32 devices in a mesh: wide: 8 (over z, core), narrow: 4 (over y, x).
Axes of the slice: x: 2, y: 2, z: 4, core: 2. Of those that a mesh axis runs over, the one named last changes fastest.
Arguments:
- latents: float32 [2, 64, 256, 16], P(None, ('wide', 'narrow')), may hold values from -6 to 6
- noise_field: float32 [2, 64, 256, 16], P(None, ('wide', 'narrow')), may hold values from -6 to 6
- labels: int32 [2, 64], P(None, ('wide', 'narrow')), may hold values from 0 to 999
- label_drop: int32 [2, 64], P(None, ('wide', 'narrow')), may hold values 0 or 1
- time_steps: int32 [2, 64], P(None, ('wide', 'narrow')), may hold values from 0 to 999
- loss_weights: float32 [2, 64], P(None, ('wide', 'narrow')), may hold values from 0.5 to 7.5, as said below
- attend_weight: float32 [768, 2304], P('narrow'), may hold values from -0.21875 to 0.21875
- attend_first: float32 [768, 2304], P('narrow'), may hold values from -9.536743e-07 to 9.536743e-07
- attend_second: float32 [768, 2304], P('narrow'), may hold values from 1.5e-16 to 2.4e-15
- attend_left: float32 [24, 32, 32], P('narrow'), may hold values from -1 to 1, as said below
- attend_right: float32 [72, 32, 32], replicated, may hold values from -1 to 1, as said below
- output_weight: float32 [768, 768], P('narrow'), may hold values from -0.625 to 0.625
- output_first: float32 [768, 768], P('narrow'), may hold values from -9.536743e-07 to 9.536743e-07
- output_second: float32 [768, 768], P('narrow'), may hold values from 1e-17 to 1.6e-16
- output_left: float32 [24, 32, 32], P('narrow'), may hold values from -1 to 1, as said below
- output_right: float32 [24, 32, 32], replicated, may hold values from -1 to 1, as said below
- expand_weight: float32 [768, 3072], P('narrow'), may hold values from -0.21875 to 0.21875
- expand_first: float32 [768, 3072], P('narrow'), may hold values from -9.536743e-07 to 9.536743e-07
- expand_second: float32 [768, 3072], P('narrow'), may hold values from 1e-17 to 1.6e-16
- expand_left: float32 [24, 32, 32], P('narrow'), may hold values from -1 to 1, as said below
- expand_right: float32 [96, 32, 32], replicated, may hold values from -1 to 1, as said below
- shrink_weight: float32 [3072, 768], P('narrow'), may hold values from -0.109375 to 0.109375
- shrink_first: float32 [3072, 768], P('narrow'), may hold values from -9.536743e-07 to 9.536743e-07
- shrink_second: float32 [3072, 768], P('narrow'), may hold values from 1e-17 to 1.6e-16
- shrink_left: float32 [96, 32, 32], P('narrow'), may hold values from -1 to 1, as said below
- shrink_right: float32 [24, 32, 32], replicated, may hold values from -1 to 1, as said below
- adaptive_weight: float32 [768, 6144], P('narrow'), may hold values from -0.21875 to 0.21875
- adaptive_first: float32 [768, 6144], P('narrow'), may hold values from -9.536743e-07 to 9.536743e-07
- adaptive_second: float32 [768, 6144], P('narrow'), may hold values from 1.5e-16 to 2.4e-15
- adaptive_left: float32 [24, 32, 32], P('narrow'), may hold values from -1 to 1, as said below
- adaptive_right: float32 [192, 32, 32], replicated, may hold values from -1 to 1, as said below
- shared_weight: float32 [1592848], P('narrow')
- shared_first: float32 [1592848], P('narrow'), may hold values from -6e-07 to 6e-07
- shared_second: float32 [1592848], P('narrow'), may hold values from 1.5e-16 to 1.2e-13
Outputs:
- attend_new: float32 [768, 2304], P('narrow')
- attend_mean: float32 [768, 2304], P('narrow')
- attend_square: float32 [768, 2304], P('narrow')
- attend_copy: bfloat16 [768, 2304], P('narrow')
- output_new: float32 [768, 768], P('narrow')
- output_mean: float32 [768, 768], P('narrow')
- output_square: float32 [768, 768], P('narrow')
- output_copy: bfloat16 [768, 768], P('narrow')
- expand_new: float32 [768, 3072], P('narrow')
- expand_mean: float32 [768, 3072], P('narrow')
- expand_square: float32 [768, 3072], P('narrow')
- expand_copy: bfloat16 [768, 3072], P('narrow')
- shrink_new: float32 [3072, 768], P('narrow')
- shrink_mean: float32 [3072, 768], P('narrow')
- shrink_square: float32 [3072, 768], P('narrow')
- shrink_copy: bfloat16 [3072, 768], P('narrow')
- adaptive_new: float32 [768, 6144], P('narrow')
- adaptive_mean: float32 [768, 6144], P('narrow')
- adaptive_square: float32 [768, 6144], P('narrow')
- adaptive_copy: bfloat16 [768, 6144], P('narrow')
- shared_new: float32 [1592848], P('narrow')
- shared_mean: float32 [1592848], P('narrow')
- shared_square: float32 [1592848], P('narrow')
- shared_copy: bfloat16 [1592848], P('narrow')
- loss_sum: float32 [], replicated
- weight_sum: float32 [], replicated
- clip_norm: float32 [], replicated
The draws below stay inside these ranges and needn't reach their ends.
Inputs may be any that keep to these rules, and one draw needn't show every extreme that they name: `loss_weights`: its scale grows from the first image to the last. `attend_left`: each block is an orthogonal matrix. `attend_right`: each block is an orthogonal matrix. `output_left`: each block is an orthogonal matrix. `output_right`: each block is an orthogonal matrix. `expand_left`: each block is an orthogonal matrix. `expand_right`: each block is an orthogonal matrix. `shrink_left`: each block is an orthogonal matrix. `shrink_right`: each block is an orthogonal matrix. `adaptive_left`: each block is an orthogonal matrix. `adaptive_right`: each block is an orthogonal matrix.
All inputs are finite; a program needn't handle non-finite values. No bound on the sum of `label_drop` on one device may be relied on, other than what follows from the above.
Results may differ from the reference program's by a relative error of at most 0.0064.
Values may be sent and summed in bfloat16 or wider, within the bound.
A program may use at most 320 MiB of HBM per device.

```python
import math
import jax
import jax.numpy as jnp
import numpy as np
from jax import lax

HEADS = 12
HEAD_DIM = 64
MLP_WIDTH = 3072
CLASSES = 1001
FREQS = 256
PATCH = 16
TIMESTEPS = 1000
BLOCK = 32
STEP_COUNT = 10
MICROBATCHES = 2
IMAGES_DEV = 2
WIDTH = 768
SEQUENCE = 256
IMAGES = 64
SHARED = 1592848
N_NARROW = 4


def householder(key, blocks):
    vector = jax.random.normal(key, (blocks, BLOCK), jnp.float32)
    scale = 2.0 / jnp.sum(vector * vector, axis=1)
    return jnp.eye(BLOCK, dtype=jnp.float32)[None] - scale[:, None, None] * vector[:, :, None] * vector[:, None, :]


def draw_attend_left(key, part):
    key = jax.random.fold_in(key, 21)
    return householder(key, WIDTH // BLOCK)


def draw_attend_right(key, part):
    key = jax.random.fold_in(key, 22)
    return householder(key, 3 * WIDTH // BLOCK)


def draw_output_left(key, part):
    key = jax.random.fold_in(key, 23)
    return householder(key, WIDTH // BLOCK)


def draw_output_right(key, part):
    key = jax.random.fold_in(key, 24)
    return householder(key, WIDTH // BLOCK)


def draw_expand_left(key, part):
    key = jax.random.fold_in(key, 25)
    return householder(key, WIDTH // BLOCK)


def draw_expand_right(key, part):
    key = jax.random.fold_in(key, 26)
    return householder(key, MLP_WIDTH // BLOCK)


def draw_shrink_left(key, part):
    key = jax.random.fold_in(key, 27)
    return householder(key, MLP_WIDTH // BLOCK)


def draw_shrink_right(key, part):
    key = jax.random.fold_in(key, 28)
    return householder(key, WIDTH // BLOCK)


def draw_adaptive_left(key, part):
    key = jax.random.fold_in(key, 29)
    return householder(key, WIDTH // BLOCK)


def draw_adaptive_right(key, part):
    key = jax.random.fold_in(key, 30)
    return householder(key, 8 * WIDTH // BLOCK)


def draw_loss_weights(key, part):
    key = jax.random.fold_in(key, 7)
    place = jnp.arange(IMAGES, dtype=jnp.float32) / max(IMAGES - 1, 1)
    rising = 1.0 + 2.0 * place
    return jax.random.uniform(key, (MICROBATCHES, IMAGES), jnp.float32, 0.5, 1.5) * rising


def draw_shared_weight(key, part):
    key = jax.random.fold_in(key, 5)
    counts = [PATCH * WIDTH, FREQS * WIDTH, WIDTH * WIDTH, CLASSES * WIDTH, WIDTH * PATCH, 13 * WIDTH + MLP_WIDTH + PATCH]
    scales = [PATCH ** (-0.5), FREQS ** (-0.5), WIDTH ** (-0.5), 0.15, WIDTH ** (-0.5), 0.1]
    spread = jnp.concatenate([jnp.full((count,), factor, jnp.float32) for count, factor in zip(counts, scales)])
    values = jax.random.normal(key, (SHARED,), jnp.float32)
    return spread * values


def draw_shared_first(key, part):
    key = jax.random.fold_in(key, 31)
    values = 6.1e-08 * jax.random.truncated_normal(key, -6.0, 6.0, (SHARED,), jnp.float32)
    return jnp.clip(values, -6e-07, 6e-07)


def draw_shared_second(key, part):
    key = jax.random.fold_in(key, 32)
    top = 2.4e-15
    level = jax.random.uniform(key, (SHARED,), jnp.float32, math.log(1.5e-16), math.log(top))
    return jnp.clip(jnp.exp(level), 1.5e-16, top)


def touch_ends(entries, stream_key, smallest, top_value):
    shape = entries.shape
    spot = [jax.random.randint(jax.random.fold_in(stream_key, axis), (), 0, shape[axis]) for axis in range(len(shape))]
    entries = entries.at[tuple(spot)].set(smallest)
    longest = shape.index(max(shape))
    spot[longest] = (spot[longest] + 1) % shape[longest]
    return entries.at[tuple(spot)].set(top_value)


def levels(key, extent, cuts, low, top_value):
    factor_of, own = 1.0, jax.random.fold_in(key, 6)
    for position, blocks in cuts:
        draws = jnp.exp(jax.random.uniform(jax.random.fold_in(own, position), (blocks,), jnp.float32, low / len(cuts), top_value / len(cuts)))
        factor_of = factor_of * jnp.repeat(draws, extent[position] // blocks).reshape([-1 if axis == position else 1 for axis in range(len(extent))])
    return factor_of


def rank_bounds(number_of, slope):
    loads = [(1 << 20) // math.isqrt(grade ** slope) + 1 for grade in range(1, number_of + 1)]
    scale = 1 + sum(loads) // (1 << 30)
    return np.cumsum(np.array([max(1, weight // scale) for weight in loads]))


def ranked(stream_key, extent, amount, skew):
    listing = rank_bounds(amount, skew)
    pick = jax.random.randint(jax.random.fold_in(stream_key, 1), extent, 0, int(listing[amount - 1]))
    standing = jnp.searchsorted(jnp.asarray(listing, jnp.int32), pick, side="right")
    return jax.random.permutation(jax.random.fold_in(stream_key, 2), amount)[standing].astype(jnp.int32)


def scatter_about(rng, extent, deviation, reach, cuts=(), held_as=jnp.bfloat16):
    values = deviation * jax.random.normal(rng, extent, jnp.float32)
    if cuts:
        values = values * levels(rng, extent, cuts, -0.22, 0.18)
    return jnp.clip(values, -reach, reach).astype(held_as)


def setup_inputs(seed: int = 0) -> dict:
    arg_keys = jax.random.split(jax.random.key(seed), 35)
    latents = scatter_about(arg_keys[0], (MICROBATCHES, IMAGES, SEQUENCE, PATCH), 1.0, 6.0, ((1, 32),), jnp.float32)
    noise_field = scatter_about(arg_keys[1], (MICROBATCHES, IMAGES, SEQUENCE, PATCH), 1.0, 6.0, ((1, 32),), jnp.float32)
    labels = touch_ends(ranked(arg_keys[2], (MICROBATCHES, IMAGES), CLASSES - 1, 2), jax.random.fold_in(arg_keys[2], 3), 0, (CLASSES - 1) - 1).astype(jnp.int32)
    label_drop = touch_ends((jax.random.randint(arg_keys[3], (MICROBATCHES, IMAGES), 0, 10) < 1).astype(jnp.int32), jax.random.fold_in(arg_keys[3], 1), 0, 1)
    time_steps = touch_ends(jax.random.randint(arg_keys[4], (MICROBATCHES, IMAGES), 0, TIMESTEPS), jax.random.fold_in(arg_keys[4], 1), 0, TIMESTEPS - 1).astype(jnp.int32)
    loss_weights = draw_loss_weights(jax.random.fold_in(arg_keys[34], 71), 0)
    attend_weight = scatter_about(arg_keys[6], (WIDTH, 3 * WIDTH), WIDTH ** -0.5, 0.21875, ((0, 4),), jnp.float32)
    attend_first = scatter_about(arg_keys[7], (WIDTH, 3 * WIDTH), (6.1e-08), 9.5367431640625e-07, ((0, 4),), jnp.float32)
    attend_second = jnp.clip(jnp.exp(math.log(2.4000000934092797e-15) - 2.7725887 * jax.random.uniform(arg_keys[8], (WIDTH, 3 * WIDTH), jnp.float32) ** levels(arg_keys[8], (WIDTH, 3 * WIDTH), ((0, 4),), -0.2, 0.2)), 1.5000000583807998e-16, 2.4000000934092797e-15)
    attend_left = draw_attend_left(jax.random.fold_in(arg_keys[34], 71), 0)
    attend_right = draw_attend_right(jax.random.fold_in(arg_keys[34], 71), 0)
    output_weight = scatter_about(arg_keys[11], (WIDTH, WIDTH), (WIDTH // 8) ** -0.5, 0.625, ((0, 4),), jnp.float32)
    output_first = scatter_about(arg_keys[12], (WIDTH, WIDTH), (6.1e-08), 9.5367431640625e-07, ((0, 4),), jnp.float32)
    output_second = jnp.clip(jnp.exp(math.log(1.5999999740402544e-16) - 2.7725887 * jax.random.uniform(arg_keys[13], (WIDTH, WIDTH), jnp.float32) ** levels(arg_keys[13], (WIDTH, WIDTH), ((0, 4),), -0.2, 0.2)), 9.99999983775159e-18, 1.5999999740402544e-16)
    output_left = draw_output_left(jax.random.fold_in(arg_keys[34], 71), 0)
    output_right = draw_output_right(jax.random.fold_in(arg_keys[34], 71), 0)
    expand_weight = scatter_about(arg_keys[16], (WIDTH, MLP_WIDTH), WIDTH ** -0.5, 0.21875, ((0, 4),), jnp.float32)
    expand_first = scatter_about(arg_keys[17], (WIDTH, MLP_WIDTH), (6.1e-08), 9.5367431640625e-07, ((0, 4),), jnp.float32)
    expand_second = jnp.clip(jnp.exp(math.log(1.5999999740402544e-16) - 2.7725887 * jax.random.uniform(arg_keys[18], (WIDTH, MLP_WIDTH), jnp.float32) ** levels(arg_keys[18], (WIDTH, MLP_WIDTH), ((0, 4),), -0.2, 0.2)), 9.99999983775159e-18, 1.5999999740402544e-16)
    expand_left = draw_expand_left(jax.random.fold_in(arg_keys[34], 71), 0)
    expand_right = draw_expand_right(jax.random.fold_in(arg_keys[34], 71), 0)
    shrink_weight = scatter_about(arg_keys[21], (MLP_WIDTH, WIDTH), MLP_WIDTH ** -0.5, 0.109375, ((0, 4),), jnp.float32)
    shrink_first = scatter_about(arg_keys[22], (MLP_WIDTH, WIDTH), (6.1e-08), 9.5367431640625e-07, ((0, 4),), jnp.float32)
    shrink_second = jnp.clip(jnp.exp(math.log(1.5999999740402544e-16) - 2.7725887 * jax.random.uniform(arg_keys[23], (MLP_WIDTH, WIDTH), jnp.float32) ** levels(arg_keys[23], (MLP_WIDTH, WIDTH), ((0, 4),), -0.2, 0.2)), 9.99999983775159e-18, 1.5999999740402544e-16)
    shrink_left = draw_shrink_left(jax.random.fold_in(arg_keys[34], 71), 0)
    shrink_right = draw_shrink_right(jax.random.fold_in(arg_keys[34], 71), 0)
    adaptive_weight = scatter_about(arg_keys[26], (WIDTH, 8 * WIDTH), WIDTH ** -0.5, 0.21875, ((0, 4),), jnp.float32)
    adaptive_first = scatter_about(arg_keys[27], (WIDTH, 8 * WIDTH), (6.1e-08), 9.5367431640625e-07, ((0, 4),), jnp.float32)
    adaptive_second = jnp.clip(jnp.exp(math.log(2.4000000934092797e-15) - 2.7725887 * jax.random.uniform(arg_keys[28], (WIDTH, 8 * WIDTH), jnp.float32) ** levels(arg_keys[28], (WIDTH, 8 * WIDTH), ((0, 4),), -0.2, 0.2)), 1.5000000583807998e-16, 2.4000000934092797e-15)
    adaptive_left = draw_adaptive_left(jax.random.fold_in(arg_keys[34], 71), 0)
    adaptive_right = draw_adaptive_right(jax.random.fold_in(arg_keys[34], 71), 0)
    shared_weight = draw_shared_weight(jax.random.fold_in(arg_keys[34], 71), 0)
    shared_first = draw_shared_first(jax.random.fold_in(arg_keys[34], 71), 0)
    shared_second = draw_shared_second(jax.random.fold_in(arg_keys[34], 71), 0)
    return dict(latents=latents, noise_field=noise_field, labels=labels, label_drop=label_drop, time_steps=time_steps, loss_weights=loss_weights, attend_weight=attend_weight, attend_first=attend_first, attend_second=attend_second, attend_left=attend_left, attend_right=attend_right, output_weight=output_weight, output_first=output_first, output_second=output_second, output_left=output_left, output_right=output_right, expand_weight=expand_weight, expand_first=expand_first, expand_second=expand_second, expand_left=expand_left, expand_right=expand_right, shrink_weight=shrink_weight, shrink_first=shrink_first, shrink_second=shrink_second, shrink_left=shrink_left, shrink_right=shrink_right, adaptive_weight=adaptive_weight, adaptive_first=adaptive_first, adaptive_second=adaptive_second, adaptive_left=adaptive_left, adaptive_right=adaptive_right, shared_weight=shared_weight, shared_first=shared_first, shared_second=shared_second)


beta_one = 0.9
beta_two = 0.999
epsilon_adam = 1e-08
learn_rate = 0.03
decay_rate = 0.01
clip_limit = 0.002
highest = lax.Precision.HIGHEST

@jax.custom_vjp
def low(v):
    return lax.optimization_barrier(v.astype(jnp.bfloat16)).astype(jnp.float32)

@jax.custom_vjp
def low_back(v):
    return v

def low_keep(v):
    return (low(v), None)

def low_pass(kept, grad):
    return (grad,)

def back_keep(v):
    return (v, None)

def back_low(kept, grad):
    return (low(grad),)
low.defvjp(low_keep, low_pass)
low_back.defvjp(back_keep, back_low)

def positions(tokens, width):
    side = math.isqrt(tokens)
    quarter = width // 4
    omega = 1.0 / 10000.0 ** (jnp.arange(quarter, dtype=jnp.float32) / quarter)
    place = jnp.arange(tokens)
    column = (place % side).astype(jnp.float32)[:, None] * omega
    row = (place // side).astype(jnp.float32)[:, None] * omega
    return jnp.concatenate([jnp.sin(column), jnp.cos(column), jnp.sin(row), jnp.cos(row)], axis=1)

def frequencies(moment, width):
    half = width // 2
    phases = jnp.exp(-math.log(10000.0) * jnp.arange(half, dtype=jnp.float32) / half)
    angles = moment[:, None] * 1000.0 * phases
    return jnp.concatenate([jnp.cos(angles), jnp.sin(angles)], axis=1)

def normalize(hidden):
    centered = hidden - lax.optimization_barrier(jnp.mean(hidden, axis=-1, keepdims=True))
    return centered * lax.rsqrt(lax.optimization_barrier(jnp.mean(centered * centered, axis=-1, keepdims=True)) + 1e-06)

def modulate(hidden, shift, scale):
    return normalize(hidden) * (1.0 + scale[:, None, :]) + shift[:, None, :]

def split_shared(shared):
    shapes = [(PATCH, WIDTH), (FREQS, WIDTH), (WIDTH, WIDTH), (CLASSES, WIDTH), (WIDTH, PATCH), (WIDTH,), (WIDTH,), (WIDTH,), (WIDTH,), (MLP_WIDTH,), (WIDTH,), (8 * WIDTH,), (PATCH,)]
    pieces = []
    start = 0
    for shape in shapes:
        count = math.prod(shape)
        pieces.append(shared[start:start + count].reshape(shape))
        start = start + count
    return pieces

def rotate(grad, left, right):
    rows, cols = grad.shape
    size = left.shape[1]
    blocks = grad.reshape(rows // size, size, cols // size, size)
    turned = jnp.einsum('iab,iajd->ibjd', left, blocks, precision=highest)
    turned = jnp.einsum('ibjc,jcd->ibjd', turned, right, precision=highest)
    return turned.reshape(rows, cols)

def unrotate(step, left, right):
    rows, cols = step.shape
    size = left.shape[1]
    blocks = step.reshape(rows // size, size, cols // size, size)
    turned = jnp.einsum('iab,ibjd->iajd', left, blocks, precision=highest)
    turned = jnp.einsum('iajd,jcd->iajc', turned, right, precision=highest)
    return turned.reshape(rows, cols)

def adam_direction(first, second):
    return first / (1.0 - beta_one ** STEP_COUNT) / (jnp.sqrt(second / (1.0 - beta_two ** STEP_COUNT)) + epsilon_adam)

def rotated_update(weight, first, second, grad, left, right):
    turned = rotate(grad, left, right)
    first = beta_one * first + (1.0 - beta_one) * turned
    second = beta_two * second + (1.0 - beta_two) * turned * turned
    weight = weight - learn_rate * (unrotate(adam_direction(first, second), left, right) + decay_rate * weight)
    return (weight, first, second)

def plain_update(weight, first, second, grad):
    first = beta_one * first + (1.0 - beta_one) * grad
    second = beta_two * second + (1.0 - beta_two) * grad * grad
    weight = weight - learn_rate * (adam_direction(first, second) + decay_rate * weight)
    return (weight, first, second)

def dense(inputs, weight):
    return jnp.einsum('...i,ij->...j', inputs, weight, precision=highest)

def group_loss(params, group):
    attend_w, output_w, expand_w, shrink_w, adaptive_w, shared = params
    pieces = split_shared(shared)
    latent, noisy, label, dropped, steps, weights = group
    moment = (steps.astype(jnp.float32) + 0.5) / TIMESTEPS
    chosen = jnp.where(dropped == 1, CLASSES - 1, label)
    weight_t = moment[:, None, None]
    blended = low((1.0 - weight_t) * latent + weight_t * noisy)
    target = noisy - latent
    images, tokens = (latent.shape[0], latent.shape[1])
    hidden = low_back(dense(blended, pieces[0]) + pieces[5]) + positions(tokens, WIDTH)
    time_pre = low_back(dense(low(frequencies(moment, FREQS)), pieces[1]) + pieces[6])
    condition = low_back(dense(low(jax.nn.silu(time_pre)), pieces[2]) + pieces[7]) + pieces[3][chosen]
    mods = low_back(dense(low(jax.nn.silu(condition)), adaptive_w) + pieces[11])
    spans = jnp.split(mods, 8, axis=1)
    normed = low(modulate(hidden, spans[0], spans[1]))
    triple = low(low_back(dense(normed, attend_w))).reshape(images, tokens, 3, HEADS, HEAD_DIM)
    query, keys, values = (triple[:, :, 0], triple[:, :, 1], triple[:, :, 2])
    scores = low_back(jnp.einsum('bqhd,bkhd->bhqk', query, keys, precision=highest) * HEAD_DIM ** (-0.5))
    probs = low(jax.nn.softmax(scores, axis=-1))
    attended = jnp.einsum('bhqk,bkhd->bqhd', probs, values, precision=highest)
    attended = low(low_back(attended)).reshape(images, tokens, WIDTH)
    branch = low_back(dense(attended, output_w) + pieces[8])
    middle = hidden + spans[2][:, None, :] * branch
    normed_two = low(modulate(middle, spans[3], spans[4]))
    expand_pre = low_back(dense(normed_two, expand_w) + pieces[9])
    branch_two = low_back(dense(low(jax.nn.gelu(expand_pre, approximate=True)), shrink_w) + pieces[10])
    upper = middle + spans[5][:, None, :] * branch_two
    final = low(modulate(upper, spans[6], spans[7]))
    output = low_back(dense(final, pieces[4]) + pieces[12])
    mismatch = output - target
    return jnp.sum(weights * lax.optimization_barrier(jnp.mean(mismatch * mismatch, axis=(1, 2))))

def reference(latents, noise_field, labels, label_drop, time_steps, loss_weights, attend_weight, attend_first, attend_second, attend_left, attend_right, output_weight, output_first, output_second, output_left, output_right, expand_weight, expand_first, expand_second, expand_left, expand_right, shrink_weight, shrink_first, shrink_second, shrink_left, shrink_right, adaptive_weight, adaptive_first, adaptive_second, adaptive_left, adaptive_right, shared_weight, shared_first, shared_second):
    matrices = (attend_weight, output_weight, expand_weight, shrink_weight, adaptive_weight)
    params = matrices + (shared_weight,)
    group_size = IMAGES_DEV * N_NARROW
    data = (latents, noise_field, labels, label_drop, time_steps, loss_weights)
    grouped = tuple((array.reshape((MICROBATCHES * IMAGES // group_size, group_size) + array.shape[2:]) for array in data))

    def total(weights):
        lowered = tuple((low(weight) for weight in weights))

        def accumulate(carry, group):
            return (carry + group_loss(lowered, group), None)
        summed, unused = lax.scan(jax.checkpoint(accumulate), jnp.zeros((), loss_weights.dtype), grouped)
        return summed
    loss_sum, pullback = jax.vjp(total, params)
    weight_sum = jnp.sum(loss_weights)
    grads = pullback(jnp.ones_like(loss_sum) / weight_sum)[0]
    clip_norm = jnp.sqrt(sum((jnp.sum(gradient * gradient) for gradient in grads)))
    factor = clip_limit / jnp.maximum(clip_norm, clip_limit)
    states = ((attend_first, attend_second, attend_left, attend_right), (output_first, output_second, output_left, output_right), (expand_first, expand_second, expand_left, expand_right), (shrink_first, shrink_second, shrink_left, shrink_right), (adaptive_first, adaptive_second, adaptive_left, adaptive_right))
    results = []
    for number in range(5):
        first, second, left, right = states[number]
        fresh = rotated_update(matrices[number], first, second, grads[number] * factor, left, right)
        results += [fresh[0], fresh[1], fresh[2], fresh[0].astype(jnp.bfloat16)]
    fresh = plain_update(shared_weight, shared_first, shared_second, grads[5] * factor)
    results += [fresh[0], fresh[1], fresh[2], fresh[0].astype(jnp.bfloat16)]
    return (results[0], results[1], results[2], results[3], results[4], results[5], results[6], results[7], results[8], results[9], results[10], results[11], results[12], results[13], results[14], results[15], results[16], results[17], results[18], results[19], results[20], results[21], results[22], results[23], loss_sum, weight_sum, clip_norm)
```

```python
from functools import partial
import math

import jax
import jax.numpy as jnp
import numpy as np
from jax import lax
from jax.experimental import pallas as pl
from jax.experimental.pallas import tpu as pltpu
from jax.sharding import PartitionSpec as P

HEADS = 12
HEAD_DIM = 64
MLP_WIDTH = 3072
CLASSES = 1001
FREQS = 256
PATCH = 16
TIMESTEPS = 1000
BLOCK = 32
STEP_COUNT = 10
WIDTH = 768
SEQUENCE = 256


beta_one = 0.9
beta_two = 0.999
epsilon_adam = 1e-08
learn_rate = 0.03
decay_rate = 0.01
clip_limit = 0.002
highest = lax.Precision.HIGHEST
bf16 = jnp.bfloat16
f32 = jnp.float32

ROW_PATCH = 0
ROW_TIME_ONE = 16
ROW_TIME_TWO = 272
ROW_TABLE = 1040
ROW_FINAL = 2041
ROW_BIAS = 2057


def positions(tokens, width):
    side = math.isqrt(tokens)
    quarter = width // 4
    omega = 1.0 / 10000.0 ** (np.arange(quarter, dtype=np.float64) / quarter)
    place = np.arange(tokens)
    column = (place % side)[:, None] * omega
    row = (place // side)[:, None] * omega
    table = np.concatenate([np.sin(column), np.cos(column), np.sin(row), np.cos(row)], axis=1)
    return jnp.asarray(table.astype(np.float32))


def frequencies(moment, width):
    half = width // 2
    phases = jnp.exp(-math.log(10000.0) * jnp.arange(half, dtype=jnp.float32) / half)
    angles = moment[:, None] * 1000.0 * phases
    return jnp.concatenate([jnp.cos(angles), jnp.sin(angles)], axis=1)


def normalize(hidden):
    centered = hidden - jnp.mean(hidden, axis=-1, keepdims=True)
    return centered * lax.rsqrt(jnp.mean(centered * centered, axis=-1, keepdims=True) + 1e-06)


def modulate(hidden, shift, scale):
    return normalize(hidden) * (1.0 + scale[:, None, :]) + shift[:, None, :]


def adam_direction(first, second):
    return (
        first
        / (1.0 - beta_one**STEP_COUNT)
        / (jnp.sqrt(second / (1.0 - beta_two**STEP_COUNT)) + epsilon_adam)
    )


def plain_update(weight, first, second, grad):
    first = beta_one * first + (1.0 - beta_one) * grad
    second = beta_two * second + (1.0 - beta_two) * grad * grad
    weight = weight - learn_rate * (adam_direction(first, second) + decay_rate * weight)
    return (weight, first, second)


def rounded(value):
    return value.astype(jnp.bfloat16)


def product(inputs, weight):
    return jnp.dot(inputs, weight, preferred_element_type=jnp.float32)


def backprod(gradient, weight):
    return jnp.einsum("...n,kn->...k", gradient, weight, preferred_element_type=jnp.float32)


def weight_grad(inputs, gradient):
    flat_in = inputs.reshape(-1, inputs.shape[-1])
    flat_grad = gradient.reshape(-1, gradient.shape[-1])
    return lax.dot_general(
        flat_in, flat_grad, (((0,), (0,)), ((), ())), preferred_element_type=jnp.float32
    )


def bias_grad(gradient):
    return jnp.sum(gradient.astype(jnp.float32).reshape(-1, gradient.shape[-1]), axis=0)


def halves(value):
    high = value.astype(bf16)
    return high, (value - high.astype(f32)).astype(bf16)


def spread_blocks(blocks):
    count = blocks.shape[0]
    size = count * BLOCK
    high, low = halves(blocks.reshape(size, BLOCK))
    place = lax.broadcasted_iota(jnp.int32, (BLOCK, size), 0)
    column = lax.broadcasted_iota(jnp.int32, (BLOCK, size), 1)
    repeat = (place == column % BLOCK).astype(bf16)
    row_block = lax.broadcasted_iota(jnp.int32, (size, size), 0) // BLOCK
    col_block = lax.broadcasted_iota(jnp.int32, (size, size), 1) // BLOCK
    inside = row_block == col_block
    high = jnp.dot(high, repeat, preferred_element_type=f32)
    low = jnp.dot(low, repeat, preferred_element_type=f32)
    return jnp.where(inside, high, 0.0), jnp.where(inside, low, 0.0)


def dot(left, right):
    return jnp.dot(left, right, preferred_element_type=f32)


def dot_t(left, right):
    return lax.dot_general(left, right, (((1,), (1,)), ((), ())), preferred_element_type=f32)


def adam_kernel(
    factor_ref,
    weight_ref,
    first_ref,
    second_ref,
    grad_ref,
    left_ref,
    right_ref,
    new_ref,
    mean_ref,
    square_ref,
    copy_ref,
    left_high,
    turn_high,
    turn_low,
):
    @pl.when(pl.program_id(1) == 0)
    def _():
        high, low = spread_blocks(left_ref[...])
        left_high[...] = high.astype(bf16)
        turn_high[...] = high.T.astype(bf16)
        turn_low[...] = low.T.astype(bf16)

    factor = factor_ref[0]
    chunk = 256
    for start in range(0, weight_ref.shape[1], chunk):
        span = pl.ds(start, chunk)
        right_high, right_low = spread_blocks(
            right_ref[start // BLOCK : (start + chunk) // BLOCK]
        )
        right_high = right_high.astype(bf16)
        right_low = right_low.astype(bf16)
        if grad_ref.dtype == bf16:
            grad = grad_ref[:, span]
            turned = dot(grad, right_high) + dot(grad, right_low)
        else:
            grad_high, grad_low = halves(grad_ref[:, span])
            turned = dot(grad_high, right_high) + (
                dot(grad_high, right_low) + dot(grad_low, right_high)
            )
        high, low = halves(turned)
        turned = dot(turn_high[...], high) + (
            dot(turn_low[...], high) + dot(turn_high[...], low)
        )
        turned = turned * factor
        first = beta_one * first_ref[:, span] + (1.0 - beta_one) * turned
        second = beta_two * second_ref[:, span] + (1.0 - beta_two) * turned * turned
        mean_ref[:, span] = first
        square_ref[:, span] = second
        step = adam_direction(first, second)
        step = dot_t(step.astype(bf16), right_high)
        step = dot(left_high[...], step.astype(bf16))
        weight = weight_ref[:, span]
        weight = weight - learn_rate * (step + decay_rate * weight)
        new_ref[:, span] = weight
        copy_ref[:, span] = weight.astype(bf16)


def rotated_update(weight, first, second, grad, base, left, right, factor, tile_rows):
    rows, cols = weight.shape
    tile_cols = WIDTH
    tile = pl.BlockSpec((tile_rows, tile_cols), lambda i, j: (i, j))
    if base is None:
        grad_tile = tile
    else:
        across = cols // tile_cols
        grad_tile = pl.BlockSpec(
            (tile_rows, tile_cols), lambda i, j: (base + i * across + j, 0)
        )
    return pl.pallas_call(
        adam_kernel,
        grid=(rows // tile_rows, cols // tile_cols),
        in_specs=[
            pl.BlockSpec(memory_space=pltpu.SMEM),
            tile,
            tile,
            tile,
            grad_tile,
            pl.BlockSpec((tile_rows // BLOCK, BLOCK, BLOCK), lambda i, j: (i, 0, 0)),
            pl.BlockSpec((tile_cols // BLOCK, BLOCK, BLOCK), lambda i, j: (j, 0, 0)),
        ],
        out_specs=[tile] * 4,
        out_shape=[jax.ShapeDtypeStruct((rows, cols), f32)] * 3
        + [jax.ShapeDtypeStruct((rows, cols), bf16)],
        scratch_shapes=[pltpu.VMEM((tile_rows, tile_rows), bf16)] * 3,
        compiler_params=pltpu.CompilerParams(vmem_limit_bytes=48 * 1024 * 1024),
        name="rotated_adam",
    )(factor.reshape(1), weight, first, second, grad, left, right)


def bits_of(extent):
    return extent.bit_length() - 1


def flipped(index, mask, count):
    for bit in range(count):
        if mask >> bit & 1:
            index = index + (1 - 2 * (index // (1 << bit) % 2)) * (1 << bit)
    return index


def greet(n_wide, n_narrow):
    barrier = pltpu.get_barrier_semaphore()
    count = 0
    for axis, extent in (("narrow", n_narrow), ("wide", n_wide)):
        me = lax.axis_index(axis)
        for bit in range(bits_of(extent)):
            pl.semaphore_signal(
                barrier,
                inc=1,
                device_id={axis: flipped(me, 1 << bit, bits_of(extent))},
                device_id_type=pl.DeviceIdType.MESH,
            )
            count = count + 1
    pl.semaphore_wait(barrier, count)


def remote(source, target, send_sem, recv_sem, axis, peer):
    return pltpu.make_async_remote_copy(
        src_ref=source,
        dst_ref=target,
        send_sem=send_sem,
        recv_sem=recv_sem,
        device_id={axis: peer},
        device_id_type=pl.DeviceIdType.MESH,
    )


def route(path, step, count):
    return (step + path) % count


ROW_TAIL = 2048
TAIL = 32
ALIGN = 16
SHEET = 384


def shard_rows(shard):
    rows = (shard + WIDTH - 2) // WIDTH + 1 + ALIGN
    return -(-rows // 32) * 32


def shard_start(number, shard):
    return number * shard // WIDTH // ALIGN * ALIGN


def flat_rows(n_narrow, shard):
    last = shard_start(n_narrow - 1, shard) + shard_rows(shard)
    return max(-(-last // ALIGN) * ALIGN, 2112)


def silu_slope(value):
    gate = jax.nn.sigmoid(value)
    return gate * (1.0 + value * (1.0 - gate))


def own_columns(value, n_narrow):
    here = lax.axis_index("narrow")
    width = value.shape[1] // n_narrow
    result = value[:, :width]
    for number in range(1, n_narrow):
        result = jnp.where(
            here == number, value[:, number * width : (number + 1) * width], result
        )
    return result


def gather_kernel(n_wide, n_narrow, images, shard, *refs):
    count = 5
    shards = refs[:count]
    adaptive_ref, info_ref = refs[count : count + 2]
    outs = refs[count + 2 : count + 14]
    flat, sheet, time_pre, condition, own_act, adaptive_low, mods_ref, total_ref = outs[4:12]
    scratch = refs[count + 14 :]
    gathered = scratch[0]
    wides = scratch[1 : count + 1]
    lows = scratch[count + 1 : 2 * count + 1]
    (
        adaptive_wide,
        info_all,
        lined,
        part,
        part_in,
        load_sem,
        keep_sem,
        send_sem,
        recv_sem,
        core_send,
        core_recv,
        info_sem,
        info_send,
        info_recv,
        part_send,
        part_recv,
    ) = scratch[2 * count + 1 :]
    fulls = (gathered,) + tuple(outs[:4])
    here = lax.axis_index("narrow")
    there = lax.axis_index("wide")
    core = there % 2
    n_bits = bits_of(n_narrow)
    w_bits = bits_of(n_wide)
    sibling = flipped(there, 1, w_bits)

    loads = [
        pltpu.make_async_copy(shards[number], wides[number], load_sem.at[number])
        for number in range(count)
    ]
    loads.append(pltpu.make_async_copy(adaptive_ref, adaptive_wide, load_sem.at[count]))
    for load in loads:
        load.start()
    slot = there * n_narrow + here
    info_own = pltpu.make_async_copy(info_ref, info_all.at[pl.ds(slot, 1)], info_sem)
    info_own.start()
    greet(n_wide, n_narrow)
    sends = []

    def region(number, owner, half, path):
        rows, cols = shards[number].shape
        return (
            pl.ds(pl.multiple_of(owner * rows + half * (rows // 2), 16), rows // 2),
            pl.ds(path * (cols // 2), cols // 2),
        )

    def narrow_step(number, step):
        for path in range(2):
            bit = route(path, step, n_bits)
            peer = flipped(here, 1 << bit, n_bits)
            done = sum(1 << route(path, earlier, n_bits) for earlier in range(step))
            for mask in range(n_narrow):
                if mask & ~done:
                    continue
                place = region(number, flipped(here, mask, n_bits), core, path)
                arrives = mask | 1 << bit
                if mask == 0:
                    rows, cols = shards[number].shape
                    source = lows[number].at[
                        pl.ds(pl.multiple_of(core * (rows // 2), 16), rows // 2),
                        pl.ds(path * (cols // 2), cols // 2),
                    ]
                else:
                    source = fulls[number].at[place]
                copy = remote(
                    source,
                    fulls[number].at[place],
                    send_sem.at[number, path, arrives - 1],
                    recv_sem.at[number, path, arrives - 1],
                    "narrow",
                    peer,
                )
                copy.start()
                sends.append(copy)

    def arrive(number, step):
        for path in range(2):
            bit = route(path, step, n_bits)
            done = sum(1 << route(path, earlier, n_bits) for earlier in range(step))
            for mask in range(n_narrow):
                if mask & ~done:
                    continue
                arrived = mask | 1 << bit
                place = region(number, flipped(here, arrived, n_bits), core, path)
                remote(
                    fulls[number].at[place],
                    fulls[number].at[place],
                    send_sem.at[number, path, arrived - 1],
                    recv_sem.at[number, path, arrived - 1],
                    "narrow",
                    flipped(here, 1 << bit, n_bits),
                ).wait_recv()
                copy = remote(
                    fulls[number].at[place],
                    fulls[number].at[place],
                    core_send.at[number, path, arrived - 1],
                    core_recv.at[number, path, arrived - 1],
                    "wide",
                    sibling,
                )
                copy.start()
                sends.append(copy)

    def from_sibling(number):
        for path in range(2):
            for mask in range(1, n_narrow):
                place = region(number, flipped(here, mask, n_bits), 1 - core, path)
                remote(
                    fulls[number].at[place],
                    fulls[number].at[place],
                    core_send.at[number, path, mask - 1],
                    core_recv.at[number, path, mask - 1],
                    "wide",
                    sibling,
                ).wait_recv()

    def cast_rows(source, target):
        def cast(index, carry):
            span = pl.ds(pl.multiple_of(index * 16, 16), 16)
            target[span, :] = source[span, :].astype(bf16)
            return carry

        lax.fori_loop(0, source.shape[0] // 16, cast, 0)

    keeps = []

    def begin(number):
        loads[number].wait()
        rows = shards[number].shape[0]
        cast_rows(wides[number], lows[number])
        keep = pltpu.make_async_copy(
            lows[number],
            fulls[number].at[pl.ds(pl.multiple_of(here * rows, 16), rows)],
            keep_sem.at[number],
        )
        keep.start()
        keeps.append(keep)
        narrow_step(number, 0)

    places = [("narrow", bit, n_bits) for bit in range(n_bits)]
    places += [("wide", bit, w_bits) for bit in range(w_bits)]

    def info_copy(position):
        axis, bit, bits = places[position]
        width = 1 << position
        base = slot // width * width
        return remote(
            info_all.at[pl.ds(base, width)],
            info_all.at[pl.ds(base, width)],
            info_send.at[position],
            info_recv.at[position],
            axis,
            flipped(lax.axis_index(axis), 1 << bit, bits),
        )

    info_own.wait()
    info_copy(0).start()
    begin(0)
    for position in range(len(places)):
        info_copy(position).wait()
        if position + 1 < len(places):
            info_copy(position + 1).start()
    begin(1)
    for step in range(n_bits):
        arrive(0, step)
        if step + 1 < n_bits:
            narrow_step(0, step + 1)
    for number in range(2, count):
        begin(number)
    from_sibling(0)
    keeps[0].wait()

    height = shards[0].shape[0]
    reached = 0
    for number in range(n_narrow):
        start = shard_start(number, shard)
        overlap = max(reached - start, 0)
        block = number * height
        if overlap:
            flat[start:reached, :] = (
                flat[start:reached, :].astype(f32)
                + gathered[block : block + overlap, :].astype(f32)
            ).astype(bf16)
        flat[start + overlap : start + height, :] = gathered[block + overlap : block + height, :]
        reached = start + height
    if reached < flat.shape[0]:
        flat[reached:, :] = jnp.zeros((flat.shape[0] - reached, WIDTH), bf16)

    devices = n_wide * n_narrow
    for number in range(devices):
        sheet[number * images : (number + 1) * images, :] = info_all[number, :images, :]
    weights = sheet[:, FREQS + 1 : FREQS + 2]
    total_ref[...] = jnp.sum(weights, axis=0, keepdims=True)
    tail = flat[ROW_TAIL : ROW_TAIL + TAIL, :].astype(f32)
    tail_row = ROW_BIAS - ROW_TAIL
    value = dot(sheet[:, :FREQS].astype(bf16), flat[ROW_TIME_ONE:ROW_TIME_TWO, :])
    value = value + tail[tail_row + 1 : tail_row + 2]
    time_pre[...] = value
    act = jax.nn.silu(value).astype(bf16)
    value = dot(act, flat[ROW_TIME_TWO:ROW_TABLE, :]) + tail[tail_row + 2 : tail_row + 3]
    labels = lax.broadcasted_iota(jnp.int32, (sheet.shape[0], 1008), 1).astype(f32)
    pick = jnp.where(sheet[:, FREQS : FREQS + 1] == labels, 1.0, 0.0).astype(bf16)
    value = value + dot(pick, flat[ROW_TABLE : ROW_TABLE + 1008, :])
    condition[...] = value
    act = own_columns(jax.nn.silu(value), n_narrow)
    own_act[...] = act.astype(bf16)
    lined[...] = act

    loads[count].wait()
    cast_rows(adaptive_wide, adaptive_low)
    group = n_narrow * images
    near = lined[pl.ds(pl.multiple_of(there * group, 8), group), :]
    blocks = []
    for number in range(n_narrow):
        blocks.append(near[number * images : (number + 1) * images])
        blocks.append(jnp.zeros((8 - images, near.shape[1]), f32))
    near = jnp.concatenate(blocks, axis=0).astype(bf16)
    for index in range(8):
        span = slice(index * WIDTH, (index + 1) * WIDTH)
        value = dot(near, adaptive_low[:, span])
        for number in range(n_narrow):
            part[0, number, :, span] = value[8 * number : 8 * number + 8]

    def part_copy(step, mask):
        bit = 1 << step
        return remote(
            part.at[step, flipped(here, mask, n_bits)],
            part_in.at[step, flipped(here, mask, n_bits)],
            part_send.at[step, mask],
            part_recv.at[step, mask],
            "narrow",
            flipped(here, bit, n_bits),
        )

    def part_back(step, mask):
        bit = 1 << step
        owner = flipped(here, mask - bit, n_bits)
        return remote(
            part_in.at[step, owner],
            part_in.at[step, owner],
            part_send.at[step, mask],
            part_recv.at[step, mask],
            "narrow",
            flipped(here, bit, n_bits),
        ), owner

    for step in range(n_bits):
        bit = 1 << step
        masks = [
            mask for mask in range(n_narrow) if mask & bit and not mask & (bit - 1)
        ]
        for mask in masks:
            copy = part_copy(step, mask)
            copy.start()
            sends.append(copy)
        for mask in masks:
            back, owner = part_back(step, mask)
            back.wait_recv()
            if step + 1 < n_bits:
                part[step + 1, owner] = part[step, owner] + part_in[step, owner]
            else:
                value = part[step, owner] + part_in[step, owner]
                for image in range(images):
                    for index in range(8):
                        mods_ref[image, index : index + 1, :] = (
                            value[image : image + 1, index * WIDTH : (index + 1) * WIDTH]
                            + tail[tail_row + 9 + index : tail_row + 10 + index]
                        )

    for step in range(n_bits):
        for number in range(1, count):
            arrive(number, step)
            if step + 1 < n_bits:
                narrow_step(number, step + 1)
    for number in range(1, count):
        from_sibling(number)
    for keep in keeps[1:]:
        keep.wait()
    for copy in sends:
        copy.wait_send()


def gather_all(n_wide, n_narrow, images, shard, shards, adaptive, info):
    count = len(shards)
    any_space = pl.BlockSpec(memory_space=pl.ANY)
    vmem = pl.BlockSpec(memory_space=pltpu.VMEM)
    devices = n_wide * n_narrow
    n_bits = bits_of(n_narrow)
    rows = adaptive.shape[0]
    dma = pltpu.SemaphoreType.DMA
    total = devices * images
    return pl.pallas_call(
        partial(gather_kernel, n_wide, n_narrow, images, shard),
        in_specs=[any_space] * (count + 2),
        out_specs=[any_space] * (count - 1) + [vmem] * 8,
        out_shape=[
            jax.ShapeDtypeStruct((piece.shape[0] * n_narrow, piece.shape[1]), bf16)
            for piece in shards[1:]
        ]
        + [
            jax.ShapeDtypeStruct((flat_rows(n_narrow, shard), WIDTH), bf16),
            jax.ShapeDtypeStruct((total, SHEET), f32),
            jax.ShapeDtypeStruct((total, WIDTH), f32),
            jax.ShapeDtypeStruct((total, WIDTH), f32),
            jax.ShapeDtypeStruct((total, rows), bf16),
            jax.ShapeDtypeStruct(adaptive.shape, bf16),
            jax.ShapeDtypeStruct((images, 8, WIDTH), f32),
            jax.ShapeDtypeStruct((1, 1), f32),
        ],
        scratch_shapes=[pltpu.VMEM((shards[0].shape[0] * n_narrow, WIDTH), bf16)]
        + [pltpu.VMEM(piece.shape, f32) for piece in shards]
        + [pltpu.VMEM(piece.shape, bf16) for piece in shards]
        + [
            pltpu.VMEM(adaptive.shape, f32),
            pltpu.VMEM((devices,) + info.shape[1:], f32),
            pltpu.VMEM((total, rows), f32),
            pltpu.VMEM((n_bits, n_narrow, 8, 8 * WIDTH), f32),
            pltpu.VMEM((n_bits, n_narrow, 8, 8 * WIDTH), f32),
            dma((count + 1,)),
            dma((count,)),
            dma((count, 2, n_narrow - 1)),
            dma((count, 2, n_narrow - 1)),
            dma((count, 2, n_narrow - 1)),
            dma((count, 2, n_narrow - 1)),
            dma,
            dma((bits_of(devices),)),
            dma((bits_of(devices),)),
            dma((n_bits, n_narrow)),
            dma((n_bits, n_narrow)),
        ],
        compiler_params=pltpu.CompilerParams(
            collective_id=0, has_side_effects=True, vmem_limit_bytes=56 * 1024 * 1024
        ),
        name="gather_weights",
    )(*shards, adaptive, info)


RING = 4


def reduce_kernel(n_wide, n_narrow, images, shard, *refs):
    grad_refs = refs[:4]
    (
        g_mods_ref,
        g_patch_ref,
        g_final_ref,
        g_bias_ref,
        adaptive_low,
        sheet,
        time_pre,
        condition,
        own_act,
        time_two,
    ) = refs[4:14]
    out_ref, adaptive_out, rows_out, window_out, totals_out, clip_out = refs[14:20]
    scratch = refs[20:]
    own, from_core, to_near, from_near, to_far, from_far, acc, acc_far = scratch[:8]
    load_sem, core_sem, near_sem, far_sem, back_sem, last_sem = scratch[8:14]
    (
        mods_all,
        small_out,
        small_in,
        act_all,
        stage,
        norm_out,
        norm_in,
        squares,
        mods_sem,
        small_sem,
        act_sem,
        rows_sem,
        norm_sem,
    ) = scratch[14:]
    here = lax.axis_index("narrow")
    there = lax.axis_index("wide")
    core = there % 2
    n_bits = bits_of(n_narrow)
    w_bits = bits_of(n_wide)
    far_steps = w_bits - 1
    sibling = flipped(there, 1, w_bits)
    chunks, _, half, width = out_ref.shape
    side = width // 2

    leaving = []
    for path in range(2):
        done = 0
        place = 0
        steps = []
        for step in range(n_bits):
            bit = 1 << route(path, step, n_bits)
            masks = [mask for mask in range(n_narrow) if mask & bit and not mask & done]
            steps.append((bit, {mask: place + spot for spot, mask in enumerate(masks)}))
            place = place + len(masks)
            done = done | bit
        leaving.append(steps)

    parts = [(0, half, 0, width)]
    gives = []
    for step in range(far_steps):
        low, rows, left, cols = parts[-1]
        mine = there // (2 << step) % 2
        if rows % 32 == 0:
            keep = (low + mine * (rows // 2), rows // 2, left, cols)
            give = (low + (1 - mine) * (rows // 2), rows // 2, left, cols)
        elif cols % 256 == 0:
            keep = (low, rows, left + mine * (cols // 2), cols // 2)
            give = (low, rows, left + (1 - mine) * (cols // 2), cols // 2)
        else:
            keep = parts[-1]
            give = parts[-1]
        parts.append(keep)
        gives.append(give)
    traded = [gives[step] is not parts[step] for step in range(far_steps)]

    def window(part):
        low, rows, left, cols = part
        if not isinstance(low, int):
            low = pl.multiple_of(low, 16)
        if not isinstance(left, int):
            left = pl.multiple_of(left, 128)
        return (pl.ds(low, rows), pl.ds(left, cols))

    def keep_copy(k, grad_ref, first):
        start = pl.multiple_of((k - first) * 2 * half + core * half, 16)
        return pltpu.make_async_copy(
            grad_ref.at[:, pl.ds(start, half), :], own.at[k % RING], load_sem.at[k]
        )

    def start_keep(k):
        first = 0
        for grad_ref in grad_refs:
            tiles = grad_ref.shape[1] // (2 * half)

            @pl.when(jnp.logical_and(k >= first, k < first + tiles))
            def _(grad_ref=grad_ref, first=first):
                keep_copy(k, grad_ref, first).start()

            first = first + tiles

    def give_copy(k, grad_ref, first):
        start = pl.multiple_of((k - first) * 2 * half + (1 - core) * half, 16)
        return remote(
            grad_ref.at[:, pl.ds(start, half), :],
            from_core.at[k],
            core_sem.at[0, k],
            core_sem.at[1, k],
            "wide",
            sibling,
        )

    def near_copy(path, k, step):
        bit, masks = leaving[path][step]
        spots = pl.ds(min(masks.values()), len(masks))
        return remote(
            to_near.at[path, k, spots],
            from_near.at[path, k, spots],
            near_sem.at[0, path, k, step],
            near_sem.at[1, path, k, step],
            "narrow",
            flipped(here, bit, n_bits),
        )

    def far_copy(k, step, part):
        return remote(
            to_far.at[(k, step) + window(part)],
            from_far.at[(k, step) + window(part)],
            far_sem.at[0, k, step],
            far_sem.at[1, k, step],
            "wide",
            flipped(there, 2 << step, w_bits),
        )

    def back_copy(k, step, part):
        place = (k, core) + window(part)
        return remote(
            out_ref.at[place],
            out_ref.at[place],
            back_sem.at[0, k, step],
            back_sem.at[1, k, step],
            "wide",
            flipped(there, 2 << step, w_bits),
        )

    def last_copy(k, side_of):
        return remote(
            out_ref.at[k, side_of],
            out_ref.at[k, side_of],
            last_sem.at[0, k],
            last_sem.at[1, k],
            "wide",
            sibling,
        )

    def place_near(path, k, step, mask, total):
        columns = pl.ds(path * side, side)
        ring = k % RING
        if step == n_bits:
            acc_far[ring, :, columns] = total
        elif mask in leaving[path][step][1]:
            to_near[path, k, leaving[path][step][1][mask]] = total.astype(bf16)
        else:
            acc[ring, mask, :, columns] = total

    def stage_core(k):
        keep_copy(k, grad_refs[0], k).wait()
        give_copy(k, grad_refs[0], k).wait_recv()
        for path in range(2):
            columns = pl.ds(path * side, side)
            for mask in range(n_narrow):
                owner = flipped(here, mask, n_bits)
                total = own[k % RING, owner, :, columns].astype(f32) + from_core[
                    k, owner, :, columns
                ].astype(f32)
                place_near(path, k, 0, mask, total)
            near_copy(path, k, 0).start()
        start_keep(k + RING - 1)

    def stage_near(step, k):
        ring = k % RING
        for path in range(2):
            columns = pl.ds(path * side, side)
            near_copy(path, k, step).wait_recv()
            bit, masks = leaving[path][step]
            for mask, spot in masks.items():
                total = acc[ring, mask - bit, :, columns] + from_near[path, k, spot].astype(f32)
                place_near(path, k, step + 1, mask - bit, total)
            if step + 1 < n_bits:
                near_copy(path, k, step + 1).start()
        if step + 1 == n_bits:
            start_far(0, k)

    def start_far(step, k):
        ring = k % RING
        if step < far_steps:
            place = window(gives[step])
            to_far[(k, step) + place] = acc_far[(ring,) + place].astype(bf16)
            far_copy(k, step, gives[step]).start()
        else:
            place = window(parts[step])
            out_ref[(k, core) + place] = acc_far[(ring,) + place].astype(bf16)
            start_back(far_steps - 1, k)

    def stage_far(step, k):
        ring = k % RING
        far_copy(k, step, parts[step + 1]).wait_recv()
        place = window(parts[step + 1])
        if traded[step]:
            mine = acc_far[(ring,) + place]
        else:
            mine = to_far[(k, step) + place].astype(f32)
        acc_far[(ring,) + place] = mine + from_far[(k, step) + place].astype(f32)
        start_far(step + 1, k)

    def start_back(step, k):
        while step >= 0 and not traded[step]:
            step = step - 1
        if step >= 0:
            back_copy(k, step, parts[step + 1]).start()
        else:
            last_copy(k, core).start()

    def stage_back(step, k):
        back_copy(k, step, gives[step]).wait_recv()
        start_back(step - 1, k)

    def add_squares(value):
        squares[...] += jnp.sum(value * value, axis=0, keepdims=True)

    def stage_last(k):
        last_copy(k, 1 - core).wait_recv()
        for number in range(2):
            add_squares(out_ref[k, number].astype(f32))

    stages = [stage_core]
    stages += [partial(stage_near, step) for step in range(n_bits)]
    stages += [partial(stage_far, step) for step in range(far_steps)]
    stages += [partial(stage_back, step) for step in reversed(range(far_steps)) if traded[step]]
    stages += [stage_last]

    places = [("narrow", bit, n_bits) for bit in range(n_bits)]
    places += [("wide", bit, w_bits) for bit in range(w_bits)]
    hops = len(places)
    slot = there * n_narrow + here
    per = images * 8
    count = n_wide * n_narrow * images

    def beside(axis, bit, bits, source, target, sem, position):
        return remote(
            source,
            target,
            sem.at[0, position],
            sem.at[1, position],
            axis,
            flipped(lax.axis_index(axis), 1 << bit, bits),
        )

    def mods_copy(position):
        width = 1 << position
        block = mods_all.at[pl.ds(slot // width * width, width)]
        return beside(*places[position], block, block, mods_sem, position)

    def small_copy(position):
        return beside(
            *places[position], small_out.at[position], small_in.at[position], small_sem, position
        )

    def act_copy(position):
        width = 1 << position
        block = act_all.at[pl.ds(here // width * width, width)]
        return beside(*places[position], block, block, act_sem, position)

    def small_total():
        return small_out[hops - 1] + small_in[hops - 1]

    def rows_copy(start, rows, position):
        return pltpu.make_async_copy(
            stage.at[pl.ds(0, rows)], rows_out.at[pl.ds(start, rows)], rows_sem.at[position]
        )

    height = window_out.shape[0]

    def window_copy():
        start = here * shard // (WIDTH * ALIGN) * ALIGN
        return pltpu.make_async_copy(
            rows_out.at[pl.ds(pl.multiple_of(start, ALIGN), height)], window_out, rows_sem.at[2]
        )

    def spread_hop(position):
        if position == 0:
            mods_all[slot] = g_mods_ref[...].astype(bf16)
            small_out[0, 0:PATCH] = g_patch_ref[...]
            small_out[0, PATCH : 2 * PATCH] = g_final_ref[...]
            small_out[0, 2 * PATCH : 2 * PATCH + 8] = g_bias_ref[...]
        else:
            mods_copy(position - 1).wait_recv()
            small_copy(position - 1).wait_recv()
            if position < hops:
                small_out[position] = small_out[position - 1] + small_in[position - 1]
        if position < hops:
            mods_copy(position).start()
            small_copy(position).start()

    def which_mod(shape):
        return lax.broadcasted_iota(jnp.int32, shape, 0) % 8

    def send_act():
        everything = mods_all[...].reshape(count * 8, WIDTH)
        kind = which_mod((count * 8, act_all.shape[2]))
        total = jnp.zeros((count * 8, act_all.shape[2]), f32)
        for index in range(8):
            span = slice(index * WIDTH, (index + 1) * WIDTH)
            value = dot_t(everything, adaptive_low[:, span])
            total = total + jnp.where(kind == index, value, 0.0)
        act_all[here] = jnp.sum(total.reshape(count, 8, -1), axis=1)
        act_copy(0).start()

    def act_hop(position):
        act_copy(position - 1).wait_recv()
        if position < n_bits:
            act_copy(position).start()

    def grad_condition():
        grad = jnp.concatenate([act_all[number] for number in range(n_narrow)], axis=1)
        return grad * silu_slope(condition[...])

    def grad_time():
        low = grad_condition().astype(bf16)
        before = time_pre[...]
        return low, (dot_t(low, time_two[...]) * silu_slope(before)).astype(bf16)

    def upper_rows():
        low, first = grad_time()
        stage[0:PATCH, :] = small_total()[0:PATCH]
        stage[ROW_TIME_ONE:ROW_TIME_TWO, :] = dot_s(sheet[:, :FREQS].astype(bf16), first)
        act = jax.nn.silu(time_pre[...]).astype(bf16)
        stage[ROW_TIME_TWO:ROW_TABLE, :] = dot_s(act, low)
        rows_copy(0, ROW_TABLE, 0).start()

    def lower_rows():
        rows_copy(0, ROW_TABLE, 0).wait()
        grad = grad_condition()
        low, first = grad_time()
        labels = lax.broadcasted_iota(jnp.int32, (count, 1008), 1).astype(f32)
        pick = jnp.where(sheet[:, FREQS : FREQS + 1] == labels, 1.0, 0.0).astype(bf16)
        high, rest = halves(grad)
        rest = grad - high.astype(f32)
        middle, rest = halves(rest)
        table = dot_s(pick, high) + (dot_s(pick, middle) + dot_s(pick, rest))
        stage[0:1008, :] = table
        small = small_total()
        base = ROW_FINAL - ROW_TABLE
        stage[base : base + PATCH, :] = small[PATCH : 2 * PATCH]
        base = ROW_BIAS - ROW_TABLE
        bias = small[2 * PATCH : 2 * PATCH + 8]
        stage[base : base + 1, :] = bias[0:1]
        stage[base + 1 : base + 2, :] = jnp.sum(first.astype(f32), axis=0, keepdims=True)
        stage[base + 2 : base + 3, :] = jnp.sum(low.astype(f32), axis=0, keepdims=True)
        stage[base + 3 : base + 4, :] = bias[1:2]
        stage[base + 4 : base + 8, :] = bias[4:8]
        stage[base + 8 : base + 9, :] = bias[2:3]
        stage[base + 9 : base + 17, :] = jnp.sum(
            mods_all[...].astype(f32).reshape(count, 8, WIDTH), axis=0
        )
        lane = lax.broadcasted_iota(jnp.int32, (1, WIDTH), 1)
        stage[base + 17 : base + 18, :] = jnp.where(lane < PATCH, bias[3:4], 0.0)
        stage[base + 18 :, :] = jnp.zeros((stage.shape[0] - base - 18, WIDTH), f32)
        totals_out[...] = bias
        rows_copy(ROW_TABLE, stage.shape[0], 1).start()

    def adaptive_rows():
        everything = mods_all[...].reshape(count * 8, WIDTH)
        act = own_act[...].astype(f32)
        act = jnp.broadcast_to(act[:, None, :], (count, 8, act.shape[1]))
        act = act.reshape(count * 8, -1).astype(bf16)
        kind = which_mod(act.shape)
        for index in range(8):
            span = slice(index * WIDTH, (index + 1) * WIDTH)
            here_act = jnp.where(kind == index, act, jnp.zeros((), bf16))
            value = dot_s(here_act, everything)
            add_squares(value)
            adaptive_out[:, span] = value.astype(bf16)
        rows_copy(ROW_TABLE, stage.shape[0], 1).wait()
        window_copy().start()

    def window_squares():
        window_copy().wait()
        start = here * shard // (WIDTH * ALIGN) * ALIGN
        first = here * shard - start * WIDTH
        value = window_out[...]
        spot = (
            lax.broadcasted_iota(jnp.int32, value.shape, 0) * WIDTH
            + lax.broadcasted_iota(jnp.int32, value.shape, 1)
        )
        inside = jnp.logical_and(spot >= first, spot < first + shard)
        add_squares(jnp.where(inside, value, 0.0))

    asides = [partial(spread_hop, position) for position in range(hops)]

    def last_hop():
        spread_hop(hops)
        send_act()

    asides += [last_hop]
    asides += [partial(act_hop, position) for position in range(1, n_bits)]

    def last_act():
        act_hop(n_bits)
        upper_rows()

    asides += [last_act, lower_rows, adaptive_rows, window_squares]

    squares[...] = jnp.zeros_like(squares)
    greet(n_wide, n_narrow)
    first = 0
    for grad_ref in grad_refs:
        tiles = grad_ref.shape[1] // (2 * half)

        def begin(k, carry, grad_ref=grad_ref, first=first):
            give_copy(k, grad_ref, first).start()
            return carry

        lax.fori_loop(first, first + tiles, begin, 0)
        first = first + tiles
    for k in range(RING - 1):
        start_keep(jnp.int32(k))

    def wave(t, carry):
        for number, stage in enumerate(stages):
            k = t - number

            @pl.when(jnp.logical_and(k >= 0, k < chunks))
            def _(stage=stage, k=k):
                stage(k)

        for number, aside in enumerate(asides):

            @pl.when(t == number)
            def _(aside=aside):
                aside()

        return carry

    lax.fori_loop(0, max(chunks + len(stages) - 1, len(asides)), wave, 0)

    def finish(k, carry):
        give_copy(k, grad_refs[0], k).wait_send()
        for path in range(2):
            for step in range(n_bits):
                near_copy(path, k, step).wait_send()
        for step in range(far_steps):
            far_copy(k, step, gives[step]).wait_send()
            if traded[step]:
                back_copy(k, step, parts[step + 1]).wait_send()
        last_copy(k, core).wait_send()
        return carry

    lax.fori_loop(0, chunks, finish, 0)
    for position in range(hops):
        mods_copy(position).wait_send()
        small_copy(position).wait_send()
    for position in range(n_bits):
        act_copy(position).wait_send()

    total = jnp.sum(squares[...], axis=1, keepdims=True)
    value = jnp.broadcast_to(total, norm_out.shape[1:])
    for position in range(n_bits):
        norm_out[position] = value
        copy = beside(
            *places[position], norm_out.at[position], norm_in.at[position], norm_sem, position
        )
        copy.start()
        copy.wait()
        value = value + norm_in[position]
    norm = jnp.sqrt(value)
    row = lax.broadcasted_iota(jnp.int32, value.shape, 0)
    clip_out[...] = jnp.where(row == 0, norm, clip_limit / jnp.maximum(norm, clip_limit))


def reduce_all(n_wide, n_narrow, images, shard, grads, asides):
    rows = WIDTH // n_narrow
    chunks = sum(grad.shape[1] for grad in grads) // rows
    half = rows // 2
    far = bits_of(n_wide) - 1
    devices = n_wide * n_narrow
    hops = bits_of(devices)
    count = devices * images
    dma = pltpu.SemaphoreType.DMA
    any_space = pl.BlockSpec(memory_space=pl.ANY)
    vmem = pl.BlockSpec(memory_space=pltpu.VMEM)
    height = flat_rows(n_narrow, shard)
    out, adaptive, _, window, totals, clip = pl.pallas_call(
        partial(reduce_kernel, n_wide, n_narrow, images, shard),
        in_specs=[any_space] * 4 + [vmem] * len(asides),
        out_specs=[vmem, vmem, any_space, vmem, vmem, vmem],
        out_shape=[
            jax.ShapeDtypeStruct((chunks, 2, half, WIDTH), bf16),
            jax.ShapeDtypeStruct((rows, 8 * WIDTH), bf16),
            jax.ShapeDtypeStruct((height, WIDTH), f32),
            jax.ShapeDtypeStruct((shard_rows(shard), WIDTH), f32),
            jax.ShapeDtypeStruct((8, WIDTH), f32),
            jax.ShapeDtypeStruct((8, 128), f32),
        ],
        scratch_shapes=[
            pltpu.VMEM((RING, n_narrow, half, WIDTH), bf16),
            pltpu.VMEM((chunks, n_narrow, half, WIDTH), bf16),
            pltpu.VMEM((2, chunks, n_narrow - 1, half, WIDTH // 2), bf16),
            pltpu.VMEM((2, chunks, n_narrow - 1, half, WIDTH // 2), bf16),
            pltpu.VMEM((chunks, far, half, WIDTH), bf16),
            pltpu.VMEM((chunks, far, half, WIDTH), bf16),
            pltpu.VMEM((RING, n_narrow, half, WIDTH), f32),
            pltpu.VMEM((RING, half, WIDTH), f32),
            dma((chunks,)),
            dma((2, chunks)),
            dma((2, 2, chunks, bits_of(n_narrow))),
            dma((2, chunks, far)),
            dma((2, chunks, far)),
            dma((2, chunks)),
            pltpu.VMEM((devices, images * 8, WIDTH), bf16),
            pltpu.VMEM((hops, 2 * PATCH + 8, WIDTH), f32),
            pltpu.VMEM((hops, 2 * PATCH + 8, WIDTH), f32),
            pltpu.VMEM((n_narrow, count, rows), f32),
            pltpu.VMEM((height - ROW_TABLE, WIDTH), f32),
            pltpu.VMEM((bits_of(n_narrow), 8, 128), f32),
            pltpu.VMEM((bits_of(n_narrow), 8, 128), f32),
            pltpu.VMEM((1, WIDTH), f32),
            dma((2, hops)),
            dma((2, hops)),
            dma((2, bits_of(n_narrow))),
            dma((3,)),
            dma((2, bits_of(n_narrow))),
        ],
        compiler_params=pltpu.CompilerParams(
            collective_id=1, has_side_effects=True, vmem_limit_bytes=62 * 1024 * 1024
        ),
        cost_estimate=pl.CostEstimate(
            flops=10**8, bytes_accessed=300 * 10**6, transcendentals=0
        ),
        name="reduce_gradients",
    )(*grads, *asides)
    return out.reshape(chunks * rows, WIDTH), adaptive, window, totals, clip


def weight_kernel(left_ref, right_ref, out_ref):
    value = dot_s(left_ref[...], right_ref[...]).astype(bf16)
    out_ref[...] = value.reshape(out_ref.shape)


def weight_blocks(n_narrow, inputs, gradient):
    tokens, depth = inputs.shape
    across = gradient.shape[1] // WIDTH
    down = depth // WIDTH
    rows = WIDTH // n_narrow
    if down == 1:
        grid = across
        left = pl.BlockSpec((tokens, WIDTH), lambda i: (0, 0))
        right = pl.BlockSpec((tokens, WIDTH), lambda i: (0, i))
        out = pl.BlockSpec((n_narrow, rows, WIDTH), lambda i: (0, i, 0))
        shape = (n_narrow, across * rows, WIDTH)
    else:
        grid = down
        left = pl.BlockSpec((tokens, WIDTH), lambda i: (0, i))
        right = pl.BlockSpec((tokens, WIDTH), lambda i: (0, 0))
        out = pl.BlockSpec((WIDTH, WIDTH), lambda i: (i, 0))
        shape = (depth, WIDTH)
    result = pl.pallas_call(
        weight_kernel,
        grid=(grid,),
        in_specs=[left, right],
        out_specs=out,
        out_shape=jax.ShapeDtypeStruct(shape, bf16),
        compiler_params=pltpu.CompilerParams(vmem_limit_bytes=48 * 1024 * 1024),
        name="weight_gradient",
    )(inputs, gradient)
    return result.reshape(n_narrow, -1, WIDTH)


def dot_s(left, right):
    return lax.dot_general(left, right, (((0,), (0,)), ((), ())), preferred_element_type=f32)


def center(hidden):
    centered = hidden - jnp.mean(hidden, axis=-1, keepdims=True)
    scale = lax.rsqrt(jnp.mean(centered * centered, axis=-1, keepdims=True) + 1e-06)
    return centered * scale, scale


def center_back(grad, normal, scale):
    return (
        grad
        - jnp.mean(grad, axis=-1, keepdims=True)
        - normal * jnp.mean(grad * normal, axis=-1, keepdims=True)
    ) * scale


def gelu_pair(value):
    rate = math.sqrt(2.0 / math.pi)
    square = value * value
    bend = jnp.tanh(rate * value * (1.0 + 0.044715 * square))
    half = 0.5 * (1.0 + bend)
    slope = half + 0.5 * value * (1.0 - bend * bend) * (rate * (1.0 + 3.0 * 0.044715 * square))
    return value * half, slope


def layer_kernel(
    numbers,
    latent_ref,
    noise_ref,
    mods_ref,
    place_ref,
    patch_ref,
    final_ref,
    tail_ref,
    attend_ref,
    output_ref,
    expand_ref,
    shrink_ref,
    normed_ref,
    mixed_ref,
    normed_two_ref,
    act_ref,
    g_branch_two_ref,
    g_pre_ref,
    g_branch_ref,
    g_triple_ref,
    g_mods_ref,
    g_patch_ref,
    g_final_ref,
    g_bias_ref,
    triple,
    probs,
    slope,
    normal_one,
    normal_two,
    hidden,
    branch,
    g_mixed,
):
    image = pl.program_id(0)
    tokens = SEQUENCE
    wide = 256

    def bias(index):
        spot = ROW_BIAS - ROW_TAIL + index
        return tail_ref[spot : spot + 1, :]

    def bias_wide(ref, first, index):
        across = WIDTH // wide
        return (
            pl.ds(first + index // across, 1),
            pl.ds(pl.multiple_of(index % across * wide, wide), wide),
        )

    def row(index):
        return mods_ref[0, index : index + 1, :]

    @pl.when(image == 0)
    def _():
        for ref in (g_patch_ref, g_final_ref, g_bias_ref):
            ref[...] = jnp.zeros_like(ref)

    moment = numbers[0, image]
    blended = ((1.0 - moment) * latent_ref[0] + moment * noise_ref[0]).astype(bf16)
    target = noise_ref[0] - latent_ref[0]
    start = dot(blended, patch_ref[...]) + bias(0) + place_ref[...]
    hidden[...] = start
    normal, scale_one = center(start)
    normal_one[...] = normal
    normed_ref[...] = (normal * (1.0 + row(1)) + row(0)).astype(bf16)

    def project(index, carry):
        span = pl.ds(pl.multiple_of(index * wide, wide), wide)
        triple[:, span] = dot(normed_ref[...], attend_ref[:, span]).astype(bf16)
        return carry

    lax.fori_loop(0, 3 * WIDTH // wide, project, 0)

    lane = lax.broadcasted_iota(jnp.int32, (tokens, 2 * HEAD_DIM), 1)
    first_half = lane < HEAD_DIM
    zero = jnp.zeros((), bf16)
    rate = HEAD_DIM ** (-0.5)

    def spans_of(pair):
        return [
            pl.ds(pl.multiple_of(part * WIDTH + pair * 2 * HEAD_DIM, 2 * HEAD_DIM), 2 * HEAD_DIM)
            for part in range(3)
        ]

    def attend(pair, carry):
        query_span, key_span, value_span = spans_of(pair)
        query = triple[:, query_span]
        keys = triple[:, key_span]
        values = triple[:, value_span]
        results = []
        for side in range(2):
            mask = first_half if side == 0 else jnp.logical_not(first_half)
            scores = dot_t(jnp.where(mask, query, zero), keys) * rate
            scores = jnp.exp(scores - jnp.max(scores, axis=-1, keepdims=True))
            weights = scores * (1.0 / jnp.sum(scores, axis=-1, keepdims=True))
            probs[2 * pair + side] = weights
            results.append(dot(weights.astype(bf16), values))
        mixed_ref[:, query_span] = jnp.where(first_half, results[0], results[1]).astype(bf16)
        return carry

    lax.fori_loop(0, HEADS // 2, attend, 0)

    value = dot(mixed_ref[...], output_ref[...]) + bias(3)
    branch[...] = value
    value = hidden[...] + row(2) * value
    hidden[...] = value
    normal, scale_two = center(value)
    normal_two[...] = normal
    normed_two_ref[...] = (normal * (1.0 + row(4)) + row(3)).astype(bf16)

    def widen(index, carry):
        span = pl.ds(pl.multiple_of(index * wide, wide), wide)
        before = dot(normed_two_ref[...], expand_ref[:, span])
        before = before + tail_ref[bias_wide(tail_ref, ROW_BIAS - ROW_TAIL + 4, index)]
        after, steep = gelu_pair(before)
        act_ref[:, span] = after.astype(bf16)
        slope[:, span] = steep
        return carry

    lax.fori_loop(0, MLP_WIDTH // wide, widen, 0)

    branch_two = dot(act_ref[...], shrink_ref[...]) + bias(8)
    upper = hidden[...] + row(5) * branch_two
    normal, scale_three = center(upper)
    final = (normal * (1.0 + row(7)) + row(6)).astype(bf16)
    mismatch = dot(final, final_ref[...]) + bias(17)[:, :PATCH] - target
    loss = numbers[2, image] * jnp.sum(mismatch * mismatch)
    grad_out = (numbers[1, image] * mismatch).astype(bf16)

    g_final_ref[...] += dot_s(final, grad_out)
    sums = jnp.sum(grad_out.astype(f32), axis=0, keepdims=True)
    spot = lax.broadcasted_iota(jnp.int32, (1, WIDTH), 1)
    sums = jnp.concatenate([sums, jnp.zeros((1, WIDTH - PATCH), f32)], axis=1)
    g_bias_ref[3:4, :] += jnp.where(spot == PATCH, loss, sums)
    grad = dot_t(grad_out, final_ref[...])
    shift_f = jnp.sum(grad, axis=0, keepdims=True)
    scale_f = jnp.sum(grad * normal, axis=0, keepdims=True)
    grad_upper = center_back((1.0 + row(7)) * grad, normal, scale_three)
    gate_two = jnp.sum(branch_two * grad_upper, axis=0, keepdims=True)
    grad_branch = (row(5) * grad_upper).astype(bf16)
    g_branch_two_ref[...] = grad_branch
    g_bias_ref[2:3, :] += jnp.sum(grad_branch.astype(f32), axis=0, keepdims=True)
    hidden[...] = grad_upper

    def narrow(index, carry):
        span = pl.ds(pl.multiple_of(index * wide, wide), wide)
        grad_act = dot_t(g_branch_two_ref[...], shrink_ref[span, :])
        grad_pre = (grad_act * slope[:, span]).astype(bf16)
        g_pre_ref[:, span] = grad_pre
        g_bias_ref[bias_wide(g_bias_ref, 4, index)] += jnp.sum(grad_pre.astype(f32), axis=0, keepdims=True)
        return carry

    lax.fori_loop(0, MLP_WIDTH // wide, narrow, 0)

    grad = dot_t(g_pre_ref[...], expand_ref[...])
    normal = normal_two[...]
    shift_two = jnp.sum(grad, axis=0, keepdims=True)
    scale_mod_two = jnp.sum(grad * normal, axis=0, keepdims=True)
    grad_middle = hidden[...] + center_back((1.0 + row(4)) * grad, normal, scale_two)
    gate_one = jnp.sum(branch[...] * grad_middle, axis=0, keepdims=True)
    grad_branch = (row(2) * grad_middle).astype(bf16)
    g_branch_ref[...] = grad_branch
    g_bias_ref[1:2, :] += jnp.sum(grad_branch.astype(f32), axis=0, keepdims=True)
    hidden[...] = grad_middle
    g_mixed[...] = dot_t(grad_branch, output_ref[...]).astype(bf16)

    def attend_back(pair, carry):
        query_span, key_span, value_span = spans_of(pair)
        query = triple[:, query_span]
        keys = triple[:, key_span]
        values = triple[:, value_span]
        grad_mixed = g_mixed[:, query_span]
        results = []
        for side in range(2):
            mask = first_half if side == 0 else jnp.logical_not(first_half)
            weights = probs[2 * pair + side]
            grad_weights = dot_t(jnp.where(mask, grad_mixed, zero), values)
            grad_values = dot_s(weights.astype(bf16), grad_mixed)
            grad_scores = weights * (
                grad_weights - jnp.sum(weights * grad_weights, axis=-1, keepdims=True)
            )
            grad_scores = grad_scores.astype(bf16)
            grad_query = dot(grad_scores, keys)
            grad_keys = dot_s(grad_scores, query)
            results.append((grad_query, grad_keys, grad_values))
        for part, span in enumerate((query_span, key_span, value_span)):
            merged = jnp.where(first_half, results[0][part], results[1][part])
            if part < 2:
                merged = merged * rate
            g_triple_ref[:, span] = merged.astype(bf16)
        return carry

    lax.fori_loop(0, HEADS // 2, attend_back, 0)

    grad = dot_t(g_triple_ref[...], attend_ref[...])
    normal = normal_one[...]
    shift_one = jnp.sum(grad, axis=0, keepdims=True)
    scale_mod_one = jnp.sum(grad * normal, axis=0, keepdims=True)
    grad_start = hidden[...] + center_back((1.0 + row(1)) * grad, normal, scale_one)
    grad_start = grad_start.astype(bf16)
    g_patch_ref[...] += dot_s(blended, grad_start)
    g_bias_ref[0:1, :] += jnp.sum(grad_start.astype(f32), axis=0, keepdims=True)
    for index, value in enumerate(
        (shift_one, scale_mod_one, gate_one, shift_two, scale_mod_two, gate_two, shift_f, scale_f)
    ):
        g_mods_ref[0, index : index + 1, :] = value


def layer(numbers, latent, noisy, mods, patch_w, final_w, tail, weights):
    images = latent.shape[0]
    tokens = images * SEQUENCE
    once = pl.Buffered(1)

    def whole(array):
        return pl.BlockSpec(
            array.shape, lambda i: (0,) * len(array.shape), pipeline_mode=once
        )

    def fixed(shape, dtype=f32):
        return pl.BlockSpec(shape, lambda i: (0,) * len(shape)), jax.ShapeDtypeStruct(shape, dtype)

    def per_image(width):
        return (
            pl.BlockSpec((SEQUENCE, width), lambda i: (i, 0)),
            jax.ShapeDtypeStruct((tokens, width), bf16),
        )

    outs = [
        per_image(WIDTH),
        per_image(WIDTH),
        per_image(WIDTH),
        per_image(MLP_WIDTH),
        per_image(WIDTH),
        per_image(MLP_WIDTH),
        per_image(WIDTH),
        per_image(3 * WIDTH),
        (
            pl.BlockSpec((1, 8, WIDTH), lambda i: (i, 0, 0)),
            jax.ShapeDtypeStruct((images, 8, WIDTH), f32),
        ),
        fixed((PATCH, WIDTH)),
        fixed((WIDTH, PATCH)),
        fixed((8, WIDTH)),
    ]
    place = positions(SEQUENCE, WIDTH)
    fixed_args = (place, patch_w, final_w, tail) + tuple(weights)
    flops = 2 * 2 * 7078 * 1000 * tokens
    return pl.pallas_call(
        layer_kernel,
        grid=(images,),
        in_specs=[
            pl.BlockSpec(memory_space=pltpu.SMEM),
            pl.BlockSpec((1, SEQUENCE, PATCH), lambda i: (i, 0, 0)),
            pl.BlockSpec((1, SEQUENCE, PATCH), lambda i: (i, 0, 0)),
            pl.BlockSpec((1, 8, WIDTH), lambda i: (i, 0, 0)),
        ]
        + [whole(array) for array in fixed_args],
        out_specs=[spec for spec, _ in outs],
        out_shape=[shape for _, shape in outs],
        scratch_shapes=[
            pltpu.VMEM((SEQUENCE, 3 * WIDTH), bf16),
            pltpu.VMEM((HEADS, SEQUENCE, SEQUENCE), f32),
            pltpu.VMEM((SEQUENCE, MLP_WIDTH), f32),
            pltpu.VMEM((SEQUENCE, WIDTH), f32),
            pltpu.VMEM((SEQUENCE, WIDTH), f32),
            pltpu.VMEM((SEQUENCE, WIDTH), f32),
            pltpu.VMEM((SEQUENCE, WIDTH), f32),
            pltpu.VMEM((SEQUENCE, WIDTH), bf16),
        ],
        compiler_params=pltpu.CompilerParams(vmem_limit_bytes=56 * 1024 * 1024),
        cost_estimate=pl.CostEstimate(
            flops=flops, bytes_accessed=60 * 10**6, transcendentals=0
        ),
        name="layer",
    )(numbers, latent, noisy, mods, *fixed_args)


def local(
    n_wide,
    n_narrow,
    latents,
    noise_field,
    labels,
    label_drop,
    time_steps,
    loss_weights,
    attend_weight,
    attend_first,
    attend_second,
    attend_left,
    attend_right,
    output_weight,
    output_first,
    output_second,
    output_left,
    output_right,
    expand_weight,
    expand_first,
    expand_second,
    expand_left,
    expand_right,
    shrink_weight,
    shrink_first,
    shrink_second,
    shrink_left,
    shrink_right,
    adaptive_weight,
    adaptive_first,
    adaptive_second,
    adaptive_left,
    adaptive_right,
    shared_weight,
    shared_first,
    shared_second,
):
    column = lax.axis_index("narrow")
    images = labels.shape[0] * labels.shape[1]

    moment = (time_steps.reshape(images).astype(f32) + 0.5) / TIMESTEPS
    chosen = jnp.where(label_drop == 1, CLASSES - 1, labels).reshape(images, 1).astype(f32)
    weights_here = loss_weights.reshape(images)
    info = jnp.concatenate(
        [rounded(frequencies(moment, FREQS)).astype(f32), chosen, weights_here[:, None]], axis=1
    )
    info = jnp.pad(info, ((0, 8 - images), (0, SHEET - info.shape[1])))[None]

    shard = shared_weight.shape[0]
    rows = shard_rows(shard)
    row_start = column * shard // (WIDTH * ALIGN) * ALIGN
    offset = column * shard - row_start * WIDTH
    margin = (ALIGN + 1) * WIDTH
    own = jnp.concatenate(
        [jnp.zeros((margin,), f32), shared_weight, jnp.zeros((rows * WIDTH - shard,), f32)]
    )
    own = lax.dynamic_slice(own, (margin - offset,), (rows * WIDTH,)).reshape(rows, WIDTH)

    *full, flat, sheet, time_pre, condition, own_act, adaptive_low, mods, total = gather_all(
        n_wide,
        n_narrow,
        images,
        shard,
        (own, attend_weight, output_weight, expand_weight, shrink_weight),
        adaptive_weight,
        info,
    )
    weight_sum = total[0, 0]

    shape = (images,) + latents.shape[2:]
    entries = SEQUENCE * PATCH
    numbers = jnp.stack(
        [moment, 2.0 * weights_here / (entries * weight_sum), weights_here / entries]
    )
    (
        normed,
        mixed,
        normed_two,
        act,
        g_branch_two,
        g_pre,
        g_branch,
        g_triple,
        g_mods,
        g_patch,
        g_final,
        g_bias,
    ) = layer(
        numbers,
        latents.reshape(shape),
        noise_field.reshape(shape),
        mods,
        flat[ROW_PATCH:ROW_TIME_ONE],
        flat[ROW_FINAL:ROW_BIAS].reshape(WIDTH, PATCH),
        flat[ROW_TAIL : ROW_TAIL + TAIL].astype(f32),
        full,
    )

    joined, grad_adaptive, window, totals, clip = reduce_all(
        n_wide,
        n_narrow,
        images,
        shard,
        (
            weight_blocks(n_narrow, normed, g_triple),
            weight_blocks(n_narrow, mixed, g_branch),
            weight_blocks(n_narrow, normed_two, g_pre),
            weight_blocks(n_narrow, act, g_branch_two),
        ),
        (
            g_mods.reshape(images * 8, WIDTH),
            g_patch,
            g_final.reshape(PATCH, WIDTH),
            g_bias,
            adaptive_low,
            sheet,
            time_pre,
            condition,
            own_act,
            flat[ROW_TIME_TWO:ROW_TABLE],
        ),
    )
    loss_sum = totals[3, PATCH]
    clip_norm = clip[0, 0]
    factor = clip[1, 0]
    grad_shared = lax.dynamic_slice(window.reshape(-1), (offset,), (shard,))

    states = (
        (attend_weight, attend_first, attend_second, attend_left, attend_right),
        (output_weight, output_first, output_second, output_left, output_right),
        (expand_weight, expand_first, expand_second, expand_left, expand_right),
        (shrink_weight, shrink_first, shrink_second, shrink_left, shrink_right),
        (adaptive_weight, adaptive_first, adaptive_second, adaptive_left, adaptive_right),
    )
    tiles = (0, 3, 4, 8)
    results = []
    for number in range(5):
        weight, first, second, left, right = states[number]
        grad, base = (grad_adaptive, None) if number == 4 else (joined, tiles[number])
        results += rotated_update(
            weight, first, second, grad, base, left, right, factor, WIDTH // n_narrow
        )
    fresh = plain_update(shared_weight, shared_first, shared_second, grad_shared * factor)
    results += [fresh[0], fresh[1], fresh[2], fresh[0].astype(jnp.bfloat16)]
    return tuple(results) + (loss_sum, weight_sum, clip_norm)


def solution(mesh):
    data = P(None, ("wide", "narrow"))
    state = (P("narrow", None),) * 3 + (P("narrow", None, None), P())
    return jax.shard_map(
        partial(local, mesh.shape["wide"], mesh.shape["narrow"]),
        mesh=mesh,
        in_specs=(P(None, ("wide", "narrow"), None, None),) * 2
        + (data,) * 4
        + state * 5
        + (P("narrow"),) * 3,
        out_specs=(P("narrow", None),) * 20 + (P("narrow"),) * 4 + (P(),) * 3,
        check_vma=False,
    )
```

```python
from functools import partial
import math

import jax
import jax.numpy as jnp
import numpy as np
from jax import lax
from jax.experimental import pallas as pl
from jax.experimental.pallas import tpu as pltpu
from jax.sharding import PartitionSpec as P

HEADS = 12
HEAD_DIM = 64
MLP_WIDTH = 3072
CLASSES = 1001
FREQS = 256
PATCH = 16
TIMESTEPS = 1000
BLOCK = 32
STEP_COUNT = 10
WIDTH = 768
SEQUENCE = 256


beta_one = 0.9
beta_two = 0.999
epsilon_adam = 1e-08
learn_rate = 0.03
decay_rate = 0.01
clip_limit = 0.002
highest = lax.Precision.HIGHEST
bf16 = jnp.bfloat16
f32 = jnp.float32

ROW_PATCH = 0
ROW_TIME_ONE = 16
ROW_TIME_TWO = 272
ROW_TABLE = 1040
ROW_FINAL = 2041
ROW_BIAS = 2057


def positions(tokens, width):
    side = math.isqrt(tokens)
    quarter = width // 4
    omega = 1.0 / 10000.0 ** (np.arange(quarter, dtype=np.float64) / quarter)
    place = np.arange(tokens)
    column = (place % side)[:, None] * omega
    row = (place // side)[:, None] * omega
    table = np.concatenate([np.sin(column), np.cos(column), np.sin(row), np.cos(row)], axis=1)
    return jnp.asarray(table.astype(np.float32))


def frequencies(moment, width):
    half = width // 2
    phases = jnp.exp(-math.log(10000.0) * jnp.arange(half, dtype=jnp.float32) / half)
    angles = moment[:, None] * 1000.0 * phases
    return jnp.concatenate([jnp.cos(angles), jnp.sin(angles)], axis=1)


def normalize(hidden):
    centered = hidden - jnp.mean(hidden, axis=-1, keepdims=True)
    return centered * lax.rsqrt(jnp.mean(centered * centered, axis=-1, keepdims=True) + 1e-06)


def modulate(hidden, shift, scale):
    return normalize(hidden) * (1.0 + scale[:, None, :]) + shift[:, None, :]


def adam_direction(first, second):
    return (first * (1.0 / (1.0 - beta_one**STEP_COUNT))) / (
        jnp.sqrt(second * (1.0 / (1.0 - beta_two**STEP_COUNT))) + epsilon_adam
    )


def plain_update(weight, first, second, grad):
    first = beta_one * first + (1.0 - beta_one) * grad
    second = beta_two * second + (1.0 - beta_two) * grad * grad
    weight = weight - learn_rate * (adam_direction(first, second) + decay_rate * weight)
    return (weight, first, second)


def rounded(value):
    return value.astype(jnp.bfloat16)


def product(inputs, weight):
    return jnp.dot(inputs, weight, preferred_element_type=jnp.float32)


def backprod(gradient, weight):
    return jnp.einsum("...n,kn->...k", gradient, weight, preferred_element_type=jnp.float32)


def weight_grad(inputs, gradient):
    flat_in = inputs.reshape(-1, inputs.shape[-1])
    flat_grad = gradient.reshape(-1, gradient.shape[-1])
    return lax.dot_general(
        flat_in, flat_grad, (((0,), (0,)), ((), ())), preferred_element_type=jnp.float32
    )


def bias_grad(gradient):
    return jnp.sum(gradient.astype(jnp.float32).reshape(-1, gradient.shape[-1]), axis=0)


def halves(value):
    high = value.astype(bf16)
    return high, (value - high.astype(f32)).astype(bf16)


def spread_left(blocks):
    size = blocks.shape[0]
    place = lax.broadcasted_iota(jnp.int32, (BLOCK, size), 0)
    column = lax.broadcasted_iota(jnp.int32, (BLOCK, size), 1)
    repeat = (place == column % BLOCK).astype(bf16)
    row_block = lax.broadcasted_iota(jnp.int32, (size, size), 0) // BLOCK
    col_block = lax.broadcasted_iota(jnp.int32, (size, size), 1) // BLOCK
    return tuple(
        jnp.where(
            row_block == col_block, jnp.dot(part, repeat, preferred_element_type=f32), 0.0
        ).astype(bf16)
        for part in halves(blocks)
    )


def spread_right(first, second):
    size = 4 * BLOCK
    row_block = lax.broadcasted_iota(jnp.int32, (size, size), 0) // BLOCK
    col_block = lax.broadcasted_iota(jnp.int32, (size, size), 1) // BLOCK
    inside = row_block == col_block
    corners = [
        jnp.where(inside, jnp.concatenate([row] * 4, axis=0), 0.0) for row in (first, second)
    ]
    empty = jnp.zeros((size, size), f32)
    return jnp.concatenate(
        [
            jnp.concatenate([corners[0], empty], axis=1),
            jnp.concatenate([empty, corners[1]], axis=1),
        ],
        axis=0,
    )


def dot(left, right):
    return jnp.dot(left, right, preferred_element_type=f32)


def dot_t(left, right):
    return lax.dot_general(left, right, (((1,), (1,)), ((), ())), preferred_element_type=f32)


STRIP = 256
TILES = ((3, 1), (1, 1), (4, 1), (1, 4), (8, 1))


def tile_places():
    places = []
    for matrix, (across, down) in enumerate(TILES):
        for number in range(across * down):
            places.append((matrix, number // across, number % across))
    return places


def left_number(tile):
    return (tile + 9) // 12 + (tile + 8) // 12 + (tile + 4) // 12 * (tile - 7)


def adam_kernel(count, *refs):
    factor_ref, turned, lefts, rights = refs[:4]
    states = [refs[4 + 3 * matrix : 7 + 3 * matrix] for matrix in range(5)]
    outs = [refs[19 + 4 * matrix : 23 + 4 * matrix] for matrix in range(5)]
    taken, given, low, take_sem, give_sem = refs[39:]
    rows = taken.shape[2]
    places = tile_places()
    factor = factor_ref[1, 0]

    def window(number):
        _, down, across = places[number]
        return (pl.ds(down * rows, rows), pl.ds(across * WIDTH, WIDTH))

    def takes(number):
        slot = number % 3
        arrays = [ref.at[window(number)] for ref in states[places[number][0]]]
        arrays.append(turned.at[number])
        return [
            pltpu.make_async_copy(array, taken.at[slot, part], take_sem.at[slot, part])
            for part, array in enumerate(arrays)
        ]

    def gives(number):
        slot = number % 2
        arrays = [ref.at[window(number)] for ref in outs[places[number][0]]]
        sources = [given.at[slot, part] for part in range(3)] + [low.at[slot]]
        return [
            pltpu.make_async_copy(source, array, give_sem.at[slot, part])
            for part, (source, array) in enumerate(zip(sources, arrays))
        ]

    def given_out(slot):
        for part in range(4):
            buffer = low.at[slot] if part == 3 else given.at[slot, part]
            pltpu.make_async_copy(buffer, buffer, give_sem.at[slot, part]).wait()

    for number in range(2):
        for copy in takes(number):
            copy.start()

    def body(tile, carry):
        for number in range(2, count):

            @pl.when(tile + 2 == number)
            def _(number=number):
                for copy in takes(number):
                    copy.start()

        slot = tile % 3
        out = tile % 2
        for part in range(4):
            buffer = taken.at[slot, part]
            pltpu.make_async_copy(buffer, buffer, take_sem.at[slot, part]).wait()

        @pl.when(tile >= 2)
        def _():
            given_out(out)

        stack = jnp.where(tile < 12, left_number(jnp.minimum(tile, 11)), 7)
        left = spread_left(lefts[stack])[0]
        for start in range(0, WIDTH, STRIP):
            span = slice(start, start + STRIP)
            group = tile * (WIDTH // BLOCK // 4) + start // BLOCK // 4
            right = spread_right(rights[group], rights[group + 1]).astype(bf16)
            grad = taken[slot, 3, :, span] * factor
            first = beta_one * taken[slot, 1, :, span] + (1.0 - beta_one) * grad
            second = beta_two * taken[slot, 2, :, span] + (1.0 - beta_two) * grad * grad
            given[out, 1, :, span] = first
            given[out, 2, :, span] = second
            step = adam_direction(first, second)
            step = dot_t(step.astype(bf16), right)
            step = dot(left, step.astype(bf16))
            weight = taken[slot, 0, :, span]
            weight = weight - learn_rate * (step + decay_rate * weight)
            given[out, 0, :, span] = weight
            low[out, :, span] = weight.astype(bf16)
        for number in range(count):

            @pl.when(tile == number)
            def _(number=number):
                for copy in gives(number):
                    copy.start()

        return carry

    lax.fori_loop(0, count, body, 0)
    for slot in range(2):
        given_out(slot)


def rotated_update(clip, turned, lefts, rights, states):
    count, rows, _ = turned.shape
    any_space = pl.BlockSpec(memory_space=pl.ANY)
    vmem = pl.BlockSpec(memory_space=pltpu.VMEM)
    shapes = []
    for weight, _, _ in states:
        shapes += [jax.ShapeDtypeStruct(weight.shape, f32)] * 3
        shapes += [jax.ShapeDtypeStruct(weight.shape, bf16)]
    dma = pltpu.SemaphoreType.DMA
    return pl.pallas_call(
        partial(adam_kernel, count),
        in_specs=[pl.BlockSpec(memory_space=pltpu.SMEM), any_space, vmem, vmem]
        + [any_space] * 15,
        out_specs=[any_space] * 20,
        out_shape=shapes,
        scratch_shapes=[
            pltpu.VMEM((3, 4, rows, WIDTH), f32),
            pltpu.VMEM((2, 3, rows, WIDTH), f32),
            pltpu.VMEM((2, rows, WIDTH), bf16),
            dma((3, 4)),
            dma((2, 4)),
        ],
        compiler_params=pltpu.CompilerParams(vmem_limit_bytes=60 * 1024 * 1024),
        name="rotated_adam",
    )(clip, turned, lefts, rights, *[array for state in states for array in state])


def bits_of(extent):
    return extent.bit_length() - 1


def flipped(index, mask, count):
    for bit in range(count):
        if mask >> bit & 1:
            index = index + (1 - 2 * (index // (1 << bit) % 2)) * (1 << bit)
    return index


def greet(n_wide, n_narrow):
    barrier = pltpu.get_barrier_semaphore()
    count = 0
    for axis, extent in (("narrow", n_narrow), ("wide", n_wide)):
        me = lax.axis_index(axis)
        for bit in range(bits_of(extent)):
            pl.semaphore_signal(
                barrier,
                inc=1,
                device_id={axis: flipped(me, 1 << bit, bits_of(extent))},
                device_id_type=pl.DeviceIdType.MESH,
            )
            count = count + 1
    pl.semaphore_wait(barrier, count)


def remote(source, target, send_sem, recv_sem, axis, peer):
    return pltpu.make_async_remote_copy(
        src_ref=source,
        dst_ref=target,
        send_sem=send_sem,
        recv_sem=recv_sem,
        device_id={axis: peer},
        device_id_type=pl.DeviceIdType.MESH,
    )


def slot_of(n_wide, n_narrow):
    here = lax.axis_index("narrow")
    there = lax.axis_index("wide")
    return there // 2 + n_wide // 2 * (here + n_narrow * (there % 2))


def hop_order(n_wide, n_narrow):
    n_bits = bits_of(n_narrow)
    w_bits = bits_of(n_wide)
    places = [("wide", bit, w_bits) for bit in range(1, w_bits)]
    places += [("narrow", bit, n_bits) for bit in range(n_bits)]
    return places + [("wide", 0, w_bits)]


def route(path, step, count):
    return (step + path) % count


ROW_TAIL = 2048
TAIL = 32
ALIGN = 16
SHEET = 384


def shard_rows(shard):
    rows = (shard + WIDTH - 2) // WIDTH + 1 + ALIGN
    return -(-rows // 32) * 32


def shard_start(number, shard):
    return number * shard // WIDTH // ALIGN * ALIGN


def flat_rows(n_narrow, shard):
    last = shard_start(n_narrow - 1, shard) + shard_rows(shard)
    return max(-(-last // ALIGN) * ALIGN, 2112)


def bases_along_lanes(shape):
    return shape[0] == BLOCK and shape[2] > BLOCK


def silu_slope(value):
    gate = jax.nn.sigmoid(value)
    return gate * (1.0 + value * (1.0 - gate))


def own_columns(value, n_narrow):
    here = lax.axis_index("narrow")
    width = value.shape[1] // n_narrow
    result = value[:, :width]
    for number in range(1, n_narrow):
        result = jnp.where(
            here == number, value[:, number * width : (number + 1) * width], result
        )
    return result


def gather_kernel(n_wide, n_narrow, images, shard, *refs):
    count = 5
    shards = refs[:count]
    adaptive_ref, info_ref = refs[count : count + 2]
    left_refs = refs[count + 2 : count + 7]
    right_refs = refs[count + 7 : count + 12]
    outs = refs[count + 12 : count + 29]
    scratch = refs[count + 29 :]
    (
        patch_out,
        final_out,
        tail_out,
        time_two_out,
        sheet,
        time_pre,
        condition,
        own_act,
        adaptive_low,
        mods_ref,
        total_ref,
        lefts_out,
        rights_out,
    ) = outs[4:17]
    gathered = scratch[0]
    wides = scratch[1 : count + 1]
    lows = scratch[count + 1 : 2 * count + 1]
    (
        flat,
        turned,
        adaptive_wide,
        info_all,
        part,
        part_in,
        load_sem,
        keep_sem,
        send_sem,
        recv_sem,
        core_send,
        core_recv,
        info_sem,
        info_send,
        info_recv,
        part_send,
        part_recv,
    ) = scratch[2 * count + 1 :]
    fulls = (gathered,) + tuple(outs[:4])
    here = lax.axis_index("narrow")
    there = lax.axis_index("wide")
    core = there % 2
    n_bits = bits_of(n_narrow)
    w_bits = bits_of(n_wide)
    sibling = flipped(there, 1, w_bits)

    loads = [
        pltpu.make_async_copy(shards[number], wides[number], load_sem.at[number])
        for number in range(count)
    ]
    loads.append(pltpu.make_async_copy(adaptive_ref, adaptive_wide, load_sem.at[count]))
    for load in loads:
        load.start()
    slot = slot_of(n_wide, n_narrow)
    info_own = pltpu.make_async_copy(info_ref, info_all.at[pl.ds(slot, 1)], info_sem)
    info_own.start()
    greet(n_wide, n_narrow)
    sends = []

    def region(number, owner, half, path):
        rows, cols = shards[number].shape
        return (
            pl.ds(pl.multiple_of(owner * rows + half * (rows // 2), 16), rows // 2),
            pl.ds(path * (cols // 2), cols // 2),
        )

    def narrow_step(number, step, own):
        for path in range(2):
            bit = route(path, step, n_bits)
            peer = flipped(here, 1 << bit, n_bits)
            done = sum(1 << route(path, earlier, n_bits) for earlier in range(step))
            for mask in range(n_narrow):
                if mask & ~done or own != (mask == 0):
                    continue
                place = region(number, flipped(here, mask, n_bits), core, path)
                arrives = mask | 1 << bit
                if mask == 0:
                    rows, cols = shards[number].shape
                    source = lows[number].at[
                        pl.ds(pl.multiple_of(core * (rows // 2), 16), rows // 2),
                        pl.ds(path * (cols // 2), cols // 2),
                    ]
                else:
                    source = fulls[number].at[place]
                copy = remote(
                    source,
                    fulls[number].at[place],
                    send_sem.at[number, path, arrives - 1],
                    recv_sem.at[number, path, arrives - 1],
                    "narrow",
                    peer,
                )
                copy.start()
                sends.append(copy)

    def arrive(number, step):
        for path in range(2):
            bit = route(path, step, n_bits)
            done = sum(1 << route(path, earlier, n_bits) for earlier in range(step))
            for mask in range(n_narrow):
                if mask & ~done:
                    continue
                arrived = mask | 1 << bit
                place = region(number, flipped(here, arrived, n_bits), core, path)
                remote(
                    fulls[number].at[place],
                    fulls[number].at[place],
                    send_sem.at[number, path, arrived - 1],
                    recv_sem.at[number, path, arrived - 1],
                    "narrow",
                    flipped(here, 1 << bit, n_bits),
                ).wait_recv()
                copy = remote(
                    fulls[number].at[place],
                    fulls[number].at[place],
                    core_send.at[number, path, arrived - 1],
                    core_recv.at[number, path, arrived - 1],
                    "wide",
                    sibling,
                )
                copy.start()
                sends.append(copy)

    def from_sibling(number):
        for path in range(2):
            for mask in range(1, n_narrow):
                place = region(number, flipped(here, mask, n_bits), 1 - core, path)
                remote(
                    fulls[number].at[place],
                    fulls[number].at[place],
                    core_send.at[number, path, mask - 1],
                    core_recv.at[number, path, mask - 1],
                    "wide",
                    sibling,
                ).wait_recv()

    def cast_rows(source, target):
        def cast(index, carry):
            span = pl.ds(pl.multiple_of(index * 16, 16), 16)
            target[span, :] = source[span, :].astype(bf16)
            return carry

        lax.fori_loop(0, source.shape[0] // 16, cast, 0)

    keeps = []

    def begin(number):
        loads[number].wait()
        rows = shards[number].shape[0]
        cast_rows(wides[number], lows[number])
        keep = pltpu.make_async_copy(
            lows[number],
            fulls[number].at[pl.ds(pl.multiple_of(here * rows, 16), rows)],
            keep_sem.at[number],
        )
        keep.start()
        keeps.append(keep)
        for step in range(n_bits):
            narrow_step(number, step, True)

    places = hop_order(n_wide, n_narrow)

    def info_copy(position):
        axis, bit, bits = places[position]
        width = 1 << position
        base = slot // width * width
        return remote(
            info_all.at[pl.ds(base, width)],
            info_all.at[pl.ds(base, width)],
            info_send.at[position],
            info_recv.at[position],
            axis,
            flipped(lax.axis_index(axis), 1 << bit, bits),
        )

    info_own.wait()
    info_copy(0).start()
    begin(0)
    for position in range(len(places)):
        info_copy(position).wait()
        if position + 1 < len(places):
            info_copy(position + 1).start()
        if position + 1 < count:
            begin(position + 1)
    for number in range(len(places) + 1, count):
        begin(number)

    def pass_on(numbers, step):
        for number in numbers:
            arrive(number, step)
            if step + 1 < n_bits:
                narrow_step(number, step + 1, False)

    for step in range(n_bits):
        pass_on([0], step)
    from_sibling(0)
    keeps[0].wait()

    height = shards[0].shape[0]
    reached = 0
    for number in range(n_narrow):
        start = shard_start(number, shard)
        overlap = max(reached - start, 0)
        block = number * height
        if overlap:
            flat[start:reached, :] = (
                flat[start:reached, :].astype(f32)
                + gathered[block : block + overlap, :].astype(f32)
            ).astype(bf16)
        flat[start + overlap : start + height, :] = gathered[block + overlap : block + height, :]
        reached = start + height
    if reached < flat.shape[0]:
        flat[reached:, :] = jnp.zeros((flat.shape[0] - reached, WIDTH), bf16)

    devices = n_wide * n_narrow
    for number in range(devices):
        sheet[number * images : (number + 1) * images, :] = info_all[number, :images, :]
    weights = sheet[:, FREQS + 1 : FREQS + 2]
    total_ref[...] = jnp.sum(weights, axis=0, keepdims=True)
    tail = flat[ROW_TAIL : ROW_TAIL + TAIL, :].astype(f32)
    tail_out[...] = tail
    patch_out[...] = flat[ROW_PATCH:ROW_TIME_ONE, :]
    time_two_out[...] = flat[ROW_TIME_TWO:ROW_TABLE, :]
    last = flat[ROW_FINAL - 9 : ROW_FINAL + 23, :].astype(f32)
    final_out[...] = last[9 : 9 + PATCH]
    tail_row = ROW_BIAS - ROW_TAIL
    value = dot(sheet[:, :FREQS].astype(bf16), flat[ROW_TIME_ONE:ROW_TIME_TWO, :])
    value = value + tail[tail_row + 1 : tail_row + 2]
    time_pre[...] = value
    act = jax.nn.silu(value).astype(bf16)
    value = dot(act, flat[ROW_TIME_TWO:ROW_TABLE, :]) + tail[tail_row + 2 : tail_row + 3]
    labels = lax.broadcasted_iota(jnp.int32, (sheet.shape[0], 1008), 1).astype(f32)
    pick = jnp.where(sheet[:, FREQS : FREQS + 1] == labels, 1.0, 0.0).astype(bf16)
    value = value + dot(pick, flat[ROW_TABLE : ROW_TABLE + 1008, :])
    condition[...] = value
    act = own_columns(jax.nn.silu(value), n_narrow)
    act = act.astype(bf16)
    own_act[...] = act

    loads[count].wait()
    cast_rows(adaptive_wide, adaptive_low)
    row = lax.broadcasted_iota(jnp.int32, (8 * n_narrow, act.shape[0]), 0)
    column = lax.broadcasted_iota(jnp.int32, (8 * n_narrow, act.shape[0]), 1)
    owner = there // 2 + n_wide // 2 * (row // 8 + n_narrow * core)
    chosen = jnp.logical_and(column == owner * images + row % 8, row % 8 < images)
    near = dot(jnp.where(chosen, 1.0, 0.0).astype(bf16), act).astype(bf16)
    for index in range(8):
        span = slice(index * WIDTH, (index + 1) * WIDTH)
        value = dot(near, adaptive_low[:, span])
        for number in range(n_narrow):
            part[0, number, :, span] = value[8 * number : 8 * number + 8]

    def lay_bases():
        place = 0
        for ref in left_refs:
            blocks = ref.shape[0]
            lefts_out[place : place + blocks * BLOCK, :] = ref[...].reshape(-1, BLOCK)
            place = place + blocks * BLOCK
        place = 0
        for matrix, ref in enumerate(right_refs):
            turning = bases_along_lanes(ref.shape)
            blocks = ref.shape[2] if turning else ref.shape[0]
            copies = TILES[matrix][1]
            for row in range(BLOCK):
                turned[0:blocks, :] = ref[row].T if turning else ref[:, row, :]
                value = jnp.concatenate(
                    [turned[pl.ds(spot, blocks // 4, stride=4), :] for spot in range(4)], axis=1
                )
                for copy in range(copies):
                    start = place + copy * blocks // 4 * BLOCK + row
                    rights_out[pl.ds(start, blocks // 4, stride=BLOCK), :] = value
            place = place + copies * blocks // 4 * BLOCK

    def part_copy(step, mask):
        bit = 1 << step
        return remote(
            part.at[step, flipped(here, mask, n_bits)],
            part_in.at[step, flipped(here, mask, n_bits)],
            part_send.at[step, mask],
            part_recv.at[step, mask],
            "narrow",
            flipped(here, bit, n_bits),
        )

    def part_back(step, mask):
        bit = 1 << step
        owner = flipped(here, mask - bit, n_bits)
        return remote(
            part_in.at[step, owner],
            part_in.at[step, owner],
            part_send.at[step, mask],
            part_recv.at[step, mask],
            "narrow",
            flipped(here, bit, n_bits),
        ), owner

    for step in range(n_bits):
        bit = 1 << step
        masks = [
            mask for mask in range(n_narrow) if mask & bit and not mask & (bit - 1)
        ]
        for mask in masks:
            copy = part_copy(step, mask)
            copy.start()
            sends.append(copy)
        pass_on(range(1, count), step)
        if step == 0:
            lay_bases()
        for mask in masks:
            back, owner = part_back(step, mask)
            back.wait_recv()
            if step + 1 < n_bits:
                part[step + 1, owner] = part[step, owner] + part_in[step, owner]
            else:
                value = part[step, owner] + part_in[step, owner]
                for image in range(images):
                    for index in range(8):
                        mods_ref[image, index : index + 1, :] = (
                            value[image : image + 1, index * WIDTH : (index + 1) * WIDTH]
                            + tail[tail_row + 9 + index : tail_row + 10 + index]
                        )

    for number in range(1, count):
        from_sibling(number)
    for keep in keeps[1:]:
        keep.wait()
    for copy in sends:
        copy.wait_send()


def gather_all(n_wide, n_narrow, images, shard, shards, adaptive, info, lefts, rights):
    count = len(shards)
    any_space = pl.BlockSpec(memory_space=pl.ANY)
    vmem = pl.BlockSpec(memory_space=pltpu.VMEM)
    devices = n_wide * n_narrow
    n_bits = bits_of(n_narrow)
    rows = adaptive.shape[0]
    dma = pltpu.SemaphoreType.DMA
    total = devices * images
    return pl.pallas_call(
        partial(gather_kernel, n_wide, n_narrow, images, shard),
        in_specs=[any_space] * (count + 2) + [vmem] * 10,
        out_specs=[any_space] * (count - 1) + [vmem] * 13,
        out_shape=[
            jax.ShapeDtypeStruct((piece.shape[0] * n_narrow, piece.shape[1]), bf16)
            for piece in shards[1:]
        ]
        + [
            jax.ShapeDtypeStruct((PATCH, WIDTH), bf16),
            jax.ShapeDtypeStruct((PATCH, WIDTH), f32),
            jax.ShapeDtypeStruct((TAIL, WIDTH), f32),
            jax.ShapeDtypeStruct((WIDTH, WIDTH), bf16),
            jax.ShapeDtypeStruct((total, SHEET), f32),
            jax.ShapeDtypeStruct((total, WIDTH), f32),
            jax.ShapeDtypeStruct((total, WIDTH), f32),
            jax.ShapeDtypeStruct((total, rows), bf16),
            jax.ShapeDtypeStruct(adaptive.shape, bf16),
            jax.ShapeDtypeStruct((images, 8, WIDTH), f32),
            jax.ShapeDtypeStruct((1, 1), f32),
            jax.ShapeDtypeStruct((8 * rows, BLOCK), f32),
            jax.ShapeDtypeStruct((len(tile_places()) * 6 * BLOCK, 4 * BLOCK), f32),
        ],
        scratch_shapes=[pltpu.VMEM((shards[0].shape[0] * n_narrow, WIDTH), bf16)]
        + [pltpu.VMEM(piece.shape, f32) for piece in shards]
        + [pltpu.VMEM(piece.shape, bf16) for piece in shards]
        + [
            pltpu.VMEM((flat_rows(n_narrow, shard), WIDTH), bf16),
            pltpu.VMEM((8 * WIDTH // BLOCK, BLOCK), f32),
            pltpu.VMEM(adaptive.shape, f32),
            pltpu.VMEM((devices,) + info.shape[1:], f32),
            pltpu.VMEM((n_bits, n_narrow, 8, 8 * WIDTH), f32),
            pltpu.VMEM((n_bits, n_narrow, 8, 8 * WIDTH), f32),
            dma((count + 1,)),
            dma((count,)),
            dma((count, 2, n_narrow - 1)),
            dma((count, 2, n_narrow - 1)),
            dma((count, 2, n_narrow - 1)),
            dma((count, 2, n_narrow - 1)),
            dma,
            dma((bits_of(devices),)),
            dma((bits_of(devices),)),
            dma((n_bits, n_narrow)),
            dma((n_bits, n_narrow)),
        ],
        compiler_params=pltpu.CompilerParams(
            collective_id=0, has_side_effects=True, vmem_limit_bytes=56 * 1024 * 1024
        ),
        name="gather_weights",
    )(*shards, adaptive, info, *lefts, *rights)


RING = 4


def reduce_kernel(n_wide, n_narrow, images, shard, *refs):
    grad_refs = refs[:4]
    (
        g_mods_ref,
        g_patch_ref,
        g_final_ref,
        g_bias_ref,
        adaptive_low,
        sheet,
        time_pre,
        condition,
        own_act,
        time_two,
        lefts,
        rights,
    ) = refs[4:16]
    turned_out, rows_out, window_out, totals_out, clip_out = refs[16:21]
    out_ref = refs[21]
    scratch = refs[22:]
    own, from_core, to_near, from_near, to_far, from_far, acc, acc_far = scratch[:8]
    load_sem, core_sem, near_sem, far_sem, back_sem, last_sem = scratch[8:14]
    (
        mods_all,
        by_mod,
        product_parts,
        first_part,
        biases,
        small_out,
        small_in,
        small_all,
        act_all,
        stage,
        norm_out,
        norm_in,
        squares,
        ring,
        mods_sem,
        mods_near_sem,
        small_sem,
        act_sem,
        rows_sem,
        norm_sem,
        ring_sem,
    ) = scratch[14:]
    here = lax.axis_index("narrow")
    there = lax.axis_index("wide")
    core = there % 2
    n_bits = bits_of(n_narrow)
    w_bits = bits_of(n_wide)
    far_steps = w_bits - 1
    sibling = flipped(there, 1, w_bits)
    chunks, _, half, width = out_ref.shape
    side = width // 2

    leaving = []
    for path in range(2):
        done = 0
        place = 0
        steps = []
        for step in range(n_bits):
            bit = 1 << route(path, step, n_bits)
            masks = [mask for mask in range(n_narrow) if mask & bit and not mask & done]
            steps.append((bit, {mask: place + spot for spot, mask in enumerate(masks)}))
            place = place + len(masks)
            done = done | bit
        leaving.append(steps)

    parts = [(0, half, 0, width)]
    gives = []
    for step in range(far_steps):
        low, rows, left, cols = parts[-1]
        mine = there // (2 << step) % 2
        if rows % 32 == 0:
            keep = (low + mine * (rows // 2), rows // 2, left, cols)
            give = (low + (1 - mine) * (rows // 2), rows // 2, left, cols)
        elif cols % 256 == 0:
            keep = (low, rows, left + mine * (cols // 2), cols // 2)
            give = (low, rows, left + (1 - mine) * (cols // 2), cols // 2)
        else:
            keep = parts[-1]
            give = parts[-1]
        parts.append(keep)
        gives.append(give)
    traded = [gives[step] is not parts[step] for step in range(far_steps)]

    def window(part):
        low, rows, left, cols = part
        if not isinstance(low, int):
            low = pl.multiple_of(low, 16)
        if not isinstance(left, int):
            left = pl.multiple_of(left, 128)
        return (pl.ds(low, rows), pl.ds(left, cols))

    def keep_copy(k, grad_ref, first):
        start = pl.multiple_of((k - first) * 2 * half + core * half, 16)
        return pltpu.make_async_copy(
            grad_ref.at[:, pl.ds(start, half), :], own.at[k % RING], load_sem.at[k]
        )

    def start_keep(k):
        first = 0
        for grad_ref in grad_refs:
            tiles = grad_ref.shape[1] // (2 * half)

            @pl.when(jnp.logical_and(k >= first, k < first + tiles))
            def _(grad_ref=grad_ref, first=first):
                keep_copy(k, grad_ref, first).start()

            first = first + tiles

    def give_copy(k, grad_ref, first):
        start = pl.multiple_of((k - first) * 2 * half + (1 - core) * half, 16)
        return remote(
            grad_ref.at[:, pl.ds(start, half), :],
            from_core.at[k],
            core_sem.at[0, k],
            core_sem.at[1, k],
            "wide",
            sibling,
        )

    def near_copy(path, k, step):
        bit, masks = leaving[path][step]
        spots = pl.ds(min(masks.values()), len(masks))
        return remote(
            to_near.at[path, k % RING, spots],
            from_near.at[path, k, spots],
            near_sem.at[0, path, k, step],
            near_sem.at[1, path, k, step],
            "narrow",
            flipped(here, bit, n_bits),
        )

    def far_copy(k, step, part):
        return remote(
            to_far.at[(k % RING, step) + window(part)],
            from_far.at[(k, step) + window(part)],
            far_sem.at[0, k, step],
            far_sem.at[1, k, step],
            "wide",
            flipped(there, 2 << step, w_bits),
        )

    def back_copy(k, step, part):
        place = (k, core) + window(part)
        return remote(
            out_ref.at[place],
            out_ref.at[place],
            back_sem.at[0, k, step],
            back_sem.at[1, k, step],
            "wide",
            flipped(there, 2 << step, w_bits),
        )

    def last_copy(k, side_of):
        return remote(
            out_ref.at[k, side_of],
            out_ref.at[k, side_of],
            last_sem.at[0, k],
            last_sem.at[1, k],
            "wide",
            sibling,
        )

    def place_near(path, k, step, mask, total):
        columns = pl.ds(path * side, side)
        ring_slot = k % RING
        if step == n_bits:
            acc_far[ring_slot, :, columns] = total
        elif mask in leaving[path][step][1]:
            to_near[path, ring_slot, leaving[path][step][1][mask]] = total.astype(bf16)
        else:
            acc[ring_slot, mask, :, columns] = total

    def before(k, wait):
        @pl.when(k >= RING)
        def _():
            wait()

    def stage_core(k):
        keep_copy(k, grad_refs[0], k).wait()
        give_copy(k, grad_refs[0], k).wait_recv()
        for path in range(2):
            before(k, lambda path=path: near_copy(path, k - RING, 0).wait_send())
            columns = pl.ds(path * side, side)
            for mask in range(n_narrow):
                owner = flipped(here, mask, n_bits)
                total = own[k % RING, owner, :, columns].astype(f32) + from_core[
                    k, owner, :, columns
                ].astype(f32)
                place_near(path, k, 0, mask, total)
            near_copy(path, k, 0).start()
        start_keep(k + RING - 1)

    def stage_near(step, k):
        ring_slot = k % RING
        for path in range(2):
            columns = pl.ds(path * side, side)
            near_copy(path, k, step).wait_recv()
            if step + 1 < n_bits:
                before(k, lambda path=path: near_copy(path, k - RING, step + 1).wait_send())
            bit, masks = leaving[path][step]
            for mask, spot in masks.items():
                total = acc[ring_slot, mask - bit, :, columns] + from_near[path, k, spot].astype(f32)
                place_near(path, k, step + 1, mask - bit, total)
            if step + 1 < n_bits:
                near_copy(path, k, step + 1).start()
        if step + 1 == n_bits:
            start_far(0, k)

    def start_far(step, k):
        ring_slot = k % RING
        if step < far_steps:
            place = window(gives[step])
            before(k, lambda: far_copy(k - RING, step, gives[step]).wait_send())
            to_far[(ring_slot, step) + place] = acc_far[(ring_slot,) + place].astype(bf16)
            far_copy(k, step, gives[step]).start()
        else:
            place = window(parts[step])
            out_ref[(k, core) + place] = acc_far[(ring_slot,) + place].astype(bf16)
            start_back(far_steps - 1, k)

    def stage_far(step, k):
        ring_slot = k % RING
        far_copy(k, step, parts[step + 1]).wait_recv()
        place = window(parts[step + 1])
        if traded[step]:
            mine = acc_far[(ring_slot,) + place]
        else:
            mine = to_far[(ring_slot, step) + place].astype(f32)
        acc_far[(ring_slot,) + place] = mine + from_far[(k, step) + place].astype(f32)
        start_far(step + 1, k)

    def start_back(step, k):
        while step >= 0 and not traded[step]:
            step = step - 1
        if step >= 0:
            back_copy(k, step, parts[step + 1]).start()
        else:
            last_copy(k, core).start()

    def stage_back(step, k):
        back_copy(k, step, gives[step]).wait_recv()
        start_back(step - 1, k)

    def add_squares(value):
        squares[...] += jnp.sum(value * value, axis=0, keepdims=True)

    def turned_copy(slot, tile):
        return pltpu.make_async_copy(ring.at[slot], turned_out.at[tile], ring_sem.at[slot])

    def turn(high, rest, stack, tile, slot, used):
        @pl.when(used)
        def _():
            turned_copy(slot, tile).wait()

        left, left_rest = spread_left(lefts[stack])
        for start in range(0, WIDTH, STRIP):
            span = slice(start, start + STRIP)
            group = tile * (WIDTH // BLOCK // 4) + start // BLOCK // 4
            right, right_rest = halves(spread_right(rights[group], rights[group + 1]))
            value = dot(high[:, span], right) + dot(high[:, span], right_rest)
            if rest is not None:
                value = value + dot(rest[:, span], right)
            part, part_rest = halves(value)
            ring[slot, :, span] = dot_s(left, part) + (
                dot_s(left_rest, part) + dot_s(left, part_rest)
            )
        turned_copy(slot, tile).start()

    def stage_last(k):
        last_copy(k, 1 - core).wait_recv()
        for number in range(2):
            add_squares(out_ref[k, number].astype(f32))
        value = out_ref[k].reshape(2 * half, width)
        turn(value, None, left_number(k), k, k % 2, k >= 2)

    stages = [stage_core]
    stages += [partial(stage_near, step) for step in range(n_bits)]
    stages += [partial(stage_far, step) for step in range(far_steps)]
    stages += [partial(stage_back, step) for step in reversed(range(far_steps)) if traded[step]]
    stages += [stage_last]

    places = hop_order(n_wide, n_narrow)
    near_places = [("narrow", bit, n_bits) for bit in range(n_bits)]
    hops = len(places)
    slot = slot_of(n_wide, n_narrow)
    count = n_wide * n_narrow * images

    def beside(axis, bit, bits, source, target, sem, position):
        return remote(
            source,
            target,
            sem.at[0, position],
            sem.at[1, position],
            axis,
            flipped(lax.axis_index(axis), 1 << bit, bits),
        )

    column_bits = n_wide // 2
    half_rows = small_out.shape[1] // 2
    own_rows = pl.ds(pl.multiple_of(half_rows * core, 8), half_rows)
    small_places = places[hops - 1 :] + places[: hops - 1]

    def mods_copy(position):
        width = 1 << position
        block = mods_all.at[pl.ds(slot // width * width, width)]
        return beside(*places[position], block, block, mods_sem, position)

    def mods_near(path, step, mask, arrived):
        owner = flipped(here, arrived if mask is None else mask, n_bits)
        bit = 1 << route(path, step, n_bits)
        block = mods_all.at[
            pl.ds(column_bits * (owner + n_narrow * core), column_bits),
            :,
            pl.ds(path * side, side),
        ]
        return remote(
            block,
            block,
            mods_near_sem.at[0, path, arrived - 1],
            mods_near_sem.at[1, path, arrived - 1],
            "narrow",
            flipped(here, bit, n_bits),
        )

    def near_masks(path, step):
        done = sum(1 << route(path, earlier, n_bits) for earlier in range(step))
        bit = 1 << route(path, step, n_bits)
        return [(mask, mask | bit) for mask in range(n_narrow) if not mask & ~done]

    def small_copy(position):
        if position == 0:
            return beside(
                *small_places[0], small_out.at[0], small_in.at[0], small_sem, position
            )
        if position == hops:
            block = small_all.at[own_rows]
            return beside(*small_places[0], block, block, small_sem, position)
        return beside(
            *small_places[position],
            small_out.at[position, own_rows],
            small_in.at[position, own_rows],
            small_sem,
            position,
        )

    def act_copy(position):
        width = 1 << position
        block = act_all.at[pl.ds(here // width * width, width)]
        return beside(*near_places[position], block, block, act_sem, position)

    def small_total():
        return small_all[...]

    def rows_copy(start, rows, position):
        return pltpu.make_async_copy(
            stage.at[pl.ds(0, rows)], rows_out.at[pl.ds(start, rows)], rows_sem.at[position]
        )

    height = window_out.shape[0]

    def window_copy():
        start = here * shard // (WIDTH * ALIGN) * ALIGN
        return pltpu.make_async_copy(
            rows_out.at[pl.ds(pl.multiple_of(start, ALIGN), height)], window_out, rows_sem.at[2]
        )

    def mods_hop(position):
        if position == 0:
            mods_all[slot] = g_mods_ref[...].astype(bf16)
        elif position <= far_steps or position == hops:
            mods_copy(position - 1).wait_recv()
        else:
            step = position - 1 - far_steps
            for path in range(2):
                for _, arrived in near_masks(path, step):
                    mods_near(path, step, None, arrived).wait_recv()
        if position < far_steps or position == hops - 1:
            mods_copy(position).start()
        elif position < hops:
            step = position - far_steps
            for path in range(2):
                for mask, arrived in near_masks(path, step):
                    mods_near(path, step, mask, arrived).start()

    def small_hop(position):
        if position == 0:
            small_out[0, 0:PATCH] = g_patch_ref[...]
            small_out[0, PATCH : 2 * PATCH] = g_final_ref[...]
            small_out[0, 2 * PATCH : 2 * PATCH + 8] = g_bias_ref[...]
            small_out[0, 2 * PATCH + 8 :] = jnp.zeros(
                (small_out.shape[1] - 2 * PATCH - 8, WIDTH), f32
            )
        else:
            small_copy(position - 1).wait_recv()
            total = small_out[position - 1, own_rows] + small_in[position - 1, own_rows]
            if position < hops:
                small_out[position, own_rows] = total
            else:
                small_all[own_rows] = total
        small_copy(position).start()

    def small_end():
        other = pl.ds(pl.multiple_of(half_rows * (1 - core), 8), half_rows)
        block = small_all.at[other]
        beside(*small_places[0], block, block, small_sem, hops).wait_recv()

    def sort_mods():
        together = 8
        size = together * images * 8
        row = lax.broadcasted_iota(jnp.int32, (size, size), 0)
        column = lax.broadcasted_iota(jnp.int32, (size, size), 1)
        span = together * images
        order = jnp.where(column == row % span * 8 + row // span, 1.0, 0.0).astype(bf16)
        for block in range(mods_all.shape[0] // together):
            value = mods_all[block * together : (block + 1) * together].reshape(size, WIDTH)
            value = dot(order, value).astype(bf16)
            for index in range(8):
                by_mod[index, block * span : (block + 1) * span, :] = value[
                    index * span : (index + 1) * span
                ]

    def send_act():
        sort_mods()
        total = jnp.zeros(act_all.shape[1:], f32)
        for index in range(8):
            span = slice(index * WIDTH, (index + 1) * WIDTH)
            total = total + dot_t(by_mod[index], adaptive_low[:, span])
        act_all[here] = total
        act_copy(0).start()

    def act_hop(position):
        act_copy(position - 1).wait_recv()
        if position < n_bits:
            act_copy(position).start()

    def start_rows():
        grad = jnp.concatenate([act_all[number] for number in range(n_narrow)], axis=1)
        grad = grad * silu_slope(condition[...])
        high, rest = halves(grad)
        before = time_pre[...]
        first = (dot_t(high, time_two[...]) * silu_slope(before)).astype(bf16)
        product_parts[0:count] = high
        product_parts[count : 2 * count] = rest
        first_part[...] = first
        biases[0:1, :] = jnp.sum(first.astype(f32), axis=0, keepdims=True)
        biases[1:2, :] = jnp.sum(high.astype(f32), axis=0, keepdims=True)

    def upper_rows():
        stage[0:PATCH, :] = small_total()[0:PATCH]
        stage[ROW_TIME_ONE:ROW_TIME_TWO, :] = dot_s(
            sheet[:, :FREQS].astype(bf16), first_part[...]
        )
        act = jax.nn.silu(time_pre[...]).astype(bf16)
        stage[ROW_TIME_TWO:ROW_TABLE, :] = dot_s(act, product_parts[0:count])
        rows_copy(0, ROW_TABLE, 0).start()

    def table_rows(half_of):
        if half_of == 0:
            rows_copy(0, ROW_TABLE, 0).wait()
        size = 504
        labels = lax.broadcasted_iota(jnp.int32, (count, size), 1) + half_of * size
        pick = jnp.where(sheet[:, FREQS : FREQS + 1] == labels.astype(f32), 1.0, 0.0)
        pick = pick.astype(bf16)
        pick = jnp.concatenate([pick, pick], axis=0)
        stage[half_of * size : (half_of + 1) * size, :] = dot_s(pick, product_parts[...])

    def lower_rows():
        small = small_total()
        base = ROW_FINAL - ROW_TABLE
        stage[base : base + PATCH, :] = small[PATCH : 2 * PATCH]
        base = ROW_BIAS - ROW_TABLE
        bias = small[2 * PATCH : 2 * PATCH + 8]
        stage[base : base + 1, :] = bias[0:1]
        stage[base + 1 : base + 3, :] = biases[0:2, :]
        stage[base + 3 : base + 4, :] = bias[1:2]
        stage[base + 4 : base + 8, :] = bias[4:8]
        stage[base + 8 : base + 9, :] = bias[2:3]
        for index in range(8):
            stage[base + 9 + index : base + 10 + index, :] = jnp.sum(
                by_mod[index].astype(f32), axis=0, keepdims=True
            )
        lane = lax.broadcasted_iota(jnp.int32, (1, WIDTH), 1)
        stage[base + 17 : base + 18, :] = jnp.where(lane < PATCH, bias[3:4], 0.0)
        stage[base + 18 :, :] = jnp.zeros((stage.shape[0] - base - 18, WIDTH), f32)
        totals_out[...] = bias
        rows_copy(ROW_TABLE, stage.shape[0], 1).start()

    first_turn = chunks

    def adaptive_columns(index):
        value = dot_s(own_act[...], by_mod[index])
        add_squares(value)
        high, rest = halves(value)
        turn(high, rest, lefts.shape[0] - 1, first_turn + index, 2 + index % 2, index >= 2)

    def start_window():
        rows_copy(ROW_TABLE, stage.shape[0], 1).wait()
        window_copy().start()

    def window_squares():
        window_copy().wait()
        start = here * shard // (WIDTH * ALIGN) * ALIGN
        first = here * shard - start * WIDTH
        value = window_out[...]
        spot = (
            lax.broadcasted_iota(jnp.int32, value.shape, 0) * WIDTH
            + lax.broadcasted_iota(jnp.int32, value.shape, 1)
        )
        inside = jnp.logical_and(spot >= first, spot < first + shard)
        add_squares(jnp.where(inside, value, 0.0))

    def together(*steps):
        return lambda: [step() for step in steps]

    asides = [
        together(partial(mods_hop, position), partial(small_hop, position))
        for position in range(hops)
    ]
    asides += [together(partial(mods_hop, hops), partial(small_hop, hops), send_act)]
    first_act = len(asides)
    asides += [partial(act_hop, position) for position in range(1, n_bits)]
    asides[-1] = together(asides[-1], small_end)
    asides += [
        together(partial(act_hop, n_bits), start_rows),
        upper_rows,
        partial(table_rows, 0),
        partial(table_rows, 1),
        lower_rows,
        start_window,
        window_squares,
    ]

    squares[...] = jnp.zeros_like(squares)
    greet(n_wide, n_narrow)
    first = 0
    for grad_ref in grad_refs:
        tiles = grad_ref.shape[1] // (2 * half)

        def begin(k, carry, grad_ref=grad_ref, first=first):
            give_copy(k, grad_ref, first).start()
            return carry

        lax.fori_loop(first, first + tiles, begin, 0)
        first = first + tiles
    for k in range(RING - 1):
        start_keep(jnp.int32(k))

    def wave(t, carry):
        for number, stage in enumerate(stages):
            k = t - number

            @pl.when(jnp.logical_and(k >= 0, k < chunks))
            def _(stage=stage, k=k):
                stage(k)

        for number, aside in enumerate(asides):

            @pl.when(t == number)
            def _(aside=aside):
                aside()

        index = t - first_act

        @pl.when(jnp.logical_and(index >= 0, index < 8))
        def _():
            adaptive_columns(index)

        return carry

    lax.fori_loop(0, max(chunks + len(stages) - 1, len(asides), first_act + 8), wave, 0)

    def finish(k, carry):
        give_copy(k, grad_refs[0], k).wait_send()
        for step in range(far_steps):
            if traded[step]:
                back_copy(k, step, parts[step + 1]).wait_send()
        last_copy(k, core).wait_send()
        return carry

    lax.fori_loop(0, chunks, finish, 0)

    def finish_ring(k, carry):
        for path in range(2):
            for step in range(n_bits):
                near_copy(path, k, step).wait_send()
        for step in range(far_steps):
            far_copy(k, step, gives[step]).wait_send()
        return carry

    lax.fori_loop(chunks - RING, chunks, finish_ring, 0)
    for position in [*range(far_steps), hops - 1]:
        mods_copy(position).wait_send()
    for path in range(2):
        for step in range(n_bits):
            for mask, arrived in near_masks(path, step):
                mods_near(path, step, mask, arrived).wait_send()
    for position in range(hops + 1):
        small_copy(position).wait_send()
    for position in range(n_bits):
        act_copy(position).wait_send()
    for slot_of_ring in range(4):
        turned_copy(slot_of_ring, 0).wait()

    total = jnp.sum(squares[...], axis=1, keepdims=True)
    value = jnp.broadcast_to(total, norm_out.shape[1:])
    for position in range(n_bits):
        norm_out[position] = value
        copy = beside(
            *near_places[position],
            norm_out.at[position],
            norm_in.at[position],
            norm_sem,
            position,
        )
        copy.start()
        copy.wait()
        value = value + norm_in[position]
    norm = jnp.sqrt(value)
    row = lax.broadcasted_iota(jnp.int32, value.shape, 0)
    clip_out[...] = jnp.where(row == 0, norm, clip_limit / jnp.maximum(norm, clip_limit))


def reduce_all(n_wide, n_narrow, images, shard, grads, asides):
    rows = WIDTH // n_narrow
    chunks = sum(grad.shape[1] for grad in grads) // rows
    half = rows // 2
    far = bits_of(n_wide) - 1
    devices = n_wide * n_narrow
    hops = bits_of(devices)
    count = devices * images
    dma = pltpu.SemaphoreType.DMA
    any_space = pl.BlockSpec(memory_space=pl.ANY)
    vmem = pl.BlockSpec(memory_space=pltpu.VMEM)
    height = flat_rows(n_narrow, shard)
    turned, _, window, totals, clip = pl.pallas_call(
        partial(reduce_kernel, n_wide, n_narrow, images, shard),
        in_specs=[any_space] * 4 + [vmem] * len(asides),
        out_specs=[any_space, any_space, vmem, vmem, vmem],
        out_shape=[
            jax.ShapeDtypeStruct((chunks + 8, rows, WIDTH), f32),
            jax.ShapeDtypeStruct((height, WIDTH), f32),
            jax.ShapeDtypeStruct((shard_rows(shard), WIDTH), f32),
            jax.ShapeDtypeStruct((8, WIDTH), f32),
            jax.ShapeDtypeStruct((8, 128), f32),
        ],
        scratch_shapes=[
            pltpu.VMEM((chunks, 2, half, WIDTH), bf16),
            pltpu.VMEM((RING, n_narrow, half, WIDTH), bf16),
            pltpu.VMEM((chunks, n_narrow, half, WIDTH), bf16),
            pltpu.VMEM((2, RING, n_narrow - 1, half, WIDTH // 2), bf16),
            pltpu.VMEM((2, chunks, n_narrow - 1, half, WIDTH // 2), bf16),
            pltpu.VMEM((RING, far, half, WIDTH), bf16),
            pltpu.VMEM((chunks, far, half, WIDTH), bf16),
            pltpu.VMEM((RING, n_narrow, half, WIDTH), f32),
            pltpu.VMEM((RING, half, WIDTH), f32),
            dma((chunks,)),
            dma((2, chunks)),
            dma((2, 2, chunks, bits_of(n_narrow))),
            dma((2, chunks, far)),
            dma((2, chunks, far)),
            dma((2, chunks)),
            pltpu.VMEM((devices, images * 8, WIDTH), bf16),
            pltpu.VMEM((8, count, WIDTH), bf16),
            pltpu.VMEM((2 * count, WIDTH), bf16),
            pltpu.VMEM((count, WIDTH), bf16),
            pltpu.VMEM((8, WIDTH), f32),
            pltpu.VMEM((hops, 3 * PATCH, WIDTH), f32),
            pltpu.VMEM((hops, 3 * PATCH, WIDTH), f32),
            pltpu.VMEM((3 * PATCH, WIDTH), f32),
            pltpu.VMEM((n_narrow, count, rows), f32),
            pltpu.VMEM((height - ROW_TABLE, WIDTH), f32),
            pltpu.VMEM((bits_of(n_narrow), 8, 128), f32),
            pltpu.VMEM((bits_of(n_narrow), 8, 128), f32),
            pltpu.VMEM((1, WIDTH), f32),
            pltpu.VMEM((4, rows, WIDTH), f32),
            dma((2, hops)),
            dma((2, 2, n_narrow - 1)),
            dma((2, hops + 1)),
            dma((2, bits_of(n_narrow))),
            dma((3,)),
            dma((2, bits_of(n_narrow))),
            dma((4,)),
        ],
        compiler_params=pltpu.CompilerParams(
            collective_id=1, has_side_effects=True, vmem_limit_bytes=62 * 1024 * 1024
        ),
        cost_estimate=pl.CostEstimate(
            flops=10**8, bytes_accessed=300 * 10**6, transcendentals=0
        ),
        name="reduce_gradients",
    )(*grads, *asides)
    return turned, window, totals, clip


def weight_kernel(*refs):
    lefts, rights, outs = refs[0:4], refs[4:8], refs[8:12]
    taken, given, take_sem, give_sem = refs[12:]
    _, pieces, rows, _ = given.shape
    units = [
        (matrix, number)
        for matrix in range(4)
        for number in range(max(lefts[matrix].shape[1], rights[matrix].shape[1]) // WIDTH)
    ]

    def takes(unit):
        matrix, number = units[unit]
        copies = []
        for side, ref in enumerate((lefts[matrix], rights[matrix])):
            start = number * WIDTH if ref.shape[1] > WIDTH else 0
            copies.append(
                pltpu.make_async_copy(
                    ref.at[:, pl.ds(start, WIDTH)],
                    taken.at[unit % 3, side],
                    take_sem.at[unit % 3, side],
                )
            )
        return copies

    def give(unit):
        matrix, number = units[unit]
        if matrix < 3:
            target = outs[matrix].at[:, pl.ds(number * rows, rows), :]
        else:
            target = outs[3].at[pl.ds(number * pieces, pieces)]
        return pltpu.make_async_copy(given.at[unit % 2], target, give_sem.at[unit % 2])

    def given_out(slot):
        pltpu.make_async_copy(given.at[slot], given.at[slot], give_sem.at[slot]).wait()

    for unit in range(2):
        for copy in takes(unit):
            copy.start()

    def body(step, carry):
        for unit in range(2, len(units)):

            @pl.when(step + 2 == unit)
            def _(unit=unit):
                for copy in takes(unit):
                    copy.start()

        slot = step % 3
        out = step % 2
        for side in range(2):
            buffer = taken.at[slot, side]
            pltpu.make_async_copy(buffer, buffer, take_sem.at[slot, side]).wait()

        @pl.when(step >= 2)
        def _():
            given_out(out)

        for start in range(0, WIDTH, STRIP):
            span = slice(start, start + STRIP)
            value = dot_s(taken[slot, 0], taken[slot, 1, :, span]).astype(bf16)
            given[out, :, :, span] = value.reshape(pieces, rows, STRIP)
        for unit in range(len(units)):

            @pl.when(step == unit)
            def _(unit=unit):
                give(unit).start()

        return carry

    lax.fori_loop(0, len(units), body, 0)
    for slot in range(2):
        given_out(slot)


def weight_blocks(n_narrow, inputs, gradients):
    rows = WIDTH // n_narrow
    tokens = inputs[0].shape[0]
    any_space = pl.BlockSpec(memory_space=pl.ANY)
    shapes = [(n_narrow, gradient.shape[1] // n_narrow, WIDTH) for gradient in gradients[:3]]
    shapes.append((inputs[3].shape[1] // rows, rows, WIDTH))
    dma = pltpu.SemaphoreType.DMA
    results = pl.pallas_call(
        weight_kernel,
        in_specs=[any_space] * 8,
        out_specs=[any_space] * 4,
        out_shape=[jax.ShapeDtypeStruct(shape, bf16) for shape in shapes],
        scratch_shapes=[
            pltpu.VMEM((3, 2, tokens, WIDTH), bf16),
            pltpu.VMEM((2, n_narrow, rows, WIDTH), bf16),
            dma((3, 2)),
            dma((2,)),
        ],
        compiler_params=pltpu.CompilerParams(vmem_limit_bytes=60 * 1024 * 1024),
        name="weight_gradient",
    )(*inputs, *gradients)
    return [result.reshape(n_narrow, -1, WIDTH) for result in results]


def dot_s(left, right):
    return lax.dot_general(left, right, (((0,), (0,)), ((), ())), preferred_element_type=f32)


def center(hidden):
    centered = hidden - jnp.mean(hidden, axis=-1, keepdims=True)
    scale = lax.rsqrt(jnp.mean(centered * centered, axis=-1, keepdims=True) + 1e-06)
    return centered * scale, scale


def center_back(grad, normal, scale):
    return (
        grad
        - jnp.mean(grad, axis=-1, keepdims=True)
        - normal * jnp.mean(grad * normal, axis=-1, keepdims=True)
    ) * scale


def gelu_pair(value):
    rate = math.sqrt(2.0 / math.pi)
    square = value * value
    bend = jnp.tanh(rate * value * (1.0 + 0.044715 * square))
    half = 0.5 * (1.0 + bend)
    slope = half + 0.5 * value * (1.0 - bend * bend) * (rate * (1.0 + 3.0 * 0.044715 * square))
    return value * half, slope


def layer_kernel(
    numbers,
    latent_ref,
    noise_ref,
    mods_ref,
    place_ref,
    patch_ref,
    final_ref,
    tail_ref,
    attend_ref,
    output_ref,
    expand_ref,
    shrink_ref,
    normed_ref,
    mixed_ref,
    normed_two_ref,
    act_ref,
    g_branch_two_ref,
    g_pre_ref,
    g_branch_ref,
    g_triple_ref,
    g_mods_ref,
    g_patch_ref,
    g_final_ref,
    g_bias_ref,
    triple,
    probs,
    slope,
    normal_one,
    normal_two,
    hidden,
    branch,
    g_mixed,
):
    image = pl.program_id(0)
    tokens = SEQUENCE
    wide = 256

    def bias(index):
        spot = ROW_BIAS - ROW_TAIL + index
        return tail_ref[spot : spot + 1, :]

    def bias_wide(ref, first, index):
        across = WIDTH // wide
        return (
            pl.ds(first + index // across, 1),
            pl.ds(pl.multiple_of(index % across * wide, wide), wide),
        )

    def row(index):
        return mods_ref[0, index : index + 1, :]

    @pl.when(image == 0)
    def _():
        for ref in (g_patch_ref, g_final_ref, g_bias_ref):
            ref[...] = jnp.zeros_like(ref)

    moment = numbers[0, image]
    blended = ((1.0 - moment) * latent_ref[0] + moment * noise_ref[0]).astype(bf16)
    target = noise_ref[0] - latent_ref[0]
    start = dot(blended, patch_ref[...]) + bias(0) + place_ref[...]
    hidden[...] = start
    normal, scale_one = center(start)
    normal_one[...] = normal
    normed_ref[...] = (normal * (1.0 + row(1)) + row(0)).astype(bf16)

    def project(index, carry):
        span = pl.ds(pl.multiple_of(index * wide, wide), wide)
        triple[:, span] = dot(normed_ref[...], attend_ref[:, span]).astype(bf16)
        return carry

    lax.fori_loop(0, 3 * WIDTH // wide, project, 0, unroll=True)

    lane = lax.broadcasted_iota(jnp.int32, (tokens, 2 * HEAD_DIM), 1)
    first_half = lane < HEAD_DIM
    zero = jnp.zeros((), bf16)
    rate = HEAD_DIM ** (-0.5)

    def spans_of(pair):
        return [
            pl.ds(pl.multiple_of(part * WIDTH + pair * 2 * HEAD_DIM, 2 * HEAD_DIM), 2 * HEAD_DIM)
            for part in range(3)
        ]

    def attend(pair, carry):
        query_span, key_span, value_span = spans_of(pair)
        query = triple[:, query_span]
        keys = triple[:, key_span]
        values = triple[:, value_span]
        results = []
        for side in range(2):
            mask = first_half if side == 0 else jnp.logical_not(first_half)
            scores = dot_t(jnp.where(mask, query, zero), keys) * rate
            scores = jnp.exp(scores - jnp.max(scores, axis=-1, keepdims=True))
            weights = scores * (1.0 / jnp.sum(scores, axis=-1, keepdims=True))
            probs[2 * pair + side] = weights
            results.append(dot(weights.astype(bf16), values))
        mixed_ref[:, query_span] = jnp.where(first_half, results[0], results[1]).astype(bf16)
        return carry

    lax.fori_loop(0, HEADS // 2, attend, 0, unroll=True)

    value = dot(mixed_ref[...], output_ref[...]) + bias(3)
    branch[...] = value
    value = hidden[...] + row(2) * value
    hidden[...] = value
    normal, scale_two = center(value)
    normal_two[...] = normal
    normed_two_ref[...] = (normal * (1.0 + row(4)) + row(3)).astype(bf16)

    def widen(index, carry):
        span = pl.ds(pl.multiple_of(index * wide, wide), wide)
        before = dot(normed_two_ref[...], expand_ref[:, span])
        before = before + tail_ref[bias_wide(tail_ref, ROW_BIAS - ROW_TAIL + 4, index)]
        after, steep = gelu_pair(before)
        act_ref[:, span] = after.astype(bf16)
        slope[:, span] = steep
        return carry

    lax.fori_loop(0, MLP_WIDTH // wide, widen, 0, unroll=True)

    branch_two = dot(act_ref[...], shrink_ref[...]) + bias(8)
    upper = hidden[...] + row(5) * branch_two
    normal, scale_three = center(upper)
    final = (normal * (1.0 + row(7)) + row(6)).astype(bf16)
    mismatch = dot(final, final_ref[...]) + bias(17)[:, :PATCH] - target
    loss = numbers[2, image] * jnp.sum(mismatch * mismatch)
    grad_out = (numbers[1, image] * mismatch).astype(bf16)

    g_final_ref[...] += dot_s(final, grad_out)
    sums = jnp.sum(grad_out.astype(f32), axis=0, keepdims=True)
    spot = lax.broadcasted_iota(jnp.int32, (1, WIDTH), 1)
    sums = jnp.concatenate([sums, jnp.zeros((1, WIDTH - PATCH), f32)], axis=1)
    g_bias_ref[3:4, :] += jnp.where(spot == PATCH, loss, sums)
    grad = dot_t(grad_out, final_ref[...])
    shift_f = jnp.sum(grad, axis=0, keepdims=True)
    scale_f = jnp.sum(grad * normal, axis=0, keepdims=True)
    grad_upper = center_back((1.0 + row(7)) * grad, normal, scale_three)
    gate_two = jnp.sum(branch_two * grad_upper, axis=0, keepdims=True)
    grad_branch = (row(5) * grad_upper).astype(bf16)
    g_branch_two_ref[...] = grad_branch
    g_bias_ref[2:3, :] += jnp.sum(grad_branch.astype(f32), axis=0, keepdims=True)
    hidden[...] = grad_upper

    def narrow(index, carry):
        span = pl.ds(pl.multiple_of(index * wide, wide), wide)
        grad_act = dot_t(g_branch_two_ref[...], shrink_ref[span, :])
        grad_pre = (grad_act * slope[:, span]).astype(bf16)
        g_pre_ref[:, span] = grad_pre
        g_bias_ref[bias_wide(g_bias_ref, 4, index)] += jnp.sum(grad_pre.astype(f32), axis=0, keepdims=True)
        return carry

    lax.fori_loop(0, MLP_WIDTH // wide, narrow, 0, unroll=True)

    grad = dot_t(g_pre_ref[...], expand_ref[...])
    normal = normal_two[...]
    shift_two = jnp.sum(grad, axis=0, keepdims=True)
    scale_mod_two = jnp.sum(grad * normal, axis=0, keepdims=True)
    grad_middle = hidden[...] + center_back((1.0 + row(4)) * grad, normal, scale_two)
    gate_one = jnp.sum(branch[...] * grad_middle, axis=0, keepdims=True)
    grad_branch = (row(2) * grad_middle).astype(bf16)
    g_branch_ref[...] = grad_branch
    g_bias_ref[1:2, :] += jnp.sum(grad_branch.astype(f32), axis=0, keepdims=True)
    hidden[...] = grad_middle
    g_mixed[...] = dot_t(grad_branch, output_ref[...]).astype(bf16)

    def attend_back(pair, carry):
        query_span, key_span, value_span = spans_of(pair)
        query = triple[:, query_span]
        keys = triple[:, key_span]
        values = triple[:, value_span]
        grad_mixed = g_mixed[:, query_span]
        results = []
        for side in range(2):
            mask = first_half if side == 0 else jnp.logical_not(first_half)
            weights = probs[2 * pair + side]
            grad_weights = dot_t(jnp.where(mask, grad_mixed, zero), values)
            grad_values = dot_s(weights.astype(bf16), grad_mixed)
            grad_scores = weights * (
                grad_weights - jnp.sum(weights * grad_weights, axis=-1, keepdims=True)
            )
            grad_scores = grad_scores.astype(bf16)
            grad_query = dot(grad_scores, keys)
            grad_keys = dot_s(grad_scores, query)
            results.append((grad_query, grad_keys, grad_values))
        for part, span in enumerate((query_span, key_span, value_span)):
            merged = jnp.where(first_half, results[0][part], results[1][part])
            if part < 2:
                merged = merged * rate
            g_triple_ref[:, span] = merged.astype(bf16)
        return carry

    lax.fori_loop(0, HEADS // 2, attend_back, 0, unroll=True)

    grad = dot_t(g_triple_ref[...], attend_ref[...])
    normal = normal_one[...]
    shift_one = jnp.sum(grad, axis=0, keepdims=True)
    scale_mod_one = jnp.sum(grad * normal, axis=0, keepdims=True)
    grad_start = hidden[...] + center_back((1.0 + row(1)) * grad, normal, scale_one)
    grad_start = grad_start.astype(bf16)
    g_patch_ref[...] += dot_s(blended, grad_start)
    g_bias_ref[0:1, :] += jnp.sum(grad_start.astype(f32), axis=0, keepdims=True)
    for index, value in enumerate(
        (shift_one, scale_mod_one, gate_one, shift_two, scale_mod_two, gate_two, shift_f, scale_f)
    ):
        g_mods_ref[0, index : index + 1, :] = value


def layer(numbers, latent, noisy, mods, patch_w, final_w, tail, weights):
    images = latent.shape[0]
    tokens = images * SEQUENCE
    once = pl.Buffered(1)

    def whole(array):
        return pl.BlockSpec(
            array.shape, lambda i: (0,) * len(array.shape), pipeline_mode=once
        )

    def fixed(shape, dtype=f32):
        return pl.BlockSpec(shape, lambda i: (0,) * len(shape)), jax.ShapeDtypeStruct(shape, dtype)

    def per_image(width):
        return (
            pl.BlockSpec((SEQUENCE, width), lambda i: (i, 0)),
            jax.ShapeDtypeStruct((tokens, width), bf16),
        )

    outs = [
        per_image(WIDTH),
        per_image(WIDTH),
        per_image(WIDTH),
        per_image(MLP_WIDTH),
        per_image(WIDTH),
        per_image(MLP_WIDTH),
        per_image(WIDTH),
        per_image(3 * WIDTH),
        (
            pl.BlockSpec((1, 8, WIDTH), lambda i: (i, 0, 0)),
            jax.ShapeDtypeStruct((images, 8, WIDTH), f32),
        ),
        fixed((PATCH, WIDTH)),
        fixed((WIDTH, PATCH)),
        fixed((8, WIDTH)),
    ]
    place = positions(SEQUENCE, WIDTH)
    fixed_args = (place, patch_w, final_w, tail) + tuple(weights)
    flops = 2 * 2 * 7078 * 1000 * tokens
    return pl.pallas_call(
        layer_kernel,
        grid=(images,),
        in_specs=[
            pl.BlockSpec(memory_space=pltpu.SMEM),
            pl.BlockSpec((1, SEQUENCE, PATCH), lambda i: (i, 0, 0)),
            pl.BlockSpec((1, SEQUENCE, PATCH), lambda i: (i, 0, 0)),
            pl.BlockSpec((1, 8, WIDTH), lambda i: (i, 0, 0)),
        ]
        + [whole(array) for array in fixed_args],
        out_specs=[spec for spec, _ in outs],
        out_shape=[shape for _, shape in outs],
        scratch_shapes=[
            pltpu.VMEM((SEQUENCE, 3 * WIDTH), bf16),
            pltpu.VMEM((HEADS, SEQUENCE, SEQUENCE), f32),
            pltpu.VMEM((SEQUENCE, MLP_WIDTH), f32),
            pltpu.VMEM((SEQUENCE, WIDTH), f32),
            pltpu.VMEM((SEQUENCE, WIDTH), f32),
            pltpu.VMEM((SEQUENCE, WIDTH), f32),
            pltpu.VMEM((SEQUENCE, WIDTH), f32),
            pltpu.VMEM((SEQUENCE, WIDTH), bf16),
        ],
        compiler_params=pltpu.CompilerParams(vmem_limit_bytes=56 * 1024 * 1024),
        cost_estimate=pl.CostEstimate(
            flops=flops, bytes_accessed=60 * 10**6, transcendentals=0
        ),
        name="layer",
    )(numbers, latent, noisy, mods, *fixed_args)


def local(
    n_wide,
    n_narrow,
    latents,
    noise_field,
    labels,
    label_drop,
    time_steps,
    loss_weights,
    attend_weight,
    attend_first,
    attend_second,
    attend_left,
    attend_right,
    output_weight,
    output_first,
    output_second,
    output_left,
    output_right,
    expand_weight,
    expand_first,
    expand_second,
    expand_left,
    expand_right,
    shrink_weight,
    shrink_first,
    shrink_second,
    shrink_left,
    shrink_right,
    adaptive_weight,
    adaptive_first,
    adaptive_second,
    adaptive_left,
    adaptive_right,
    shared_weight,
    shared_first,
    shared_second,
):
    column = lax.axis_index("narrow")
    images = labels.shape[0] * labels.shape[1]

    moment = (time_steps.reshape(images).astype(f32) + 0.5) / TIMESTEPS
    chosen = jnp.where(label_drop == 1, CLASSES - 1, labels).reshape(images, 1).astype(f32)
    weights_here = loss_weights.reshape(images)
    info = jnp.concatenate(
        [rounded(frequencies(moment, FREQS)).astype(f32), chosen, weights_here[:, None]], axis=1
    )
    info = jnp.pad(info, ((0, 8 - images), (0, SHEET - info.shape[1])))[None]

    shard = shared_weight.shape[0]
    rows = shard_rows(shard)
    row_start = column * shard // (WIDTH * ALIGN) * ALIGN
    offset = column * shard - row_start * WIDTH
    margin = -(-(ALIGN + 1) * WIDTH // 1024) * 1024
    own = lax.pad(shared_weight, f32(0.0), [(margin, rows * WIDTH - shard, 0)])
    own = lax.dynamic_slice(own, (margin - offset,), (rows * WIDTH,)).reshape(rows, WIDTH)

    (
        *full,
        patch_w,
        final_rows,
        tail,
        time_two,
        sheet,
        time_pre,
        condition,
        own_act,
        adaptive_low,
        mods,
        total,
        lefts,
        rights,
    ) = gather_all(
        n_wide,
        n_narrow,
        images,
        shard,
        (own, attend_weight, output_weight, expand_weight, shrink_weight),
        adaptive_weight,
        info,
        (attend_left, output_left, expand_left, shrink_left, adaptive_left),
        [
            blocks.transpose(1, 2, 0) if blocks.shape[0] > BLOCK else blocks
            for blocks in (attend_right, output_right, expand_right, shrink_right, adaptive_right)
        ],
    )
    lefts = lefts.reshape(8, -1, BLOCK)
    rights = rights.reshape(-1, BLOCK, 4 * BLOCK)
    weight_sum = total[0, 0]

    shape = (images,) + latents.shape[2:]
    entries = SEQUENCE * PATCH
    numbers = jnp.stack(
        [moment, 2.0 * weights_here / (entries * weight_sum), weights_here / entries]
    )
    (
        normed,
        mixed,
        normed_two,
        act,
        g_branch_two,
        g_pre,
        g_branch,
        g_triple,
        g_mods,
        g_patch,
        g_final,
        g_bias,
    ) = layer(
        numbers,
        latents.reshape(shape),
        noise_field.reshape(shape),
        mods,
        patch_w,
        final_rows.astype(bf16).reshape(WIDTH, PATCH),
        tail,
        full,
    )

    turned, window, totals, clip = reduce_all(
        n_wide,
        n_narrow,
        images,
        shard,
        weight_blocks(
            n_narrow,
            (normed, mixed, normed_two, act),
            (g_triple, g_branch, g_pre, g_branch_two),
        ),
        (
            g_mods.reshape(images * 8, WIDTH),
            g_patch,
            g_final.reshape(PATCH, WIDTH),
            g_bias,
            adaptive_low,
            sheet,
            time_pre,
            condition,
            own_act,
            time_two,
            lefts,
            rights,
        ),
    )
    loss_sum = totals[3, PATCH]
    clip_norm = clip[0, 0]
    factor = clip[1, 0]
    grad_shared = lax.dynamic_slice(window.reshape(-1), (offset,), (shard,))

    results = rotated_update(
        clip,
        turned,
        lefts,
        rights,
        (
            (attend_weight, attend_first, attend_second),
            (output_weight, output_first, output_second),
            (expand_weight, expand_first, expand_second),
            (shrink_weight, shrink_first, shrink_second),
            (adaptive_weight, adaptive_first, adaptive_second),
        ),
    )
    fresh = plain_update(shared_weight, shared_first, shared_second, grad_shared * factor)
    results = [*results, fresh[0], fresh[1], fresh[2], fresh[0].astype(jnp.bfloat16)]
    return tuple(results) + (loss_sum, weight_sum, clip_norm)


def solution(mesh):
    data = P(None, ("wide", "narrow"))
    state = (P("narrow", None),) * 3 + (P("narrow", None, None), P())
    return jax.shard_map(
        partial(local, mesh.shape["wide"], mesh.shape["narrow"]),
        mesh=mesh,
        in_specs=(P(None, ("wide", "narrow"), None, None),) * 2
        + (data,) * 4
        + state * 5
        + (P("narrow"),) * 3,
        out_specs=(P("narrow", None),) * 20 + (P("narrow"),) * 4 + (P(),) * 3,
        check_vma=False,
    )
```

```python
from functools import partial
import math

import jax
import jax.numpy as jnp
import numpy as np
from jax import lax
from jax.experimental import pallas as pl
from jax.experimental.pallas import tpu as pltpu
from jax.sharding import PartitionSpec as P

HEADS = 12
HEAD_DIM = 64
MLP_WIDTH = 3072
CLASSES = 1001
FREQS = 256
PATCH = 16
TIMESTEPS = 1000
BLOCK = 32
STEP_COUNT = 10
WIDTH = 768
SEQUENCE = 256


beta_one = 0.9
beta_two = 0.999
epsilon_adam = 1e-08
learn_rate = 0.03
decay_rate = 0.01
clip_limit = 0.002
highest = lax.Precision.HIGHEST
bf16 = jnp.bfloat16
f32 = jnp.float32

ROW_PATCH = 0
ROW_TIME_ONE = 16
ROW_TIME_TWO = 272
ROW_TABLE = 1040
ROW_FINAL = 2041
ROW_BIAS = 2057


def positions(tokens, width):
    side = math.isqrt(tokens)
    quarter = width // 4
    omega = 1.0 / 10000.0 ** (np.arange(quarter, dtype=np.float64) / quarter)
    place = np.arange(tokens)
    column = (place % side)[:, None] * omega
    row = (place // side)[:, None] * omega
    table = np.concatenate([np.sin(column), np.cos(column), np.sin(row), np.cos(row)], axis=1)
    return jnp.asarray(table.astype(np.float32))


def frequencies(moment, width):
    half = width // 2
    phases = jnp.exp(-math.log(10000.0) * jnp.arange(half, dtype=jnp.float32) / half)
    angles = moment[:, None] * 1000.0 * phases
    return jnp.concatenate([jnp.cos(angles), jnp.sin(angles)], axis=1)


def normalize(hidden):
    centered = hidden - jnp.mean(hidden, axis=-1, keepdims=True)
    return centered * lax.rsqrt(jnp.mean(centered * centered, axis=-1, keepdims=True) + 1e-06)


def modulate(hidden, shift, scale):
    return normalize(hidden) * (1.0 + scale[:, None, :]) + shift[:, None, :]


def adam_direction(first, second):
    return (first * (1.0 / (1.0 - beta_one**STEP_COUNT))) / (
        jnp.sqrt(second * (1.0 / (1.0 - beta_two**STEP_COUNT))) + epsilon_adam
    )


def plain_update(weight, first, second, grad):
    first = beta_one * first + (1.0 - beta_one) * grad
    second = beta_two * second + (1.0 - beta_two) * grad * grad
    weight = weight - learn_rate * (adam_direction(first, second) + decay_rate * weight)
    return (weight, first, second)


def rounded(value):
    return value.astype(jnp.bfloat16)


def product(inputs, weight):
    return jnp.dot(inputs, weight, preferred_element_type=jnp.float32)


def backprod(gradient, weight):
    return jnp.einsum("...n,kn->...k", gradient, weight, preferred_element_type=jnp.float32)


def weight_grad(inputs, gradient):
    flat_in = inputs.reshape(-1, inputs.shape[-1])
    flat_grad = gradient.reshape(-1, gradient.shape[-1])
    return lax.dot_general(
        flat_in, flat_grad, (((0,), (0,)), ((), ())), preferred_element_type=jnp.float32
    )


def bias_grad(gradient):
    return jnp.sum(gradient.astype(jnp.float32).reshape(-1, gradient.shape[-1]), axis=0)


def halves(value):
    high = value.astype(bf16)
    return high, (value - high.astype(f32)).astype(bf16)


def spread_left(blocks):
    size = blocks.shape[0]
    place = lax.broadcasted_iota(jnp.int32, (BLOCK, size), 0)
    column = lax.broadcasted_iota(jnp.int32, (BLOCK, size), 1)
    repeat = (place == column % BLOCK).astype(bf16)
    row_block = lax.broadcasted_iota(jnp.int32, (size, size), 0) // BLOCK
    col_block = lax.broadcasted_iota(jnp.int32, (size, size), 1) // BLOCK
    return tuple(
        jnp.where(
            row_block == col_block, jnp.dot(part, repeat, preferred_element_type=f32), 0.0
        ).astype(bf16)
        for part in halves(blocks)
    )


def spread_right(first, second):
    size = 4 * BLOCK
    row_block = lax.broadcasted_iota(jnp.int32, (size, size), 0) // BLOCK
    col_block = lax.broadcasted_iota(jnp.int32, (size, size), 1) // BLOCK
    inside = row_block == col_block
    corners = [
        jnp.where(inside, jnp.concatenate([row] * 4, axis=0), 0.0) for row in (first, second)
    ]
    empty = jnp.zeros((size, size), f32)
    return jnp.concatenate(
        [
            jnp.concatenate([corners[0], empty], axis=1),
            jnp.concatenate([empty, corners[1]], axis=1),
        ],
        axis=0,
    )


def dot(left, right):
    return jnp.dot(left, right, preferred_element_type=f32)


def dot_t(left, right):
    return lax.dot_general(left, right, (((1,), (1,)), ((), ())), preferred_element_type=f32)


STRIP = 256
TILES = ((3, 1), (1, 1), (4, 1), (1, 4), (8, 1))


def tile_places():
    places = []
    for matrix, (across, down) in enumerate(TILES):
        for number in range(across * down):
            places.append((matrix, number // across, number % across))
    return places


def left_number(tile):
    return (tile + 9) // 12 + (tile + 8) // 12 + (tile + 4) // 12 * (tile - 7)


def adam_kernel(count, *refs):
    factor_ref, turned, lefts, rights = refs[:4]
    states = [refs[4 + 3 * matrix : 7 + 3 * matrix] for matrix in range(5)]
    outs = [refs[19 + 4 * matrix : 23 + 4 * matrix] for matrix in range(5)]
    taken, given, low, take_sem, give_sem = refs[39:]
    rows = taken.shape[2]
    places = tile_places()
    factor = factor_ref[1, 0]

    def window(number):
        _, down, across = places[number]
        return (pl.ds(down * rows, rows), pl.ds(across * WIDTH, WIDTH))

    def takes(number):
        slot = number % 3
        arrays = [ref.at[window(number)] for ref in states[places[number][0]]]
        arrays.append(turned.at[number])
        return [
            pltpu.make_async_copy(array, taken.at[slot, part], take_sem.at[slot, part])
            for part, array in enumerate(arrays)
        ]

    def gives(number):
        slot = number % 2
        arrays = [ref.at[window(number)] for ref in outs[places[number][0]]]
        sources = [given.at[slot, part] for part in range(3)] + [low.at[slot]]
        return [
            pltpu.make_async_copy(source, array, give_sem.at[slot, part])
            for part, (source, array) in enumerate(zip(sources, arrays))
        ]

    def given_out(slot):
        for part in range(4):
            buffer = low.at[slot] if part == 3 else given.at[slot, part]
            pltpu.make_async_copy(buffer, buffer, give_sem.at[slot, part]).wait()

    for number in range(2):
        for copy in takes(number):
            copy.start()

    def body(tile, carry):
        for number in range(2, count):

            @pl.when(tile + 2 == number)
            def _(number=number):
                for copy in takes(number):
                    copy.start()

        slot = tile % 3
        out = tile % 2
        for part in range(4):
            buffer = taken.at[slot, part]
            pltpu.make_async_copy(buffer, buffer, take_sem.at[slot, part]).wait()

        @pl.when(tile >= 2)
        def _():
            given_out(out)

        stack = jnp.where(tile < 12, left_number(jnp.minimum(tile, 11)), 7)
        left = spread_left(lefts[stack])[0]
        for start in range(0, WIDTH, STRIP):
            span = slice(start, start + STRIP)
            group = tile * (WIDTH // BLOCK // 4) + start // BLOCK // 4
            right = spread_right(rights[group], rights[group + 1]).astype(bf16)
            grad = taken[slot, 3, :, span] * factor
            first = beta_one * taken[slot, 1, :, span] + (1.0 - beta_one) * grad
            second = beta_two * taken[slot, 2, :, span] + (1.0 - beta_two) * grad * grad
            given[out, 1, :, span] = first
            given[out, 2, :, span] = second
            step = adam_direction(first, second)
            step = dot_t(step.astype(bf16), right)
            step = dot(left, step.astype(bf16))
            weight = taken[slot, 0, :, span]
            weight = weight - learn_rate * (step + decay_rate * weight)
            given[out, 0, :, span] = weight
            low[out, :, span] = weight.astype(bf16)
        for number in range(count):

            @pl.when(tile == number)
            def _(number=number):
                for copy in gives(number):
                    copy.start()

        return carry

    lax.fori_loop(0, count, body, 0)
    for slot in range(2):
        given_out(slot)


def rotated_update(clip, turned, lefts, rights, states):
    count, rows, _ = turned.shape
    any_space = pl.BlockSpec(memory_space=pl.ANY)
    vmem = pl.BlockSpec(memory_space=pltpu.VMEM)
    shapes = []
    for weight, _, _ in states:
        shapes += [jax.ShapeDtypeStruct(weight.shape, f32)] * 3
        shapes += [jax.ShapeDtypeStruct(weight.shape, bf16)]
    dma = pltpu.SemaphoreType.DMA
    return pl.pallas_call(
        partial(adam_kernel, count),
        in_specs=[pl.BlockSpec(memory_space=pltpu.SMEM), any_space, vmem, vmem]
        + [any_space] * 15,
        out_specs=[any_space] * 20,
        out_shape=shapes,
        scratch_shapes=[
            pltpu.VMEM((3, 4, rows, WIDTH), f32),
            pltpu.VMEM((2, 3, rows, WIDTH), f32),
            pltpu.VMEM((2, rows, WIDTH), bf16),
            dma((3, 4)),
            dma((2, 4)),
        ],
        compiler_params=pltpu.CompilerParams(vmem_limit_bytes=60 * 1024 * 1024),
        name="rotated_adam",
    )(clip, turned, lefts, rights, *[array for state in states for array in state])


def bits_of(extent):
    return extent.bit_length() - 1


def flipped(index, mask, count):
    for bit in range(count):
        if mask >> bit & 1:
            index = index + (1 - 2 * (index // (1 << bit) % 2)) * (1 << bit)
    return index


def greet(n_wide, n_narrow):
    barrier = pltpu.get_barrier_semaphore()
    count = 0
    for axis, extent in (("narrow", n_narrow), ("wide", n_wide)):
        me = lax.axis_index(axis)
        for bit in range(bits_of(extent)):
            pl.semaphore_signal(
                barrier,
                inc=1,
                device_id={axis: flipped(me, 1 << bit, bits_of(extent))},
                device_id_type=pl.DeviceIdType.MESH,
            )
            count = count + 1
    pl.semaphore_wait(barrier, count)


def remote(source, target, send_sem, recv_sem, axis, peer):
    return pltpu.make_async_remote_copy(
        src_ref=source,
        dst_ref=target,
        send_sem=send_sem,
        recv_sem=recv_sem,
        device_id={axis: peer},
        device_id_type=pl.DeviceIdType.MESH,
    )


def slot_of(n_wide, n_narrow):
    here = lax.axis_index("narrow")
    there = lax.axis_index("wide")
    return there // 2 + n_wide // 2 * (here + n_narrow * (there % 2))


def hop_order(n_wide, n_narrow):
    n_bits = bits_of(n_narrow)
    w_bits = bits_of(n_wide)
    places = [("wide", bit, w_bits) for bit in range(1, w_bits)]
    places += [("narrow", bit, n_bits) for bit in range(n_bits)]
    return places + [("wide", 0, w_bits)]


def route(path, step, count):
    return (step + path) % count


ROW_TAIL = 2048
TAIL = 32
ALIGN = 16
SHEET = 384


def shard_rows(shard):
    rows = (shard + WIDTH - 2) // WIDTH + 1 + ALIGN
    return -(-rows // 32) * 32


def shard_start(number, shard):
    return number * shard // WIDTH // ALIGN * ALIGN


def flat_rows(n_narrow, shard):
    last = shard_start(n_narrow - 1, shard) + shard_rows(shard)
    return max(-(-last // ALIGN) * ALIGN, 2112)


def center(hidden):
    centered = hidden - jnp.mean(hidden, axis=-1, keepdims=True)
    scale = lax.rsqrt(jnp.mean(centered * centered, axis=-1, keepdims=True) + 1e-06)
    return centered * scale, scale


def pair_spans(pair):
    return [
        pl.ds(pl.multiple_of(part * WIDTH + pair * 2 * HEAD_DIM, 2 * HEAD_DIM), 2 * HEAD_DIM)
        for part in range(3)
    ]


def head_masks(tokens):
    lane = lax.broadcasted_iota(jnp.int32, (tokens, 2 * HEAD_DIM), 1)
    return lane < HEAD_DIM, lane >= HEAD_DIM


def bases_along_lanes(shape):
    return shape[0] == BLOCK and shape[2] > BLOCK


def silu_slope(value):
    gate = jax.nn.sigmoid(value)
    return gate * (1.0 + value * (1.0 - gate))


def own_columns(value, n_narrow):
    here = lax.axis_index("narrow")
    width = value.shape[1] // n_narrow
    result = value[:, :width]
    for number in range(1, n_narrow):
        result = jnp.where(
            here == number, value[:, number * width : (number + 1) * width], result
        )
    return result


def gather_kernel(n_wide, n_narrow, images, shard, *refs):
    count = 5
    shards = refs[:count]
    adaptive_ref, info_ref = refs[count : count + 2]
    left_refs = refs[count + 2 : count + 7]
    right_refs = refs[count + 7 : count + 12]
    moment_ref, latent_ref, noise_ref, place_ref = refs[count + 12 : count + 16]
    outs = refs[count + 16 : count + 37]
    scratch = refs[count + 37 :]
    (
        patch_out,
        final_out,
        tail_out,
        time_two_out,
        sheet,
        time_pre,
        condition,
        own_act,
        adaptive_low,
        mods_ref,
        total_ref,
        lefts_out,
        rights_out,
        normed_out,
        triple_out,
        mixed_out,
        probs_out,
    ) = outs[4:21]
    gathered = scratch[0]
    wides = scratch[1 : count + 1]
    lows = scratch[count + 1 : 2 * count + 1]
    (
        flat,
        turned,
        attend_full,
        normed,
        triple,
        mixed,
        probs,
        adaptive_wide,
        info_all,
        part,
        part_in,
        load_sem,
        keep_sem,
        send_sem,
        recv_sem,
        core_send,
        core_recv,
        info_sem,
        info_send,
        info_recv,
        part_send,
        part_recv,
        attend_sem,
        image_sem,
    ) = scratch[2 * count + 1 :]
    fulls = (gathered, attend_full) + tuple(outs[1:4])
    here = lax.axis_index("narrow")
    there = lax.axis_index("wide")
    core = there % 2
    n_bits = bits_of(n_narrow)
    w_bits = bits_of(n_wide)
    sibling = flipped(there, 1, w_bits)

    loads = [
        pltpu.make_async_copy(shards[number], wides[number], load_sem.at[number])
        for number in range(count)
    ]
    loads.append(pltpu.make_async_copy(adaptive_ref, adaptive_wide, load_sem.at[count]))
    for load in loads:
        load.start()
    slot = slot_of(n_wide, n_narrow)
    info_own = pltpu.make_async_copy(info_ref, info_all.at[pl.ds(slot, 1)], info_sem)
    info_own.start()
    greet(n_wide, n_narrow)
    sends = []

    def region(number, owner, half, path):
        rows, cols = shards[number].shape
        return (
            pl.ds(pl.multiple_of(owner * rows + half * (rows // 2), 16), rows // 2),
            pl.ds(path * (cols // 2), cols // 2),
        )

    def narrow_step(number, step, own):
        for path in range(2):
            bit = route(path, step, n_bits)
            peer = flipped(here, 1 << bit, n_bits)
            done = sum(1 << route(path, earlier, n_bits) for earlier in range(step))
            for mask in range(n_narrow):
                if mask & ~done or own != (mask == 0):
                    continue
                place = region(number, flipped(here, mask, n_bits), core, path)
                arrives = mask | 1 << bit
                if mask == 0:
                    rows, cols = shards[number].shape
                    source = lows[number].at[
                        pl.ds(pl.multiple_of(core * (rows // 2), 16), rows // 2),
                        pl.ds(path * (cols // 2), cols // 2),
                    ]
                else:
                    source = fulls[number].at[place]
                copy = remote(
                    source,
                    fulls[number].at[place],
                    send_sem.at[number, path, arrives - 1],
                    recv_sem.at[number, path, arrives - 1],
                    "narrow",
                    peer,
                )
                copy.start()
                sends.append(copy)

    def arrive(number, step):
        for path in range(2):
            bit = route(path, step, n_bits)
            done = sum(1 << route(path, earlier, n_bits) for earlier in range(step))
            for mask in range(n_narrow):
                if mask & ~done:
                    continue
                arrived = mask | 1 << bit
                place = region(number, flipped(here, arrived, n_bits), core, path)
                remote(
                    fulls[number].at[place],
                    fulls[number].at[place],
                    send_sem.at[number, path, arrived - 1],
                    recv_sem.at[number, path, arrived - 1],
                    "narrow",
                    flipped(here, 1 << bit, n_bits),
                ).wait_recv()
                copy = remote(
                    fulls[number].at[place],
                    fulls[number].at[place],
                    core_send.at[number, path, arrived - 1],
                    core_recv.at[number, path, arrived - 1],
                    "wide",
                    sibling,
                )
                copy.start()
                sends.append(copy)

    def from_sibling(number):
        for path in range(2):
            for mask in range(1, n_narrow):
                place = region(number, flipped(here, mask, n_bits), 1 - core, path)
                remote(
                    fulls[number].at[place],
                    fulls[number].at[place],
                    core_send.at[number, path, mask - 1],
                    core_recv.at[number, path, mask - 1],
                    "wide",
                    sibling,
                ).wait_recv()

    def cast_rows(source, target):
        def cast(index, carry):
            span = pl.ds(pl.multiple_of(index * 16, 16), 16)
            target[span, :] = source[span, :].astype(bf16)
            return carry

        lax.fori_loop(0, source.shape[0] // 16, cast, 0)

    keeps = []

    def begin(number):
        loads[number].wait()
        rows = shards[number].shape[0]
        cast_rows(wides[number], lows[number])
        keep = pltpu.make_async_copy(
            lows[number],
            fulls[number].at[pl.ds(pl.multiple_of(here * rows, 16), rows)],
            keep_sem.at[number],
        )
        keep.start()
        keeps.append(keep)
        narrow_step(number, 0, True)

    def begin_rest(number):
        for step in range(1, n_bits):
            narrow_step(number, step, True)

    places = hop_order(n_wide, n_narrow)

    def info_copy(position):
        axis, bit, bits = places[position]
        width = 1 << position
        base = slot // width * width
        return remote(
            info_all.at[pl.ds(base, width)],
            info_all.at[pl.ds(base, width)],
            info_send.at[position],
            info_recv.at[position],
            axis,
            flipped(lax.axis_index(axis), 1 << bit, bits),
        )

    def pass_on(numbers, step):
        for number in numbers:
            arrive(number, step)
            if step + 1 < n_bits:
                narrow_step(number, step + 1, False)

    info_own.wait()
    info_copy(0).start()
    begin(0)
    begin_rest(0)
    waiting = [lambda step=step: pass_on([0], step) for step in range(n_bits - 1)]
    waiting += [lambda: (begin(1), begin_rest(1)), lambda: (begin(2), begin_rest(2))]
    waiting += [lambda: begin(3), lambda: begin(4)]
    for position in range(len(places)):
        info_copy(position).wait()
        if position + 1 < len(places):
            info_copy(position + 1).start()
        if waiting:
            waiting.pop(0)()
    for step in waiting:
        step()
    pass_on([0], n_bits - 1)
    from_sibling(0)
    keeps[0].wait()

    height = shards[0].shape[0]
    reached = 0
    for number in range(n_narrow):
        start = shard_start(number, shard)
        overlap = max(reached - start, 0)
        block = number * height
        if overlap:
            flat[start:reached, :] = (
                flat[start:reached, :].astype(f32)
                + gathered[block : block + overlap, :].astype(f32)
            ).astype(bf16)
        flat[start + overlap : start + height, :] = gathered[block + overlap : block + height, :]
        reached = start + height
    if reached < flat.shape[0]:
        flat[reached:, :] = jnp.zeros((flat.shape[0] - reached, WIDTH), bf16)

    devices = n_wide * n_narrow
    for number in range(devices):
        sheet[number * images : (number + 1) * images, :] = info_all[number, :images, :]
    weights = sheet[:, FREQS + 1 : FREQS + 2]
    total_ref[...] = jnp.sum(weights, axis=0, keepdims=True)
    tail = flat[ROW_TAIL : ROW_TAIL + TAIL, :].astype(f32)
    tail_out[...] = tail
    patch_out[...] = flat[ROW_PATCH:ROW_TIME_ONE, :]
    time_two_out[...] = flat[ROW_TIME_TWO:ROW_TABLE, :]
    last = flat[ROW_FINAL - 9 : ROW_FINAL + 23, :].astype(f32)
    final_out[...] = last[9 : 9 + PATCH]
    tail_row = ROW_BIAS - ROW_TAIL
    value = dot(sheet[:, :FREQS].astype(bf16), flat[ROW_TIME_ONE:ROW_TIME_TWO, :])
    value = value + tail[tail_row + 1 : tail_row + 2]
    time_pre[...] = value
    act = jax.nn.silu(value).astype(bf16)
    value = dot(act, flat[ROW_TIME_TWO:ROW_TABLE, :]) + tail[tail_row + 2 : tail_row + 3]
    labels = lax.broadcasted_iota(jnp.int32, (sheet.shape[0], 1008), 1).astype(f32)
    pick = jnp.where(sheet[:, FREQS : FREQS + 1] == labels, 1.0, 0.0).astype(bf16)
    value = value + dot(pick, flat[ROW_TABLE : ROW_TABLE + 1008, :])
    condition[...] = value
    act = own_columns(jax.nn.silu(value), n_narrow)
    act = act.astype(bf16)
    own_act[...] = act

    loads[count].wait()
    cast_rows(adaptive_wide, adaptive_low)
    row = lax.broadcasted_iota(jnp.int32, (8 * n_narrow, act.shape[0]), 0)
    column = lax.broadcasted_iota(jnp.int32, (8 * n_narrow, act.shape[0]), 1)
    owner = there // 2 + n_wide // 2 * (row // 8 + n_narrow * core)
    chosen = column == owner * images + row % images
    near = dot(jnp.where(chosen, 1.0, 0.0).astype(bf16), act).astype(bf16)
    across = images

    def piece(index):
        first = index // across * images
        start = index % across * WIDTH
        return slice(first, first + images), slice(start, start + WIDTH)

    for index in range(8):
        value = dot(near, adaptive_low[:, index * WIDTH : (index + 1) * WIDTH])
        rows_of, span = piece(index)
        for number in range(n_narrow):
            start = 8 * number + rows_of.start
            part[0, number, rows_of, span] = value[start : start + images]

    def lay_bases():
        place = 0
        for ref in left_refs:
            blocks = ref.shape[0]
            lefts_out[place : place + blocks * BLOCK, :] = ref[...].reshape(-1, BLOCK)
            place = place + blocks * BLOCK
        place = 0
        for matrix, ref in enumerate(right_refs):
            turning = bases_along_lanes(ref.shape)
            blocks = ref.shape[2] if turning else ref.shape[0]
            copies = TILES[matrix][1]
            for row in range(BLOCK):
                turned[0:blocks, :] = ref[row].T if turning else ref[:, row, :]
                value = jnp.concatenate(
                    [turned[pl.ds(spot, blocks // 4, stride=4), :] for spot in range(4)], axis=1
                )
                for copy in range(copies):
                    start = place + copy * blocks // 4 * BLOCK + row
                    rights_out[pl.ds(start, blocks // 4, stride=BLOCK), :] = value
            place = place + copies * blocks // 4 * BLOCK

    def part_copy(step, mask):
        bit = 1 << step
        return remote(
            part.at[step, flipped(here, mask, n_bits)],
            part_in.at[step, flipped(here, mask, n_bits)],
            part_send.at[step, mask],
            part_recv.at[step, mask],
            "narrow",
            flipped(here, bit, n_bits),
        )

    def part_back(step, mask):
        bit = 1 << step
        owner = flipped(here, mask - bit, n_bits)
        return remote(
            part_in.at[step, owner],
            part_in.at[step, owner],
            part_send.at[step, mask],
            part_recv.at[step, mask],
            "narrow",
            flipped(here, bit, n_bits),
        ), owner

    for step in range(n_bits):
        bit = 1 << step
        masks = [
            mask for mask in range(n_narrow) if mask & bit and not mask & (bit - 1)
        ]
        for mask in masks:
            copy = part_copy(step, mask)
            copy.start()
            sends.append(copy)
        pass_on([1, 2] if step + 1 < n_bits else [], step)
        for mask in masks:
            back, owner = part_back(step, mask)
            back.wait_recv()
            if step + 1 < n_bits:
                part[step + 1, owner] = part[step, owner] + part_in[step, owner]
            else:
                value = part[step, owner] + part_in[step, owner]
                for index in range(8):
                    rows_of, span = piece(index)
                    for image in range(images):
                        start = rows_of.start + image
                        mods_ref[image, index : index + 1, :] = (
                            value[start : start + 1, span]
                            + tail[tail_row + 9 + index : tail_row + 10 + index]
                        )

    begin_rest(3)
    begin_rest(4)
    for step in range(n_bits - 1):
        pass_on([3, 4], step)
    pass_on([1], n_bits - 1)
    lay_bases()

    from_sibling(1)
    keeps[1].wait()
    attend_out = pltpu.make_async_copy(attend_full, outs[0], attend_sem)
    attend_out.start()
    masks = head_masks(SEQUENCE)
    rate = HEAD_DIM ** (-0.5)

    def image_copies(image):
        slot = image % 2
        tokens = pl.ds(pl.multiple_of(image * SEQUENCE, SEQUENCE), SEQUENCE)
        heads = pl.ds(image * HEADS, HEADS)
        pairs = (
            (normed, normed_out.at[tokens]),
            (triple, triple_out.at[tokens]),
            (mixed, mixed_out.at[tokens]),
            (probs, probs_out.at[heads]),
        )
        return [
            pltpu.make_async_copy(source.at[slot], target, image_sem.at[slot, number])
            for number, (source, target) in enumerate(pairs)
        ]

    def one_image(image, carry):
        slot = image % 2

        @pl.when(image >= 2)
        def _():
            for copy in image_copies(image - 2):
                copy.wait()

        moment = moment_ref[image]
        blended = (1.0 - moment) * latent_ref[image] + moment * noise_ref[image]
        start = dot(blended.astype(bf16), patch_out[...]) + tail_out[tail_row : tail_row + 1, :]
        normal, _ = center(start + place_ref[...])
        shift = mods_ref[image, 0:1, :]
        scale = mods_ref[image, 1:2, :]
        normed[slot] = (normal * (1.0 + scale) + shift).astype(bf16)

        for index in range(3 * WIDTH // STRIP):
            span = slice(index * STRIP, (index + 1) * STRIP)
            triple[slot, :, span] = dot(normed[slot], attend_full[:, span]).astype(bf16)
        for pair in range(HEADS // 2):
            query_span, key_span, value_span = pair_spans(pair)
            query = triple[slot, :, query_span]
            keys = triple[slot, :, key_span]
            values = triple[slot, :, value_span]
            results = []
            for side, mask in enumerate(masks):
                scores = dot_t(jnp.where(mask, query, jnp.zeros((), bf16)), keys) * rate
                scores = jnp.exp(scores - jnp.max(scores, axis=-1, keepdims=True))
                shares = scores * (1.0 / jnp.sum(scores, axis=-1, keepdims=True))
                shares = shares.astype(bf16)
                probs[slot, 2 * pair + side] = shares
                results.append(dot(shares, values))
            mixed[slot, :, query_span] = jnp.where(masks[0], results[0], results[1]).astype(bf16)
        for copy in image_copies(image):
            copy.start()
        return carry

    lax.fori_loop(0, images, one_image, 0)
    pass_on(range(2, count), n_bits - 1)
    for number in range(2, count):
        from_sibling(number)
    for keep in keeps[2:]:
        keep.wait()
    for copy in sends:
        copy.wait_send()
    for image in range(max(images - 2, 0), images):
        for copy in image_copies(image):
            copy.wait()
    attend_out.wait()


def gather_all(n_wide, n_narrow, images, shard, shards, adaptive, info, lefts, rights, data):
    count = len(shards)
    any_space = pl.BlockSpec(memory_space=pl.ANY)
    vmem = pl.BlockSpec(memory_space=pltpu.VMEM)
    devices = n_wide * n_narrow
    n_bits = bits_of(n_narrow)
    rows = adaptive.shape[0]
    dma = pltpu.SemaphoreType.DMA
    total = devices * images
    return pl.pallas_call(
        partial(gather_kernel, n_wide, n_narrow, images, shard),
        in_specs=[any_space] * (count + 2)
        + [vmem] * 10
        + [pl.BlockSpec(memory_space=pltpu.SMEM)]
        + [vmem] * 3,
        out_specs=[any_space] * (count - 1) + [vmem] * 13 + [any_space] * 4,
        out_shape=[
            jax.ShapeDtypeStruct((piece.shape[0] * n_narrow, piece.shape[1]), bf16)
            for piece in shards[1:]
        ]
        + [
            jax.ShapeDtypeStruct((PATCH, WIDTH), bf16),
            jax.ShapeDtypeStruct((PATCH, WIDTH), f32),
            jax.ShapeDtypeStruct((TAIL, WIDTH), f32),
            jax.ShapeDtypeStruct((WIDTH, WIDTH), bf16),
            jax.ShapeDtypeStruct((total, SHEET), f32),
            jax.ShapeDtypeStruct((total, WIDTH), f32),
            jax.ShapeDtypeStruct((total, WIDTH), f32),
            jax.ShapeDtypeStruct((total, rows), bf16),
            jax.ShapeDtypeStruct(adaptive.shape, bf16),
            jax.ShapeDtypeStruct((images, 8, WIDTH), f32),
            jax.ShapeDtypeStruct((1, 1), f32),
            jax.ShapeDtypeStruct((8 * rows, BLOCK), f32),
            jax.ShapeDtypeStruct((len(tile_places()) * 6 * BLOCK, 4 * BLOCK), f32),
            jax.ShapeDtypeStruct((images * SEQUENCE, WIDTH), bf16),
            jax.ShapeDtypeStruct((images * SEQUENCE, 3 * WIDTH), bf16),
            jax.ShapeDtypeStruct((images * SEQUENCE, WIDTH), bf16),
            jax.ShapeDtypeStruct((images * HEADS, SEQUENCE, SEQUENCE), bf16),
        ],
        scratch_shapes=[pltpu.VMEM((shards[0].shape[0] * n_narrow, WIDTH), bf16)]
        + [pltpu.VMEM(piece.shape, f32) for piece in shards]
        + [pltpu.VMEM(piece.shape, bf16) for piece in shards]
        + [
            pltpu.VMEM((flat_rows(n_narrow, shard), WIDTH), bf16),
            pltpu.VMEM((8 * WIDTH // BLOCK, BLOCK), f32),
            pltpu.VMEM((WIDTH, 3 * WIDTH), bf16),
            pltpu.VMEM((2, SEQUENCE, WIDTH), bf16),
            pltpu.VMEM((2, SEQUENCE, 3 * WIDTH), bf16),
            pltpu.VMEM((2, SEQUENCE, WIDTH), bf16),
            pltpu.VMEM((2, HEADS, SEQUENCE, SEQUENCE), bf16),
            pltpu.VMEM(adaptive.shape, f32),
            pltpu.VMEM((devices,) + info.shape[1:], f32),
            pltpu.VMEM((n_bits, n_narrow, 8, images * WIDTH), f32),
            pltpu.VMEM((n_bits, n_narrow, 8, images * WIDTH), f32),
            dma((count + 1,)),
            dma((count,)),
            dma((count, 2, n_narrow - 1)),
            dma((count, 2, n_narrow - 1)),
            dma((count, 2, n_narrow - 1)),
            dma((count, 2, n_narrow - 1)),
            dma,
            dma((bits_of(devices),)),
            dma((bits_of(devices),)),
            dma((n_bits, n_narrow)),
            dma((n_bits, n_narrow)),
            dma,
            dma((2, 4)),
        ],
        compiler_params=pltpu.CompilerParams(
            collective_id=0, has_side_effects=True, vmem_limit_bytes=60 * 1024 * 1024
        ),
        name="gather_weights",
    )(*shards, adaptive, info, *lefts, *rights, *data)


RING = 4


def reduce_kernel(n_wide, n_narrow, images, shard, *refs):
    grad_refs = refs[:4]
    (
        g_mods_ref,
        g_patch_ref,
        g_final_ref,
        g_bias_ref,
        adaptive_low,
        sheet,
        time_pre,
        condition,
        own_act,
        time_two,
        lefts,
        rights,
    ) = refs[4:16]
    turned_out, rows_out, window_out, totals_out, clip_out = refs[16:21]
    out_ref = refs[21]
    scratch = refs[22:]
    own, from_core, to_near, from_near, to_far, from_far, acc, acc_far = scratch[:8]
    load_sem, core_sem, near_sem, far_sem, back_sem, last_sem = scratch[8:14]
    (
        mods_all,
        by_mod,
        product_parts,
        first_part,
        biases,
        small_out,
        small_in,
        small_all,
        act_all,
        stage,
        norm_out,
        norm_in,
        squares,
        ring,
        mods_sem,
        mods_near_sem,
        small_sem,
        act_sem,
        rows_sem,
        norm_sem,
        ring_sem,
    ) = scratch[14:]
    here = lax.axis_index("narrow")
    there = lax.axis_index("wide")
    core = there % 2
    n_bits = bits_of(n_narrow)
    w_bits = bits_of(n_wide)
    far_steps = w_bits - 1
    sibling = flipped(there, 1, w_bits)
    chunks, _, half, width = out_ref.shape
    side = width // 2

    leaving = []
    for path in range(2):
        done = 0
        place = 0
        steps = []
        for step in range(n_bits):
            bit = 1 << route(path, step, n_bits)
            masks = [mask for mask in range(n_narrow) if mask & bit and not mask & done]
            steps.append((bit, {mask: place + spot for spot, mask in enumerate(masks)}))
            place = place + len(masks)
            done = done | bit
        leaving.append(steps)

    parts = [(0, half, 0, width)]
    gives = []
    for step in range(far_steps):
        low, rows, left, cols = parts[-1]
        mine = there // (2 << step) % 2
        if rows % 32 == 0:
            keep = (low + mine * (rows // 2), rows // 2, left, cols)
            give = (low + (1 - mine) * (rows // 2), rows // 2, left, cols)
        elif cols % 256 == 0:
            keep = (low, rows, left + mine * (cols // 2), cols // 2)
            give = (low, rows, left + (1 - mine) * (cols // 2), cols // 2)
        else:
            keep = parts[-1]
            give = parts[-1]
        parts.append(keep)
        gives.append(give)
    traded = [gives[step] is not parts[step] for step in range(far_steps)]

    def window(part):
        low, rows, left, cols = part
        if not isinstance(low, int):
            low = pl.multiple_of(low, 16)
        if not isinstance(left, int):
            left = pl.multiple_of(left, 128)
        return (pl.ds(low, rows), pl.ds(left, cols))

    def keep_copy(k, grad_ref, first):
        start = pl.multiple_of((k - first) * 2 * half + core * half, 16)
        return pltpu.make_async_copy(
            grad_ref.at[:, pl.ds(start, half), :], own.at[k % RING], load_sem.at[k]
        )

    def start_keep(k):
        first = 0
        for grad_ref in grad_refs:
            tiles = grad_ref.shape[1] // (2 * half)

            @pl.when(jnp.logical_and(k >= first, k < first + tiles))
            def _(grad_ref=grad_ref, first=first):
                keep_copy(k, grad_ref, first).start()

            first = first + tiles

    def give_copy(k, grad_ref, first):
        start = pl.multiple_of((k - first) * 2 * half + (1 - core) * half, 16)
        return remote(
            grad_ref.at[:, pl.ds(start, half), :],
            from_core.at[k],
            core_sem.at[0, k],
            core_sem.at[1, k],
            "wide",
            sibling,
        )

    def near_copy(path, k, step):
        bit, masks = leaving[path][step]
        spots = pl.ds(min(masks.values()), len(masks))
        return remote(
            to_near.at[path, k % RING, spots],
            from_near.at[path, k, spots],
            near_sem.at[0, path, k, step],
            near_sem.at[1, path, k, step],
            "narrow",
            flipped(here, bit, n_bits),
        )

    def far_copy(k, step, part):
        return remote(
            to_far.at[(k % RING, step) + window(part)],
            from_far.at[(k, step) + window(part)],
            far_sem.at[0, k, step],
            far_sem.at[1, k, step],
            "wide",
            flipped(there, 2 << step, w_bits),
        )

    def back_copy(k, step, part):
        place = (k, core) + window(part)
        return remote(
            out_ref.at[place],
            out_ref.at[place],
            back_sem.at[0, k, step],
            back_sem.at[1, k, step],
            "wide",
            flipped(there, 2 << step, w_bits),
        )

    def last_copy(k, side_of):
        return remote(
            out_ref.at[k, side_of],
            out_ref.at[k, side_of],
            last_sem.at[0, k],
            last_sem.at[1, k],
            "wide",
            sibling,
        )

    def place_near(path, k, step, mask, total):
        columns = pl.ds(path * side, side)
        ring_slot = k % RING
        if step == n_bits:
            acc_far[ring_slot, :, columns] = total
        elif mask in leaving[path][step][1]:
            to_near[path, ring_slot, leaving[path][step][1][mask]] = total.astype(bf16)
        else:
            acc[ring_slot, mask, :, columns] = total

    def before(k, wait):
        @pl.when(k >= RING)
        def _():
            wait()

    def stage_core(k):
        keep_copy(k, grad_refs[0], k).wait()
        give_copy(k, grad_refs[0], k).wait_recv()
        for path in range(2):
            before(k, lambda path=path: near_copy(path, k - RING, 0).wait_send())
            columns = pl.ds(path * side, side)
            for mask in range(n_narrow):
                owner = flipped(here, mask, n_bits)
                total = own[k % RING, owner, :, columns].astype(f32) + from_core[
                    k, owner, :, columns
                ].astype(f32)
                place_near(path, k, 0, mask, total)
            near_copy(path, k, 0).start()
        start_keep(k + RING - 1)

    def stage_near(step, k):
        ring_slot = k % RING
        for path in range(2):
            columns = pl.ds(path * side, side)
            near_copy(path, k, step).wait_recv()
            if step + 1 < n_bits:
                before(k, lambda path=path: near_copy(path, k - RING, step + 1).wait_send())
            bit, masks = leaving[path][step]
            for mask, spot in masks.items():
                total = acc[ring_slot, mask - bit, :, columns] + from_near[path, k, spot].astype(f32)
                place_near(path, k, step + 1, mask - bit, total)
            if step + 1 < n_bits:
                near_copy(path, k, step + 1).start()
        if step + 1 == n_bits:
            start_far(0, k)

    def start_far(step, k):
        ring_slot = k % RING
        if step < far_steps:
            place = window(gives[step])
            before(k, lambda: far_copy(k - RING, step, gives[step]).wait_send())
            to_far[(ring_slot, step) + place] = acc_far[(ring_slot,) + place].astype(bf16)
            far_copy(k, step, gives[step]).start()
        else:
            place = window(parts[step])
            out_ref[(k, core) + place] = acc_far[(ring_slot,) + place].astype(bf16)
            start_back(far_steps - 1, k)

    def stage_far(step, k):
        ring_slot = k % RING
        far_copy(k, step, parts[step + 1]).wait_recv()
        place = window(parts[step + 1])
        if traded[step]:
            mine = acc_far[(ring_slot,) + place]
        else:
            mine = to_far[(ring_slot, step) + place].astype(f32)
        acc_far[(ring_slot,) + place] = mine + from_far[(k, step) + place].astype(f32)
        start_far(step + 1, k)

    def start_back(step, k):
        while step >= 0 and not traded[step]:
            step = step - 1
        if step >= 0:
            back_copy(k, step, parts[step + 1]).start()
        else:
            last_copy(k, core).start()

    def stage_back(step, k):
        back_copy(k, step, gives[step]).wait_recv()
        start_back(step - 1, k)

    def add_squares(value):
        squares[...] += jnp.sum(value * value, axis=0, keepdims=True)

    def turned_copy(slot, tile):
        return pltpu.make_async_copy(ring.at[slot], turned_out.at[tile], ring_sem.at[slot])

    def turn(high, rest, stack, tile, slot, used):
        @pl.when(used)
        def _():
            turned_copy(slot, tile).wait()

        left, left_rest = spread_left(lefts[stack])
        for start in range(0, WIDTH, STRIP):
            span = slice(start, start + STRIP)
            group = tile * (WIDTH // BLOCK // 4) + start // BLOCK // 4
            right, right_rest = halves(spread_right(rights[group], rights[group + 1]))
            value = dot(high[:, span], right) + dot(high[:, span], right_rest)
            if rest is not None:
                value = value + dot(rest[:, span], right)
            part, part_rest = halves(value)
            ring[slot, :, span] = dot_s(left, part) + (
                dot_s(left_rest, part) + dot_s(left, part_rest)
            )
        turned_copy(slot, tile).start()

    def stage_last(k):
        last_copy(k, 1 - core).wait_recv()
        for number in range(2):
            add_squares(out_ref[k, number].astype(f32))
        value = out_ref[k].reshape(2 * half, width)
        turn(value, None, left_number(k), k, k % 2, k >= 2)

    stages = [stage_core]
    stages += [partial(stage_near, step) for step in range(n_bits)]
    stages += [partial(stage_far, step) for step in range(far_steps)]
    stages += [partial(stage_back, step) for step in reversed(range(far_steps)) if traded[step]]
    stages += [stage_last]

    places = hop_order(n_wide, n_narrow)
    near_places = [("narrow", bit, n_bits) for bit in range(n_bits)]
    hops = len(places)
    slot = slot_of(n_wide, n_narrow)
    count = n_wide * n_narrow * images

    def beside(axis, bit, bits, source, target, sem, position):
        return remote(
            source,
            target,
            sem.at[0, position],
            sem.at[1, position],
            axis,
            flipped(lax.axis_index(axis), 1 << bit, bits),
        )

    column_bits = n_wide // 2
    half_rows = small_out.shape[1] // 2
    own_rows = pl.ds(pl.multiple_of(half_rows * core, 8), half_rows)
    small_places = places[hops - 1 :] + places[: hops - 1]

    def mods_copy(position):
        width = 1 << position
        block = mods_all.at[pl.ds(slot // width * width, width)]
        return beside(*places[position], block, block, mods_sem, position)

    def mods_near(path, step, mask, arrived):
        owner = flipped(here, arrived if mask is None else mask, n_bits)
        bit = 1 << route(path, step, n_bits)
        block = mods_all.at[
            pl.ds(column_bits * (owner + n_narrow * core), column_bits),
            :,
            pl.ds(path * side, side),
        ]
        return remote(
            block,
            block,
            mods_near_sem.at[0, path, arrived - 1],
            mods_near_sem.at[1, path, arrived - 1],
            "narrow",
            flipped(here, bit, n_bits),
        )

    def near_masks(path, step):
        done = sum(1 << route(path, earlier, n_bits) for earlier in range(step))
        bit = 1 << route(path, step, n_bits)
        return [(mask, mask | bit) for mask in range(n_narrow) if not mask & ~done]

    def small_copy(position):
        if position == 0:
            return beside(
                *small_places[0], small_out.at[0], small_in.at[0], small_sem, position
            )
        if position == hops:
            block = small_all.at[own_rows]
            return beside(*small_places[0], block, block, small_sem, position)
        return beside(
            *small_places[position],
            small_out.at[position, own_rows],
            small_in.at[position, own_rows],
            small_sem,
            position,
        )

    def act_copy(position):
        width = 1 << position
        block = act_all.at[pl.ds(here // width * width, width)]
        return beside(*near_places[position], block, block, act_sem, position)

    def small_total():
        return small_all[...]

    def rows_copy(start, rows, position):
        return pltpu.make_async_copy(
            stage.at[pl.ds(0, rows)], rows_out.at[pl.ds(start, rows)], rows_sem.at[position]
        )

    height = window_out.shape[0]

    def window_copy():
        start = here * shard // (WIDTH * ALIGN) * ALIGN
        return pltpu.make_async_copy(
            rows_out.at[pl.ds(pl.multiple_of(start, ALIGN), height)], window_out, rows_sem.at[2]
        )

    def mods_hop(position):
        if position == 0:
            mods_all[slot] = g_mods_ref[...].astype(bf16)
        elif position <= far_steps or position == hops:
            mods_copy(position - 1).wait_recv()
        else:
            step = position - 1 - far_steps
            for path in range(2):
                for _, arrived in near_masks(path, step):
                    mods_near(path, step, None, arrived).wait_recv()
        if position < far_steps or position == hops - 1:
            mods_copy(position).start()
        elif position < hops:
            step = position - far_steps
            for path in range(2):
                for mask, arrived in near_masks(path, step):
                    mods_near(path, step, mask, arrived).start()

    def small_hop(position):
        if position == 0:
            small_out[0, 0:PATCH] = g_patch_ref[...]
            small_out[0, PATCH : 2 * PATCH] = g_final_ref[...]
            small_out[0, 2 * PATCH : 2 * PATCH + 8] = g_bias_ref[...]
            small_out[0, 2 * PATCH + 8 :] = jnp.zeros(
                (small_out.shape[1] - 2 * PATCH - 8, WIDTH), f32
            )
        else:
            small_copy(position - 1).wait_recv()
            total = small_out[position - 1, own_rows] + small_in[position - 1, own_rows]
            if position < hops:
                small_out[position, own_rows] = total
            else:
                small_all[own_rows] = total
        small_copy(position).start()

    def small_end():
        other = pl.ds(pl.multiple_of(half_rows * (1 - core), 8), half_rows)
        block = small_all.at[other]
        beside(*small_places[0], block, block, small_sem, hops).wait_recv()

    def sort_mods():
        together = 8
        size = together * images * 8
        row = lax.broadcasted_iota(jnp.int32, (size, size), 0)
        column = lax.broadcasted_iota(jnp.int32, (size, size), 1)
        span = together * images
        order = jnp.where(column == row % span * 8 + row // span, 1.0, 0.0).astype(bf16)
        for block in range(mods_all.shape[0] // together):
            value = mods_all[block * together : (block + 1) * together].reshape(size, WIDTH)
            value = dot(order, value).astype(bf16)
            for index in range(8):
                by_mod[index, block * span : (block + 1) * span, :] = value[
                    index * span : (index + 1) * span
                ]

    def send_act():
        sort_mods()
        total = jnp.zeros(act_all.shape[1:], f32)
        for index in range(8):
            span = slice(index * WIDTH, (index + 1) * WIDTH)
            total = total + dot_t(by_mod[index], adaptive_low[:, span])
        act_all[here] = total
        act_copy(0).start()

    def act_hop(position):
        act_copy(position - 1).wait_recv()
        if position < n_bits:
            act_copy(position).start()

    def start_rows():
        grad = jnp.concatenate([act_all[number] for number in range(n_narrow)], axis=1)
        grad = grad * silu_slope(condition[...])
        high, rest = halves(grad)
        before = time_pre[...]
        first = (dot_t(high, time_two[...]) * silu_slope(before)).astype(bf16)
        product_parts[0:count] = high
        product_parts[count : 2 * count] = rest
        first_part[...] = first
        biases[0:1, :] = jnp.sum(first.astype(f32), axis=0, keepdims=True)
        biases[1:2, :] = jnp.sum(high.astype(f32), axis=0, keepdims=True)

    def upper_rows():
        stage[0:PATCH, :] = small_total()[0:PATCH]
        stage[ROW_TIME_ONE:ROW_TIME_TWO, :] = dot_s(
            sheet[:, :FREQS].astype(bf16), first_part[...]
        )
        act = jax.nn.silu(time_pre[...]).astype(bf16)
        stage[ROW_TIME_TWO:ROW_TABLE, :] = dot_s(act, product_parts[0:count])
        rows_copy(0, ROW_TABLE, 0).start()

    def table_rows(half_of):
        if half_of == 0:
            rows_copy(0, ROW_TABLE, 0).wait()
        size = 504
        labels = lax.broadcasted_iota(jnp.int32, (count, size), 1) + half_of * size
        pick = jnp.where(sheet[:, FREQS : FREQS + 1] == labels.astype(f32), 1.0, 0.0)
        pick = pick.astype(bf16)
        pick = jnp.concatenate([pick, pick], axis=0)
        stage[half_of * size : (half_of + 1) * size, :] = dot_s(pick, product_parts[...])

    def lower_rows():
        small = small_total()
        base = ROW_FINAL - ROW_TABLE
        stage[base : base + PATCH, :] = small[PATCH : 2 * PATCH]
        base = ROW_BIAS - ROW_TABLE
        bias = small[2 * PATCH : 2 * PATCH + 8]
        stage[base : base + 1, :] = bias[0:1]
        stage[base + 1 : base + 3, :] = biases[0:2, :]
        stage[base + 3 : base + 4, :] = bias[1:2]
        stage[base + 4 : base + 8, :] = bias[4:8]
        stage[base + 8 : base + 9, :] = bias[2:3]
        for index in range(8):
            stage[base + 9 + index : base + 10 + index, :] = jnp.sum(
                by_mod[index].astype(f32), axis=0, keepdims=True
            )
        lane = lax.broadcasted_iota(jnp.int32, (1, WIDTH), 1)
        stage[base + 17 : base + 18, :] = jnp.where(lane < PATCH, bias[3:4], 0.0)
        stage[base + 18 :, :] = jnp.zeros((stage.shape[0] - base - 18, WIDTH), f32)
        totals_out[...] = bias
        rows_copy(ROW_TABLE, stage.shape[0], 1).start()

    first_turn = chunks

    def adaptive_columns(index):
        value = dot_s(own_act[...], by_mod[index])
        add_squares(value)
        high, rest = halves(value)
        turn(high, rest, lefts.shape[0] - 1, first_turn + index, 2 + index % 2, index >= 2)

    def start_window():
        rows_copy(ROW_TABLE, stage.shape[0], 1).wait()
        window_copy().start()

    def window_squares():
        window_copy().wait()
        start = here * shard // (WIDTH * ALIGN) * ALIGN
        first = here * shard - start * WIDTH
        value = window_out[...]
        spot = (
            lax.broadcasted_iota(jnp.int32, value.shape, 0) * WIDTH
            + lax.broadcasted_iota(jnp.int32, value.shape, 1)
        )
        inside = jnp.logical_and(spot >= first, spot < first + shard)
        add_squares(jnp.where(inside, value, 0.0))

    def together(*steps):
        return lambda: [step() for step in steps]

    asides = [
        together(partial(mods_hop, position), partial(small_hop, position))
        for position in range(hops)
    ]
    asides += [together(partial(mods_hop, hops), partial(small_hop, hops), send_act)]
    first_act = len(asides)
    asides += [partial(act_hop, position) for position in range(1, n_bits)]
    asides[-1] = together(asides[-1], small_end)
    asides += [
        together(partial(act_hop, n_bits), start_rows),
        upper_rows,
        partial(table_rows, 0),
        partial(table_rows, 1),
        lower_rows,
        start_window,
        window_squares,
    ]

    squares[...] = jnp.zeros_like(squares)
    greet(n_wide, n_narrow)
    first = 0
    for grad_ref in grad_refs:
        tiles = grad_ref.shape[1] // (2 * half)

        def begin(k, carry, grad_ref=grad_ref, first=first):
            give_copy(k, grad_ref, first).start()
            return carry

        lax.fori_loop(first, first + tiles, begin, 0)
        first = first + tiles
    for k in range(RING - 1):
        start_keep(jnp.int32(k))

    def wave(t, carry):
        for number, stage in enumerate(stages):
            k = t - number

            @pl.when(jnp.logical_and(k >= 0, k < chunks))
            def _(stage=stage, k=k):
                stage(k)

        for number, aside in enumerate(asides):

            @pl.when(t == number)
            def _(aside=aside):
                aside()

        index = t - first_act

        @pl.when(jnp.logical_and(index >= 0, index < 8))
        def _():
            adaptive_columns(index)

        return carry

    lax.fori_loop(0, max(chunks + len(stages) - 1, len(asides), first_act + 8), wave, 0)

    def finish(k, carry):
        give_copy(k, grad_refs[0], k).wait_send()
        for step in range(far_steps):
            if traded[step]:
                back_copy(k, step, parts[step + 1]).wait_send()
        last_copy(k, core).wait_send()
        return carry

    lax.fori_loop(0, chunks, finish, 0)

    def finish_ring(k, carry):
        for path in range(2):
            for step in range(n_bits):
                near_copy(path, k, step).wait_send()
        for step in range(far_steps):
            far_copy(k, step, gives[step]).wait_send()
        return carry

    lax.fori_loop(chunks - RING, chunks, finish_ring, 0)
    for position in [*range(far_steps), hops - 1]:
        mods_copy(position).wait_send()
    for path in range(2):
        for step in range(n_bits):
            for mask, arrived in near_masks(path, step):
                mods_near(path, step, mask, arrived).wait_send()
    for position in range(hops + 1):
        small_copy(position).wait_send()
    for position in range(n_bits):
        act_copy(position).wait_send()
    for slot_of_ring in range(4):
        turned_copy(slot_of_ring, 0).wait()

    total = jnp.sum(squares[...], axis=1, keepdims=True)
    value = jnp.broadcast_to(total, norm_out.shape[1:])
    for position in range(n_bits):
        norm_out[position] = value
        copy = beside(
            *near_places[position],
            norm_out.at[position],
            norm_in.at[position],
            norm_sem,
            position,
        )
        copy.start()
        copy.wait()
        value = value + norm_in[position]
    norm = jnp.sqrt(value)
    row = lax.broadcasted_iota(jnp.int32, value.shape, 0)
    clip_out[...] = jnp.where(row == 0, norm, clip_limit / jnp.maximum(norm, clip_limit))


def reduce_all(n_wide, n_narrow, images, shard, grads, asides):
    rows = WIDTH // n_narrow
    chunks = sum(grad.shape[1] for grad in grads) // rows
    half = rows // 2
    far = bits_of(n_wide) - 1
    devices = n_wide * n_narrow
    hops = bits_of(devices)
    count = devices * images
    dma = pltpu.SemaphoreType.DMA
    any_space = pl.BlockSpec(memory_space=pl.ANY)
    vmem = pl.BlockSpec(memory_space=pltpu.VMEM)
    height = flat_rows(n_narrow, shard)
    turned, _, window, totals, clip = pl.pallas_call(
        partial(reduce_kernel, n_wide, n_narrow, images, shard),
        in_specs=[any_space] * 4 + [vmem] * len(asides),
        out_specs=[any_space, any_space, vmem, vmem, vmem],
        out_shape=[
            jax.ShapeDtypeStruct((chunks + 8, rows, WIDTH), f32),
            jax.ShapeDtypeStruct((height, WIDTH), f32),
            jax.ShapeDtypeStruct((shard_rows(shard), WIDTH), f32),
            jax.ShapeDtypeStruct((8, WIDTH), f32),
            jax.ShapeDtypeStruct((8, 128), f32),
        ],
        scratch_shapes=[
            pltpu.VMEM((chunks, 2, half, WIDTH), bf16),
            pltpu.VMEM((RING, n_narrow, half, WIDTH), bf16),
            pltpu.VMEM((chunks, n_narrow, half, WIDTH), bf16),
            pltpu.VMEM((2, RING, n_narrow - 1, half, WIDTH // 2), bf16),
            pltpu.VMEM((2, chunks, n_narrow - 1, half, WIDTH // 2), bf16),
            pltpu.VMEM((RING, far, half, WIDTH), bf16),
            pltpu.VMEM((chunks, far, half, WIDTH), bf16),
            pltpu.VMEM((RING, n_narrow, half, WIDTH), f32),
            pltpu.VMEM((RING, half, WIDTH), f32),
            dma((chunks,)),
            dma((2, chunks)),
            dma((2, 2, chunks, bits_of(n_narrow))),
            dma((2, chunks, far)),
            dma((2, chunks, far)),
            dma((2, chunks)),
            pltpu.VMEM((devices, images * 8, WIDTH), bf16),
            pltpu.VMEM((8, count, WIDTH), bf16),
            pltpu.VMEM((2 * count, WIDTH), bf16),
            pltpu.VMEM((count, WIDTH), bf16),
            pltpu.VMEM((8, WIDTH), f32),
            pltpu.VMEM((hops, 3 * PATCH, WIDTH), f32),
            pltpu.VMEM((hops, 3 * PATCH, WIDTH), f32),
            pltpu.VMEM((3 * PATCH, WIDTH), f32),
            pltpu.VMEM((n_narrow, count, rows), f32),
            pltpu.VMEM((height - ROW_TABLE, WIDTH), f32),
            pltpu.VMEM((bits_of(n_narrow), 8, 128), f32),
            pltpu.VMEM((bits_of(n_narrow), 8, 128), f32),
            pltpu.VMEM((1, WIDTH), f32),
            pltpu.VMEM((4, rows, WIDTH), f32),
            dma((2, hops)),
            dma((2, 2, n_narrow - 1)),
            dma((2, hops + 1)),
            dma((2, bits_of(n_narrow))),
            dma((3,)),
            dma((2, bits_of(n_narrow))),
            dma((4,)),
        ],
        compiler_params=pltpu.CompilerParams(
            collective_id=1, has_side_effects=True, vmem_limit_bytes=62 * 1024 * 1024
        ),
        cost_estimate=pl.CostEstimate(
            flops=10**8, bytes_accessed=300 * 10**6, transcendentals=0
        ),
        name="reduce_gradients",
    )(*grads, *asides)
    return turned, window, totals, clip


def weight_kernel(*refs):
    lefts, rights, outs = refs[0:4], refs[4:8], refs[8:12]
    taken, given, take_sem, give_sem = refs[12:]
    _, pieces, rows, _ = given.shape
    units = [
        (matrix, number)
        for matrix in range(4)
        for number in range(max(lefts[matrix].shape[1], rights[matrix].shape[1]) // WIDTH)
    ]

    def takes(unit):
        matrix, number = units[unit]
        copies = []
        for side, ref in enumerate((lefts[matrix], rights[matrix])):
            start = number * WIDTH if ref.shape[1] > WIDTH else 0
            copies.append(
                pltpu.make_async_copy(
                    ref.at[:, pl.ds(start, WIDTH)],
                    taken.at[unit % 3, side],
                    take_sem.at[unit % 3, side],
                )
            )
        return copies

    def give(unit):
        matrix, number = units[unit]
        if matrix < 3:
            target = outs[matrix].at[:, pl.ds(number * rows, rows), :]
        else:
            target = outs[3].at[pl.ds(number * pieces, pieces)]
        return pltpu.make_async_copy(given.at[unit % 2], target, give_sem.at[unit % 2])

    def given_out(slot):
        pltpu.make_async_copy(given.at[slot], given.at[slot], give_sem.at[slot]).wait()

    for unit in range(2):
        for copy in takes(unit):
            copy.start()

    def body(step, carry):
        for unit in range(2, len(units)):

            @pl.when(step + 2 == unit)
            def _(unit=unit):
                for copy in takes(unit):
                    copy.start()

        slot = step % 3
        out = step % 2
        for side in range(2):
            buffer = taken.at[slot, side]
            pltpu.make_async_copy(buffer, buffer, take_sem.at[slot, side]).wait()

        @pl.when(step >= 2)
        def _():
            given_out(out)

        for start in range(0, WIDTH, STRIP):
            span = slice(start, start + STRIP)
            value = dot_s(taken[slot, 0], taken[slot, 1, :, span]).astype(bf16)
            given[out, :, :, span] = value.reshape(pieces, rows, STRIP)
        for unit in range(len(units)):

            @pl.when(step == unit)
            def _(unit=unit):
                give(unit).start()

        return carry

    lax.fori_loop(0, len(units), body, 0)
    for slot in range(2):
        given_out(slot)


def weight_blocks(n_narrow, inputs, gradients):
    rows = WIDTH // n_narrow
    tokens = inputs[0].shape[0]
    any_space = pl.BlockSpec(memory_space=pl.ANY)
    shapes = [(n_narrow, gradient.shape[1] // n_narrow, WIDTH) for gradient in gradients[:3]]
    shapes.append((inputs[3].shape[1] // rows, rows, WIDTH))
    dma = pltpu.SemaphoreType.DMA
    results = pl.pallas_call(
        weight_kernel,
        in_specs=[any_space] * 8,
        out_specs=[any_space] * 4,
        out_shape=[jax.ShapeDtypeStruct(shape, bf16) for shape in shapes],
        scratch_shapes=[
            pltpu.VMEM((3, 2, tokens, WIDTH), bf16),
            pltpu.VMEM((2, n_narrow, rows, WIDTH), bf16),
            dma((3, 2)),
            dma((2,)),
        ],
        compiler_params=pltpu.CompilerParams(vmem_limit_bytes=60 * 1024 * 1024),
        name="weight_gradient",
    )(*inputs, *gradients)
    return [result.reshape(n_narrow, -1, WIDTH) for result in results]


def dot_s(left, right):
    return lax.dot_general(left, right, (((0,), (0,)), ((), ())), preferred_element_type=f32)


def center_back(grad, normal, scale):
    return (
        grad
        - jnp.mean(grad, axis=-1, keepdims=True)
        - normal * jnp.mean(grad * normal, axis=-1, keepdims=True)
    ) * scale


def gelu_pair(value):
    rate = math.sqrt(2.0 / math.pi)
    square = value * value
    bend = jnp.tanh(rate * value * (1.0 + 0.044715 * square))
    half = 0.5 * (1.0 + bend)
    slope = half + 0.5 * value * (1.0 - bend * bend) * (rate * (1.0 + 3.0 * 0.044715 * square))
    return value * half, slope


def layer_kernel(
    numbers,
    latent_ref,
    noise_ref,
    mods_ref,
    triple,
    mixed_ref,
    probs,
    place_ref,
    patch_ref,
    final_ref,
    tail_ref,
    attend_ref,
    output_ref,
    expand_ref,
    shrink_ref,
    normed_two_ref,
    act_ref,
    g_branch_two_ref,
    g_pre_ref,
    g_branch_ref,
    g_triple_ref,
    g_mods_ref,
    g_patch_ref,
    g_final_ref,
    g_bias_ref,
    slope,
    normal_one,
    normal_two,
    hidden,
    branch,
    g_mixed,
):
    image = pl.program_id(0)
    tokens = SEQUENCE
    wide = 256

    def bias(index):
        spot = ROW_BIAS - ROW_TAIL + index
        return tail_ref[spot : spot + 1, :]

    def bias_wide(ref, first, index):
        across = WIDTH // wide
        return (
            pl.ds(first + index // across, 1),
            pl.ds(pl.multiple_of(index % across * wide, wide), wide),
        )

    def row(index):
        return mods_ref[0, index : index + 1, :]

    @pl.when(image == 0)
    def _():
        for ref in (g_patch_ref, g_final_ref, g_bias_ref):
            ref[...] = jnp.zeros_like(ref)

    moment = numbers[0, image]
    blended = ((1.0 - moment) * latent_ref[0] + moment * noise_ref[0]).astype(bf16)
    target = noise_ref[0] - latent_ref[0]
    start = dot(blended, patch_ref[...]) + bias(0) + place_ref[...]
    hidden[...] = start
    normal, scale_one = center(start)
    normal_one[...] = normal
    zero = jnp.zeros((), bf16)
    masks = head_masks(tokens)
    first_half = masks[0]
    rate = HEAD_DIM ** (-0.5)

    value = dot(mixed_ref[...], output_ref[...]) + bias(3)
    branch[...] = value
    value = hidden[...] + row(2) * value
    hidden[...] = value
    normal, scale_two = center(value)
    normal_two[...] = normal
    normed_two_ref[...] = (normal * (1.0 + row(4)) + row(3)).astype(bf16)

    def widen(index, carry):
        span = pl.ds(pl.multiple_of(index * wide, wide), wide)
        before = dot(normed_two_ref[...], expand_ref[:, span])
        before = before + tail_ref[bias_wide(tail_ref, ROW_BIAS - ROW_TAIL + 4, index)]
        after, steep = gelu_pair(before)
        act_ref[:, span] = after.astype(bf16)
        slope[:, span] = steep
        return carry

    lax.fori_loop(0, MLP_WIDTH // wide, widen, 0, unroll=True)

    branch_two = dot(act_ref[...], shrink_ref[...]) + bias(8)
    upper = hidden[...] + row(5) * branch_two
    normal, scale_three = center(upper)
    final = (normal * (1.0 + row(7)) + row(6)).astype(bf16)
    mismatch = dot(final, final_ref[...]) + bias(17)[:, :PATCH] - target
    loss = numbers[2, image] * jnp.sum(mismatch * mismatch)
    grad_out = (numbers[1, image] * mismatch).astype(bf16)

    g_final_ref[...] += dot_s(final, grad_out)
    sums = jnp.sum(grad_out.astype(f32), axis=0, keepdims=True)
    spot = lax.broadcasted_iota(jnp.int32, (1, WIDTH), 1)
    sums = jnp.concatenate([sums, jnp.zeros((1, WIDTH - PATCH), f32)], axis=1)
    g_bias_ref[3:4, :] += jnp.where(spot == PATCH, loss, sums)
    grad = dot_t(grad_out, final_ref[...])
    shift_f = jnp.sum(grad, axis=0, keepdims=True)
    scale_f = jnp.sum(grad * normal, axis=0, keepdims=True)
    grad_upper = center_back((1.0 + row(7)) * grad, normal, scale_three)
    gate_two = jnp.sum(branch_two * grad_upper, axis=0, keepdims=True)
    grad_branch = (row(5) * grad_upper).astype(bf16)
    g_branch_two_ref[...] = grad_branch
    g_bias_ref[2:3, :] += jnp.sum(grad_branch.astype(f32), axis=0, keepdims=True)
    hidden[...] = grad_upper

    def narrow(index, carry):
        span = pl.ds(pl.multiple_of(index * wide, wide), wide)
        grad_act = dot_t(g_branch_two_ref[...], shrink_ref[span, :])
        grad_pre = (grad_act * slope[:, span]).astype(bf16)
        g_pre_ref[:, span] = grad_pre
        g_bias_ref[bias_wide(g_bias_ref, 4, index)] += jnp.sum(grad_pre.astype(f32), axis=0, keepdims=True)
        return carry

    lax.fori_loop(0, MLP_WIDTH // wide, narrow, 0, unroll=True)

    grad = dot_t(g_pre_ref[...], expand_ref[...])
    normal = normal_two[...]
    shift_two = jnp.sum(grad, axis=0, keepdims=True)
    scale_mod_two = jnp.sum(grad * normal, axis=0, keepdims=True)
    grad_middle = hidden[...] + center_back((1.0 + row(4)) * grad, normal, scale_two)
    gate_one = jnp.sum(branch[...] * grad_middle, axis=0, keepdims=True)
    grad_branch = (row(2) * grad_middle).astype(bf16)
    g_branch_ref[...] = grad_branch
    g_bias_ref[1:2, :] += jnp.sum(grad_branch.astype(f32), axis=0, keepdims=True)
    hidden[...] = grad_middle
    g_mixed[...] = dot_t(grad_branch, output_ref[...]).astype(bf16)

    def attend_back(pair, carry):
        query_span, key_span, value_span = pair_spans(pair)
        query = triple[:, query_span]
        keys = triple[:, key_span]
        values = triple[:, value_span]
        grad_mixed = g_mixed[:, query_span]
        results = []
        for side in range(2):
            low_weights = probs[2 * pair + side]
            weights = low_weights.astype(f32)
            grad_weights = dot_t(jnp.where(masks[side], grad_mixed, zero), values)
            grad_values = dot_s(low_weights, grad_mixed)
            grad_scores = weights * (
                grad_weights - jnp.sum(weights * grad_weights, axis=-1, keepdims=True)
            )
            grad_scores = grad_scores.astype(bf16)
            grad_query = dot(grad_scores, keys)
            grad_keys = dot_s(grad_scores, query)
            results.append((grad_query, grad_keys, grad_values))
        for part, span in enumerate((query_span, key_span, value_span)):
            merged = jnp.where(first_half, results[0][part], results[1][part])
            if part < 2:
                merged = merged * rate
            g_triple_ref[:, span] = merged.astype(bf16)
        return carry

    lax.fori_loop(0, HEADS // 2, attend_back, 0, unroll=True)

    grad = dot_t(g_triple_ref[...], attend_ref[...])
    normal = normal_one[...]
    shift_one = jnp.sum(grad, axis=0, keepdims=True)
    scale_mod_one = jnp.sum(grad * normal, axis=0, keepdims=True)
    grad_start = hidden[...] + center_back((1.0 + row(1)) * grad, normal, scale_one)
    grad_start = grad_start.astype(bf16)
    g_patch_ref[...] += dot_s(blended, grad_start)
    g_bias_ref[0:1, :] += jnp.sum(grad_start.astype(f32), axis=0, keepdims=True)
    for index, value in enumerate(
        (shift_one, scale_mod_one, gate_one, shift_two, scale_mod_two, gate_two, shift_f, scale_f)
    ):
        g_mods_ref[0, index : index + 1, :] = value


def layer(numbers, latent, noisy, mods, attention, patch_w, final_w, tail, weights):
    images = latent.shape[0]
    tokens = images * SEQUENCE
    once = pl.Buffered(1)

    def whole(array):
        return pl.BlockSpec(
            array.shape, lambda i: (0,) * len(array.shape), pipeline_mode=once
        )

    def fixed(shape, dtype=f32):
        return pl.BlockSpec(shape, lambda i: (0,) * len(shape)), jax.ShapeDtypeStruct(shape, dtype)

    def per_image(width):
        return (
            pl.BlockSpec((SEQUENCE, width), lambda i: (i, 0)),
            jax.ShapeDtypeStruct((tokens, width), bf16),
        )

    outs = [
        per_image(WIDTH),
        per_image(MLP_WIDTH),
        per_image(WIDTH),
        per_image(MLP_WIDTH),
        per_image(WIDTH),
        per_image(3 * WIDTH),
        (
            pl.BlockSpec((1, 8, WIDTH), lambda i: (i, 0, 0)),
            jax.ShapeDtypeStruct((images, 8, WIDTH), f32),
        ),
        fixed((PATCH, WIDTH)),
        fixed((WIDTH, PATCH)),
        fixed((8, WIDTH)),
    ]
    place = positions(SEQUENCE, WIDTH)
    fixed_args = (place, patch_w, final_w, tail) + tuple(weights)
    flops = 2 * 2 * 7078 * 1000 * tokens
    return pl.pallas_call(
        layer_kernel,
        grid=(images,),
        in_specs=[
            pl.BlockSpec(memory_space=pltpu.SMEM),
            pl.BlockSpec((1, SEQUENCE, PATCH), lambda i: (i, 0, 0)),
            pl.BlockSpec((1, SEQUENCE, PATCH), lambda i: (i, 0, 0)),
            pl.BlockSpec((1, 8, WIDTH), lambda i: (i, 0, 0)),
            pl.BlockSpec((SEQUENCE, 3 * WIDTH), lambda i: (i, 0)),
            pl.BlockSpec((SEQUENCE, WIDTH), lambda i: (i, 0)),
            pl.BlockSpec((HEADS, SEQUENCE, SEQUENCE), lambda i: (i, 0, 0)),
        ]
        + [whole(array) for array in fixed_args],
        out_specs=[spec for spec, _ in outs],
        out_shape=[shape for _, shape in outs],
        scratch_shapes=[
            pltpu.VMEM((SEQUENCE, MLP_WIDTH), f32),
            pltpu.VMEM((SEQUENCE, WIDTH), f32),
            pltpu.VMEM((SEQUENCE, WIDTH), f32),
            pltpu.VMEM((SEQUENCE, WIDTH), f32),
            pltpu.VMEM((SEQUENCE, WIDTH), f32),
            pltpu.VMEM((SEQUENCE, WIDTH), bf16),
        ],
        compiler_params=pltpu.CompilerParams(vmem_limit_bytes=56 * 1024 * 1024),
        cost_estimate=pl.CostEstimate(
            flops=flops, bytes_accessed=60 * 10**6, transcendentals=0
        ),
        name="layer",
    )(numbers, latent, noisy, mods, *attention, *fixed_args)


def local(
    n_wide,
    n_narrow,
    latents,
    noise_field,
    labels,
    label_drop,
    time_steps,
    loss_weights,
    attend_weight,
    attend_first,
    attend_second,
    attend_left,
    attend_right,
    output_weight,
    output_first,
    output_second,
    output_left,
    output_right,
    expand_weight,
    expand_first,
    expand_second,
    expand_left,
    expand_right,
    shrink_weight,
    shrink_first,
    shrink_second,
    shrink_left,
    shrink_right,
    adaptive_weight,
    adaptive_first,
    adaptive_second,
    adaptive_left,
    adaptive_right,
    shared_weight,
    shared_first,
    shared_second,
):
    column = lax.axis_index("narrow")
    images = labels.shape[0] * labels.shape[1]

    moment = (time_steps.reshape(images).astype(f32) + 0.5) / TIMESTEPS
    chosen = jnp.where(label_drop == 1, CLASSES - 1, labels).reshape(images, 1).astype(f32)
    weights_here = loss_weights.reshape(images)
    info = jnp.concatenate(
        [rounded(frequencies(moment, FREQS)).astype(f32), chosen, weights_here[:, None]], axis=1
    )
    info = jnp.pad(info, ((0, 8 - images), (0, SHEET - info.shape[1])))[None]

    shape = (images,) + latents.shape[2:]

    shard = shared_weight.shape[0]
    rows = shard_rows(shard)
    row_start = column * shard // (WIDTH * ALIGN) * ALIGN
    offset = column * shard - row_start * WIDTH
    margin = -(-(ALIGN + 1) * WIDTH // 1024) * 1024
    own = lax.pad(shared_weight, f32(0.0), [(margin, rows * WIDTH - shard, 0)])
    own = lax.dynamic_slice(own, (margin - offset,), (rows * WIDTH,)).reshape(rows, WIDTH)

    (
        *full,
        patch_w,
        final_rows,
        tail,
        time_two,
        sheet,
        time_pre,
        condition,
        own_act,
        adaptive_low,
        mods,
        total,
        lefts,
        rights,
        normed,
        triple,
        mixed,
        probs,
    ) = gather_all(
        n_wide,
        n_narrow,
        images,
        shard,
        (own, attend_weight, output_weight, expand_weight, shrink_weight),
        adaptive_weight,
        info,
        (attend_left, output_left, expand_left, shrink_left, adaptive_left),
        [
            blocks.transpose(1, 2, 0) if blocks.shape[0] > BLOCK else blocks
            for blocks in (attend_right, output_right, expand_right, shrink_right, adaptive_right)
        ],
        (
            moment,
            latents.reshape(shape),
            noise_field.reshape(shape),
            positions(SEQUENCE, WIDTH),
        ),
    )
    lefts = lefts.reshape(8, -1, BLOCK)
    rights = rights.reshape(-1, BLOCK, 4 * BLOCK)
    weight_sum = total[0, 0]

    entries = SEQUENCE * PATCH
    numbers = jnp.stack(
        [moment, 2.0 * weights_here / (entries * weight_sum), weights_here / entries]
    )
    (
        normed_two,
        act,
        g_branch_two,
        g_pre,
        g_branch,
        g_triple,
        g_mods,
        g_patch,
        g_final,
        g_bias,
    ) = layer(
        numbers,
        latents.reshape(shape),
        noise_field.reshape(shape),
        mods,
        (triple, mixed, probs),
        patch_w,
        final_rows.astype(bf16).reshape(WIDTH, PATCH),
        tail,
        full,
    )

    turned, window, totals, clip = reduce_all(
        n_wide,
        n_narrow,
        images,
        shard,
        weight_blocks(
            n_narrow,
            (normed, mixed, normed_two, act),
            (g_triple, g_branch, g_pre, g_branch_two),
        ),
        (
            g_mods.reshape(images * 8, WIDTH),
            g_patch,
            g_final.reshape(PATCH, WIDTH),
            g_bias,
            adaptive_low,
            sheet,
            time_pre,
            condition,
            own_act,
            time_two,
            lefts,
            rights,
        ),
    )
    loss_sum = totals[3, PATCH]
    clip_norm = clip[0, 0]
    factor = clip[1, 0]
    grad_shared = lax.dynamic_slice(window.reshape(-1), (offset,), (shard,))

    results = rotated_update(
        clip,
        turned,
        lefts,
        rights,
        (
            (attend_weight, attend_first, attend_second),
            (output_weight, output_first, output_second),
            (expand_weight, expand_first, expand_second),
            (shrink_weight, shrink_first, shrink_second),
            (adaptive_weight, adaptive_first, adaptive_second),
        ),
    )
    fresh = plain_update(shared_weight, shared_first, shared_second, grad_shared * factor)
    results = [*results, fresh[0], fresh[1], fresh[2], fresh[0].astype(jnp.bfloat16)]
    return tuple(results) + (loss_sum, weight_sum, clip_norm)


def solution(mesh):
    data = P(None, ("wide", "narrow"))
    state = (P("narrow", None),) * 3 + (P("narrow", None, None), P())
    return jax.shard_map(
        partial(local, mesh.shape["wide"], mesh.shape["narrow"]),
        mesh=mesh,
        in_specs=(P(None, ("wide", "narrow"), None, None),) * 2
        + (data,) * 4
        + state * 5
        + (P("narrow"),) * 3,
        out_specs=(P("narrow", None),) * 20 + (P("narrow"),) * 4 + (P(),) * 3,
        check_vma=False,
    )
```

```python
from functools import partial
import math

import jax
import jax.numpy as jnp
import numpy as np
from jax import lax
from jax.experimental import pallas as pl
from jax.experimental.pallas import tpu as pltpu
from jax.sharding import PartitionSpec as P

HEADS = 12
HEAD_DIM = 64
MLP_WIDTH = 3072
CLASSES = 1001
FREQS = 256
PATCH = 16
TIMESTEPS = 1000
BLOCK = 32
STEP_COUNT = 10
WIDTH = 768
SEQUENCE = 256


beta_one = 0.9
beta_two = 0.999
epsilon_adam = 1e-08
learn_rate = 0.03
decay_rate = 0.01
clip_limit = 0.002
highest = lax.Precision.HIGHEST
bf16 = jnp.bfloat16
f32 = jnp.float32

ROW_PATCH = 0
ROW_TIME_ONE = 16
ROW_TIME_TWO = 272
ROW_TABLE = 1040
ROW_FINAL = 2041
ROW_BIAS = 2057


def positions(tokens, width):
    side = math.isqrt(tokens)
    quarter = width // 4
    omega = 1.0 / 10000.0 ** (np.arange(quarter, dtype=np.float64) / quarter)
    place = np.arange(tokens)
    column = (place % side)[:, None] * omega
    row = (place // side)[:, None] * omega
    table = np.concatenate([np.sin(column), np.cos(column), np.sin(row), np.cos(row)], axis=1)
    return jnp.asarray(table.astype(np.float32))


def frequencies(moment, width):
    half = width // 2
    phases = jnp.exp(-math.log(10000.0) * jnp.arange(half, dtype=jnp.float32) / half)
    angles = moment[:, None] * 1000.0 * phases
    return jnp.concatenate([jnp.cos(angles), jnp.sin(angles)], axis=1)


def normalize(hidden):
    centered = hidden - jnp.mean(hidden, axis=-1, keepdims=True)
    return centered * lax.rsqrt(jnp.mean(centered * centered, axis=-1, keepdims=True) + 1e-06)


def modulate(hidden, shift, scale):
    return normalize(hidden) * (1.0 + scale[:, None, :]) + shift[:, None, :]


def adam_direction(first, second):
    return (first * (1.0 / (1.0 - beta_one**STEP_COUNT))) / (
        jnp.sqrt(second * (1.0 / (1.0 - beta_two**STEP_COUNT))) + epsilon_adam
    )


def plain_update(weight, first, second, grad):
    first = beta_one * first + (1.0 - beta_one) * grad
    second = beta_two * second + (1.0 - beta_two) * grad * grad
    weight = weight - learn_rate * (adam_direction(first, second) + decay_rate * weight)
    return (weight, first, second)


def rounded(value):
    return value.astype(jnp.bfloat16)


def product(inputs, weight):
    return jnp.dot(inputs, weight, preferred_element_type=jnp.float32)


def backprod(gradient, weight):
    return jnp.einsum("...n,kn->...k", gradient, weight, preferred_element_type=jnp.float32)


def weight_grad(inputs, gradient):
    flat_in = inputs.reshape(-1, inputs.shape[-1])
    flat_grad = gradient.reshape(-1, gradient.shape[-1])
    return lax.dot_general(
        flat_in, flat_grad, (((0,), (0,)), ((), ())), preferred_element_type=jnp.float32
    )


def bias_grad(gradient):
    return jnp.sum(gradient.astype(jnp.float32).reshape(-1, gradient.shape[-1]), axis=0)


def halves(value):
    high = value.astype(bf16)
    return high, (value - high.astype(f32)).astype(bf16)


def spread_left(blocks):
    size = blocks.shape[0]
    place = lax.broadcasted_iota(jnp.int32, (BLOCK, size), 0)
    column = lax.broadcasted_iota(jnp.int32, (BLOCK, size), 1)
    repeat = (place == column % BLOCK).astype(bf16)
    row_block = lax.broadcasted_iota(jnp.int32, (size, size), 0) // BLOCK
    col_block = lax.broadcasted_iota(jnp.int32, (size, size), 1) // BLOCK
    return tuple(
        jnp.where(
            row_block == col_block, jnp.dot(part, repeat, preferred_element_type=f32), 0.0
        ).astype(bf16)
        for part in halves(blocks)
    )


def spread_right(first, second):
    size = 4 * BLOCK
    row_block = lax.broadcasted_iota(jnp.int32, (size, size), 0) // BLOCK
    col_block = lax.broadcasted_iota(jnp.int32, (size, size), 1) // BLOCK
    inside = row_block == col_block
    corners = [
        jnp.where(inside, jnp.concatenate([row] * 4, axis=0), 0.0) for row in (first, second)
    ]
    empty = jnp.zeros((size, size), f32)
    return jnp.concatenate(
        [
            jnp.concatenate([corners[0], empty], axis=1),
            jnp.concatenate([empty, corners[1]], axis=1),
        ],
        axis=0,
    )


def dot(left, right):
    return jnp.dot(left, right, preferred_element_type=f32)


def dot_t(left, right):
    return lax.dot_general(left, right, (((1,), (1,)), ((), ())), preferred_element_type=f32)


STRIP = 256
TILES = ((3, 1), (1, 1), (4, 1), (1, 4), (8, 1))


def tile_places():
    places = []
    for matrix, (across, down) in enumerate(TILES):
        for number in range(across * down):
            places.append((matrix, number // across, number % across))
    return places


def left_number(tile):
    return (tile + 9) // 12 + (tile + 8) // 12 + (tile + 4) // 12 * (tile - 7)


def adam_kernel(count, *refs):
    factor_ref, turned, lefts, rights = refs[:4]
    states = [refs[4 + 3 * matrix : 7 + 3 * matrix] for matrix in range(5)]
    outs = [refs[19 + 4 * matrix : 23 + 4 * matrix] for matrix in range(5)]
    taken, given, low, take_sem, give_sem = refs[39:]
    rows = taken.shape[2]
    places = tile_places()
    factor = factor_ref[1, 0]

    def window(number):
        _, down, across = places[number]
        return (pl.ds(down * rows, rows), pl.ds(across * WIDTH, WIDTH))

    def takes(number):
        slot = number % 3
        arrays = [ref.at[window(number)] for ref in states[places[number][0]]]
        arrays.append(turned.at[number])
        return [
            pltpu.make_async_copy(array, taken.at[slot, part], take_sem.at[slot, part])
            for part, array in enumerate(arrays)
        ]

    def gives(number):
        slot = number % 2
        arrays = [ref.at[window(number)] for ref in outs[places[number][0]]]
        sources = [given.at[slot, part] for part in range(3)] + [low.at[slot]]
        return [
            pltpu.make_async_copy(source, array, give_sem.at[slot, part])
            for part, (source, array) in enumerate(zip(sources, arrays))
        ]

    def given_out(slot):
        for part in range(4):
            buffer = low.at[slot] if part == 3 else given.at[slot, part]
            pltpu.make_async_copy(buffer, buffer, give_sem.at[slot, part]).wait()

    for number in range(2):
        for copy in takes(number):
            copy.start()

    def body(tile, carry):
        for number in range(2, count):

            @pl.when(tile + 2 == number)
            def _(number=number):
                for copy in takes(number):
                    copy.start()

        slot = tile % 3
        out = tile % 2
        for part in range(4):
            buffer = taken.at[slot, part]
            pltpu.make_async_copy(buffer, buffer, take_sem.at[slot, part]).wait()

        @pl.when(tile >= 2)
        def _():
            given_out(out)

        stack = jnp.where(tile < 12, left_number(jnp.minimum(tile, 11)), 7)
        left = spread_left(lefts[stack])[0]
        for start in range(0, WIDTH, STRIP):
            span = slice(start, start + STRIP)
            group = tile * (WIDTH // BLOCK // 4) + start // BLOCK // 4
            right = spread_right(rights[group], rights[group + 1]).astype(bf16)
            grad = taken[slot, 3, :, span] * factor
            first = beta_one * taken[slot, 1, :, span] + (1.0 - beta_one) * grad
            second = beta_two * taken[slot, 2, :, span] + (1.0 - beta_two) * grad * grad
            given[out, 1, :, span] = first
            given[out, 2, :, span] = second
            step = adam_direction(first, second)
            step = dot_t(step.astype(bf16), right)
            step = dot(left, step.astype(bf16))
            weight = taken[slot, 0, :, span]
            weight = weight - learn_rate * (step + decay_rate * weight)
            given[out, 0, :, span] = weight
            low[out, :, span] = weight.astype(bf16)
        for number in range(count):

            @pl.when(tile == number)
            def _(number=number):
                for copy in gives(number):
                    copy.start()

        return carry

    lax.fori_loop(0, count, body, 0)
    for slot in range(2):
        given_out(slot)


def rotated_update(clip, turned, lefts, rights, states):
    count, rows, _ = turned.shape
    any_space = pl.BlockSpec(memory_space=pl.ANY)
    vmem = pl.BlockSpec(memory_space=pltpu.VMEM)
    shapes = []
    for weight, _, _ in states:
        shapes += [jax.ShapeDtypeStruct(weight.shape, f32)] * 3
        shapes += [jax.ShapeDtypeStruct(weight.shape, bf16)]
    dma = pltpu.SemaphoreType.DMA
    return pl.pallas_call(
        partial(adam_kernel, count),
        in_specs=[pl.BlockSpec(memory_space=pltpu.SMEM), any_space, vmem, vmem]
        + [any_space] * 15,
        out_specs=[any_space] * 20,
        out_shape=shapes,
        scratch_shapes=[
            pltpu.VMEM((3, 4, rows, WIDTH), f32),
            pltpu.VMEM((2, 3, rows, WIDTH), f32),
            pltpu.VMEM((2, rows, WIDTH), bf16),
            dma((3, 4)),
            dma((2, 4)),
        ],
        compiler_params=pltpu.CompilerParams(vmem_limit_bytes=60 * 1024 * 1024),
        name="rotated_adam",
    )(clip, turned, lefts, rights, *[array for state in states for array in state])


def bits_of(extent):
    return extent.bit_length() - 1


def flipped(index, mask, count):
    for bit in range(count):
        if mask >> bit & 1:
            index = index + (1 - 2 * (index // (1 << bit) % 2)) * (1 << bit)
    return index


def greet(n_wide, n_narrow):
    barrier = pltpu.get_barrier_semaphore()
    count = 0
    for axis, extent in (("narrow", n_narrow), ("wide", n_wide)):
        me = lax.axis_index(axis)
        for bit in range(bits_of(extent)):
            pl.semaphore_signal(
                barrier,
                inc=1,
                device_id={axis: flipped(me, 1 << bit, bits_of(extent))},
                device_id_type=pl.DeviceIdType.MESH,
            )
            count = count + 1
    pl.semaphore_wait(barrier, count)


def remote(source, target, send_sem, recv_sem, axis, peer):
    return pltpu.make_async_remote_copy(
        src_ref=source,
        dst_ref=target,
        send_sem=send_sem,
        recv_sem=recv_sem,
        device_id={axis: peer},
        device_id_type=pl.DeviceIdType.MESH,
    )


def slot_of(n_wide, n_narrow):
    here = lax.axis_index("narrow")
    there = lax.axis_index("wide")
    return there // 2 + n_wide // 2 * (here + n_narrow * (there % 2))


def hop_order(n_wide, n_narrow):
    n_bits = bits_of(n_narrow)
    w_bits = bits_of(n_wide)
    places = [("wide", bit, w_bits) for bit in range(1, w_bits)]
    places += [("narrow", bit, n_bits) for bit in range(n_bits)]
    return places + [("wide", 0, w_bits)]


def route(path, step, count):
    return (step + path) % count


ROW_TAIL = 2048
TAIL = 32
ALIGN = 16
SHEET = 384


def shard_rows(shard):
    rows = (shard + WIDTH - 2) // WIDTH + 1 + ALIGN
    return -(-rows // 32) * 32


def shard_start(number, shard):
    return number * shard // WIDTH // ALIGN * ALIGN


def flat_rows(n_narrow, shard):
    last = shard_start(n_narrow - 1, shard) + shard_rows(shard)
    return max(-(-last // ALIGN) * ALIGN, 2112)


def center(hidden):
    centered = hidden - jnp.mean(hidden, axis=-1, keepdims=True)
    scale = lax.rsqrt(jnp.mean(centered * centered, axis=-1, keepdims=True) + 1e-06)
    return centered * scale, scale


def pair_spans(pair):
    return [
        pl.ds(pl.multiple_of(part * WIDTH + pair * 2 * HEAD_DIM, 2 * HEAD_DIM), 2 * HEAD_DIM)
        for part in range(3)
    ]


def head_masks(tokens):
    lane = lax.broadcasted_iota(jnp.int32, (tokens, 2 * HEAD_DIM), 1)
    return lane < HEAD_DIM, lane >= HEAD_DIM


def bases_along_lanes(shape):
    return shape[0] == BLOCK and shape[2] > BLOCK


def silu_slope(value):
    gate = jax.nn.sigmoid(value)
    return gate * (1.0 + value * (1.0 - gate))


def own_columns(value, n_narrow):
    here = lax.axis_index("narrow")
    width = value.shape[1] // n_narrow
    result = value[:, :width]
    for number in range(1, n_narrow):
        result = jnp.where(
            here == number, value[:, number * width : (number + 1) * width], result
        )
    return result


def gather_kernel(n_wide, n_narrow, images, shard, *refs):
    count = 5
    shards = refs[:count]
    adaptive_ref, info_ref = refs[count : count + 2]
    left_refs = refs[count + 2 : count + 7]
    right_refs = refs[count + 7 : count + 12]
    moment_ref, latent_ref, noise_ref, place_ref = refs[count + 12 : count + 16]
    outs = refs[count + 16 : count + 37]
    scratch = refs[count + 37 :]
    (
        patch_out,
        final_out,
        tail_out,
        time_two_out,
        sheet,
        time_pre,
        condition,
        own_act,
        adaptive_low,
        mods_ref,
        total_ref,
        lefts_out,
        rights_out,
        normed_out,
        triple_out,
        mixed_out,
        probs_out,
    ) = outs[4:21]
    gathered = scratch[0]
    wides = scratch[1 : count + 1]
    lows = scratch[count + 1 : 2 * count + 1]
    (
        flat,
        turned,
        attend_full,
        normed,
        triple,
        mixed,
        probs,
        adaptive_wide,
        info_all,
        part,
        part_in,
        load_sem,
        keep_sem,
        send_sem,
        recv_sem,
        core_send,
        core_recv,
        info_sem,
        info_send,
        info_recv,
        part_send,
        part_recv,
        attend_sem,
        image_sem,
    ) = scratch[2 * count + 1 :]
    fulls = (gathered, attend_full) + tuple(outs[1:4])
    here = lax.axis_index("narrow")
    there = lax.axis_index("wide")
    core = there % 2
    n_bits = bits_of(n_narrow)
    w_bits = bits_of(n_wide)
    sibling = flipped(there, 1, w_bits)

    loads = [
        pltpu.make_async_copy(shards[number], wides[number], load_sem.at[number])
        for number in range(count)
    ]
    loads.append(pltpu.make_async_copy(adaptive_ref, adaptive_wide, load_sem.at[count]))
    for load in loads:
        load.start()
    slot = slot_of(n_wide, n_narrow)
    info_own = pltpu.make_async_copy(info_ref, info_all.at[pl.ds(slot, 1)], info_sem)
    info_own.start()
    greet(n_wide, n_narrow)
    sends = []

    def region(number, owner, half, path):
        rows, cols = shards[number].shape
        return (
            pl.ds(pl.multiple_of(owner * rows + half * (rows // 2), 16), rows // 2),
            pl.ds(path * (cols // 2), cols // 2),
        )

    def narrow_step(number, step, own):
        for path in range(2):
            bit = route(path, step, n_bits)
            peer = flipped(here, 1 << bit, n_bits)
            done = sum(1 << route(path, earlier, n_bits) for earlier in range(step))
            for mask in range(n_narrow):
                if mask & ~done or own != (mask == 0):
                    continue
                place = region(number, flipped(here, mask, n_bits), core, path)
                arrives = mask | 1 << bit
                if mask == 0:
                    rows, cols = shards[number].shape
                    source = lows[number].at[
                        pl.ds(pl.multiple_of(core * (rows // 2), 16), rows // 2),
                        pl.ds(path * (cols // 2), cols // 2),
                    ]
                else:
                    source = fulls[number].at[place]
                copy = remote(
                    source,
                    fulls[number].at[place],
                    send_sem.at[number, path, arrives - 1],
                    recv_sem.at[number, path, arrives - 1],
                    "narrow",
                    peer,
                )
                copy.start()
                sends.append(copy)

    def arrive(number, step):
        for path in range(2):
            bit = route(path, step, n_bits)
            done = sum(1 << route(path, earlier, n_bits) for earlier in range(step))
            for mask in range(n_narrow):
                if mask & ~done:
                    continue
                arrived = mask | 1 << bit
                place = region(number, flipped(here, arrived, n_bits), core, path)
                remote(
                    fulls[number].at[place],
                    fulls[number].at[place],
                    send_sem.at[number, path, arrived - 1],
                    recv_sem.at[number, path, arrived - 1],
                    "narrow",
                    flipped(here, 1 << bit, n_bits),
                ).wait_recv()
                copy = remote(
                    fulls[number].at[place],
                    fulls[number].at[place],
                    core_send.at[number, path, arrived - 1],
                    core_recv.at[number, path, arrived - 1],
                    "wide",
                    sibling,
                )
                copy.start()
                sends.append(copy)

    def from_sibling(number):
        for path in range(2):
            for mask in range(1, n_narrow):
                place = region(number, flipped(here, mask, n_bits), 1 - core, path)
                remote(
                    fulls[number].at[place],
                    fulls[number].at[place],
                    core_send.at[number, path, mask - 1],
                    core_recv.at[number, path, mask - 1],
                    "wide",
                    sibling,
                ).wait_recv()

    def cast_rows(source, target):
        def cast(index, carry):
            span = pl.ds(pl.multiple_of(index * 16, 16), 16)
            target[span, :] = source[span, :].astype(bf16)
            return carry

        lax.fori_loop(0, source.shape[0] // 16, cast, 0)

    keeps = []

    def begin(number):
        loads[number].wait()
        rows = shards[number].shape[0]
        cast_rows(wides[number], lows[number])
        keep = pltpu.make_async_copy(
            lows[number],
            fulls[number].at[pl.ds(pl.multiple_of(here * rows, 16), rows)],
            keep_sem.at[number],
        )
        keep.start()
        keeps.append(keep)
        narrow_step(number, 0, True)

    def begin_rest(number):
        for step in range(1, n_bits):
            narrow_step(number, step, True)

    places = hop_order(n_wide, n_narrow)

    def info_copy(position):
        axis, bit, bits = places[position]
        width = 1 << position
        base = slot // width * width
        return remote(
            info_all.at[pl.ds(base, width)],
            info_all.at[pl.ds(base, width)],
            info_send.at[position],
            info_recv.at[position],
            axis,
            flipped(lax.axis_index(axis), 1 << bit, bits),
        )

    def pass_on(numbers, step):
        for number in numbers:
            arrive(number, step)
            if step + 1 < n_bits:
                narrow_step(number, step + 1, False)

    info_own.wait()
    info_copy(0).start()
    begin(0)
    begin_rest(0)
    waiting = [lambda step=step: pass_on([0], step) for step in range(n_bits - 1)]
    waiting += [lambda: (begin(1), begin_rest(1)), lambda: (begin(2), begin_rest(2))]
    waiting += [lambda: begin(3), lambda: begin(4)]
    for position in range(len(places)):
        info_copy(position).wait()
        if position + 1 < len(places):
            info_copy(position + 1).start()
        if waiting:
            waiting.pop(0)()
    for step in waiting:
        step()
    pass_on([0], n_bits - 1)
    from_sibling(0)
    keeps[0].wait()

    height = shards[0].shape[0]
    reached = 0
    for number in range(n_narrow):
        start = shard_start(number, shard)
        overlap = max(reached - start, 0)
        block = number * height
        if overlap:
            flat[start:reached, :] = (
                flat[start:reached, :].astype(f32)
                + gathered[block : block + overlap, :].astype(f32)
            ).astype(bf16)
        flat[start + overlap : start + height, :] = gathered[block + overlap : block + height, :]
        reached = start + height
    if reached < flat.shape[0]:
        flat[reached:, :] = jnp.zeros((flat.shape[0] - reached, WIDTH), bf16)

    devices = n_wide * n_narrow
    for number in range(devices):
        sheet[number * images : (number + 1) * images, :] = info_all[number, :images, :]
    weights = sheet[:, FREQS + 1 : FREQS + 2]
    total_ref[...] = jnp.sum(weights, axis=0, keepdims=True)
    tail = flat[ROW_TAIL : ROW_TAIL + TAIL, :].astype(f32)
    tail_out[...] = tail
    patch_out[...] = flat[ROW_PATCH:ROW_TIME_ONE, :]
    time_two_out[...] = flat[ROW_TIME_TWO:ROW_TABLE, :]
    last = flat[ROW_FINAL - 9 : ROW_FINAL + 23, :].astype(f32)
    final_out[...] = last[9 : 9 + PATCH]
    tail_row = ROW_BIAS - ROW_TAIL
    value = dot(sheet[:, :FREQS].astype(bf16), flat[ROW_TIME_ONE:ROW_TIME_TWO, :])
    value = value + tail[tail_row + 1 : tail_row + 2]
    time_pre[...] = value
    act = jax.nn.silu(value).astype(bf16)
    value = dot(act, flat[ROW_TIME_TWO:ROW_TABLE, :]) + tail[tail_row + 2 : tail_row + 3]
    labels = lax.broadcasted_iota(jnp.int32, (sheet.shape[0], 1008), 1).astype(f32)
    pick = jnp.where(sheet[:, FREQS : FREQS + 1] == labels, 1.0, 0.0).astype(bf16)
    value = value + dot(pick, flat[ROW_TABLE : ROW_TABLE + 1008, :])
    condition[...] = value
    act = own_columns(jax.nn.silu(value), n_narrow)
    act = act.astype(bf16)
    own_act[...] = act

    loads[count].wait()
    cast_rows(adaptive_wide, adaptive_low)
    row = lax.broadcasted_iota(jnp.int32, (8 * n_narrow, act.shape[0]), 0)
    column = lax.broadcasted_iota(jnp.int32, (8 * n_narrow, act.shape[0]), 1)
    owner = there // 2 + n_wide // 2 * (row // 8 + n_narrow * core)
    chosen = column == owner * images + row % images
    near = dot(jnp.where(chosen, 1.0, 0.0).astype(bf16), act).astype(bf16)
    across = images

    def piece(index):
        first = index // across * images
        start = index % across * WIDTH
        return slice(first, first + images), slice(start, start + WIDTH)

    for index in range(8):
        value = dot(near, adaptive_low[:, index * WIDTH : (index + 1) * WIDTH])
        rows_of, span = piece(index)
        for number in range(n_narrow):
            start = 8 * number + rows_of.start
            part[0, number, rows_of, span] = value[start : start + images]

    def lay_bases():
        place = 0
        for ref in left_refs:
            blocks = ref.shape[0]
            lefts_out[place : place + blocks * BLOCK, :] = ref[...].reshape(-1, BLOCK)
            place = place + blocks * BLOCK
        place = 0
        for matrix, ref in enumerate(right_refs):
            turning = bases_along_lanes(ref.shape)
            blocks = ref.shape[2] if turning else ref.shape[0]
            copies = TILES[matrix][1]
            for row in range(BLOCK):
                turned[0:blocks, :] = ref[row].T if turning else ref[:, row, :]
                value = jnp.concatenate(
                    [turned[pl.ds(spot, blocks // 4, stride=4), :] for spot in range(4)], axis=1
                )
                for copy in range(copies):
                    start = place + copy * blocks // 4 * BLOCK + row
                    rights_out[pl.ds(start, blocks // 4, stride=BLOCK), :] = value
            place = place + copies * blocks // 4 * BLOCK

    def part_copy(step, mask):
        bit = 1 << step
        return remote(
            part.at[step, flipped(here, mask, n_bits)],
            part_in.at[step, flipped(here, mask, n_bits)],
            part_send.at[step, mask],
            part_recv.at[step, mask],
            "narrow",
            flipped(here, bit, n_bits),
        )

    def part_back(step, mask):
        bit = 1 << step
        owner = flipped(here, mask - bit, n_bits)
        return remote(
            part_in.at[step, owner],
            part_in.at[step, owner],
            part_send.at[step, mask],
            part_recv.at[step, mask],
            "narrow",
            flipped(here, bit, n_bits),
        ), owner

    for step in range(n_bits):
        bit = 1 << step
        masks = [
            mask for mask in range(n_narrow) if mask & bit and not mask & (bit - 1)
        ]
        for mask in masks:
            copy = part_copy(step, mask)
            copy.start()
            sends.append(copy)
        pass_on([1, 2] if step + 1 < n_bits else [], step)
        for mask in masks:
            back, owner = part_back(step, mask)
            back.wait_recv()
            if step + 1 < n_bits:
                part[step + 1, owner] = part[step, owner] + part_in[step, owner]
            else:
                value = part[step, owner] + part_in[step, owner]
                for index in range(8):
                    rows_of, span = piece(index)
                    for image in range(images):
                        start = rows_of.start + image
                        mods_ref[image, index : index + 1, :] = (
                            value[start : start + 1, span]
                            + tail[tail_row + 9 + index : tail_row + 10 + index]
                        )

    begin_rest(3)
    begin_rest(4)
    for step in range(n_bits - 1):
        pass_on([3, 4], step)
    pass_on([1], n_bits - 1)
    lay_bases()

    from_sibling(1)
    keeps[1].wait()
    attend_out = pltpu.make_async_copy(attend_full, outs[0], attend_sem)
    attend_out.start()
    masks = head_masks(SEQUENCE)
    rate = HEAD_DIM ** (-0.5)

    def image_copies(image):
        slot = image % 2
        tokens = pl.ds(pl.multiple_of(image * SEQUENCE, SEQUENCE), SEQUENCE)
        heads = pl.ds(image * HEADS, HEADS)
        pairs = (
            (normed, normed_out.at[tokens]),
            (triple, triple_out.at[tokens]),
            (mixed, mixed_out.at[tokens]),
            (probs, probs_out.at[heads]),
        )
        return [
            pltpu.make_async_copy(source.at[slot], target, image_sem.at[slot, number])
            for number, (source, target) in enumerate(pairs)
        ]

    def one_image(image, carry):
        slot = image % 2

        @pl.when(image >= 2)
        def _():
            for copy in image_copies(image - 2):
                copy.wait()

        moment = moment_ref[image]
        blended = (1.0 - moment) * latent_ref[image] + moment * noise_ref[image]
        start = dot(blended.astype(bf16), patch_out[...]) + tail_out[tail_row : tail_row + 1, :]
        normal, _ = center(start + place_ref[...])
        shift = mods_ref[image, 0:1, :]
        scale = mods_ref[image, 1:2, :]
        normed[slot] = (normal * (1.0 + scale) + shift).astype(bf16)

        for index in range(3 * WIDTH // STRIP):
            span = slice(index * STRIP, (index + 1) * STRIP)
            triple[slot, :, span] = dot(normed[slot], attend_full[:, span]).astype(bf16)
        for pair in range(HEADS // 2):
            query_span, key_span, value_span = pair_spans(pair)
            query = triple[slot, :, query_span]
            keys = triple[slot, :, key_span]
            values = triple[slot, :, value_span]
            results = []
            for side, mask in enumerate(masks):
                scores = dot_t(jnp.where(mask, query, jnp.zeros((), bf16)), keys) * rate
                scores = jnp.exp(scores - jnp.max(scores, axis=-1, keepdims=True))
                shares = scores * (1.0 / jnp.sum(scores, axis=-1, keepdims=True))
                shares = shares.astype(bf16)
                probs[slot, 2 * pair + side] = shares
                results.append(dot(shares, values))
            mixed[slot, :, query_span] = jnp.where(masks[0], results[0], results[1]).astype(bf16)
        for copy in image_copies(image):
            copy.start()
        return carry

    lax.fori_loop(0, images, one_image, 0)
    pass_on(range(2, count), n_bits - 1)
    for number in range(2, count):
        from_sibling(number)
    for keep in keeps[2:]:
        keep.wait()
    for copy in sends:
        copy.wait_send()
    for image in range(max(images - 2, 0), images):
        for copy in image_copies(image):
            copy.wait()
    attend_out.wait()


def gather_all(n_wide, n_narrow, images, shard, shards, adaptive, info, lefts, rights, data):
    count = len(shards)
    any_space = pl.BlockSpec(memory_space=pl.ANY)
    vmem = pl.BlockSpec(memory_space=pltpu.VMEM)
    devices = n_wide * n_narrow
    n_bits = bits_of(n_narrow)
    rows = adaptive.shape[0]
    dma = pltpu.SemaphoreType.DMA
    total = devices * images
    return pl.pallas_call(
        partial(gather_kernel, n_wide, n_narrow, images, shard),
        in_specs=[any_space] * (count + 2)
        + [vmem] * 10
        + [pl.BlockSpec(memory_space=pltpu.SMEM)]
        + [vmem] * 3,
        out_specs=[any_space] * (count - 1) + [vmem] * 13 + [any_space] * 4,
        out_shape=[
            jax.ShapeDtypeStruct((piece.shape[0] * n_narrow, piece.shape[1]), bf16)
            for piece in shards[1:]
        ]
        + [
            jax.ShapeDtypeStruct((PATCH, WIDTH), bf16),
            jax.ShapeDtypeStruct((PATCH, WIDTH), f32),
            jax.ShapeDtypeStruct((TAIL, WIDTH), f32),
            jax.ShapeDtypeStruct((WIDTH, WIDTH), bf16),
            jax.ShapeDtypeStruct((total, SHEET), f32),
            jax.ShapeDtypeStruct((total, WIDTH), f32),
            jax.ShapeDtypeStruct((total, WIDTH), f32),
            jax.ShapeDtypeStruct((total, rows), bf16),
            jax.ShapeDtypeStruct(adaptive.shape, bf16),
            jax.ShapeDtypeStruct((images, 8, WIDTH), f32),
            jax.ShapeDtypeStruct((1, 1), f32),
            jax.ShapeDtypeStruct((8 * rows, BLOCK), f32),
            jax.ShapeDtypeStruct((len(tile_places()) * 6 * BLOCK, 4 * BLOCK), f32),
            jax.ShapeDtypeStruct((images * SEQUENCE, WIDTH), bf16),
            jax.ShapeDtypeStruct((images * SEQUENCE, 3 * WIDTH), bf16),
            jax.ShapeDtypeStruct((images * SEQUENCE, WIDTH), bf16),
            jax.ShapeDtypeStruct((images * HEADS, SEQUENCE, SEQUENCE), bf16),
        ],
        scratch_shapes=[pltpu.VMEM((shards[0].shape[0] * n_narrow, WIDTH), bf16)]
        + [pltpu.VMEM(piece.shape, f32) for piece in shards]
        + [pltpu.VMEM(piece.shape, bf16) for piece in shards]
        + [
            pltpu.VMEM((flat_rows(n_narrow, shard), WIDTH), bf16),
            pltpu.VMEM((8 * WIDTH // BLOCK, BLOCK), f32),
            pltpu.VMEM((WIDTH, 3 * WIDTH), bf16),
            pltpu.VMEM((2, SEQUENCE, WIDTH), bf16),
            pltpu.VMEM((2, SEQUENCE, 3 * WIDTH), bf16),
            pltpu.VMEM((2, SEQUENCE, WIDTH), bf16),
            pltpu.VMEM((2, HEADS, SEQUENCE, SEQUENCE), bf16),
            pltpu.VMEM(adaptive.shape, f32),
            pltpu.VMEM((devices,) + info.shape[1:], f32),
            pltpu.VMEM((n_bits, n_narrow, 8, images * WIDTH), f32),
            pltpu.VMEM((n_bits, n_narrow, 8, images * WIDTH), f32),
            dma((count + 1,)),
            dma((count,)),
            dma((count, 2, n_narrow - 1)),
            dma((count, 2, n_narrow - 1)),
            dma((count, 2, n_narrow - 1)),
            dma((count, 2, n_narrow - 1)),
            dma,
            dma((bits_of(devices),)),
            dma((bits_of(devices),)),
            dma((n_bits, n_narrow)),
            dma((n_bits, n_narrow)),
            dma,
            dma((2, 4)),
        ],
        compiler_params=pltpu.CompilerParams(
            collective_id=0, has_side_effects=True, vmem_limit_bytes=60 * 1024 * 1024
        ),
        name="gather_weights",
    )(*shards, adaptive, info, *lefts, *rights, *data)


RING = 4


def reduce_kernel(n_wide, n_narrow, images, shard, *refs):
    input_refs, gradient_refs = refs[0:4], refs[4:8]
    (
        g_mods_ref,
        g_patch_ref,
        g_final_ref,
        g_bias_ref,
        adaptive_low,
        sheet,
        time_pre,
        condition,
        own_act,
        time_two,
        lefts,
        rights,
    ) = refs[8:20]
    turned_out, rows_out, window_out, totals_out, clip_out = refs[20:25]
    out_ref, pair, act_in, last_in, blocks, to_core = refs[25:31]
    scratch = refs[31:]
    own, from_core, to_near, from_near, to_far, from_far, acc, acc_far = scratch[:8]
    load_sem, core_sem, near_sem, far_sem, back_sem, last_sem = scratch[8:14]
    (
        mods_all,
        by_mod,
        product_parts,
        first_part,
        biases,
        small_first,
        small_out,
        small_in,
        small_all,
        act_all,
        stage,
        norm_out,
        norm_in,
        squares,
        ring,
        mods_sem,
        mods_near_sem,
        small_sem,
        act_sem,
        rows_sem,
        norm_sem,
        ring_sem,
    ) = scratch[14:]
    here = lax.axis_index("narrow")
    there = lax.axis_index("wide")
    core = there % 2
    n_bits = bits_of(n_narrow)
    w_bits = bits_of(n_wide)
    far_steps = w_bits - 1
    sibling = flipped(there, 1, w_bits)
    chunks, _, half, width = out_ref.shape
    side = width // 2

    leaving = []
    for path in range(2):
        done = 0
        place = 0
        steps = []
        for step in range(n_bits):
            bit = 1 << route(path, step, n_bits)
            masks = [mask for mask in range(n_narrow) if mask & bit and not mask & done]
            steps.append((bit, {mask: place + spot for spot, mask in enumerate(masks)}))
            place = place + len(masks)
            done = done | bit
        leaving.append(steps)

    parts = [(0, half, 0, width)]
    gives = []
    for step in range(far_steps):
        low, rows, left, cols = parts[-1]
        mine = there // (2 << step) % 2
        if rows % 32 == 0:
            keep = (low + mine * (rows // 2), rows // 2, left, cols)
            give = (low + (1 - mine) * (rows // 2), rows // 2, left, cols)
        elif cols % 256 == 0:
            keep = (low, rows, left + mine * (cols // 2), cols // 2)
            give = (low, rows, left + (1 - mine) * (cols // 2), cols // 2)
        else:
            keep = parts[-1]
            give = parts[-1]
        parts.append(keep)
        gives.append(give)
    traded = [gives[step] is not parts[step] for step in range(far_steps)]

    def window(part):
        low, rows, left, cols = part
        if not isinstance(low, int):
            low = pl.multiple_of(low, 16)
        if not isinstance(left, int):
            left = pl.multiple_of(left, 128)
        return (pl.ds(low, rows), pl.ds(left, cols))

    def give_copy(k):
        return remote(
            to_core.at[k % 2],
            from_core.at[k % RING],
            core_sem.at[0, k],
            core_sem.at[1, k],
            "wide",
            sibling,
        )

    products = [(0, 0), (0, 1), (0, 2), (1, 0), (2, 0), (2, 1), (2, 2), (2, 3)]
    lasting = act_in.shape[1]

    def start_pair(k):
        for number, (matrix, across) in enumerate(products):

            @pl.when(k == number)
            def _(number=number, matrix=matrix, across=across):
                slot_of = number % 2
                pltpu.make_async_copy(
                    input_refs[matrix], pair.at[slot_of, 0], load_sem.at[slot_of, 0]
                ).start()
                pltpu.make_async_copy(
                    gradient_refs[matrix].at[:, pl.ds(across * WIDTH, WIDTH)],
                    pair.at[slot_of, 1],
                    load_sem.at[slot_of, 1],
                ).start()

    def act_load(number):
        return pltpu.make_async_copy(
            input_refs[3].at[:, pl.ds(pl.multiple_of(number * lasting, lasting), lasting)],
            act_in,
            load_sem.at[2, 0],
        )

    def last_load():
        return pltpu.make_async_copy(gradient_refs[3], last_in, load_sem.at[2, 1])

    def put_halves(k, owner, span, lower, upper):
        own[k % 2, owner, :, span] = jnp.where(core == 0, lower, upper).astype(f32)
        to_core[k % 2, owner, :, span] = jnp.where(core == 0, upper, lower).astype(bf16)

    def stage_product(k):
        start_pair(k + 1)

        @pl.when(k >= 2)
        def _():
            give_copy(k - 2).wait_send()

        @pl.when(k < len(products))
        def _():
            slot_of = k % 2
            for side_of in range(2):
                buffer = pair.at[slot_of, side_of]
                pltpu.make_async_copy(buffer, buffer, load_sem.at[slot_of, side_of]).wait()
            for start in range(0, WIDTH, STRIP):
                span = slice(start, start + STRIP)
                value = dot_s(pair[slot_of, 0], pair[slot_of, 1, :, span])
                for owner in range(n_narrow):
                    top = owner * 2 * half
                    put_halves(
                        k,
                        owner,
                        span,
                        value[top : top + half],
                        value[top + half : top + 2 * half],
                    )

        @pl.when(k >= len(products))
        def _():
            for owner in range(n_narrow):
                block = owner * 4 + k - len(products)
                put_halves(
                    k,
                    owner,
                    slice(None),
                    blocks[block, 0:half, :].astype(f32),
                    blocks[block, half : 2 * half, :].astype(f32),
                )

        give_copy(k).start()

    def last_product(number):
        act_load(number).wait()
        for start in range(0, WIDTH, STRIP):
            span = slice(start, start + STRIP)
            value = dot_s(act_in[...], last_in[:, span]).astype(bf16)
            for piece in range(n_narrow):
                top = piece * 2 * half
                blocks[number * n_narrow + piece, :, span] = value[top : top + 2 * half]

        @pl.when(number < 3)
        def _():
            act_load(number + 1).start()

    def near_copy(path, k, step):
        bit, masks = leaving[path][step]
        spots = pl.ds(min(masks.values()), len(masks))
        return remote(
            to_near.at[path, k % RING, spots],
            from_near.at[path, k % RING, spots],
            near_sem.at[0, path, k, step],
            near_sem.at[1, path, k, step],
            "narrow",
            flipped(here, bit, n_bits),
        )

    def far_copy(k, step, part):
        return remote(
            to_far.at[(k % RING, step) + window(part)],
            from_far.at[(k % RING, step) + window(part)],
            far_sem.at[0, k, step],
            far_sem.at[1, k, step],
            "wide",
            flipped(there, 2 << step, w_bits),
        )

    def back_copy(k, step, part):
        place = (k, core) + window(part)
        return remote(
            out_ref.at[place],
            out_ref.at[place],
            back_sem.at[0, k, step],
            back_sem.at[1, k, step],
            "wide",
            flipped(there, 2 << step, w_bits),
        )

    def last_copy(k, side_of):
        return remote(
            out_ref.at[k, side_of],
            out_ref.at[k, side_of],
            last_sem.at[0, k],
            last_sem.at[1, k],
            "wide",
            sibling,
        )

    def place_near(path, k, step, mask, total):
        columns = pl.ds(path * side, side)
        ring_slot = k % RING
        if step == n_bits:
            acc_far[ring_slot, :, columns] = total
        elif mask in leaving[path][step][1]:
            to_near[path, ring_slot, leaving[path][step][1][mask]] = total.astype(bf16)
        else:
            acc[ring_slot, mask, :, columns] = total

    def before(k, wait):
        @pl.when(k >= RING)
        def _():
            wait()

    def stage_core(k):
        give_copy(k).wait_recv()
        for path in range(2):
            before(k, lambda path=path: near_copy(path, k - RING, 0).wait_send())
            columns = pl.ds(path * side, side)
            for mask in range(n_narrow):
                owner = flipped(here, mask, n_bits)
                total = own[k % 2, owner, :, columns] + from_core[
                    k % RING, owner, :, columns
                ].astype(f32)
                place_near(path, k, 0, mask, total)
            near_copy(path, k, 0).start()

    def stage_near(step, k):
        ring_slot = k % RING
        for path in range(2):
            columns = pl.ds(path * side, side)
            near_copy(path, k, step).wait_recv()
            if step + 1 < n_bits:
                before(k, lambda path=path: near_copy(path, k - RING, step + 1).wait_send())
            bit, masks = leaving[path][step]
            for mask, spot in masks.items():
                total = acc[ring_slot, mask - bit, :, columns] + from_near[path, ring_slot, spot].astype(f32)
                place_near(path, k, step + 1, mask - bit, total)
            if step + 1 < n_bits:
                near_copy(path, k, step + 1).start()
        if step + 1 == n_bits:
            start_far(0, k)

    def start_far(step, k):
        ring_slot = k % RING
        if step < far_steps:
            place = window(gives[step])
            before(k, lambda: far_copy(k - RING, step, gives[step]).wait_send())
            to_far[(ring_slot, step) + place] = acc_far[(ring_slot,) + place].astype(bf16)
            far_copy(k, step, gives[step]).start()
        else:
            place = window(parts[step])
            out_ref[(k, core) + place] = acc_far[(ring_slot,) + place].astype(bf16)
            start_back(far_steps - 1, k)

    def stage_far(step, k):
        ring_slot = k % RING
        far_copy(k, step, parts[step + 1]).wait_recv()
        place = window(parts[step + 1])
        if traded[step]:
            mine = acc_far[(ring_slot,) + place]
        else:
            mine = to_far[(ring_slot, step) + place].astype(f32)
        acc_far[(ring_slot,) + place] = mine + from_far[(ring_slot, step) + place].astype(f32)
        start_far(step + 1, k)

    def start_back(step, k):
        while step >= 0 and not traded[step]:
            step = step - 1
        if step >= 0:
            back_copy(k, step, parts[step + 1]).start()
        else:
            last_copy(k, core).start()

    def stage_back(step, k):
        back_copy(k, step, gives[step]).wait_recv()
        start_back(step - 1, k)

    def add_squares(value):
        squares[...] += jnp.sum(value * value, axis=0, keepdims=True)

    def turned_copy(slot, tile):
        return pltpu.make_async_copy(ring.at[slot], turned_out.at[tile], ring_sem.at[slot])

    def turn(high, rest, stack, tile, slot, used):
        @pl.when(used)
        def _():
            turned_copy(slot, tile).wait()

        left, left_rest = spread_left(lefts[stack])
        for start in range(0, WIDTH, STRIP):
            span = slice(start, start + STRIP)
            group = tile * (WIDTH // BLOCK // 4) + start // BLOCK // 4
            right, right_rest = halves(spread_right(rights[group], rights[group + 1]))
            value = dot(high[:, span], right) + dot(high[:, span], right_rest)
            if rest is not None:
                value = value + dot(rest[:, span], right)
            part, part_rest = halves(value)
            ring[slot, :, span] = dot_s(left, part) + (
                dot_s(left_rest, part) + dot_s(left, part_rest)
            )
        turned_copy(slot, tile).start()

    def stage_last(k):
        last_copy(k, 1 - core).wait_recv()
        for number in range(2):
            add_squares(out_ref[k, number].astype(f32))
        value = out_ref[k].reshape(2 * half, width)
        turn(value, None, left_number(k), k, k % 2, k >= 2)

    stages = [stage_product, stage_core]
    stages += [partial(stage_near, step) for step in range(n_bits)]
    stages += [partial(stage_far, step) for step in range(far_steps)]
    stages += [partial(stage_back, step) for step in reversed(range(far_steps)) if traded[step]]
    stages += [stage_last]

    places = hop_order(n_wide, n_narrow)
    near_places = [("narrow", bit, n_bits) for bit in range(n_bits)]
    hops = len(places)
    slot = slot_of(n_wide, n_narrow)
    count = n_wide * n_narrow * images

    def beside(axis, bit, bits, source, target, sem, position):
        return remote(
            source,
            target,
            sem.at[0, position],
            sem.at[1, position],
            axis,
            flipped(lax.axis_index(axis), 1 << bit, bits),
        )

    column_bits = n_wide // 2
    half_rows = small_out.shape[1]
    own_rows = pl.ds(pl.multiple_of(half_rows * core, 8), half_rows)
    small_places = places[hops - 1 :] + places[: hops - 1]

    def mods_copy(position):
        width = 1 << position
        block = mods_all.at[pl.ds(slot // width * width, width)]
        return beside(*places[position], block, block, mods_sem, position)

    def mods_near(path, step, mask, arrived):
        owner = flipped(here, arrived if mask is None else mask, n_bits)
        bit = 1 << route(path, step, n_bits)
        block = mods_all.at[
            pl.ds(column_bits * (owner + n_narrow * core), column_bits),
            :,
            pl.ds(path * side, side),
        ]
        return remote(
            block,
            block,
            mods_near_sem.at[0, path, arrived - 1],
            mods_near_sem.at[1, path, arrived - 1],
            "narrow",
            flipped(here, bit, n_bits),
        )

    def near_masks(path, step):
        done = sum(1 << route(path, earlier, n_bits) for earlier in range(step))
        bit = 1 << route(path, step, n_bits)
        return [(mask, mask | bit) for mask in range(n_narrow) if not mask & ~done]

    def small_copy(position):
        if position == 0:
            return beside(
                *small_places[0], small_first.at[0], small_first.at[1], small_sem, position
            )
        if position == hops:
            block = small_all.at[own_rows]
            return beside(*small_places[0], block, block, small_sem, position)
        return beside(
            *small_places[position],
            small_out.at[position],
            small_in.at[position],
            small_sem,
            position,
        )

    def act_copy(position):
        width = 1 << position
        block = act_all.at[pl.ds(here // width * width, width)]
        return beside(*near_places[position], block, block, act_sem, position)

    def small_total():
        return small_all[...]

    def rows_copy(start, rows, position):
        return pltpu.make_async_copy(
            stage.at[pl.ds(0, rows)], rows_out.at[pl.ds(start, rows)], rows_sem.at[position]
        )

    height = window_out.shape[0]

    def window_copies():
        start = here * shard // (WIDTH * ALIGN) * ALIGN
        source = rows_out.at[pl.ds(pl.multiple_of(start, ALIGN), height)]
        return [
            pltpu.make_async_copy(source, stage.at[pl.ds(0, height)], rows_sem.at[2]),
            pltpu.make_async_copy(stage.at[pl.ds(0, height)], window_out, rows_sem.at[3]),
        ]

    def mods_hop(position):
        if position == 0:
            mods_all[slot] = g_mods_ref[...].astype(bf16)
        elif position <= far_steps or position == hops:
            mods_copy(position - 1).wait_recv()
        else:
            step = position - 1 - far_steps
            for path in range(2):
                for _, arrived in near_masks(path, step):
                    mods_near(path, step, None, arrived).wait_recv()
        if position < far_steps or position == hops - 1:
            mods_copy(position).start()
        elif position < hops:
            step = position - far_steps
            for path in range(2):
                for mask, arrived in near_masks(path, step):
                    mods_near(path, step, mask, arrived).start()

    def small_hop(position):
        if position == 0:
            small_first[0, 0:PATCH] = g_patch_ref[...]
            small_first[0, PATCH : 2 * PATCH] = g_final_ref[...]
            small_first[0, 2 * PATCH : 2 * PATCH + 8] = g_bias_ref[...]
            small_first[0, 2 * PATCH + 8 :] = jnp.zeros(
                (small_first.shape[1] - 2 * PATCH - 8, WIDTH), f32
            )
        else:
            small_copy(position - 1).wait_recv()
            if position == 1:
                total = small_first[0, own_rows] + small_first[1, own_rows]
            else:
                total = small_out[position - 1] + small_in[position - 1]
            if position < hops:
                small_out[position] = total
            else:
                small_all[own_rows] = total
        small_copy(position).start()

    def small_end():
        other = pl.ds(pl.multiple_of(half_rows * (1 - core), 8), half_rows)
        block = small_all.at[other]
        beside(*small_places[0], block, block, small_sem, hops).wait_recv()

    def sort_mods():
        together = 8
        size = together * images * 8
        row = lax.broadcasted_iota(jnp.int32, (size, size), 0)
        column = lax.broadcasted_iota(jnp.int32, (size, size), 1)
        span = together * images
        order = jnp.where(column == row % span * 8 + row // span, 1.0, 0.0).astype(bf16)
        for block in range(mods_all.shape[0] // together):
            value = mods_all[block * together : (block + 1) * together].reshape(size, WIDTH)
            value = dot(order, value).astype(bf16)
            for index in range(8):
                by_mod[index, block * span : (block + 1) * span, :] = value[
                    index * span : (index + 1) * span
                ]

    def send_act():
        sort_mods()
        total = jnp.zeros(act_all.shape[1:], f32)
        for index in range(8):
            span = slice(index * WIDTH, (index + 1) * WIDTH)
            total = total + dot_t(by_mod[index], adaptive_low[:, span])
        act_all[here] = total
        act_copy(0).start()

    def act_hop(position):
        act_copy(position - 1).wait_recv()
        if position < n_bits:
            act_copy(position).start()

    def start_rows():
        grad = jnp.concatenate([act_all[number] for number in range(n_narrow)], axis=1)
        grad = grad * silu_slope(condition[...])
        high, rest = halves(grad)
        before = time_pre[...]
        first = (dot_t(high, time_two[...]) * silu_slope(before)).astype(bf16)
        product_parts[0:count] = high
        product_parts[count : 2 * count] = rest
        first_part[...] = first
        biases[0:1, :] = jnp.sum(first.astype(f32), axis=0, keepdims=True)
        biases[1:2, :] = jnp.sum(high.astype(f32), axis=0, keepdims=True)

    def upper_rows():
        stage[0:PATCH, :] = small_total()[0:PATCH]
        stage[ROW_TIME_ONE:ROW_TIME_TWO, :] = dot_s(
            sheet[:, :FREQS].astype(bf16), first_part[...]
        )
        act = jax.nn.silu(time_pre[...]).astype(bf16)
        stage[ROW_TIME_TWO:ROW_TABLE, :] = dot_s(act, product_parts[0:count])
        rows_copy(0, ROW_TABLE, 0).start()

    def table_rows(half_of):
        if half_of == 0:
            rows_copy(0, ROW_TABLE, 0).wait()
        size = 504
        labels = lax.broadcasted_iota(jnp.int32, (count, size), 1) + half_of * size
        pick = jnp.where(sheet[:, FREQS : FREQS + 1] == labels.astype(f32), 1.0, 0.0)
        pick = pick.astype(bf16)
        pick = jnp.concatenate([pick, pick], axis=0)
        stage[half_of * size : (half_of + 1) * size, :] = dot_s(pick, product_parts[...])

    def lower_rows():
        small = small_total()
        base = ROW_FINAL - ROW_TABLE
        stage[base : base + PATCH, :] = small[PATCH : 2 * PATCH]
        base = ROW_BIAS - ROW_TABLE
        bias = small[2 * PATCH : 2 * PATCH + 8]
        stage[base : base + 1, :] = bias[0:1]
        stage[base + 1 : base + 3, :] = biases[0:2, :]
        stage[base + 3 : base + 4, :] = bias[1:2]
        stage[base + 4 : base + 8, :] = bias[4:8]
        stage[base + 8 : base + 9, :] = bias[2:3]
        for index in range(8):
            stage[base + 9 + index : base + 10 + index, :] = jnp.sum(
                by_mod[index].astype(f32), axis=0, keepdims=True
            )
        lane = lax.broadcasted_iota(jnp.int32, (1, WIDTH), 1)
        stage[base + 17 : base + 18, :] = jnp.where(lane < PATCH, bias[3:4], 0.0)
        stage[base + 18 :, :] = jnp.zeros((stage.shape[0] - base - 18, WIDTH), f32)
        totals_out[...] = bias
        rows_copy(ROW_TABLE, stage.shape[0], 1).start()

    first_turn = chunks

    def adaptive_columns(index):
        value = dot_s(own_act[...], by_mod[index])
        add_squares(value)
        high, rest = halves(value)
        turn(high, rest, lefts.shape[0] - 1, first_turn + index, 2 + index % 2, index >= 2)

    def start_window():
        rows_copy(ROW_TABLE, stage.shape[0], 1).wait()
        window_copies()[0].start()

    def window_squares():
        window_copies()[0].wait()
        window_copies()[1].start()
        start = here * shard // (WIDTH * ALIGN) * ALIGN
        first = here * shard - start * WIDTH
        value = stage[0:height, :]
        spot = (
            lax.broadcasted_iota(jnp.int32, value.shape, 0) * WIDTH
            + lax.broadcasted_iota(jnp.int32, value.shape, 1)
        )
        inside = jnp.logical_and(spot >= first, spot < first + shard)
        add_squares(jnp.where(inside, value, 0.0))

    def together(*steps):
        return lambda: [step() for step in steps]

    asides = [
        together(partial(mods_hop, position), partial(small_hop, position))
        for position in range(hops)
    ]
    asides += [together(partial(mods_hop, hops), partial(small_hop, hops), send_act)]
    first_act = len(asides)
    asides += [partial(act_hop, position) for position in range(1, n_bits)]
    asides[-1] = together(asides[-1], small_end)
    asides += [
        together(partial(act_hop, n_bits), start_rows),
        upper_rows,
        partial(table_rows, 0),
        partial(table_rows, 1),
        lower_rows,
        start_window,
        window_squares,
    ]

    squares[...] = jnp.zeros_like(squares)
    greet(n_wide, n_narrow)
    start_pair(jnp.int32(0))
    last_load().start()
    act_load(0).start()

    def wave(t, carry):
        for number, stage in [*enumerate(stages)][1:] + [(0, stages[0])]:
            k = t - number

            @pl.when(jnp.logical_and(k >= 0, k < chunks))
            def _(stage=stage, k=k):
                stage(k)

        @pl.when(t == 1)
        def _():
            last_load().wait()

        @pl.when(jnp.logical_and(t % 2 == 1, t < 8))
        def _():
            last_product(t // 2)

        for number, aside in enumerate(asides):

            @pl.when(t == number)
            def _(aside=aside):
                aside()

        index = t - first_act

        @pl.when(jnp.logical_and(index >= 0, index < 8))
        def _():
            adaptive_columns(index)

        return carry

    lax.fori_loop(0, max(chunks + len(stages) - 1, len(asides), first_act + 8), wave, 0)

    def finish(k, carry):
        for step in range(far_steps):
            if traded[step]:
                back_copy(k, step, parts[step + 1]).wait_send()
        last_copy(k, core).wait_send()
        return carry

    lax.fori_loop(0, chunks, finish, 0)
    for k in range(chunks - 2, chunks):
        give_copy(k).wait_send()

    def finish_ring(k, carry):
        for path in range(2):
            for step in range(n_bits):
                near_copy(path, k, step).wait_send()
        for step in range(far_steps):
            far_copy(k, step, gives[step]).wait_send()
        return carry

    lax.fori_loop(chunks - RING, chunks, finish_ring, 0)
    for position in [*range(far_steps), hops - 1]:
        mods_copy(position).wait_send()
    for path in range(2):
        for step in range(n_bits):
            for mask, arrived in near_masks(path, step):
                mods_near(path, step, mask, arrived).wait_send()
    for position in range(hops + 1):
        small_copy(position).wait_send()
    for position in range(n_bits):
        act_copy(position).wait_send()
    for slot_of_ring in range(4):
        turned_copy(slot_of_ring, 0).wait()
    window_copies()[1].wait()

    total = jnp.sum(squares[...], axis=1, keepdims=True)
    value = jnp.broadcast_to(total, norm_out.shape[1:])
    for position in range(n_bits):
        norm_out[position] = value
        copy = beside(
            *near_places[position],
            norm_out.at[position],
            norm_in.at[position],
            norm_sem,
            position,
        )
        copy.start()
        copy.wait()
        value = value + norm_in[position]
    norm = jnp.sqrt(value)
    row = lax.broadcasted_iota(jnp.int32, value.shape, 0)
    clip_out[...] = jnp.where(row == 0, norm, clip_limit / jnp.maximum(norm, clip_limit))


def reduce_all(n_wide, n_narrow, images, shard, inputs, gradients, asides):
    rows = WIDTH // n_narrow
    chunks = 12
    tokens = inputs[0].shape[0]
    half = rows // 2
    far = bits_of(n_wide) - 1
    devices = n_wide * n_narrow
    hops = bits_of(devices)
    count = devices * images
    dma = pltpu.SemaphoreType.DMA
    any_space = pl.BlockSpec(memory_space=pl.ANY)
    vmem = pl.BlockSpec(memory_space=pltpu.VMEM)
    height = flat_rows(n_narrow, shard)
    turned, _, window, totals, clip = pl.pallas_call(
        partial(reduce_kernel, n_wide, n_narrow, images, shard),
        in_specs=[any_space] * 8 + [vmem] * len(asides),
        out_specs=[any_space, any_space, any_space, vmem, vmem],
        out_shape=[
            jax.ShapeDtypeStruct((chunks + 8, rows, WIDTH), f32),
            jax.ShapeDtypeStruct((height, WIDTH), f32),
            jax.ShapeDtypeStruct((shard_rows(shard), WIDTH), f32),
            jax.ShapeDtypeStruct((8, WIDTH), f32),
            jax.ShapeDtypeStruct((8, 128), f32),
        ],
        scratch_shapes=[
            pltpu.VMEM((chunks, 2, half, WIDTH), bf16),
            pltpu.VMEM((2, 2, tokens, WIDTH), bf16),
            pltpu.VMEM((tokens, WIDTH), bf16),
            pltpu.VMEM((tokens, WIDTH), bf16),
            pltpu.VMEM((4 * n_narrow, rows, WIDTH), bf16),
            pltpu.VMEM((2, n_narrow, half, WIDTH), bf16),
            pltpu.VMEM((2, n_narrow, half, WIDTH), f32),
            pltpu.VMEM((RING, n_narrow, half, WIDTH), bf16),
            pltpu.VMEM((2, RING, n_narrow - 1, half, WIDTH // 2), bf16),
            pltpu.VMEM((2, RING, n_narrow - 1, half, WIDTH // 2), bf16),
            pltpu.VMEM((RING, far, half, WIDTH), bf16),
            pltpu.VMEM((RING, far, half, WIDTH), bf16),
            pltpu.VMEM((RING, n_narrow, half, WIDTH), f32),
            pltpu.VMEM((RING, half, WIDTH), f32),
            dma((3, 2)),
            dma((2, chunks)),
            dma((2, 2, chunks, bits_of(n_narrow))),
            dma((2, chunks, far)),
            dma((2, chunks, far)),
            dma((2, chunks)),
            pltpu.VMEM((devices, images * 8, WIDTH), bf16),
            pltpu.VMEM((8, count, WIDTH), bf16),
            pltpu.VMEM((2 * count, WIDTH), bf16),
            pltpu.VMEM((count, WIDTH), bf16),
            pltpu.VMEM((8, WIDTH), f32),
            pltpu.VMEM((2, 3 * PATCH, WIDTH), f32),
            pltpu.VMEM((hops, 3 * PATCH // 2, WIDTH), f32),
            pltpu.VMEM((hops, 3 * PATCH // 2, WIDTH), f32),
            pltpu.VMEM((3 * PATCH, WIDTH), f32),
            pltpu.VMEM((n_narrow, count, rows), f32),
            pltpu.VMEM((height - ROW_TABLE, WIDTH), f32),
            pltpu.VMEM((bits_of(n_narrow), 8, 128), f32),
            pltpu.VMEM((bits_of(n_narrow), 8, 128), f32),
            pltpu.VMEM((1, WIDTH), f32),
            pltpu.VMEM((4, rows, WIDTH), f32),
            dma((2, hops)),
            dma((2, 2, n_narrow - 1)),
            dma((2, hops + 1)),
            dma((2, bits_of(n_narrow))),
            dma((4,)),
            dma((2, bits_of(n_narrow))),
            dma((4,)),
        ],
        compiler_params=pltpu.CompilerParams(
            collective_id=1, has_side_effects=True, vmem_limit_bytes=63 * 1024 * 1024
        ),
        cost_estimate=pl.CostEstimate(
            flops=10**8, bytes_accessed=300 * 10**6, transcendentals=0
        ),
        name="reduce_gradients",
    )(*inputs, *gradients, *asides)
    return turned, window, totals, clip


def dot_s(left, right):
    return lax.dot_general(left, right, (((0,), (0,)), ((), ())), preferred_element_type=f32)


def center_back(grad, normal, scale):
    return (
        grad
        - jnp.mean(grad, axis=-1, keepdims=True)
        - normal * jnp.mean(grad * normal, axis=-1, keepdims=True)
    ) * scale


def gelu_pair(value):
    rate = math.sqrt(2.0 / math.pi)
    square = value * value
    bend = jnp.tanh(rate * value * (1.0 + 0.044715 * square))
    half = 0.5 * (1.0 + bend)
    slope = half + 0.5 * value * (1.0 - bend * bend) * (rate * (1.0 + 3.0 * 0.044715 * square))
    return value * half, slope


def layer_kernel(
    numbers,
    latent_ref,
    noise_ref,
    mods_ref,
    triple,
    mixed_ref,
    probs,
    place_ref,
    patch_ref,
    final_ref,
    tail_ref,
    attend_ref,
    output_ref,
    expand_ref,
    shrink_ref,
    normed_two_ref,
    act_ref,
    g_branch_two_ref,
    g_pre_ref,
    g_branch_ref,
    g_triple_ref,
    g_mods_ref,
    g_patch_ref,
    g_final_ref,
    g_bias_ref,
    slope,
    normal_one,
    normal_two,
    hidden,
    branch,
    g_mixed,
):
    image = pl.program_id(0)
    tokens = SEQUENCE
    wide = 256

    def bias(index):
        spot = ROW_BIAS - ROW_TAIL + index
        return tail_ref[spot : spot + 1, :]

    def bias_wide(ref, first, index):
        across = WIDTH // wide
        return (
            pl.ds(first + index // across, 1),
            pl.ds(pl.multiple_of(index % across * wide, wide), wide),
        )

    def row(index):
        return mods_ref[0, index : index + 1, :]

    @pl.when(image == 0)
    def _():
        for ref in (g_patch_ref, g_final_ref, g_bias_ref):
            ref[...] = jnp.zeros_like(ref)

    moment = numbers[0, image]
    blended = ((1.0 - moment) * latent_ref[0] + moment * noise_ref[0]).astype(bf16)
    target = noise_ref[0] - latent_ref[0]
    start = dot(blended, patch_ref[...]) + bias(0) + place_ref[...]
    hidden[...] = start
    normal, scale_one = center(start)
    normal_one[...] = normal
    zero = jnp.zeros((), bf16)
    masks = head_masks(tokens)
    first_half = masks[0]
    rate = HEAD_DIM ** (-0.5)

    value = dot(mixed_ref[...], output_ref[...]) + bias(3)
    branch[...] = value
    value = hidden[...] + row(2) * value
    hidden[...] = value
    normal, scale_two = center(value)
    normal_two[...] = normal
    normed_two_ref[...] = (normal * (1.0 + row(4)) + row(3)).astype(bf16)

    def widen(index, carry):
        span = pl.ds(pl.multiple_of(index * wide, wide), wide)
        before = dot(normed_two_ref[...], expand_ref[:, span])
        before = before + tail_ref[bias_wide(tail_ref, ROW_BIAS - ROW_TAIL + 4, index)]
        after, steep = gelu_pair(before)
        act_ref[:, span] = after.astype(bf16)
        slope[:, span] = steep
        return carry

    lax.fori_loop(0, MLP_WIDTH // wide, widen, 0, unroll=6)

    branch_two = dot(act_ref[...], shrink_ref[...]) + bias(8)
    upper = hidden[...] + row(5) * branch_two
    normal, scale_three = center(upper)
    final = (normal * (1.0 + row(7)) + row(6)).astype(bf16)
    mismatch = dot(final, final_ref[...]) + bias(17)[:, :PATCH] - target
    loss = numbers[2, image] * jnp.sum(mismatch * mismatch)
    grad_out = (numbers[1, image] * mismatch).astype(bf16)

    g_final_ref[...] += dot_s(final, grad_out)
    sums = jnp.sum(grad_out.astype(f32), axis=0, keepdims=True)
    spot = lax.broadcasted_iota(jnp.int32, (1, WIDTH), 1)
    sums = jnp.concatenate([sums, jnp.zeros((1, WIDTH - PATCH), f32)], axis=1)
    g_bias_ref[3:4, :] += jnp.where(spot == PATCH, loss, sums)
    grad = dot_t(grad_out, final_ref[...])
    shift_f = jnp.sum(grad, axis=0, keepdims=True)
    scale_f = jnp.sum(grad * normal, axis=0, keepdims=True)
    grad_upper = center_back((1.0 + row(7)) * grad, normal, scale_three)
    gate_two = jnp.sum(branch_two * grad_upper, axis=0, keepdims=True)
    grad_branch = (row(5) * grad_upper).astype(bf16)
    g_branch_two_ref[...] = grad_branch
    g_bias_ref[2:3, :] += jnp.sum(grad_branch.astype(f32), axis=0, keepdims=True)
    hidden[...] = grad_upper

    def narrow(index, carry):
        span = pl.ds(pl.multiple_of(index * wide, wide), wide)
        grad_act = dot_t(g_branch_two_ref[...], shrink_ref[span, :])
        grad_pre = (grad_act * slope[:, span]).astype(bf16)
        g_pre_ref[:, span] = grad_pre
        g_bias_ref[bias_wide(g_bias_ref, 4, index)] += jnp.sum(grad_pre.astype(f32), axis=0, keepdims=True)
        return carry

    lax.fori_loop(0, MLP_WIDTH // wide, narrow, 0, unroll=6)

    grad = dot_t(g_pre_ref[...], expand_ref[...])
    normal = normal_two[...]
    shift_two = jnp.sum(grad, axis=0, keepdims=True)
    scale_mod_two = jnp.sum(grad * normal, axis=0, keepdims=True)
    grad_middle = hidden[...] + center_back((1.0 + row(4)) * grad, normal, scale_two)
    gate_one = jnp.sum(branch[...] * grad_middle, axis=0, keepdims=True)
    grad_branch = (row(2) * grad_middle).astype(bf16)
    g_branch_ref[...] = grad_branch
    g_bias_ref[1:2, :] += jnp.sum(grad_branch.astype(f32), axis=0, keepdims=True)
    hidden[...] = grad_middle
    g_mixed[...] = dot_t(grad_branch, output_ref[...]).astype(bf16)

    def attend_back(pair, carry):
        query_span, key_span, value_span = pair_spans(pair)
        query = triple[:, query_span]
        keys = triple[:, key_span]
        values = triple[:, value_span]
        grad_mixed = g_mixed[:, query_span]
        results = []
        for side in range(2):
            low_weights = probs[2 * pair + side]
            weights = low_weights.astype(f32)
            grad_weights = dot_t(jnp.where(masks[side], grad_mixed, zero), values)
            grad_values = dot_s(low_weights, grad_mixed)
            grad_scores = weights * (
                grad_weights - jnp.sum(weights * grad_weights, axis=-1, keepdims=True)
            )
            grad_scores = grad_scores.astype(bf16)
            grad_query = dot(grad_scores, keys)
            grad_keys = dot_s(grad_scores, query)
            results.append((grad_query, grad_keys, grad_values))
        for part, span in enumerate((query_span, key_span, value_span)):
            merged = jnp.where(first_half, results[0][part], results[1][part])
            if part < 2:
                merged = merged * rate
            g_triple_ref[:, span] = merged.astype(bf16)
        return carry

    lax.fori_loop(0, HEADS // 2, attend_back, 0, unroll=3)

    grad = dot_t(g_triple_ref[...], attend_ref[...])
    normal = normal_one[...]
    shift_one = jnp.sum(grad, axis=0, keepdims=True)
    scale_mod_one = jnp.sum(grad * normal, axis=0, keepdims=True)
    grad_start = hidden[...] + center_back((1.0 + row(1)) * grad, normal, scale_one)
    grad_start = grad_start.astype(bf16)
    g_patch_ref[...] += dot_s(blended, grad_start)
    g_bias_ref[0:1, :] += jnp.sum(grad_start.astype(f32), axis=0, keepdims=True)
    for index, value in enumerate(
        (shift_one, scale_mod_one, gate_one, shift_two, scale_mod_two, gate_two, shift_f, scale_f)
    ):
        g_mods_ref[0, index : index + 1, :] = value


def layer(numbers, latent, noisy, mods, attention, patch_w, final_w, tail, weights):
    images = latent.shape[0]
    tokens = images * SEQUENCE
    once = pl.Buffered(1)

    def whole(array):
        return pl.BlockSpec(
            array.shape, lambda i: (0,) * len(array.shape), pipeline_mode=once
        )

    def fixed(shape, dtype=f32):
        return pl.BlockSpec(shape, lambda i: (0,) * len(shape)), jax.ShapeDtypeStruct(shape, dtype)

    def per_image(width):
        return (
            pl.BlockSpec((SEQUENCE, width), lambda i: (i, 0)),
            jax.ShapeDtypeStruct((tokens, width), bf16),
        )

    outs = [
        per_image(WIDTH),
        per_image(MLP_WIDTH),
        per_image(WIDTH),
        per_image(MLP_WIDTH),
        per_image(WIDTH),
        per_image(3 * WIDTH),
        (
            pl.BlockSpec((1, 8, WIDTH), lambda i: (i, 0, 0)),
            jax.ShapeDtypeStruct((images, 8, WIDTH), f32),
        ),
        fixed((PATCH, WIDTH)),
        fixed((WIDTH, PATCH)),
        fixed((8, WIDTH)),
    ]
    place = positions(SEQUENCE, WIDTH)
    fixed_args = (place, patch_w, final_w, tail) + tuple(weights)
    flops = 2 * 2 * 7078 * 1000 * tokens
    return pl.pallas_call(
        layer_kernel,
        grid=(images,),
        in_specs=[
            pl.BlockSpec(memory_space=pltpu.SMEM),
            pl.BlockSpec((1, SEQUENCE, PATCH), lambda i: (i, 0, 0)),
            pl.BlockSpec((1, SEQUENCE, PATCH), lambda i: (i, 0, 0)),
            pl.BlockSpec((1, 8, WIDTH), lambda i: (i, 0, 0)),
            pl.BlockSpec((SEQUENCE, 3 * WIDTH), lambda i: (i, 0)),
            pl.BlockSpec((SEQUENCE, WIDTH), lambda i: (i, 0)),
            pl.BlockSpec((HEADS, SEQUENCE, SEQUENCE), lambda i: (i, 0, 0)),
        ]
        + [whole(array) for array in fixed_args],
        out_specs=[spec for spec, _ in outs],
        out_shape=[shape for _, shape in outs],
        scratch_shapes=[
            pltpu.VMEM((SEQUENCE, MLP_WIDTH), f32),
            pltpu.VMEM((SEQUENCE, WIDTH), f32),
            pltpu.VMEM((SEQUENCE, WIDTH), f32),
            pltpu.VMEM((SEQUENCE, WIDTH), f32),
            pltpu.VMEM((SEQUENCE, WIDTH), f32),
            pltpu.VMEM((SEQUENCE, WIDTH), bf16),
        ],
        compiler_params=pltpu.CompilerParams(vmem_limit_bytes=56 * 1024 * 1024),
        cost_estimate=pl.CostEstimate(
            flops=flops, bytes_accessed=60 * 10**6, transcendentals=0
        ),
        name="layer",
    )(numbers, latent, noisy, mods, *attention, *fixed_args)


def local(
    n_wide,
    n_narrow,
    latents,
    noise_field,
    labels,
    label_drop,
    time_steps,
    loss_weights,
    attend_weight,
    attend_first,
    attend_second,
    attend_left,
    attend_right,
    output_weight,
    output_first,
    output_second,
    output_left,
    output_right,
    expand_weight,
    expand_first,
    expand_second,
    expand_left,
    expand_right,
    shrink_weight,
    shrink_first,
    shrink_second,
    shrink_left,
    shrink_right,
    adaptive_weight,
    adaptive_first,
    adaptive_second,
    adaptive_left,
    adaptive_right,
    shared_weight,
    shared_first,
    shared_second,
):
    column = lax.axis_index("narrow")
    images = labels.shape[0] * labels.shape[1]

    moment = (time_steps.reshape(images).astype(f32) + 0.5) / TIMESTEPS
    chosen = jnp.where(label_drop == 1, CLASSES - 1, labels).reshape(images, 1).astype(f32)
    weights_here = loss_weights.reshape(images)
    info = jnp.concatenate(
        [rounded(frequencies(moment, FREQS)).astype(f32), chosen, weights_here[:, None]], axis=1
    )
    info = jnp.pad(info, ((0, 8 - images), (0, SHEET - info.shape[1])))[None]

    shape = (images,) + latents.shape[2:]

    shard = shared_weight.shape[0]
    rows = shard_rows(shard)
    row_start = column * shard // (WIDTH * ALIGN) * ALIGN
    offset = column * shard - row_start * WIDTH
    margin = -(-(ALIGN + 1) * WIDTH // 1024) * 1024
    own = lax.pad(shared_weight, f32(0.0), [(margin, rows * WIDTH - shard, 0)])
    own = lax.dynamic_slice(own, (margin - offset,), (rows * WIDTH,)).reshape(rows, WIDTH)

    (
        *full,
        patch_w,
        final_rows,
        tail,
        time_two,
        sheet,
        time_pre,
        condition,
        own_act,
        adaptive_low,
        mods,
        total,
        lefts,
        rights,
        normed,
        triple,
        mixed,
        probs,
    ) = gather_all(
        n_wide,
        n_narrow,
        images,
        shard,
        (own, attend_weight, output_weight, expand_weight, shrink_weight),
        adaptive_weight,
        info,
        (attend_left, output_left, expand_left, shrink_left, adaptive_left),
        [
            blocks.transpose(1, 2, 0) if blocks.shape[0] > BLOCK else blocks
            for blocks in (attend_right, output_right, expand_right, shrink_right, adaptive_right)
        ],
        (
            moment,
            latents.reshape(shape),
            noise_field.reshape(shape),
            positions(SEQUENCE, WIDTH),
        ),
    )
    lefts = lefts.reshape(8, -1, BLOCK)
    rights = rights.reshape(-1, BLOCK, 4 * BLOCK)
    weight_sum = total[0, 0]

    entries = SEQUENCE * PATCH
    numbers = jnp.stack(
        [moment, 2.0 * weights_here / (entries * weight_sum), weights_here / entries]
    )
    (
        normed_two,
        act,
        g_branch_two,
        g_pre,
        g_branch,
        g_triple,
        g_mods,
        g_patch,
        g_final,
        g_bias,
    ) = layer(
        numbers,
        latents.reshape(shape),
        noise_field.reshape(shape),
        mods,
        (triple, mixed, probs),
        patch_w,
        final_rows.astype(bf16).reshape(WIDTH, PATCH),
        tail,
        full,
    )

    turned, window, totals, clip = reduce_all(
        n_wide,
        n_narrow,
        images,
        shard,
        (normed, mixed, normed_two, act),
        (g_triple, g_branch, g_pre, g_branch_two),
        (
            g_mods.reshape(images * 8, WIDTH),
            g_patch,
            g_final.reshape(PATCH, WIDTH),
            g_bias,
            adaptive_low,
            sheet,
            time_pre,
            condition,
            own_act,
            time_two,
            lefts,
            rights,
        ),
    )
    loss_sum = totals[3, PATCH]
    clip_norm = clip[0, 0]
    factor = clip[1, 0]
    grad_shared = lax.dynamic_slice(window.reshape(-1), (offset,), (shard,))

    results = rotated_update(
        clip,
        turned,
        lefts,
        rights,
        (
            (attend_weight, attend_first, attend_second),
            (output_weight, output_first, output_second),
            (expand_weight, expand_first, expand_second),
            (shrink_weight, shrink_first, shrink_second),
            (adaptive_weight, adaptive_first, adaptive_second),
        ),
    )
    fresh = plain_update(shared_weight, shared_first, shared_second, grad_shared * factor)
    results = [*results, fresh[0], fresh[1], fresh[2], fresh[0].astype(jnp.bfloat16)]
    return tuple(results) + (loss_sum, weight_sum, clip_norm)


def solution(mesh):
    data = P(None, ("wide", "narrow"))
    state = (P("narrow", None),) * 3 + (P("narrow", None, None), P())
    return jax.shard_map(
        partial(local, mesh.shape["wide"], mesh.shape["narrow"]),
        mesh=mesh,
        in_specs=(P(None, ("wide", "narrow"), None, None),) * 2
        + (data,) * 4
        + state * 5
        + (P("narrow"),) * 3,
        out_specs=(P("narrow", None),) * 20 + (P("narrow"),) * 4 + (P(),) * 3,
        check_vma=False,
    )
```

```python
from functools import partial
import math

import jax
import jax.numpy as jnp
import numpy as np
from jax import lax
from jax.experimental import pallas as pl
from jax.experimental.pallas import tpu as pltpu
from jax.sharding import PartitionSpec as P

HEADS = 12
HEAD_DIM = 64
MLP_WIDTH = 3072
CLASSES = 1001
FREQS = 256
PATCH = 16
TIMESTEPS = 1000
BLOCK = 32
STEP_COUNT = 10
WIDTH = 768
SEQUENCE = 256


beta_one = 0.9
beta_two = 0.999
epsilon_adam = 1e-08
learn_rate = 0.03
decay_rate = 0.01
clip_limit = 0.002
highest = lax.Precision.HIGHEST
bf16 = jnp.bfloat16
f32 = jnp.float32

ROW_PATCH = 0
ROW_TIME_ONE = 16
ROW_TIME_TWO = 272
ROW_TABLE = 1040
ROW_FINAL = 2041
ROW_BIAS = 2057


def positions(tokens, width):
    side = math.isqrt(tokens)
    quarter = width // 4
    omega = 1.0 / 10000.0 ** (np.arange(quarter, dtype=np.float64) / quarter)
    place = np.arange(tokens)
    column = (place % side)[:, None] * omega
    row = (place // side)[:, None] * omega
    table = np.concatenate([np.sin(column), np.cos(column), np.sin(row), np.cos(row)], axis=1)
    return jnp.asarray(table.astype(np.float32))


def frequencies(moment, width):
    half = width // 2
    phases = jnp.exp(-math.log(10000.0) * jnp.arange(half, dtype=jnp.float32) / half)
    angles = moment[:, None] * 1000.0 * phases
    return jnp.concatenate([jnp.cos(angles), jnp.sin(angles)], axis=1)


def normalize(hidden):
    centered = hidden - jnp.mean(hidden, axis=-1, keepdims=True)
    return centered * lax.rsqrt(jnp.mean(centered * centered, axis=-1, keepdims=True) + 1e-06)


def modulate(hidden, shift, scale):
    return normalize(hidden) * (1.0 + scale[:, None, :]) + shift[:, None, :]


def adam_direction(first, second):
    return (first * (1.0 / (1.0 - beta_one**STEP_COUNT))) / (
        jnp.sqrt(second * (1.0 / (1.0 - beta_two**STEP_COUNT))) + epsilon_adam
    )


def plain_update(weight, first, second, grad):
    first = beta_one * first + (1.0 - beta_one) * grad
    second = beta_two * second + (1.0 - beta_two) * grad * grad
    weight = weight - learn_rate * (adam_direction(first, second) + decay_rate * weight)
    return (weight, first, second)


def rounded(value):
    return value.astype(jnp.bfloat16)


def product(inputs, weight):
    return jnp.dot(inputs, weight, preferred_element_type=jnp.float32)


def backprod(gradient, weight):
    return jnp.einsum("...n,kn->...k", gradient, weight, preferred_element_type=jnp.float32)


def weight_grad(inputs, gradient):
    flat_in = inputs.reshape(-1, inputs.shape[-1])
    flat_grad = gradient.reshape(-1, gradient.shape[-1])
    return lax.dot_general(
        flat_in, flat_grad, (((0,), (0,)), ((), ())), preferred_element_type=jnp.float32
    )


def bias_grad(gradient):
    return jnp.sum(gradient.astype(jnp.float32).reshape(-1, gradient.shape[-1]), axis=0)


def halves(value):
    high = value.astype(bf16)
    return high, (value - high.astype(f32)).astype(bf16)


def spread_left(blocks):
    size = blocks.shape[0]
    place = lax.broadcasted_iota(jnp.int32, (BLOCK, size), 0)
    column = lax.broadcasted_iota(jnp.int32, (BLOCK, size), 1)
    repeat = (place == column % BLOCK).astype(bf16)
    row_block = lax.broadcasted_iota(jnp.int32, (size, size), 0) // BLOCK
    col_block = lax.broadcasted_iota(jnp.int32, (size, size), 1) // BLOCK
    return tuple(
        jnp.where(
            row_block == col_block, jnp.dot(part, repeat, preferred_element_type=f32), 0.0
        ).astype(bf16)
        for part in halves(blocks)
    )


def spread_right(first, second):
    size = 4 * BLOCK
    row_block = lax.broadcasted_iota(jnp.int32, (size, size), 0) // BLOCK
    col_block = lax.broadcasted_iota(jnp.int32, (size, size), 1) // BLOCK
    inside = row_block == col_block
    corners = [
        jnp.where(inside, jnp.concatenate([row] * 4, axis=0), 0.0) for row in (first, second)
    ]
    empty = jnp.zeros((size, size), f32)
    return jnp.concatenate(
        [
            jnp.concatenate([corners[0], empty], axis=1),
            jnp.concatenate([empty, corners[1]], axis=1),
        ],
        axis=0,
    )


def dot(left, right):
    return jnp.dot(left, right, preferred_element_type=f32)


def dot_t(left, right):
    return lax.dot_general(left, right, (((1,), (1,)), ((), ())), preferred_element_type=f32)


STRIP = 256
TILES = ((3, 1), (1, 1), (4, 1), (1, 4), (8, 1))


def tile_places():
    places = []
    for matrix, (across, down) in enumerate(TILES):
        for number in range(across * down):
            places.append((matrix, number // across, number % across))
    return places


def left_number(tile):
    return (tile + 9) // 12 + (tile + 8) // 12 + (tile + 4) // 12 * (tile - 7)


def adam_kernel(count, *refs):
    factor_ref, turned, lefts, rights = refs[:4]
    states = [refs[4 + 3 * matrix : 7 + 3 * matrix] for matrix in range(5)]
    outs = [refs[19 + 4 * matrix : 23 + 4 * matrix] for matrix in range(5)]
    taken, given, low, take_sem, give_sem = refs[39:]
    rows = taken.shape[2]
    places = tile_places()
    factor = factor_ref[1, 0]

    def window(number):
        _, down, across = places[number]
        return (pl.ds(down * rows, rows), pl.ds(across * WIDTH, WIDTH))

    def takes(number):
        slot = number % 3
        arrays = [ref.at[window(number)] for ref in states[places[number][0]]]
        arrays.append(turned.at[number])
        return [
            pltpu.make_async_copy(array, taken.at[slot, part], take_sem.at[slot, part])
            for part, array in enumerate(arrays)
        ]

    def gives(number):
        slot = number % 2
        arrays = [ref.at[window(number)] for ref in outs[places[number][0]]]
        sources = [given.at[slot, part] for part in range(3)] + [low.at[slot]]
        return [
            pltpu.make_async_copy(source, array, give_sem.at[slot, part])
            for part, (source, array) in enumerate(zip(sources, arrays))
        ]

    def given_out(slot):
        for part in range(4):
            buffer = low.at[slot] if part == 3 else given.at[slot, part]
            pltpu.make_async_copy(buffer, buffer, give_sem.at[slot, part]).wait()

    for number in range(2):
        for copy in takes(number):
            copy.start()

    def body(tile, carry):
        for number in range(2, count):

            @pl.when(tile + 2 == number)
            def _(number=number):
                for copy in takes(number):
                    copy.start()

        slot = tile % 3
        out = tile % 2
        for part in range(4):
            buffer = taken.at[slot, part]
            pltpu.make_async_copy(buffer, buffer, take_sem.at[slot, part]).wait()

        @pl.when(tile >= 2)
        def _():
            given_out(out)

        stack = jnp.where(tile < 12, left_number(jnp.minimum(tile, 11)), 7)
        left = spread_left(lefts[stack])[0]
        for start in range(0, WIDTH, STRIP):
            span = slice(start, start + STRIP)
            group = tile * (WIDTH // BLOCK // 4) + start // BLOCK // 4
            right = spread_right(rights[group], rights[group + 1]).astype(bf16)
            grad = taken[slot, 3, :, span] * factor
            first = beta_one * taken[slot, 1, :, span] + (1.0 - beta_one) * grad
            second = beta_two * taken[slot, 2, :, span] + (1.0 - beta_two) * grad * grad
            given[out, 1, :, span] = first
            given[out, 2, :, span] = second
            step = adam_direction(first, second)
            step = dot_t(step.astype(bf16), right)
            step = dot(left, step.astype(bf16))
            weight = taken[slot, 0, :, span]
            weight = weight - learn_rate * (step + decay_rate * weight)
            given[out, 0, :, span] = weight
            low[out, :, span] = weight.astype(bf16)
        for number in range(count):

            @pl.when(tile == number)
            def _(number=number):
                for copy in gives(number):
                    copy.start()

        return carry

    lax.fori_loop(0, count, body, 0)
    for slot in range(2):
        given_out(slot)


def rotated_update(clip, turned, lefts, rights, states):
    count, rows, _ = turned.shape
    any_space = pl.BlockSpec(memory_space=pl.ANY)
    vmem = pl.BlockSpec(memory_space=pltpu.VMEM)
    shapes = []
    for weight, _, _ in states:
        shapes += [jax.ShapeDtypeStruct(weight.shape, f32)] * 3
        shapes += [jax.ShapeDtypeStruct(weight.shape, bf16)]
    dma = pltpu.SemaphoreType.DMA
    return pl.pallas_call(
        partial(adam_kernel, count),
        in_specs=[pl.BlockSpec(memory_space=pltpu.SMEM), any_space, vmem, vmem]
        + [any_space] * 15,
        out_specs=[any_space] * 20,
        out_shape=shapes,
        scratch_shapes=[
            pltpu.VMEM((3, 4, rows, WIDTH), f32),
            pltpu.VMEM((2, 3, rows, WIDTH), f32),
            pltpu.VMEM((2, rows, WIDTH), bf16),
            dma((3, 4)),
            dma((2, 4)),
        ],
        compiler_params=pltpu.CompilerParams(vmem_limit_bytes=60 * 1024 * 1024),
        name="rotated_adam",
    )(clip, turned, lefts, rights, *[array for state in states for array in state])


def bits_of(extent):
    return extent.bit_length() - 1


def flipped(index, mask, count):
    for bit in range(count):
        if mask >> bit & 1:
            index = index + (1 - 2 * (index // (1 << bit) % 2)) * (1 << bit)
    return index


def greet(n_wide, n_narrow):
    barrier = pltpu.get_barrier_semaphore()
    count = 0
    for axis, extent in (("narrow", n_narrow), ("wide", n_wide)):
        me = lax.axis_index(axis)
        for bit in range(bits_of(extent)):
            pl.semaphore_signal(
                barrier,
                inc=1,
                device_id={axis: flipped(me, 1 << bit, bits_of(extent))},
                device_id_type=pl.DeviceIdType.MESH,
            )
            count = count + 1
    pl.semaphore_wait(barrier, count)


def remote(source, target, send_sem, recv_sem, axis, peer):
    return pltpu.make_async_remote_copy(
        src_ref=source,
        dst_ref=target,
        send_sem=send_sem,
        recv_sem=recv_sem,
        device_id={axis: peer},
        device_id_type=pl.DeviceIdType.MESH,
    )


def slot_of(n_wide, n_narrow):
    here = lax.axis_index("narrow")
    there = lax.axis_index("wide")
    return there // 2 + n_wide // 2 * (here + n_narrow * (there % 2))


def hop_order(n_wide, n_narrow):
    n_bits = bits_of(n_narrow)
    w_bits = bits_of(n_wide)
    places = [("wide", bit, w_bits) for bit in range(1, w_bits)]
    places += [("narrow", bit, n_bits) for bit in range(n_bits)]
    return places + [("wide", 0, w_bits)]


def route(path, step, count):
    return (step + path) % count


ROW_TAIL = 2048
TAIL = 32
ALIGN = 16
SHEET = 384


def shard_rows(shard):
    rows = (shard + WIDTH - 2) // WIDTH + 1 + ALIGN
    return -(-rows // 32) * 32


def shard_start(number, shard):
    return number * shard // WIDTH // ALIGN * ALIGN


def flat_rows(n_narrow, shard):
    last = shard_start(n_narrow - 1, shard) + shard_rows(shard)
    return max(-(-last // ALIGN) * ALIGN, 2112)


def center(hidden):
    centered = hidden - jnp.mean(hidden, axis=-1, keepdims=True)
    scale = lax.rsqrt(jnp.mean(centered * centered, axis=-1, keepdims=True) + 1e-06)
    return centered * scale, scale


def pair_spans(pair):
    return [
        pl.ds(pl.multiple_of(part * WIDTH + pair * 2 * HEAD_DIM, 2 * HEAD_DIM), 2 * HEAD_DIM)
        for part in range(3)
    ]


def head_masks(tokens):
    lane = lax.broadcasted_iota(jnp.int32, (tokens, 2 * HEAD_DIM), 1)
    return lane < HEAD_DIM, lane >= HEAD_DIM


def bases_along_lanes(shape):
    return shape[0] == BLOCK and shape[2] > BLOCK


def silu_slope(value):
    gate = jax.nn.sigmoid(value)
    return gate * (1.0 + value * (1.0 - gate))


def own_columns(value, n_narrow):
    here = lax.axis_index("narrow")
    width = value.shape[1] // n_narrow
    result = value[:, :width]
    for number in range(1, n_narrow):
        result = jnp.where(
            here == number, value[:, number * width : (number + 1) * width], result
        )
    return result


def gather_kernel(n_wide, n_narrow, images, shard, *refs):
    count = 5
    shards = refs[:count]
    adaptive_ref, info_ref = refs[count : count + 2]
    left_refs = refs[count + 2 : count + 7]
    right_refs = refs[count + 7 : count + 12]
    moment_ref, latent_ref, noise_ref, place_ref = refs[count + 12 : count + 16]
    outs = refs[count + 16 : count + 37]
    scratch = refs[count + 37 :]
    (
        patch_out,
        final_out,
        tail_out,
        time_two_out,
        sheet,
        time_pre,
        condition,
        own_act,
        adaptive_low,
        mods_ref,
        total_ref,
        lefts_out,
        rights_out,
        normed_out,
        triple_out,
        mixed_out,
        probs_out,
    ) = outs[4:21]
    gathered = scratch[0]
    wides = scratch[1 : count + 1]
    lows = scratch[count + 1 : 2 * count + 1]
    (
        flat,
        turned,
        attend_full,
        normed,
        triple,
        mixed,
        probs,
        adaptive_wide,
        info_all,
        part,
        part_in,
        load_sem,
        keep_sem,
        send_sem,
        recv_sem,
        core_send,
        core_recv,
        info_sem,
        info_send,
        info_recv,
        part_send,
        part_recv,
        attend_sem,
        image_sem,
        *early,
    ) = scratch[2 * count + 1 :]
    fulls = (gathered, attend_full) + tuple(outs[1:4])
    early_targets = (time_two_out, sheet, time_pre, condition, own_act, adaptive_low, lefts_out, rights_out)
    early_buffers, early_sem = early[:8], early[8]
    (
        time_two_out,
        sheet,
        time_pre,
        condition,
        own_act,
        adaptive_low,
        lefts_out,
        rights_out,
    ) = early_buffers
    early_copies = [
        pltpu.make_async_copy(source, target, early_sem.at[number])
        for number, (source, target) in enumerate(zip(early_buffers, early_targets))
    ]
    here = lax.axis_index("narrow")
    there = lax.axis_index("wide")
    core = there % 2
    n_bits = bits_of(n_narrow)
    w_bits = bits_of(n_wide)
    sibling = flipped(there, 1, w_bits)

    loads = [
        pltpu.make_async_copy(shards[number], wides[number], load_sem.at[number])
        for number in range(count)
    ]
    loads.append(pltpu.make_async_copy(adaptive_ref, adaptive_wide, load_sem.at[count]))
    for load in loads:
        load.start()
    slot = slot_of(n_wide, n_narrow)
    info_own = pltpu.make_async_copy(info_ref, info_all.at[pl.ds(slot, 1)], info_sem)
    info_own.start()
    greet(n_wide, n_narrow)
    sends = []

    def region(number, owner, half, path):
        rows, cols = shards[number].shape
        return (
            pl.ds(pl.multiple_of(owner * rows + half * (rows // 2), 16), rows // 2),
            pl.ds(path * (cols // 2), cols // 2),
        )

    def narrow_step(number, step, own):
        for path in range(2):
            bit = route(path, step, n_bits)
            peer = flipped(here, 1 << bit, n_bits)
            done = sum(1 << route(path, earlier, n_bits) for earlier in range(step))
            for mask in range(n_narrow):
                if mask & ~done or own != (mask == 0):
                    continue
                place = region(number, flipped(here, mask, n_bits), core, path)
                arrives = mask | 1 << bit
                if mask == 0:
                    rows, cols = shards[number].shape
                    source = lows[number].at[
                        pl.ds(pl.multiple_of(core * (rows // 2), 16), rows // 2),
                        pl.ds(path * (cols // 2), cols // 2),
                    ]
                else:
                    source = fulls[number].at[place]
                copy = remote(
                    source,
                    fulls[number].at[place],
                    send_sem.at[number, path, arrives - 1],
                    recv_sem.at[number, path, arrives - 1],
                    "narrow",
                    peer,
                )
                copy.start()
                sends.append(copy)

    def arrive(number, step):
        for path in range(2):
            bit = route(path, step, n_bits)
            done = sum(1 << route(path, earlier, n_bits) for earlier in range(step))
            for mask in range(n_narrow):
                if mask & ~done:
                    continue
                arrived = mask | 1 << bit
                place = region(number, flipped(here, arrived, n_bits), core, path)
                remote(
                    fulls[number].at[place],
                    fulls[number].at[place],
                    send_sem.at[number, path, arrived - 1],
                    recv_sem.at[number, path, arrived - 1],
                    "narrow",
                    flipped(here, 1 << bit, n_bits),
                ).wait_recv()
                copy = remote(
                    fulls[number].at[place],
                    fulls[number].at[place],
                    core_send.at[number, path, arrived - 1],
                    core_recv.at[number, path, arrived - 1],
                    "wide",
                    sibling,
                )
                copy.start()
                sends.append(copy)

    def from_sibling(number):
        for path in range(2):
            for mask in range(1, n_narrow):
                place = region(number, flipped(here, mask, n_bits), 1 - core, path)
                remote(
                    fulls[number].at[place],
                    fulls[number].at[place],
                    core_send.at[number, path, mask - 1],
                    core_recv.at[number, path, mask - 1],
                    "wide",
                    sibling,
                ).wait_recv()

    def cast_rows(source, target):
        def cast(index, carry):
            span = pl.ds(pl.multiple_of(index * 16, 16), 16)
            target[span, :] = source[span, :].astype(bf16)
            return carry

        lax.fori_loop(0, source.shape[0] // 16, cast, 0)

    keeps = []

    def begin(number):
        loads[number].wait()
        rows = shards[number].shape[0]
        cast_rows(wides[number], lows[number])
        keep = pltpu.make_async_copy(
            lows[number],
            fulls[number].at[pl.ds(pl.multiple_of(here * rows, 16), rows)],
            keep_sem.at[number],
        )
        keep.start()
        keeps.append(keep)
        narrow_step(number, 0, True)

    def begin_rest(number):
        for step in range(1, n_bits):
            narrow_step(number, step, True)

    places = hop_order(n_wide, n_narrow)

    def info_copy(position):
        axis, bit, bits = places[position]
        width = 1 << position
        base = slot // width * width
        return remote(
            info_all.at[pl.ds(base, width)],
            info_all.at[pl.ds(base, width)],
            info_send.at[position],
            info_recv.at[position],
            axis,
            flipped(lax.axis_index(axis), 1 << bit, bits),
        )

    def pass_on(numbers, step):
        for number in numbers:
            arrive(number, step)
            if step + 1 < n_bits:
                narrow_step(number, step + 1, False)

    info_own.wait()
    info_copy(0).start()
    begin(0)
    begin_rest(0)
    waiting = [lambda step=step: pass_on([0], step) for step in range(n_bits - 1)]
    waiting += [lambda: (begin(1), begin_rest(1)), lambda: (begin(2), begin_rest(2))]
    waiting += [lambda: begin(3), lambda: begin(4)]
    for position in range(len(places)):
        info_copy(position).wait()
        if position + 1 < len(places):
            info_copy(position + 1).start()
        if waiting:
            waiting.pop(0)()
    for step in waiting:
        step()
    pass_on([0], n_bits - 1)
    from_sibling(0)
    keeps[0].wait()

    height = shards[0].shape[0]
    reached = 0
    for number in range(n_narrow):
        start = shard_start(number, shard)
        overlap = max(reached - start, 0)
        block = number * height
        if overlap:
            flat[start:reached, :] = (
                flat[start:reached, :].astype(f32)
                + gathered[block : block + overlap, :].astype(f32)
            ).astype(bf16)
        flat[start + overlap : start + height, :] = gathered[block + overlap : block + height, :]
        reached = start + height
    if reached < flat.shape[0]:
        flat[reached:, :] = jnp.zeros((flat.shape[0] - reached, WIDTH), bf16)

    devices = n_wide * n_narrow
    for number in range(devices):
        sheet[number * images : (number + 1) * images, :] = info_all[number, :images, :]
    weights = sheet[:, FREQS + 1 : FREQS + 2]
    total_ref[...] = jnp.sum(weights, axis=0, keepdims=True)
    tail = flat[ROW_TAIL : ROW_TAIL + TAIL, :].astype(f32)
    tail_out[...] = tail
    patch_out[...] = flat[ROW_PATCH:ROW_TIME_ONE, :]
    time_two_out[...] = flat[ROW_TIME_TWO:ROW_TABLE, :]
    last = flat[ROW_FINAL - 9 : ROW_FINAL + 23, :].astype(f32)
    final_out[...] = last[9 : 9 + PATCH]
    tail_row = ROW_BIAS - ROW_TAIL
    value = dot(sheet[:, :FREQS].astype(bf16), flat[ROW_TIME_ONE:ROW_TIME_TWO, :])
    value = value + tail[tail_row + 1 : tail_row + 2]
    time_pre[...] = value
    act = jax.nn.silu(value).astype(bf16)
    value = dot(act, flat[ROW_TIME_TWO:ROW_TABLE, :]) + tail[tail_row + 2 : tail_row + 3]
    labels = lax.broadcasted_iota(jnp.int32, (sheet.shape[0], 1008), 1).astype(f32)
    pick = jnp.where(sheet[:, FREQS : FREQS + 1] == labels, 1.0, 0.0).astype(bf16)
    value = value + dot(pick, flat[ROW_TABLE : ROW_TABLE + 1008, :])
    condition[...] = value
    act = own_columns(jax.nn.silu(value), n_narrow)
    act = act.astype(bf16)
    own_act[...] = act

    loads[count].wait()
    cast_rows(adaptive_wide, adaptive_low)
    row = lax.broadcasted_iota(jnp.int32, (8 * n_narrow, act.shape[0]), 0)
    column = lax.broadcasted_iota(jnp.int32, (8 * n_narrow, act.shape[0]), 1)
    owner = there // 2 + n_wide // 2 * (row // 8 + n_narrow * core)
    chosen = column == owner * images + row % images
    near = dot(jnp.where(chosen, 1.0, 0.0).astype(bf16), act).astype(bf16)
    across = images

    def piece(index):
        first = index // across * images
        start = index % across * WIDTH
        return slice(first, first + images), slice(start, start + WIDTH)

    for index in range(8):
        value = dot(near, adaptive_low[:, index * WIDTH : (index + 1) * WIDTH])
        rows_of, span = piece(index)
        for number in range(n_narrow):
            start = 8 * number + rows_of.start
            part[0, number, rows_of, span] = value[start : start + images]

    def lay_bases():
        place = 0
        for ref in left_refs:
            blocks = ref.shape[0]
            lefts_out[place : place + blocks * BLOCK, :] = ref[...].reshape(-1, BLOCK)
            place = place + blocks * BLOCK
        place = 0
        for matrix, ref in enumerate(right_refs):
            turning = bases_along_lanes(ref.shape)
            blocks = ref.shape[2] if turning else ref.shape[0]
            copies = TILES[matrix][1]
            for row in range(BLOCK):
                turned[0:blocks, :] = ref[row].T if turning else ref[:, row, :]
                value = jnp.concatenate(
                    [turned[pl.ds(spot, blocks // 4, stride=4), :] for spot in range(4)], axis=1
                )
                for copy in range(copies):
                    start = place + copy * blocks // 4 * BLOCK + row
                    rights_out[pl.ds(start, blocks // 4, stride=BLOCK), :] = value
            place = place + copies * blocks // 4 * BLOCK

    def part_copy(step, mask):
        bit = 1 << step
        return remote(
            part.at[step, flipped(here, mask, n_bits)],
            part_in.at[step, flipped(here, mask, n_bits)],
            part_send.at[step, mask],
            part_recv.at[step, mask],
            "narrow",
            flipped(here, bit, n_bits),
        )

    def part_back(step, mask):
        bit = 1 << step
        owner = flipped(here, mask - bit, n_bits)
        return remote(
            part_in.at[step, owner],
            part_in.at[step, owner],
            part_send.at[step, mask],
            part_recv.at[step, mask],
            "narrow",
            flipped(here, bit, n_bits),
        ), owner

    for step in range(n_bits):
        bit = 1 << step
        masks = [
            mask for mask in range(n_narrow) if mask & bit and not mask & (bit - 1)
        ]
        for mask in masks:
            copy = part_copy(step, mask)
            copy.start()
            sends.append(copy)
        pass_on([1, 2] if step + 1 < n_bits else [], step)
        for mask in masks:
            back, owner = part_back(step, mask)
            back.wait_recv()
            if step + 1 < n_bits:
                part[step + 1, owner] = part[step, owner] + part_in[step, owner]
            else:
                value = part[step, owner] + part_in[step, owner]
                for index in range(8):
                    rows_of, span = piece(index)
                    for image in range(images):
                        start = rows_of.start + image
                        mods_ref[image, index : index + 1, :] = (
                            value[start : start + 1, span]
                            + tail[tail_row + 9 + index : tail_row + 10 + index]
                        )

    begin_rest(3)
    begin_rest(4)
    for step in range(n_bits - 1):
        pass_on([3, 4], step)
    pass_on([1], n_bits - 1)
    lay_bases()

    for copy in early_copies:
        copy.start()

    from_sibling(1)
    keeps[1].wait()
    attend_out = pltpu.make_async_copy(attend_full, outs[0], attend_sem)
    attend_out.start()
    masks = head_masks(SEQUENCE)
    rate = HEAD_DIM ** (-0.5)

    def image_copies(image):
        slot = image % 2
        tokens = pl.ds(pl.multiple_of(image * SEQUENCE, SEQUENCE), SEQUENCE)
        heads = pl.ds(image * HEADS, HEADS)
        pairs = (
            (normed, normed_out.at[tokens]),
            (triple, triple_out.at[tokens]),
            (mixed, mixed_out.at[tokens]),
            (probs, probs_out.at[heads]),
        )
        return [
            pltpu.make_async_copy(source.at[slot], target, image_sem.at[slot, number])
            for number, (source, target) in enumerate(pairs)
        ]

    def one_image(image, carry):
        slot = image % 2

        @pl.when(image >= 2)
        def _():
            for copy in image_copies(image - 2):
                copy.wait()

        moment = moment_ref[image]
        blended = (1.0 - moment) * latent_ref[image] + moment * noise_ref[image]
        start = dot(blended.astype(bf16), patch_out[...]) + tail_out[tail_row : tail_row + 1, :]
        normal, _ = center(start + place_ref[...])
        shift = mods_ref[image, 0:1, :]
        scale = mods_ref[image, 1:2, :]
        normed[slot] = (normal * (1.0 + scale) + shift).astype(bf16)

        for index in range(3 * WIDTH // STRIP):
            span = slice(index * STRIP, (index + 1) * STRIP)
            triple[slot, :, span] = dot(normed[slot], attend_full[:, span]).astype(bf16)
        for pair in range(HEADS // 2):
            query_span, key_span, value_span = pair_spans(pair)
            query = triple[slot, :, query_span]
            keys = triple[slot, :, key_span]
            values = triple[slot, :, value_span]
            results = []
            for side, mask in enumerate(masks):
                scores = dot_t(jnp.where(mask, query, jnp.zeros((), bf16)), keys) * rate
                scores = jnp.exp(scores - jnp.max(scores, axis=-1, keepdims=True))
                shares = scores * (1.0 / jnp.sum(scores, axis=-1, keepdims=True))
                shares = shares.astype(bf16)
                probs[slot, 2 * pair + side] = shares
                results.append(dot(shares, values))
            mixed[slot, :, query_span] = jnp.where(masks[0], results[0], results[1]).astype(bf16)
        for copy in image_copies(image):
            copy.start()
        return carry

    lax.fori_loop(0, images, one_image, 0)
    pass_on(range(2, count), n_bits - 1)
    for number in range(2, count):
        from_sibling(number)
    for keep in keeps[2:]:
        keep.wait()
    for copy in sends:
        copy.wait_send()
    for image in range(max(images - 2, 0), images):
        for copy in image_copies(image):
            copy.wait()
    attend_out.wait()
    for copy in early_copies:
        copy.wait()


def gather_all(n_wide, n_narrow, images, shard, shards, adaptive, info, lefts, rights, data):
    count = len(shards)
    any_space = pl.BlockSpec(memory_space=pl.ANY)
    vmem = pl.BlockSpec(memory_space=pltpu.VMEM)
    devices = n_wide * n_narrow
    n_bits = bits_of(n_narrow)
    rows = adaptive.shape[0]
    dma = pltpu.SemaphoreType.DMA
    total = devices * images
    early = (3, 4, 5, 6, 7, 8, 11, 12)
    early_shapes = [
        ((WIDTH, WIDTH), bf16),
        ((total, SHEET), f32),
        ((total, WIDTH), f32),
        ((total, WIDTH), f32),
        ((total, rows), bf16),
        (adaptive.shape, bf16),
        ((8 * rows, BLOCK), f32),
        ((len(tile_places()) * 6 * BLOCK, 4 * BLOCK), f32),
    ]
    return pl.pallas_call(
        partial(gather_kernel, n_wide, n_narrow, images, shard),
        in_specs=[any_space] * (count + 2)
        + [vmem] * 10
        + [pl.BlockSpec(memory_space=pltpu.SMEM)]
        + [vmem] * 3,
        out_specs=[any_space] * (count - 1)
        + [any_space if number in early else vmem for number in range(13)]
        + [any_space] * 4,
        out_shape=[
            jax.ShapeDtypeStruct((piece.shape[0] * n_narrow, piece.shape[1]), bf16)
            for piece in shards[1:]
        ]
        + [
            jax.ShapeDtypeStruct((PATCH, WIDTH), bf16),
            jax.ShapeDtypeStruct((PATCH, WIDTH), f32),
            jax.ShapeDtypeStruct((TAIL, WIDTH), f32),
            jax.ShapeDtypeStruct((WIDTH, WIDTH), bf16),
            jax.ShapeDtypeStruct((total, SHEET), f32),
            jax.ShapeDtypeStruct((total, WIDTH), f32),
            jax.ShapeDtypeStruct((total, WIDTH), f32),
            jax.ShapeDtypeStruct((total, rows), bf16),
            jax.ShapeDtypeStruct(adaptive.shape, bf16),
            jax.ShapeDtypeStruct((images, 8, WIDTH), f32),
            jax.ShapeDtypeStruct((1, 1), f32),
            jax.ShapeDtypeStruct((8 * rows, BLOCK), f32),
            jax.ShapeDtypeStruct((len(tile_places()) * 6 * BLOCK, 4 * BLOCK), f32),
            jax.ShapeDtypeStruct((images * SEQUENCE, WIDTH), bf16),
            jax.ShapeDtypeStruct((images * SEQUENCE, 3 * WIDTH), bf16),
            jax.ShapeDtypeStruct((images * SEQUENCE, WIDTH), bf16),
            jax.ShapeDtypeStruct((images * HEADS, SEQUENCE, SEQUENCE), bf16),
        ],
        scratch_shapes=[pltpu.VMEM((shards[0].shape[0] * n_narrow, WIDTH), bf16)]
        + [pltpu.VMEM(piece.shape, f32) for piece in shards]
        + [pltpu.VMEM(piece.shape, bf16) for piece in shards]
        + [
            pltpu.VMEM((flat_rows(n_narrow, shard), WIDTH), bf16),
            pltpu.VMEM((8 * WIDTH // BLOCK, BLOCK), f32),
            pltpu.VMEM((WIDTH, 3 * WIDTH), bf16),
            pltpu.VMEM((2, SEQUENCE, WIDTH), bf16),
            pltpu.VMEM((2, SEQUENCE, 3 * WIDTH), bf16),
            pltpu.VMEM((2, SEQUENCE, WIDTH), bf16),
            pltpu.VMEM((2, HEADS, SEQUENCE, SEQUENCE), bf16),
            pltpu.VMEM(adaptive.shape, f32),
            pltpu.VMEM((devices,) + info.shape[1:], f32),
            pltpu.VMEM((n_bits, n_narrow, 8, images * WIDTH), f32),
            pltpu.VMEM((n_bits, n_narrow, 8, images * WIDTH), f32),
            dma((count + 1,)),
            dma((count,)),
            dma((count, 2, n_narrow - 1)),
            dma((count, 2, n_narrow - 1)),
            dma((count, 2, n_narrow - 1)),
            dma((count, 2, n_narrow - 1)),
            dma,
            dma((bits_of(devices),)),
            dma((bits_of(devices),)),
            dma((n_bits, n_narrow)),
            dma((n_bits, n_narrow)),
            dma,
            dma((2, 4)),
            *[pltpu.VMEM(shape, dtype) for shape, dtype in early_shapes],
            dma((8,)),
        ],
        compiler_params=pltpu.CompilerParams(
            collective_id=0, has_side_effects=True, vmem_limit_bytes=60 * 1024 * 1024
        ),
        name="gather_weights",
    )(*shards, adaptive, info, *lefts, *rights, *data)


RING = 4


def reduce_kernel(n_wide, n_narrow, images, shard, *refs):
    input_refs, gradient_refs = refs[0:4], refs[4:8]
    (
        g_mods_ref,
        g_patch_ref,
        g_final_ref,
        g_bias_ref,
        adaptive_low,
        sheet,
        time_pre,
        condition,
        own_act,
        time_two,
        lefts,
        rights,
    ) = refs[8:20]
    turned_out, rows_out, window_out, totals_out, clip_out = refs[20:25]
    out_ref, pair, act_in, last_in, blocks, to_core = refs[25:31]
    late_inputs = refs[12:20]
    late_buffers = refs[31:39]
    (
        adaptive_low,
        sheet,
        time_pre,
        condition,
        own_act,
        time_two,
        lefts,
        rights,
    ) = late_buffers
    scratch = refs[39:]
    own, from_core, to_near, from_near, to_far, from_far, acc, acc_far = scratch[:8]
    load_sem, core_sem, near_sem, far_sem, back_sem, last_sem = scratch[8:14]
    (
        mods_all,
        by_mod,
        product_parts,
        first_part,
        biases,
        small_first,
        small_out,
        small_in,
        small_all,
        late_sem,
        act_all,
        stage,
        norm_out,
        norm_in,
        squares,
        ring,
        mods_sem,
        mods_near_sem,
        small_sem,
        act_sem,
        rows_sem,
        norm_sem,
        ring_sem,
    ) = scratch[14:]
    here = lax.axis_index("narrow")
    there = lax.axis_index("wide")
    core = there % 2
    n_bits = bits_of(n_narrow)
    w_bits = bits_of(n_wide)
    far_steps = w_bits - 1
    sibling = flipped(there, 1, w_bits)
    chunks, _, half, width = out_ref.shape
    side = width // 2

    leaving = []
    for path in range(2):
        done = 0
        place = 0
        steps = []
        for step in range(n_bits):
            bit = 1 << route(path, step, n_bits)
            masks = [mask for mask in range(n_narrow) if mask & bit and not mask & done]
            steps.append((bit, {mask: place + spot for spot, mask in enumerate(masks)}))
            place = place + len(masks)
            done = done | bit
        leaving.append(steps)

    parts = [(0, half, 0, width)]
    gives = []
    for step in range(far_steps):
        low, rows, left, cols = parts[-1]
        mine = there // (2 << step) % 2
        if rows % 32 == 0:
            keep = (low + mine * (rows // 2), rows // 2, left, cols)
            give = (low + (1 - mine) * (rows // 2), rows // 2, left, cols)
        elif cols % 256 == 0:
            keep = (low, rows, left + mine * (cols // 2), cols // 2)
            give = (low, rows, left + (1 - mine) * (cols // 2), cols // 2)
        else:
            keep = parts[-1]
            give = parts[-1]
        parts.append(keep)
        gives.append(give)
    traded = [gives[step] is not parts[step] for step in range(far_steps)]

    def window(part):
        low, rows, left, cols = part
        if not isinstance(low, int):
            low = pl.multiple_of(low, 16)
        if not isinstance(left, int):
            left = pl.multiple_of(left, 128)
        return (pl.ds(low, rows), pl.ds(left, cols))

    def give_copy(k):
        return remote(
            to_core.at[k % 2],
            from_core.at[k % RING],
            core_sem.at[0, k],
            core_sem.at[1, k],
            "wide",
            sibling,
        )

    products = [(0, 0), (0, 1), (0, 2), (1, 0), (2, 0), (2, 1), (2, 2), (2, 3)]
    lasting = act_in.shape[1]

    def start_pair(k):
        for number, (matrix, across) in enumerate(products):

            @pl.when(k == number)
            def _(number=number, matrix=matrix, across=across):
                slot_of = number % 2
                pltpu.make_async_copy(
                    input_refs[matrix], pair.at[slot_of, 0], load_sem.at[slot_of, 0]
                ).start()
                pltpu.make_async_copy(
                    gradient_refs[matrix].at[:, pl.ds(across * WIDTH, WIDTH)],
                    pair.at[slot_of, 1],
                    load_sem.at[slot_of, 1],
                ).start()

    def act_load(number):
        return pltpu.make_async_copy(
            input_refs[3].at[:, pl.ds(pl.multiple_of(number * lasting, lasting), lasting)],
            act_in,
            load_sem.at[2, 0],
        )

    def last_load():
        return pltpu.make_async_copy(gradient_refs[3], last_in, load_sem.at[2, 1])

    def put_halves(k, owner, span, lower, upper):
        own[k % 2, owner, :, span] = jnp.where(core == 0, lower, upper).astype(f32)
        to_core[k % 2, owner, :, span] = jnp.where(core == 0, upper, lower).astype(bf16)

    def stage_product(k):
        start_pair(k + 1)

        @pl.when(k >= 2)
        def _():
            give_copy(k - 2).wait_send()

        @pl.when(k < len(products))
        def _():
            slot_of = k % 2
            for side_of in range(2):
                buffer = pair.at[slot_of, side_of]
                pltpu.make_async_copy(buffer, buffer, load_sem.at[slot_of, side_of]).wait()
            for start in range(0, WIDTH, STRIP):
                span = slice(start, start + STRIP)
                value = dot_s(pair[slot_of, 0], pair[slot_of, 1, :, span])
                for owner in range(n_narrow):
                    top = owner * 2 * half
                    put_halves(
                        k,
                        owner,
                        span,
                        value[top : top + half],
                        value[top + half : top + 2 * half],
                    )

        @pl.when(k >= len(products))
        def _():
            for owner in range(n_narrow):
                block = owner * 4 + k - len(products)
                put_halves(
                    k,
                    owner,
                    slice(None),
                    blocks[block, 0:half, :].astype(f32),
                    blocks[block, half : 2 * half, :].astype(f32),
                )

        give_copy(k).start()

    def last_product(number):
        act_load(number).wait()
        for start in range(0, WIDTH, STRIP):
            span = slice(start, start + STRIP)
            value = dot_s(act_in[...], last_in[:, span]).astype(bf16)
            for piece in range(n_narrow):
                top = piece * 2 * half
                blocks[number * n_narrow + piece, :, span] = value[top : top + 2 * half]

        @pl.when(number < 3)
        def _():
            act_load(number + 1).start()

    def near_copy(path, k, step):
        bit, masks = leaving[path][step]
        spots = pl.ds(min(masks.values()), len(masks))
        return remote(
            to_near.at[path, k % RING, spots],
            from_near.at[path, k % RING, spots],
            near_sem.at[0, path, k, step],
            near_sem.at[1, path, k, step],
            "narrow",
            flipped(here, bit, n_bits),
        )

    def far_copy(k, step, part):
        return remote(
            to_far.at[(k % RING, step) + window(part)],
            from_far.at[(k % RING, step) + window(part)],
            far_sem.at[0, k, step],
            far_sem.at[1, k, step],
            "wide",
            flipped(there, 2 << step, w_bits),
        )

    def back_copy(k, step, part):
        place = (k, core) + window(part)
        return remote(
            out_ref.at[place],
            out_ref.at[place],
            back_sem.at[0, k, step],
            back_sem.at[1, k, step],
            "wide",
            flipped(there, 2 << step, w_bits),
        )

    def last_copy(k, side_of):
        return remote(
            out_ref.at[k, side_of],
            out_ref.at[k, side_of],
            last_sem.at[0, k],
            last_sem.at[1, k],
            "wide",
            sibling,
        )

    def place_near(path, k, step, mask, total):
        columns = pl.ds(path * side, side)
        ring_slot = k % RING
        if step == n_bits:
            acc_far[ring_slot, :, columns] = total
        elif mask in leaving[path][step][1]:
            to_near[path, ring_slot, leaving[path][step][1][mask]] = total.astype(bf16)
        else:
            acc[ring_slot, mask, :, columns] = total

    def before(k, wait):
        @pl.when(k >= RING)
        def _():
            wait()

    def stage_core(k):
        give_copy(k).wait_recv()
        for path in range(2):
            before(k, lambda path=path: near_copy(path, k - RING, 0).wait_send())
            columns = pl.ds(path * side, side)
            for mask in range(n_narrow):
                owner = flipped(here, mask, n_bits)
                total = own[k % 2, owner, :, columns] + from_core[
                    k % RING, owner, :, columns
                ].astype(f32)
                place_near(path, k, 0, mask, total)
            near_copy(path, k, 0).start()

    def stage_near(step, k):
        ring_slot = k % RING
        for path in range(2):
            columns = pl.ds(path * side, side)
            near_copy(path, k, step).wait_recv()
            if step + 1 < n_bits:
                before(k, lambda path=path: near_copy(path, k - RING, step + 1).wait_send())
            bit, masks = leaving[path][step]
            for mask, spot in masks.items():
                total = acc[ring_slot, mask - bit, :, columns] + from_near[path, ring_slot, spot].astype(f32)
                place_near(path, k, step + 1, mask - bit, total)
            if step + 1 < n_bits:
                near_copy(path, k, step + 1).start()
        if step + 1 == n_bits:
            start_far(0, k)

    def start_far(step, k):
        ring_slot = k % RING
        if step < far_steps:
            place = window(gives[step])
            before(k, lambda: far_copy(k - RING, step, gives[step]).wait_send())
            to_far[(ring_slot, step) + place] = acc_far[(ring_slot,) + place].astype(bf16)
            far_copy(k, step, gives[step]).start()
        else:
            place = window(parts[step])
            out_ref[(k, core) + place] = acc_far[(ring_slot,) + place].astype(bf16)
            start_back(far_steps - 1, k)

    def stage_far(step, k):
        ring_slot = k % RING
        far_copy(k, step, parts[step + 1]).wait_recv()
        place = window(parts[step + 1])
        if traded[step]:
            mine = acc_far[(ring_slot,) + place]
        else:
            mine = to_far[(ring_slot, step) + place].astype(f32)
        acc_far[(ring_slot,) + place] = mine + from_far[(ring_slot, step) + place].astype(f32)
        start_far(step + 1, k)

    def start_back(step, k):
        while step >= 0 and not traded[step]:
            step = step - 1
        if step >= 0:
            back_copy(k, step, parts[step + 1]).start()
        else:
            last_copy(k, core).start()

    def stage_back(step, k):
        back_copy(k, step, gives[step]).wait_recv()
        start_back(step - 1, k)

    def add_squares(value):
        squares[...] += jnp.sum(value * value, axis=0, keepdims=True)

    def turned_copy(slot, tile):
        return pltpu.make_async_copy(ring.at[slot], turned_out.at[tile], ring_sem.at[slot])

    def turn(high, rest, stack, tile, slot, used):
        @pl.when(used)
        def _():
            turned_copy(slot, tile).wait()

        left, left_rest = spread_left(lefts[stack])
        for start in range(0, WIDTH, STRIP):
            span = slice(start, start + STRIP)
            group = tile * (WIDTH // BLOCK // 4) + start // BLOCK // 4
            right, right_rest = halves(spread_right(rights[group], rights[group + 1]))
            value = dot(high[:, span], right) + dot(high[:, span], right_rest)
            if rest is not None:
                value = value + dot(rest[:, span], right)
            part, part_rest = halves(value)
            ring[slot, :, span] = dot_s(left, part) + (
                dot_s(left_rest, part) + dot_s(left, part_rest)
            )
        turned_copy(slot, tile).start()

    def stage_last(k):
        last_copy(k, 1 - core).wait_recv()
        for number in range(2):
            add_squares(out_ref[k, number].astype(f32))
        value = out_ref[k].reshape(2 * half, width)
        turn(value, None, left_number(k), k, k % 2, k >= 2)

    stages = [stage_product, stage_core]
    stages += [partial(stage_near, step) for step in range(n_bits)]
    stages += [partial(stage_far, step) for step in range(far_steps)]
    stages += [partial(stage_back, step) for step in reversed(range(far_steps)) if traded[step]]
    stages += [stage_last]

    places = hop_order(n_wide, n_narrow)
    near_places = [("narrow", bit, n_bits) for bit in range(n_bits)]
    hops = len(places)
    slot = slot_of(n_wide, n_narrow)
    count = n_wide * n_narrow * images

    def beside(axis, bit, bits, source, target, sem, position):
        return remote(
            source,
            target,
            sem.at[0, position],
            sem.at[1, position],
            axis,
            flipped(lax.axis_index(axis), 1 << bit, bits),
        )

    column_bits = n_wide // 2
    half_rows = small_out.shape[1]
    own_rows = pl.ds(pl.multiple_of(half_rows * core, 8), half_rows)
    small_places = places[hops - 1 :] + places[: hops - 1]

    def mods_copy(position):
        width = 1 << position
        block = mods_all.at[pl.ds(slot // width * width, width)]
        return beside(*places[position], block, block, mods_sem, position)

    def mods_near(path, step, mask, arrived):
        owner = flipped(here, arrived if mask is None else mask, n_bits)
        bit = 1 << route(path, step, n_bits)
        block = mods_all.at[
            pl.ds(column_bits * (owner + n_narrow * core), column_bits),
            :,
            pl.ds(path * side, side),
        ]
        return remote(
            block,
            block,
            mods_near_sem.at[0, path, arrived - 1],
            mods_near_sem.at[1, path, arrived - 1],
            "narrow",
            flipped(here, bit, n_bits),
        )

    def near_masks(path, step):
        done = sum(1 << route(path, earlier, n_bits) for earlier in range(step))
        bit = 1 << route(path, step, n_bits)
        return [(mask, mask | bit) for mask in range(n_narrow) if not mask & ~done]

    def small_copy(position):
        if position == 0:
            return beside(
                *small_places[0], small_first.at[0], small_first.at[1], small_sem, position
            )
        if position == hops:
            block = small_all.at[own_rows]
            return beside(*small_places[0], block, block, small_sem, position)
        return beside(
            *small_places[position],
            small_out.at[position],
            small_in.at[position],
            small_sem,
            position,
        )

    def act_copy(position):
        width = 1 << position
        block = act_all.at[pl.ds(here // width * width, width)]
        return beside(*near_places[position], block, block, act_sem, position)

    def small_total():
        return small_all[...]

    def rows_copy(start, rows, position):
        return pltpu.make_async_copy(
            stage.at[pl.ds(0, rows)], rows_out.at[pl.ds(start, rows)], rows_sem.at[position]
        )

    height = window_out.shape[0]

    def window_copies():
        start = here * shard // (WIDTH * ALIGN) * ALIGN
        source = rows_out.at[pl.ds(pl.multiple_of(start, ALIGN), height)]
        return [
            pltpu.make_async_copy(source, stage.at[pl.ds(0, height)], rows_sem.at[2]),
            pltpu.make_async_copy(stage.at[pl.ds(0, height)], window_out, rows_sem.at[3]),
        ]

    def mods_hop(position):
        if position == 0:
            mods_all[slot] = g_mods_ref[...].astype(bf16)
        elif position <= far_steps or position == hops:
            mods_copy(position - 1).wait_recv()
        else:
            step = position - 1 - far_steps
            for path in range(2):
                for _, arrived in near_masks(path, step):
                    mods_near(path, step, None, arrived).wait_recv()
        if position < far_steps or position == hops - 1:
            mods_copy(position).start()
        elif position < hops:
            step = position - far_steps
            for path in range(2):
                for mask, arrived in near_masks(path, step):
                    mods_near(path, step, mask, arrived).start()

    def small_hop(position):
        if position == 0:
            small_first[0, 0:PATCH] = g_patch_ref[...]
            small_first[0, PATCH : 2 * PATCH] = g_final_ref[...]
            small_first[0, 2 * PATCH : 2 * PATCH + 8] = g_bias_ref[...]
            small_first[0, 2 * PATCH + 8 :] = jnp.zeros(
                (small_first.shape[1] - 2 * PATCH - 8, WIDTH), f32
            )
        else:
            small_copy(position - 1).wait_recv()
            if position == 1:
                total = small_first[0, own_rows] + small_first[1, own_rows]
            else:
                total = small_out[position - 1] + small_in[position - 1]
            if position < hops:
                small_out[position] = total
            else:
                small_all[own_rows] = total
        small_copy(position).start()

    def small_end():
        other = pl.ds(pl.multiple_of(half_rows * (1 - core), 8), half_rows)
        block = small_all.at[other]
        beside(*small_places[0], block, block, small_sem, hops).wait_recv()

    def sort_mods():
        together = 8
        size = together * images * 8
        row = lax.broadcasted_iota(jnp.int32, (size, size), 0)
        column = lax.broadcasted_iota(jnp.int32, (size, size), 1)
        span = together * images
        order = jnp.where(column == row % span * 8 + row // span, 1.0, 0.0).astype(bf16)
        for block in range(mods_all.shape[0] // together):
            value = mods_all[block * together : (block + 1) * together].reshape(size, WIDTH)
            value = dot(order, value).astype(bf16)
            for index in range(8):
                by_mod[index, block * span : (block + 1) * span, :] = value[
                    index * span : (index + 1) * span
                ]

    def send_act():
        sort_mods()
        total = jnp.zeros(act_all.shape[1:], f32)
        for index in range(8):
            span = slice(index * WIDTH, (index + 1) * WIDTH)
            total = total + dot_t(by_mod[index], adaptive_low[:, span])
        act_all[here] = total
        act_copy(0).start()

    def act_hop(position):
        act_copy(position - 1).wait_recv()
        if position < n_bits:
            act_copy(position).start()

    def start_rows():
        grad = jnp.concatenate([act_all[number] for number in range(n_narrow)], axis=1)
        grad = grad * silu_slope(condition[...])
        high, rest = halves(grad)
        before = time_pre[...]
        first = (dot_t(high, time_two[...]) * silu_slope(before)).astype(bf16)
        product_parts[0:count] = high
        product_parts[count : 2 * count] = rest
        first_part[...] = first
        biases[0:1, :] = jnp.sum(first.astype(f32), axis=0, keepdims=True)
        biases[1:2, :] = jnp.sum(high.astype(f32), axis=0, keepdims=True)

    def upper_rows():
        stage[0:PATCH, :] = small_total()[0:PATCH]
        stage[ROW_TIME_ONE:ROW_TIME_TWO, :] = dot_s(
            sheet[:, :FREQS].astype(bf16), first_part[...]
        )
        act = jax.nn.silu(time_pre[...]).astype(bf16)
        stage[ROW_TIME_TWO:ROW_TABLE, :] = dot_s(act, product_parts[0:count])
        rows_copy(0, ROW_TABLE, 0).start()

    def table_rows(half_of):
        if half_of == 0:
            rows_copy(0, ROW_TABLE, 0).wait()
        size = 504
        labels = lax.broadcasted_iota(jnp.int32, (count, size), 1) + half_of * size
        pick = jnp.where(sheet[:, FREQS : FREQS + 1] == labels.astype(f32), 1.0, 0.0)
        pick = pick.astype(bf16)
        pick = jnp.concatenate([pick, pick], axis=0)
        stage[half_of * size : (half_of + 1) * size, :] = dot_s(pick, product_parts[...])

    def lower_rows():
        small = small_total()
        base = ROW_FINAL - ROW_TABLE
        stage[base : base + PATCH, :] = small[PATCH : 2 * PATCH]
        base = ROW_BIAS - ROW_TABLE
        bias = small[2 * PATCH : 2 * PATCH + 8]
        stage[base : base + 1, :] = bias[0:1]
        stage[base + 1 : base + 3, :] = biases[0:2, :]
        stage[base + 3 : base + 4, :] = bias[1:2]
        stage[base + 4 : base + 8, :] = bias[4:8]
        stage[base + 8 : base + 9, :] = bias[2:3]
        for index in range(8):
            stage[base + 9 + index : base + 10 + index, :] = jnp.sum(
                by_mod[index].astype(f32), axis=0, keepdims=True
            )
        lane = lax.broadcasted_iota(jnp.int32, (1, WIDTH), 1)
        stage[base + 17 : base + 18, :] = jnp.where(lane < PATCH, bias[3:4], 0.0)
        stage[base + 18 :, :] = jnp.zeros((stage.shape[0] - base - 18, WIDTH), f32)
        totals_out[...] = bias
        rows_copy(ROW_TABLE, stage.shape[0], 1).start()

    first_turn = chunks

    def adaptive_columns(index):
        value = dot_s(own_act[...], by_mod[index])
        add_squares(value)
        high, rest = halves(value)
        turn(high, rest, lefts.shape[0] - 1, first_turn + index, 2 + index % 2, index >= 2)

    def start_window():
        rows_copy(ROW_TABLE, stage.shape[0], 1).wait()
        window_copies()[0].start()

    def window_squares():
        window_copies()[0].wait()
        window_copies()[1].start()
        start = here * shard // (WIDTH * ALIGN) * ALIGN
        first = here * shard - start * WIDTH
        value = stage[0:height, :]
        spot = (
            lax.broadcasted_iota(jnp.int32, value.shape, 0) * WIDTH
            + lax.broadcasted_iota(jnp.int32, value.shape, 1)
        )
        inside = jnp.logical_and(spot >= first, spot < first + shard)
        add_squares(jnp.where(inside, value, 0.0))

    def together(*steps):
        return lambda: [step() for step in steps]

    asides = [
        together(partial(mods_hop, position), partial(small_hop, position))
        for position in range(hops)
    ]
    asides += [together(partial(mods_hop, hops), partial(small_hop, hops), send_act)]
    first_act = len(asides)
    asides += [partial(act_hop, position) for position in range(1, n_bits)]
    asides[-1] = together(asides[-1], small_end)
    asides += [
        together(partial(act_hop, n_bits), start_rows),
        upper_rows,
        partial(table_rows, 0),
        partial(table_rows, 1),
        lower_rows,
        start_window,
        window_squares,
    ]

    squares[...] = jnp.zeros_like(squares)
    greet(n_wide, n_narrow)
    start_pair(jnp.int32(0))
    last_load().start()
    act_load(0).start()
    late_copies = [
        pltpu.make_async_copy(source, target, late_sem.at[number])
        for number, (source, target) in enumerate(zip(late_inputs, late_buffers))
    ]
    for copy in late_copies:
        copy.start()

    def wave(t, carry):
        for number, stage in [*enumerate(stages)][1:] + [(0, stages[0])]:
            k = t - number

            @pl.when(jnp.logical_and(k >= 0, k < chunks))
            def _(stage=stage, k=k):
                stage(k)

        @pl.when(t == 1)
        def _():
            last_load().wait()
            for copy in late_copies:
                copy.wait()

        @pl.when(jnp.logical_and(t % 2 == 1, t < 8))
        def _():
            last_product(t // 2)

        for number, aside in enumerate(asides):

            @pl.when(t == number + 2)
            def _(aside=aside):
                aside()

        index = t - first_act - 2

        @pl.when(jnp.logical_and(index >= 0, index < 8))
        def _():
            adaptive_columns(index)

        return carry

    lax.fori_loop(0, max(chunks + len(stages) - 1, len(asides) + 2, first_act + 8 + 2), wave, 0)

    def finish(k, carry):
        for step in range(far_steps):
            if traded[step]:
                back_copy(k, step, parts[step + 1]).wait_send()
        last_copy(k, core).wait_send()
        return carry

    lax.fori_loop(0, chunks, finish, 0)
    for k in range(chunks - 2, chunks):
        give_copy(k).wait_send()

    def finish_ring(k, carry):
        for path in range(2):
            for step in range(n_bits):
                near_copy(path, k, step).wait_send()
        for step in range(far_steps):
            far_copy(k, step, gives[step]).wait_send()
        return carry

    lax.fori_loop(chunks - RING, chunks, finish_ring, 0)
    for position in [*range(far_steps), hops - 1]:
        mods_copy(position).wait_send()
    for path in range(2):
        for step in range(n_bits):
            for mask, arrived in near_masks(path, step):
                mods_near(path, step, mask, arrived).wait_send()
    for position in range(hops + 1):
        small_copy(position).wait_send()
    for position in range(n_bits):
        act_copy(position).wait_send()
    for slot_of_ring in range(4):
        turned_copy(slot_of_ring, 0).wait()
    window_copies()[1].wait()

    total = jnp.sum(squares[...], axis=1, keepdims=True)
    value = jnp.broadcast_to(total, norm_out.shape[1:])
    for position in range(n_bits):
        norm_out[position] = value
        copy = beside(
            *near_places[position],
            norm_out.at[position],
            norm_in.at[position],
            norm_sem,
            position,
        )
        copy.start()
        copy.wait()
        value = value + norm_in[position]
    norm = jnp.sqrt(value)
    row = lax.broadcasted_iota(jnp.int32, value.shape, 0)
    clip_out[...] = jnp.where(row == 0, norm, clip_limit / jnp.maximum(norm, clip_limit))


def reduce_all(n_wide, n_narrow, images, shard, inputs, gradients, asides):
    rows = WIDTH // n_narrow
    chunks = 12
    tokens = inputs[0].shape[0]
    half = rows // 2
    far = bits_of(n_wide) - 1
    devices = n_wide * n_narrow
    hops = bits_of(devices)
    count = devices * images
    dma = pltpu.SemaphoreType.DMA
    any_space = pl.BlockSpec(memory_space=pl.ANY)
    vmem = pl.BlockSpec(memory_space=pltpu.VMEM)
    height = flat_rows(n_narrow, shard)
    turned, _, window, totals, clip = pl.pallas_call(
        partial(reduce_kernel, n_wide, n_narrow, images, shard),
        in_specs=[any_space] * 8 + [vmem] * 4 + [any_space] * (len(asides) - 4),
        out_specs=[any_space, any_space, any_space, vmem, vmem],
        out_shape=[
            jax.ShapeDtypeStruct((chunks + 8, rows, WIDTH), f32),
            jax.ShapeDtypeStruct((height, WIDTH), f32),
            jax.ShapeDtypeStruct((shard_rows(shard), WIDTH), f32),
            jax.ShapeDtypeStruct((8, WIDTH), f32),
            jax.ShapeDtypeStruct((8, 128), f32),
        ],
        scratch_shapes=[
            pltpu.VMEM((chunks, 2, half, WIDTH), bf16),
            pltpu.VMEM((2, 2, tokens, WIDTH), bf16),
            pltpu.VMEM((tokens, WIDTH), bf16),
            pltpu.VMEM((tokens, WIDTH), bf16),
            pltpu.VMEM((4 * n_narrow, rows, WIDTH), bf16),
            pltpu.VMEM((2, n_narrow, half, WIDTH), bf16),
            *[pltpu.VMEM(array.shape, array.dtype) for array in asides[4:]],
            pltpu.VMEM((2, n_narrow, half, WIDTH), f32),
            pltpu.VMEM((RING, n_narrow, half, WIDTH), bf16),
            pltpu.VMEM((2, RING, n_narrow - 1, half, WIDTH // 2), bf16),
            pltpu.VMEM((2, RING, n_narrow - 1, half, WIDTH // 2), bf16),
            pltpu.VMEM((RING, far, half, WIDTH), bf16),
            pltpu.VMEM((RING, far, half, WIDTH), bf16),
            pltpu.VMEM((RING, n_narrow, half, WIDTH), f32),
            pltpu.VMEM((RING, half, WIDTH), f32),
            dma((3, 2)),
            dma((2, chunks)),
            dma((2, 2, chunks, bits_of(n_narrow))),
            dma((2, chunks, far)),
            dma((2, chunks, far)),
            dma((2, chunks)),
            pltpu.VMEM((devices, images * 8, WIDTH), bf16),
            pltpu.VMEM((8, count, WIDTH), bf16),
            pltpu.VMEM((2 * count, WIDTH), bf16),
            pltpu.VMEM((count, WIDTH), bf16),
            pltpu.VMEM((8, WIDTH), f32),
            pltpu.VMEM((2, 3 * PATCH, WIDTH), f32),
            pltpu.VMEM((hops, 3 * PATCH // 2, WIDTH), f32),
            pltpu.VMEM((hops, 3 * PATCH // 2, WIDTH), f32),
            pltpu.VMEM((3 * PATCH, WIDTH), f32),
            dma((len(asides) - 4,)),
            pltpu.VMEM((n_narrow, count, rows), f32),
            pltpu.VMEM((height - ROW_TABLE, WIDTH), f32),
            pltpu.VMEM((bits_of(n_narrow), 8, 128), f32),
            pltpu.VMEM((bits_of(n_narrow), 8, 128), f32),
            pltpu.VMEM((1, WIDTH), f32),
            pltpu.VMEM((4, rows, WIDTH), f32),
            dma((2, hops)),
            dma((2, 2, n_narrow - 1)),
            dma((2, hops + 1)),
            dma((2, bits_of(n_narrow))),
            dma((4,)),
            dma((2, bits_of(n_narrow))),
            dma((4,)),
        ],
        compiler_params=pltpu.CompilerParams(
            collective_id=1, has_side_effects=True, vmem_limit_bytes=63 * 1024 * 1024
        ),
        cost_estimate=pl.CostEstimate(
            flops=10**8, bytes_accessed=300 * 10**6, transcendentals=0
        ),
        name="reduce_gradients",
    )(*inputs, *gradients, *asides)
    return turned, window, totals, clip


def dot_s(left, right):
    return lax.dot_general(left, right, (((0,), (0,)), ((), ())), preferred_element_type=f32)


def center_back(grad, normal, scale):
    return (
        grad
        - jnp.mean(grad, axis=-1, keepdims=True)
        - normal * jnp.mean(grad * normal, axis=-1, keepdims=True)
    ) * scale


def gelu_pair(value):
    rate = math.sqrt(2.0 / math.pi)
    square = value * value
    bend = jnp.tanh(rate * value * (1.0 + 0.044715 * square))
    half = 0.5 * (1.0 + bend)
    slope = half + 0.5 * value * (1.0 - bend * bend) * (rate * (1.0 + 3.0 * 0.044715 * square))
    return value * half, slope


def layer_kernel(
    numbers,
    latent_ref,
    noise_ref,
    mods_ref,
    triple,
    mixed_ref,
    probs,
    place_ref,
    patch_ref,
    final_ref,
    tail_ref,
    attend_ref,
    output_ref,
    expand_ref,
    shrink_ref,
    normed_two_ref,
    act_ref,
    g_branch_two_ref,
    g_pre_ref,
    g_branch_ref,
    g_triple_ref,
    g_mods_ref,
    g_patch_ref,
    g_final_ref,
    g_bias_ref,
    slope,
    normal_one,
    normal_two,
    hidden,
    branch,
    g_mixed,
):
    image = pl.program_id(0)
    tokens = SEQUENCE
    wide = 256

    def bias(index):
        spot = ROW_BIAS - ROW_TAIL + index
        return tail_ref[spot : spot + 1, :]

    def bias_wide(ref, first, index):
        across = WIDTH // wide
        return (
            pl.ds(first + index // across, 1),
            pl.ds(pl.multiple_of(index % across * wide, wide), wide),
        )

    def row(index):
        return mods_ref[0, index : index + 1, :]

    @pl.when(image == 0)
    def _():
        for ref in (g_patch_ref, g_final_ref, g_bias_ref):
            ref[...] = jnp.zeros_like(ref)

    moment = numbers[0, image]
    blended = ((1.0 - moment) * latent_ref[0] + moment * noise_ref[0]).astype(bf16)
    target = noise_ref[0] - latent_ref[0]
    start = dot(blended, patch_ref[...]) + bias(0) + place_ref[...]
    hidden[...] = start
    normal, scale_one = center(start)
    normal_one[...] = normal
    zero = jnp.zeros((), bf16)
    masks = head_masks(tokens)
    first_half = masks[0]
    rate = HEAD_DIM ** (-0.5)

    value = dot(mixed_ref[...], output_ref[...]) + bias(3)
    branch[...] = value
    value = hidden[...] + row(2) * value
    hidden[...] = value
    normal, scale_two = center(value)
    normal_two[...] = normal
    normed_two_ref[...] = (normal * (1.0 + row(4)) + row(3)).astype(bf16)

    def widen(index, carry):
        span = pl.ds(pl.multiple_of(index * wide, wide), wide)
        before = dot(normed_two_ref[...], expand_ref[:, span])
        before = before + tail_ref[bias_wide(tail_ref, ROW_BIAS - ROW_TAIL + 4, index)]
        after, steep = gelu_pair(before)
        act_ref[:, span] = after.astype(bf16)
        slope[:, span] = steep
        return carry

    lax.fori_loop(0, MLP_WIDTH // wide, widen, 0, unroll=True)

    branch_two = dot(act_ref[...], shrink_ref[...]) + bias(8)
    upper = hidden[...] + row(5) * branch_two
    normal, scale_three = center(upper)
    final = (normal * (1.0 + row(7)) + row(6)).astype(bf16)
    mismatch = dot(final, final_ref[...]) + bias(17)[:, :PATCH] - target
    loss = numbers[2, image] * jnp.sum(mismatch * mismatch)
    grad_out = (numbers[1, image] * mismatch).astype(bf16)

    g_final_ref[...] += dot_s(final, grad_out)
    sums = jnp.sum(grad_out.astype(f32), axis=0, keepdims=True)
    spot = lax.broadcasted_iota(jnp.int32, (1, WIDTH), 1)
    sums = jnp.concatenate([sums, jnp.zeros((1, WIDTH - PATCH), f32)], axis=1)
    g_bias_ref[3:4, :] += jnp.where(spot == PATCH, loss, sums)
    grad = dot_t(grad_out, final_ref[...])
    shift_f = jnp.sum(grad, axis=0, keepdims=True)
    scale_f = jnp.sum(grad * normal, axis=0, keepdims=True)
    grad_upper = center_back((1.0 + row(7)) * grad, normal, scale_three)
    gate_two = jnp.sum(branch_two * grad_upper, axis=0, keepdims=True)
    grad_branch = (row(5) * grad_upper).astype(bf16)
    g_branch_two_ref[...] = grad_branch
    g_bias_ref[2:3, :] += jnp.sum(grad_branch.astype(f32), axis=0, keepdims=True)
    hidden[...] = grad_upper

    def narrow(index, carry):
        span = pl.ds(pl.multiple_of(index * wide, wide), wide)
        grad_act = dot_t(g_branch_two_ref[...], shrink_ref[span, :])
        grad_pre = (grad_act * slope[:, span]).astype(bf16)
        g_pre_ref[:, span] = grad_pre
        g_bias_ref[bias_wide(g_bias_ref, 4, index)] += jnp.sum(grad_pre.astype(f32), axis=0, keepdims=True)
        return carry

    lax.fori_loop(0, MLP_WIDTH // wide, narrow, 0, unroll=True)

    grad = dot_t(g_pre_ref[...], expand_ref[...])
    normal = normal_two[...]
    shift_two = jnp.sum(grad, axis=0, keepdims=True)
    scale_mod_two = jnp.sum(grad * normal, axis=0, keepdims=True)
    grad_middle = hidden[...] + center_back((1.0 + row(4)) * grad, normal, scale_two)
    gate_one = jnp.sum(branch[...] * grad_middle, axis=0, keepdims=True)
    grad_branch = (row(2) * grad_middle).astype(bf16)
    g_branch_ref[...] = grad_branch
    g_bias_ref[1:2, :] += jnp.sum(grad_branch.astype(f32), axis=0, keepdims=True)
    hidden[...] = grad_middle
    g_mixed[...] = dot_t(grad_branch, output_ref[...]).astype(bf16)

    def attend_back(pair, carry):
        query_span, key_span, value_span = pair_spans(pair)
        query = triple[:, query_span]
        keys = triple[:, key_span]
        values = triple[:, value_span]
        grad_mixed = g_mixed[:, query_span]
        results = []
        for side in range(2):
            low_weights = probs[2 * pair + side]
            weights = low_weights.astype(f32)
            grad_weights = dot_t(jnp.where(masks[side], grad_mixed, zero), values)
            grad_values = dot_s(low_weights, grad_mixed)
            grad_scores = weights * (
                grad_weights - jnp.sum(weights * grad_weights, axis=-1, keepdims=True)
            )
            grad_scores = grad_scores.astype(bf16)
            grad_query = dot(grad_scores, keys)
            grad_keys = dot_s(grad_scores, query)
            results.append((grad_query, grad_keys, grad_values))
        for part, span in enumerate((query_span, key_span, value_span)):
            merged = jnp.where(first_half, results[0][part], results[1][part])
            if part < 2:
                merged = merged * rate
            g_triple_ref[:, span] = merged.astype(bf16)
        return carry

    lax.fori_loop(0, HEADS // 2, attend_back, 0, unroll=3)

    grad = dot_t(g_triple_ref[...], attend_ref[...])
    normal = normal_one[...]
    shift_one = jnp.sum(grad, axis=0, keepdims=True)
    scale_mod_one = jnp.sum(grad * normal, axis=0, keepdims=True)
    grad_start = hidden[...] + center_back((1.0 + row(1)) * grad, normal, scale_one)
    grad_start = grad_start.astype(bf16)
    g_patch_ref[...] += dot_s(blended, grad_start)
    g_bias_ref[0:1, :] += jnp.sum(grad_start.astype(f32), axis=0, keepdims=True)
    for index, value in enumerate(
        (shift_one, scale_mod_one, gate_one, shift_two, scale_mod_two, gate_two, shift_f, scale_f)
    ):
        g_mods_ref[0, index : index + 1, :] = value


def layer(numbers, latent, noisy, mods, attention, patch_w, final_w, tail, weights):
    images = latent.shape[0]
    tokens = images * SEQUENCE
    once = pl.Buffered(1)

    def whole(array):
        return pl.BlockSpec(
            array.shape, lambda i: (0,) * len(array.shape), pipeline_mode=once
        )

    def fixed(shape, dtype=f32):
        return pl.BlockSpec(shape, lambda i: (0,) * len(shape)), jax.ShapeDtypeStruct(shape, dtype)

    def per_image(width):
        return (
            pl.BlockSpec((SEQUENCE, width), lambda i: (i, 0)),
            jax.ShapeDtypeStruct((tokens, width), bf16),
        )

    outs = [
        per_image(WIDTH),
        per_image(MLP_WIDTH),
        per_image(WIDTH),
        per_image(MLP_WIDTH),
        per_image(WIDTH),
        per_image(3 * WIDTH),
        (
            pl.BlockSpec((1, 8, WIDTH), lambda i: (i, 0, 0)),
            jax.ShapeDtypeStruct((images, 8, WIDTH), f32),
        ),
        fixed((PATCH, WIDTH)),
        fixed((WIDTH, PATCH)),
        fixed((8, WIDTH)),
    ]
    place = positions(SEQUENCE, WIDTH)
    fixed_args = (place, patch_w, final_w, tail) + tuple(weights)
    flops = 2 * 2 * 7078 * 1000 * tokens
    return pl.pallas_call(
        layer_kernel,
        grid=(images,),
        in_specs=[
            pl.BlockSpec(memory_space=pltpu.SMEM),
            pl.BlockSpec((1, SEQUENCE, PATCH), lambda i: (i, 0, 0)),
            pl.BlockSpec((1, SEQUENCE, PATCH), lambda i: (i, 0, 0)),
            pl.BlockSpec((1, 8, WIDTH), lambda i: (i, 0, 0)),
            pl.BlockSpec((SEQUENCE, 3 * WIDTH), lambda i: (i, 0)),
            pl.BlockSpec((SEQUENCE, WIDTH), lambda i: (i, 0)),
            pl.BlockSpec((HEADS, SEQUENCE, SEQUENCE), lambda i: (i, 0, 0)),
        ]
        + [whole(array) for array in fixed_args],
        out_specs=[spec for spec, _ in outs],
        out_shape=[shape for _, shape in outs],
        scratch_shapes=[
            pltpu.VMEM((SEQUENCE, MLP_WIDTH), f32),
            pltpu.VMEM((SEQUENCE, WIDTH), f32),
            pltpu.VMEM((SEQUENCE, WIDTH), f32),
            pltpu.VMEM((SEQUENCE, WIDTH), f32),
            pltpu.VMEM((SEQUENCE, WIDTH), f32),
            pltpu.VMEM((SEQUENCE, WIDTH), bf16),
        ],
        compiler_params=pltpu.CompilerParams(vmem_limit_bytes=56 * 1024 * 1024),
        cost_estimate=pl.CostEstimate(
            flops=flops, bytes_accessed=60 * 10**6, transcendentals=0
        ),
        name="layer",
    )(numbers, latent, noisy, mods, *attention, *fixed_args)


def local(
    n_wide,
    n_narrow,
    latents,
    noise_field,
    labels,
    label_drop,
    time_steps,
    loss_weights,
    attend_weight,
    attend_first,
    attend_second,
    attend_left,
    attend_right,
    output_weight,
    output_first,
    output_second,
    output_left,
    output_right,
    expand_weight,
    expand_first,
    expand_second,
    expand_left,
    expand_right,
    shrink_weight,
    shrink_first,
    shrink_second,
    shrink_left,
    shrink_right,
    adaptive_weight,
    adaptive_first,
    adaptive_second,
    adaptive_left,
    adaptive_right,
    shared_weight,
    shared_first,
    shared_second,
):
    column = lax.axis_index("narrow")
    images = labels.shape[0] * labels.shape[1]

    moment = (time_steps.reshape(images).astype(f32) + 0.5) / TIMESTEPS
    chosen = jnp.where(label_drop == 1, CLASSES - 1, labels).reshape(images, 1).astype(f32)
    weights_here = loss_weights.reshape(images)
    info = jnp.concatenate(
        [rounded(frequencies(moment, FREQS)).astype(f32), chosen, weights_here[:, None]], axis=1
    )
    info = jnp.pad(info, ((0, 8 - images), (0, SHEET - info.shape[1])))[None]

    shape = (images,) + latents.shape[2:]

    shard = shared_weight.shape[0]
    rows = shard_rows(shard)
    row_start = column * shard // (WIDTH * ALIGN) * ALIGN
    offset = column * shard - row_start * WIDTH
    margin = -(-(ALIGN + 1) * WIDTH // 1024) * 1024
    own = lax.pad(shared_weight, f32(0.0), [(margin, rows * WIDTH - shard, 0)])
    own = lax.dynamic_slice(own, (margin - offset,), (rows * WIDTH,)).reshape(rows, WIDTH)

    (
        *full,
        patch_w,
        final_rows,
        tail,
        time_two,
        sheet,
        time_pre,
        condition,
        own_act,
        adaptive_low,
        mods,
        total,
        lefts,
        rights,
        normed,
        triple,
        mixed,
        probs,
    ) = gather_all(
        n_wide,
        n_narrow,
        images,
        shard,
        (own, attend_weight, output_weight, expand_weight, shrink_weight),
        adaptive_weight,
        info,
        (attend_left, output_left, expand_left, shrink_left, adaptive_left),
        [
            blocks.transpose(1, 2, 0) if blocks.shape[0] > BLOCK else blocks
            for blocks in (attend_right, output_right, expand_right, shrink_right, adaptive_right)
        ],
        (
            moment,
            latents.reshape(shape),
            noise_field.reshape(shape),
            positions(SEQUENCE, WIDTH),
        ),
    )
    lefts = lefts.reshape(8, -1, BLOCK)
    rights = rights.reshape(-1, BLOCK, 4 * BLOCK)
    weight_sum = total[0, 0]

    entries = SEQUENCE * PATCH
    numbers = jnp.stack(
        [moment, 2.0 * weights_here / (entries * weight_sum), weights_here / entries]
    )
    (
        normed_two,
        act,
        g_branch_two,
        g_pre,
        g_branch,
        g_triple,
        g_mods,
        g_patch,
        g_final,
        g_bias,
    ) = layer(
        numbers,
        latents.reshape(shape),
        noise_field.reshape(shape),
        mods,
        (triple, mixed, probs),
        patch_w,
        final_rows.astype(bf16).reshape(WIDTH, PATCH),
        tail,
        full,
    )

    turned, window, totals, clip = reduce_all(
        n_wide,
        n_narrow,
        images,
        shard,
        (normed, mixed, normed_two, act),
        (g_triple, g_branch, g_pre, g_branch_two),
        (
            g_mods.reshape(images * 8, WIDTH),
            g_patch,
            g_final.reshape(PATCH, WIDTH),
            g_bias,
            adaptive_low,
            sheet,
            time_pre,
            condition,
            own_act,
            time_two,
            lefts,
            rights,
        ),
    )
    loss_sum = totals[3, PATCH]
    clip_norm = clip[0, 0]
    factor = clip[1, 0]
    grad_shared = lax.dynamic_slice(window.reshape(-1), (offset,), (shard,))

    results = rotated_update(
        clip,
        turned,
        lefts,
        rights,
        (
            (attend_weight, attend_first, attend_second),
            (output_weight, output_first, output_second),
            (expand_weight, expand_first, expand_second),
            (shrink_weight, shrink_first, shrink_second),
            (adaptive_weight, adaptive_first, adaptive_second),
        ),
    )
    fresh = plain_update(shared_weight, shared_first, shared_second, grad_shared * factor)
    results = [*results, fresh[0], fresh[1], fresh[2], fresh[0].astype(jnp.bfloat16)]
    return tuple(results) + (loss_sum, weight_sum, clip_norm)


def solution(mesh):
    data = P(None, ("wide", "narrow"))
    state = (P("narrow", None),) * 3 + (P("narrow", None, None), P())
    return jax.shard_map(
        partial(local, mesh.shape["wide"], mesh.shape["narrow"]),
        mesh=mesh,
        in_specs=(P(None, ("wide", "narrow"), None, None),) * 2
        + (data,) * 4
        + state * 5
        + (P("narrow"),) * 3,
        out_specs=(P("narrow", None),) * 20 + (P("narrow"),) * 4 + (P(),) * 3,
        check_vma=False,
    )
```

```python
from functools import partial
import math

import jax
import jax.numpy as jnp
import numpy as np
from jax import lax
from jax.experimental import pallas as pl
from jax.experimental.pallas import tpu as pltpu
from jax.sharding import PartitionSpec as P

HEADS = 12
HEAD_DIM = 64
MLP_WIDTH = 3072
CLASSES = 1001
FREQS = 256
PATCH = 16
TIMESTEPS = 1000
BLOCK = 32
STEP_COUNT = 10
WIDTH = 768
SEQUENCE = 256


beta_one = 0.9
beta_two = 0.999
epsilon_adam = 1e-08
learn_rate = 0.03
decay_rate = 0.01
clip_limit = 0.002
highest = lax.Precision.HIGHEST
bf16 = jnp.bfloat16
f32 = jnp.float32

ROW_PATCH = 0
ROW_TIME_ONE = 16
ROW_TIME_TWO = 272
ROW_TABLE = 1040
ROW_FINAL = 2041
ROW_BIAS = 2057


def positions(tokens, width):
    side = math.isqrt(tokens)
    quarter = width // 4
    omega = 1.0 / 10000.0 ** (np.arange(quarter, dtype=np.float64) / quarter)
    place = np.arange(tokens)
    column = (place % side)[:, None] * omega
    row = (place // side)[:, None] * omega
    table = np.concatenate([np.sin(column), np.cos(column), np.sin(row), np.cos(row)], axis=1)
    return jnp.asarray(table.astype(np.float32))


def frequencies(moment, width):
    half = width // 2
    phases = jnp.exp(-math.log(10000.0) * jnp.arange(half, dtype=jnp.float32) / half)
    angles = moment[:, None] * 1000.0 * phases
    return jnp.concatenate([jnp.cos(angles), jnp.sin(angles)], axis=1)


def normalize(hidden):
    centered = hidden - jnp.mean(hidden, axis=-1, keepdims=True)
    return centered * lax.rsqrt(jnp.mean(centered * centered, axis=-1, keepdims=True) + 1e-06)


def modulate(hidden, shift, scale):
    return normalize(hidden) * (1.0 + scale[:, None, :]) + shift[:, None, :]


def adam_direction(first, second):
    return (first * (1.0 / (1.0 - beta_one**STEP_COUNT))) / (
        jnp.sqrt(second * (1.0 / (1.0 - beta_two**STEP_COUNT))) + epsilon_adam
    )


def plain_update(weight, first, second, grad):
    first = beta_one * first + (1.0 - beta_one) * grad
    second = beta_two * second + (1.0 - beta_two) * grad * grad
    weight = weight - learn_rate * (adam_direction(first, second) + decay_rate * weight)
    return (weight, first, second)


def rounded(value):
    return value.astype(jnp.bfloat16)


def product(inputs, weight):
    return jnp.dot(inputs, weight, preferred_element_type=jnp.float32)


def backprod(gradient, weight):
    return jnp.einsum("...n,kn->...k", gradient, weight, preferred_element_type=jnp.float32)


def weight_grad(inputs, gradient):
    flat_in = inputs.reshape(-1, inputs.shape[-1])
    flat_grad = gradient.reshape(-1, gradient.shape[-1])
    return lax.dot_general(
        flat_in, flat_grad, (((0,), (0,)), ((), ())), preferred_element_type=jnp.float32
    )


def bias_grad(gradient):
    return jnp.sum(gradient.astype(jnp.float32).reshape(-1, gradient.shape[-1]), axis=0)


def halves(value):
    high = value.astype(bf16)
    return high, (value - high.astype(f32)).astype(bf16)


def spread_left(blocks):
    size = blocks.shape[0]
    place = lax.broadcasted_iota(jnp.int32, (BLOCK, size), 0)
    column = lax.broadcasted_iota(jnp.int32, (BLOCK, size), 1)
    repeat = (place == column % BLOCK).astype(bf16)
    row_block = lax.broadcasted_iota(jnp.int32, (size, size), 0) // BLOCK
    col_block = lax.broadcasted_iota(jnp.int32, (size, size), 1) // BLOCK
    return tuple(
        jnp.where(
            row_block == col_block, jnp.dot(part, repeat, preferred_element_type=f32), 0.0
        ).astype(bf16)
        for part in halves(blocks)
    )


def spread_right(first, second):
    size = 4 * BLOCK
    row_block = lax.broadcasted_iota(jnp.int32, (size, size), 0) // BLOCK
    col_block = lax.broadcasted_iota(jnp.int32, (size, size), 1) // BLOCK
    inside = row_block == col_block
    corners = [
        jnp.where(inside, jnp.concatenate([row] * 4, axis=0), 0.0) for row in (first, second)
    ]
    empty = jnp.zeros((size, size), f32)
    return jnp.concatenate(
        [
            jnp.concatenate([corners[0], empty], axis=1),
            jnp.concatenate([empty, corners[1]], axis=1),
        ],
        axis=0,
    )


def dot(left, right):
    return jnp.dot(left, right, preferred_element_type=f32)


def dot_t(left, right):
    return lax.dot_general(left, right, (((1,), (1,)), ((), ())), preferred_element_type=f32)


STRIP = 256
TILES = ((3, 1), (1, 1), (4, 1), (1, 4), (8, 1))


def tile_places():
    places = []
    for matrix, (across, down) in enumerate(TILES):
        for number in range(across * down):
            places.append((matrix, number // across, number % across))
    return places


def left_number(tile):
    return (tile + 9) // 12 + (tile + 8) // 12 + (tile + 4) // 12 * (tile - 7)


def adam_kernel(count, *refs):
    factor_ref, turned, lefts, rights = refs[:4]
    states = [refs[4 + 3 * matrix : 7 + 3 * matrix] for matrix in range(5)]
    outs = [refs[19 + 4 * matrix : 23 + 4 * matrix] for matrix in range(5)]
    taken, given, low, take_sem, give_sem = refs[39:]
    rows = taken.shape[2]
    places = tile_places()
    factor = factor_ref[1, 0]

    def window(number):
        _, down, across = places[number]
        return (pl.ds(down * rows, rows), pl.ds(across * WIDTH, WIDTH))

    def takes(number):
        slot = number % 3
        arrays = [ref.at[window(number)] for ref in states[places[number][0]]]
        arrays.append(turned.at[number])
        return [
            pltpu.make_async_copy(array, taken.at[slot, part], take_sem.at[slot, part])
            for part, array in enumerate(arrays)
        ]

    def gives(number):
        slot = number % 2
        arrays = [ref.at[window(number)] for ref in outs[places[number][0]]]
        sources = [given.at[slot, part] for part in range(3)] + [low.at[slot]]
        return [
            pltpu.make_async_copy(source, array, give_sem.at[slot, part])
            for part, (source, array) in enumerate(zip(sources, arrays))
        ]

    def given_out(slot):
        for part in range(4):
            buffer = low.at[slot] if part == 3 else given.at[slot, part]
            pltpu.make_async_copy(buffer, buffer, give_sem.at[slot, part]).wait()

    for number in range(2):
        for copy in takes(number):
            copy.start()

    def body(tile, carry):
        for number in range(2, count):

            @pl.when(tile + 2 == number)
            def _(number=number):
                for copy in takes(number):
                    copy.start()

        slot = tile % 3
        out = tile % 2
        for part in range(4):
            buffer = taken.at[slot, part]
            pltpu.make_async_copy(buffer, buffer, take_sem.at[slot, part]).wait()

        @pl.when(tile >= 2)
        def _():
            given_out(out)

        stack = jnp.where(tile < 12, left_number(jnp.minimum(tile, 11)), 7)
        left = spread_left(lefts[stack])[0]
        for start in range(0, WIDTH, STRIP):
            span = slice(start, start + STRIP)
            group = tile * (WIDTH // BLOCK // 4) + start // BLOCK // 4
            right = spread_right(rights[group], rights[group + 1]).astype(bf16)
            grad = taken[slot, 3, :, span] * factor
            first = beta_one * taken[slot, 1, :, span] + (1.0 - beta_one) * grad
            second = beta_two * taken[slot, 2, :, span] + (1.0 - beta_two) * grad * grad
            given[out, 1, :, span] = first
            given[out, 2, :, span] = second
            step = adam_direction(first, second)
            step = dot_t(step.astype(bf16), right)
            step = dot(left, step.astype(bf16))
            weight = taken[slot, 0, :, span]
            weight = weight - learn_rate * (step + decay_rate * weight)
            given[out, 0, :, span] = weight
            low[out, :, span] = weight.astype(bf16)
        for number in range(count):

            @pl.when(tile == number)
            def _(number=number):
                for copy in gives(number):
                    copy.start()

        return carry

    lax.fori_loop(0, count, body, 0)
    for slot in range(2):
        given_out(slot)


def rotated_update(clip, turned, lefts, rights, states):
    count, rows, _ = turned.shape
    any_space = pl.BlockSpec(memory_space=pl.ANY)
    vmem = pl.BlockSpec(memory_space=pltpu.VMEM)
    shapes = []
    for weight, _, _ in states:
        shapes += [jax.ShapeDtypeStruct(weight.shape, f32)] * 3
        shapes += [jax.ShapeDtypeStruct(weight.shape, bf16)]
    dma = pltpu.SemaphoreType.DMA
    return pl.pallas_call(
        partial(adam_kernel, count),
        in_specs=[pl.BlockSpec(memory_space=pltpu.SMEM), any_space, vmem, vmem]
        + [any_space] * 15,
        out_specs=[any_space] * 20,
        out_shape=shapes,
        scratch_shapes=[
            pltpu.VMEM((3, 4, rows, WIDTH), f32),
            pltpu.VMEM((2, 3, rows, WIDTH), f32),
            pltpu.VMEM((2, rows, WIDTH), bf16),
            dma((3, 4)),
            dma((2, 4)),
        ],
        compiler_params=pltpu.CompilerParams(vmem_limit_bytes=60 * 1024 * 1024),
        name="rotated_adam",
    )(clip, turned, lefts, rights, *[array for state in states for array in state])


def bits_of(extent):
    return extent.bit_length() - 1


def flipped(index, mask, count):
    for bit in range(count):
        if mask >> bit & 1:
            index = index + (1 - 2 * (index // (1 << bit) % 2)) * (1 << bit)
    return index


def greet(n_wide, n_narrow):
    barrier = pltpu.get_barrier_semaphore()
    count = 0
    for axis, extent in (("narrow", n_narrow), ("wide", n_wide)):
        me = lax.axis_index(axis)
        for bit in range(bits_of(extent)):
            pl.semaphore_signal(
                barrier,
                inc=1,
                device_id={axis: flipped(me, 1 << bit, bits_of(extent))},
                device_id_type=pl.DeviceIdType.MESH,
            )
            count = count + 1
    pl.semaphore_wait(barrier, count)


def remote(source, target, send_sem, recv_sem, axis, peer):
    return pltpu.make_async_remote_copy(
        src_ref=source,
        dst_ref=target,
        send_sem=send_sem,
        recv_sem=recv_sem,
        device_id={axis: peer},
        device_id_type=pl.DeviceIdType.MESH,
    )


def slot_of(n_wide, n_narrow):
    here = lax.axis_index("narrow")
    there = lax.axis_index("wide")
    return there // 2 + n_wide // 2 * (here + n_narrow * (there % 2))


def hop_order(n_wide, n_narrow):
    n_bits = bits_of(n_narrow)
    w_bits = bits_of(n_wide)
    places = [("wide", bit, w_bits) for bit in range(1, w_bits)]
    places += [("narrow", bit, n_bits) for bit in range(n_bits)]
    return places + [("wide", 0, w_bits)]


def route(path, step, count):
    return (step + path) % count


ROW_TAIL = 2048
TAIL = 32
ALIGN = 16
SHEET = 384


def shard_rows(shard):
    rows = (shard + WIDTH - 2) // WIDTH + 1 + ALIGN
    return -(-rows // 32) * 32


def shard_start(number, shard):
    return number * shard // WIDTH // ALIGN * ALIGN


def flat_rows(n_narrow, shard):
    last = shard_start(n_narrow - 1, shard) + shard_rows(shard)
    return max(-(-last // ALIGN) * ALIGN, 2112)


def center(hidden):
    centered = hidden - jnp.mean(hidden, axis=-1, keepdims=True)
    scale = lax.rsqrt(jnp.mean(centered * centered, axis=-1, keepdims=True) + 1e-06)
    return centered * scale, scale


def pair_spans(pair):
    return [
        pl.ds(pl.multiple_of(part * WIDTH + pair * 2 * HEAD_DIM, 2 * HEAD_DIM), 2 * HEAD_DIM)
        for part in range(3)
    ]


def head_masks(tokens):
    lane = lax.broadcasted_iota(jnp.int32, (tokens, 2 * HEAD_DIM), 1)
    return lane < HEAD_DIM, lane >= HEAD_DIM


def bases_along_lanes(shape):
    return shape[0] == BLOCK and shape[2] > BLOCK


def silu_slope(value):
    gate = jax.nn.sigmoid(value)
    return gate * (1.0 + value * (1.0 - gate))


def own_columns(value, n_narrow):
    here = lax.axis_index("narrow")
    width = value.shape[1] // n_narrow
    result = value[:, :width]
    for number in range(1, n_narrow):
        result = jnp.where(
            here == number, value[:, number * width : (number + 1) * width], result
        )
    return result


def gather_kernel(n_wide, n_narrow, images, shard, *refs):
    count = 5
    shards = refs[:count]
    adaptive_ref, info_ref = refs[count : count + 2]
    left_refs = refs[count + 2 : count + 7]
    right_refs = refs[count + 7 : count + 12]
    moment_ref, latent_ref, noise_ref, place_ref = refs[count + 12 : count + 16]
    outs = refs[count + 16 : count + 37]
    scratch = refs[count + 37 :]
    (
        patch_out,
        final_out,
        tail_out,
        time_two_out,
        sheet,
        time_pre,
        condition,
        own_act,
        adaptive_low,
        mods_ref,
        total_ref,
        lefts_out,
        rights_out,
        normed_out,
        triple_out,
        mixed_out,
        probs_out,
    ) = outs[4:21]
    gathered = scratch[0]
    wides = scratch[1 : count + 1]
    lows = scratch[count + 1 : 2 * count + 1]
    (
        flat,
        turned,
        attend_full,
        normed,
        triple,
        mixed,
        probs,
        adaptive_wide,
        info_all,
        part,
        part_in,
        load_sem,
        keep_sem,
        send_sem,
        recv_sem,
        core_send,
        core_recv,
        info_sem,
        info_send,
        info_recv,
        part_send,
        part_recv,
        attend_sem,
        image_sem,
        *early,
    ) = scratch[2 * count + 1 :]
    fulls = (gathered, attend_full) + tuple(outs[1:4])
    early_targets = (time_two_out, sheet, time_pre, condition, own_act, adaptive_low, lefts_out, rights_out)
    early_buffers, early_sem = early[:8], early[8]
    (
        time_two_out,
        sheet,
        time_pre,
        condition,
        own_act,
        adaptive_low,
        lefts_out,
        rights_out,
    ) = early_buffers
    early_copies = [
        pltpu.make_async_copy(source, target, early_sem.at[number])
        for number, (source, target) in enumerate(zip(early_buffers, early_targets))
    ]
    here = lax.axis_index("narrow")
    there = lax.axis_index("wide")
    core = there % 2
    n_bits = bits_of(n_narrow)
    w_bits = bits_of(n_wide)
    sibling = flipped(there, 1, w_bits)

    loads = [
        pltpu.make_async_copy(shards[number], wides[number], load_sem.at[number])
        for number in range(count)
    ]
    loads.append(pltpu.make_async_copy(adaptive_ref, adaptive_wide, load_sem.at[count]))
    for load in loads:
        load.start()
    slot = slot_of(n_wide, n_narrow)
    info_own = pltpu.make_async_copy(info_ref, info_all.at[pl.ds(slot, 1)], info_sem)
    info_own.start()
    greet(n_wide, n_narrow)
    sends = []

    def region(number, owner, half, path):
        rows, cols = shards[number].shape
        return (
            pl.ds(pl.multiple_of(owner * rows + half * (rows // 2), 16), rows // 2),
            pl.ds(path * (cols // 2), cols // 2),
        )

    def narrow_step(number, step, own):
        for path in range(2):
            bit = route(path, step, n_bits)
            peer = flipped(here, 1 << bit, n_bits)
            done = sum(1 << route(path, earlier, n_bits) for earlier in range(step))
            for mask in range(n_narrow):
                if mask & ~done or own != (mask == 0):
                    continue
                place = region(number, flipped(here, mask, n_bits), core, path)
                arrives = mask | 1 << bit
                if mask == 0:
                    rows, cols = shards[number].shape
                    source = lows[number].at[
                        pl.ds(pl.multiple_of(core * (rows // 2), 16), rows // 2),
                        pl.ds(path * (cols // 2), cols // 2),
                    ]
                else:
                    source = fulls[number].at[place]
                copy = remote(
                    source,
                    fulls[number].at[place],
                    send_sem.at[number, path, arrives - 1],
                    recv_sem.at[number, path, arrives - 1],
                    "narrow",
                    peer,
                )
                copy.start()
                sends.append(copy)

    def arrive(number, step):
        for path in range(2):
            bit = route(path, step, n_bits)
            done = sum(1 << route(path, earlier, n_bits) for earlier in range(step))
            for mask in range(n_narrow):
                if mask & ~done:
                    continue
                arrived = mask | 1 << bit
                place = region(number, flipped(here, arrived, n_bits), core, path)
                remote(
                    fulls[number].at[place],
                    fulls[number].at[place],
                    send_sem.at[number, path, arrived - 1],
                    recv_sem.at[number, path, arrived - 1],
                    "narrow",
                    flipped(here, 1 << bit, n_bits),
                ).wait_recv()
                copy = remote(
                    fulls[number].at[place],
                    fulls[number].at[place],
                    core_send.at[number, path, arrived - 1],
                    core_recv.at[number, path, arrived - 1],
                    "wide",
                    sibling,
                )
                copy.start()
                sends.append(copy)

    def from_sibling(number):
        for path in range(2):
            for mask in range(1, n_narrow):
                place = region(number, flipped(here, mask, n_bits), 1 - core, path)
                remote(
                    fulls[number].at[place],
                    fulls[number].at[place],
                    core_send.at[number, path, mask - 1],
                    core_recv.at[number, path, mask - 1],
                    "wide",
                    sibling,
                ).wait_recv()

    def cast_rows(source, target):
        def cast(index, carry):
            span = pl.ds(pl.multiple_of(index * 16, 16), 16)
            target[span, :] = source[span, :].astype(bf16)
            return carry

        lax.fori_loop(0, source.shape[0] // 16, cast, 0)

    keeps = []

    def begin(number):
        loads[number].wait()
        rows = shards[number].shape[0]
        cast_rows(wides[number], lows[number])
        keep = pltpu.make_async_copy(
            lows[number],
            fulls[number].at[pl.ds(pl.multiple_of(here * rows, 16), rows)],
            keep_sem.at[number],
        )
        keep.start()
        keeps.append(keep)
        narrow_step(number, 0, True)

    def begin_rest(number):
        for step in range(1, n_bits):
            narrow_step(number, step, True)

    places = hop_order(n_wide, n_narrow)

    def info_copy(position):
        axis, bit, bits = places[position]
        width = 1 << position
        base = slot // width * width
        return remote(
            info_all.at[pl.ds(base, width)],
            info_all.at[pl.ds(base, width)],
            info_send.at[position],
            info_recv.at[position],
            axis,
            flipped(lax.axis_index(axis), 1 << bit, bits),
        )

    def pass_on(numbers, step):
        for number in numbers:
            arrive(number, step)
            if step + 1 < n_bits:
                narrow_step(number, step + 1, False)

    info_own.wait()
    info_copy(0).start()
    begin(0)
    begin_rest(0)
    waiting = [lambda step=step: pass_on([0], step) for step in range(n_bits - 1)]
    waiting += [lambda: (begin(1), begin_rest(1)), lambda: (begin(2), begin_rest(2))]
    waiting += [lambda: begin(3), lambda: begin(4)]
    for position in range(len(places)):
        info_copy(position).wait()
        if position + 1 < len(places):
            info_copy(position + 1).start()
        if waiting:
            waiting.pop(0)()
    for step in waiting:
        step()
    pass_on([0], n_bits - 1)
    from_sibling(0)
    keeps[0].wait()

    height = shards[0].shape[0]
    reached = 0
    for number in range(n_narrow):
        start = shard_start(number, shard)
        overlap = max(reached - start, 0)
        block = number * height
        if overlap:
            flat[start:reached, :] = (
                flat[start:reached, :].astype(f32)
                + gathered[block : block + overlap, :].astype(f32)
            ).astype(bf16)
        flat[start + overlap : start + height, :] = gathered[block + overlap : block + height, :]
        reached = start + height
    if reached < flat.shape[0]:
        flat[reached:, :] = jnp.zeros((flat.shape[0] - reached, WIDTH), bf16)

    devices = n_wide * n_narrow
    for number in range(devices):
        sheet[number * images : (number + 1) * images, :] = info_all[number, :images, :]
    weights = sheet[:, FREQS + 1 : FREQS + 2]
    total_ref[...] = jnp.sum(weights, axis=0, keepdims=True)
    tail = flat[ROW_TAIL : ROW_TAIL + TAIL, :].astype(f32)
    tail_out[...] = tail
    patch_out[...] = flat[ROW_PATCH:ROW_TIME_ONE, :]
    time_two_out[...] = flat[ROW_TIME_TWO:ROW_TABLE, :]
    last = flat[ROW_FINAL - 9 : ROW_FINAL + 23, :].astype(f32)
    final_out[...] = last[9 : 9 + PATCH]
    tail_row = ROW_BIAS - ROW_TAIL
    value = dot(sheet[:, :FREQS].astype(bf16), flat[ROW_TIME_ONE:ROW_TIME_TWO, :])
    value = value + tail[tail_row + 1 : tail_row + 2]
    time_pre[...] = value
    act = jax.nn.silu(value).astype(bf16)
    value = dot(act, flat[ROW_TIME_TWO:ROW_TABLE, :]) + tail[tail_row + 2 : tail_row + 3]
    labels = lax.broadcasted_iota(jnp.int32, (sheet.shape[0], 1008), 1).astype(f32)
    pick = jnp.where(sheet[:, FREQS : FREQS + 1] == labels, 1.0, 0.0).astype(bf16)
    value = value + dot(pick, flat[ROW_TABLE : ROW_TABLE + 1008, :])
    condition[...] = value
    act = own_columns(jax.nn.silu(value), n_narrow)
    act = act.astype(bf16)
    own_act[...] = act

    loads[count].wait()
    cast_rows(adaptive_wide, adaptive_low)
    row = lax.broadcasted_iota(jnp.int32, (8 * n_narrow, act.shape[0]), 0)
    column = lax.broadcasted_iota(jnp.int32, (8 * n_narrow, act.shape[0]), 1)
    owner = there // 2 + n_wide // 2 * (row // 8 + n_narrow * core)
    chosen = column == owner * images + row % images
    near = dot(jnp.where(chosen, 1.0, 0.0).astype(bf16), act).astype(bf16)
    across = images

    def piece(index):
        first = index // across * images
        start = index % across * WIDTH
        return slice(first, first + images), slice(start, start + WIDTH)

    for index in range(8):
        value = dot(near, adaptive_low[:, index * WIDTH : (index + 1) * WIDTH])
        rows_of, span = piece(index)
        for number in range(n_narrow):
            start = 8 * number + rows_of.start
            part[0, number, rows_of, span] = value[start : start + images]

    def lay_bases():
        place = 0
        for ref in left_refs:
            blocks = ref.shape[0]
            lefts_out[place : place + blocks * BLOCK, :] = ref[...].reshape(-1, BLOCK)
            place = place + blocks * BLOCK
        place = 0
        for matrix, ref in enumerate(right_refs):
            turning = bases_along_lanes(ref.shape)
            blocks = ref.shape[2] if turning else ref.shape[0]
            copies = TILES[matrix][1]
            for row in range(BLOCK):
                turned[0:blocks, :] = ref[row].T if turning else ref[:, row, :]
                value = jnp.concatenate(
                    [turned[pl.ds(spot, blocks // 4, stride=4), :] for spot in range(4)], axis=1
                )
                for copy in range(copies):
                    start = place + copy * blocks // 4 * BLOCK + row
                    rights_out[pl.ds(start, blocks // 4, stride=BLOCK), :] = value
            place = place + copies * blocks // 4 * BLOCK

    def part_copy(step, mask):
        bit = 1 << step
        return remote(
            part.at[step, flipped(here, mask, n_bits)],
            part_in.at[step, flipped(here, mask, n_bits)],
            part_send.at[step, mask],
            part_recv.at[step, mask],
            "narrow",
            flipped(here, bit, n_bits),
        )

    def part_back(step, mask):
        bit = 1 << step
        owner = flipped(here, mask - bit, n_bits)
        return remote(
            part_in.at[step, owner],
            part_in.at[step, owner],
            part_send.at[step, mask],
            part_recv.at[step, mask],
            "narrow",
            flipped(here, bit, n_bits),
        ), owner

    for step in range(n_bits):
        bit = 1 << step
        masks = [
            mask for mask in range(n_narrow) if mask & bit and not mask & (bit - 1)
        ]
        for mask in masks:
            copy = part_copy(step, mask)
            copy.start()
            sends.append(copy)
        pass_on([1, 2] if step + 1 < n_bits else [], step)
        for mask in masks:
            back, owner = part_back(step, mask)
            back.wait_recv()
            if step + 1 < n_bits:
                part[step + 1, owner] = part[step, owner] + part_in[step, owner]
            else:
                value = part[step, owner] + part_in[step, owner]
                for index in range(8):
                    rows_of, span = piece(index)
                    for image in range(images):
                        start = rows_of.start + image
                        mods_ref[image, index : index + 1, :] = (
                            value[start : start + 1, span]
                            + tail[tail_row + 9 + index : tail_row + 10 + index]
                        )

    begin_rest(3)
    begin_rest(4)
    for step in range(n_bits - 1):
        pass_on([3, 4], step)
    pass_on([1], n_bits - 1)
    lay_bases()

    for copy in early_copies:
        copy.start()

    from_sibling(1)
    keeps[1].wait()
    attend_out = pltpu.make_async_copy(attend_full, outs[0], attend_sem)
    attend_out.start()
    masks = head_masks(SEQUENCE)
    rate = HEAD_DIM ** (-0.5)

    def image_copies(image):
        slot = image % 2
        tokens = pl.ds(pl.multiple_of(image * SEQUENCE, SEQUENCE), SEQUENCE)
        heads = pl.ds(image * HEADS, HEADS)
        pairs = (
            (normed, normed_out.at[tokens]),
            (triple, triple_out.at[tokens]),
            (mixed, mixed_out.at[tokens]),
            (probs, probs_out.at[heads]),
        )
        return [
            pltpu.make_async_copy(source.at[slot], target, image_sem.at[slot, number])
            for number, (source, target) in enumerate(pairs)
        ]

    def one_image(image, carry):
        slot = image % 2

        @pl.when(image >= 2)
        def _():
            for copy in image_copies(image - 2):
                copy.wait()

        moment = moment_ref[image]
        blended = (1.0 - moment) * latent_ref[image] + moment * noise_ref[image]
        start = dot(blended.astype(bf16), patch_out[...]) + tail_out[tail_row : tail_row + 1, :]
        normal, _ = center(start + place_ref[...])
        shift = mods_ref[image, 0:1, :]
        scale = mods_ref[image, 1:2, :]
        normed[slot] = (normal * (1.0 + scale) + shift).astype(bf16)

        for index in range(3 * WIDTH // STRIP):
            span = slice(index * STRIP, (index + 1) * STRIP)
            triple[slot, :, span] = dot(normed[slot], attend_full[:, span]).astype(bf16)
        for pair in range(HEADS // 2):
            query_span, key_span, value_span = pair_spans(pair)
            query = triple[slot, :, query_span]
            keys = triple[slot, :, key_span]
            values = triple[slot, :, value_span]
            results = []
            for side, mask in enumerate(masks):
                scores = dot_t(jnp.where(mask, query, jnp.zeros((), bf16)), keys) * rate
                scores = jnp.exp(scores - jnp.max(scores, axis=-1, keepdims=True))
                shares = scores * (1.0 / jnp.sum(scores, axis=-1, keepdims=True))
                shares = shares.astype(bf16)
                probs[slot, 2 * pair + side] = shares
                results.append(dot(shares, values))
            mixed[slot, :, query_span] = jnp.where(masks[0], results[0], results[1]).astype(bf16)
        for copy in image_copies(image):
            copy.start()
        return carry

    lax.fori_loop(0, images, one_image, 0)
    pass_on(range(2, count), n_bits - 1)
    for number in range(2, count):
        from_sibling(number)
    for keep in keeps[2:]:
        keep.wait()
    for copy in sends:
        copy.wait_send()
    for image in range(max(images - 2, 0), images):
        for copy in image_copies(image):
            copy.wait()
    attend_out.wait()
    for copy in early_copies:
        copy.wait()


def gather_all(n_wide, n_narrow, images, shard, shards, adaptive, info, lefts, rights, data):
    count = len(shards)
    any_space = pl.BlockSpec(memory_space=pl.ANY)
    vmem = pl.BlockSpec(memory_space=pltpu.VMEM)
    devices = n_wide * n_narrow
    n_bits = bits_of(n_narrow)
    rows = adaptive.shape[0]
    dma = pltpu.SemaphoreType.DMA
    total = devices * images
    early = (3, 4, 5, 6, 7, 8, 11, 12)
    early_shapes = [
        ((WIDTH, WIDTH), bf16),
        ((total, SHEET), f32),
        ((total, WIDTH), f32),
        ((total, WIDTH), f32),
        ((total, rows), bf16),
        (adaptive.shape, bf16),
        ((8 * rows, BLOCK), f32),
        ((len(tile_places()) * 6 * BLOCK, 4 * BLOCK), f32),
    ]
    return pl.pallas_call(
        partial(gather_kernel, n_wide, n_narrow, images, shard),
        in_specs=[any_space] * (count + 2)
        + [vmem] * 10
        + [pl.BlockSpec(memory_space=pltpu.SMEM)]
        + [vmem] * 3,
        out_specs=[any_space] * (count - 1)
        + [any_space if number in early else vmem for number in range(13)]
        + [any_space] * 4,
        out_shape=[
            jax.ShapeDtypeStruct((piece.shape[0] * n_narrow, piece.shape[1]), bf16)
            for piece in shards[1:]
        ]
        + [
            jax.ShapeDtypeStruct((PATCH, WIDTH), bf16),
            jax.ShapeDtypeStruct((PATCH, WIDTH), f32),
            jax.ShapeDtypeStruct((TAIL, WIDTH), f32),
            jax.ShapeDtypeStruct((WIDTH, WIDTH), bf16),
            jax.ShapeDtypeStruct((total, SHEET), f32),
            jax.ShapeDtypeStruct((total, WIDTH), f32),
            jax.ShapeDtypeStruct((total, WIDTH), f32),
            jax.ShapeDtypeStruct((total, rows), bf16),
            jax.ShapeDtypeStruct(adaptive.shape, bf16),
            jax.ShapeDtypeStruct((images, 8, WIDTH), f32),
            jax.ShapeDtypeStruct((1, 1), f32),
            jax.ShapeDtypeStruct((8 * rows, BLOCK), f32),
            jax.ShapeDtypeStruct((len(tile_places()) * 6 * BLOCK, 4 * BLOCK), f32),
            jax.ShapeDtypeStruct((images * SEQUENCE, WIDTH), bf16),
            jax.ShapeDtypeStruct((images * SEQUENCE, 3 * WIDTH), bf16),
            jax.ShapeDtypeStruct((images * SEQUENCE, WIDTH), bf16),
            jax.ShapeDtypeStruct((images * HEADS, SEQUENCE, SEQUENCE), bf16),
        ],
        scratch_shapes=[pltpu.VMEM((shards[0].shape[0] * n_narrow, WIDTH), bf16)]
        + [pltpu.VMEM(piece.shape, f32) for piece in shards]
        + [pltpu.VMEM(piece.shape, bf16) for piece in shards]
        + [
            pltpu.VMEM((flat_rows(n_narrow, shard), WIDTH), bf16),
            pltpu.VMEM((8 * WIDTH // BLOCK, BLOCK), f32),
            pltpu.VMEM((WIDTH, 3 * WIDTH), bf16),
            pltpu.VMEM((2, SEQUENCE, WIDTH), bf16),
            pltpu.VMEM((2, SEQUENCE, 3 * WIDTH), bf16),
            pltpu.VMEM((2, SEQUENCE, WIDTH), bf16),
            pltpu.VMEM((2, HEADS, SEQUENCE, SEQUENCE), bf16),
            pltpu.VMEM(adaptive.shape, f32),
            pltpu.VMEM((devices,) + info.shape[1:], f32),
            pltpu.VMEM((n_bits, n_narrow, 8, images * WIDTH), f32),
            pltpu.VMEM((n_bits, n_narrow, 8, images * WIDTH), f32),
            dma((count + 1,)),
            dma((count,)),
            dma((count, 2, n_narrow - 1)),
            dma((count, 2, n_narrow - 1)),
            dma((count, 2, n_narrow - 1)),
            dma((count, 2, n_narrow - 1)),
            dma,
            dma((bits_of(devices),)),
            dma((bits_of(devices),)),
            dma((n_bits, n_narrow)),
            dma((n_bits, n_narrow)),
            dma,
            dma((2, 4)),
            *[pltpu.VMEM(shape, dtype) for shape, dtype in early_shapes],
            dma((8,)),
        ],
        compiler_params=pltpu.CompilerParams(
            collective_id=0, has_side_effects=True, vmem_limit_bytes=60 * 1024 * 1024
        ),
        name="gather_weights",
    )(*shards, adaptive, info, *lefts, *rights, *data)


RING = 4


def reduce_kernel(n_wide, n_narrow, images, shard, *refs):
    input_refs, gradient_refs = refs[0:4], refs[4:8]
    (
        g_mods_ref,
        g_patch_ref,
        g_final_ref,
        g_bias_ref,
        adaptive_low,
        sheet,
        time_pre,
        condition,
        own_act,
        time_two,
        lefts,
        rights,
    ) = refs[8:20]
    turned_out, rows_out, window_out, totals_out, clip_out = refs[20:25]
    out_ref, pair, act_in, last_in, blocks, to_core = refs[25:31]
    late_inputs = refs[12:20]
    late_buffers = refs[31:39]
    (
        adaptive_low,
        sheet,
        time_pre,
        condition,
        own_act,
        time_two,
        lefts,
        rights,
    ) = late_buffers
    scratch = refs[39:]
    own, from_core, to_near, from_near, to_far, from_far, acc, acc_far = scratch[:8]
    load_sem, core_sem, near_sem, far_sem, back_sem, last_sem = scratch[8:14]
    (
        mods_all,
        by_mod,
        product_parts,
        first_part,
        biases,
        small_first,
        small_out,
        small_in,
        small_all,
        late_sem,
        act_all,
        stage,
        norm_out,
        norm_in,
        squares,
        ring,
        mods_sem,
        mods_near_sem,
        small_sem,
        act_sem,
        rows_sem,
        norm_sem,
        ring_sem,
    ) = scratch[14:]
    here = lax.axis_index("narrow")
    there = lax.axis_index("wide")
    core = there % 2
    n_bits = bits_of(n_narrow)
    w_bits = bits_of(n_wide)
    far_steps = w_bits - 1
    sibling = flipped(there, 1, w_bits)
    chunks, _, half, width = out_ref.shape
    side = width // 2

    leaving = []
    for path in range(2):
        done = 0
        place = 0
        steps = []
        for step in range(n_bits):
            bit = 1 << route(path, step, n_bits)
            masks = [mask for mask in range(n_narrow) if mask & bit and not mask & done]
            steps.append((bit, {mask: place + spot for spot, mask in enumerate(masks)}))
            place = place + len(masks)
            done = done | bit
        leaving.append(steps)

    parts = [(0, half, 0, width)]
    gives = []
    for step in range(far_steps):
        low, rows, left, cols = parts[-1]
        mine = there // (2 << step) % 2
        if rows % 32 == 0:
            keep = (low + mine * (rows // 2), rows // 2, left, cols)
            give = (low + (1 - mine) * (rows // 2), rows // 2, left, cols)
        elif cols % 256 == 0:
            keep = (low, rows, left + mine * (cols // 2), cols // 2)
            give = (low, rows, left + (1 - mine) * (cols // 2), cols // 2)
        else:
            keep = parts[-1]
            give = parts[-1]
        parts.append(keep)
        gives.append(give)
    traded = [gives[step] is not parts[step] for step in range(far_steps)]

    def window(part):
        low, rows, left, cols = part
        if not isinstance(low, int):
            low = pl.multiple_of(low, 16)
        if not isinstance(left, int):
            left = pl.multiple_of(left, 128)
        return (pl.ds(low, rows), pl.ds(left, cols))

    def give_copy(k):
        return remote(
            to_core.at[k % 2],
            from_core.at[k % RING],
            core_sem.at[0, k],
            core_sem.at[1, k],
            "wide",
            sibling,
        )

    products = [(0, 0), (0, 1), (0, 2), (1, 0), (2, 0), (2, 1), (2, 2), (2, 3)]
    lasting = act_in.shape[1]

    def start_pair(k):
        for number, (matrix, across) in enumerate(products):

            @pl.when(k == number)
            def _(number=number, matrix=matrix, across=across):
                slot_of = number % 2
                pltpu.make_async_copy(
                    input_refs[matrix], pair.at[slot_of, 0], load_sem.at[slot_of, 0]
                ).start()
                pltpu.make_async_copy(
                    gradient_refs[matrix].at[:, pl.ds(across * WIDTH, WIDTH)],
                    pair.at[slot_of, 1],
                    load_sem.at[slot_of, 1],
                ).start()

    def act_load(number):
        return pltpu.make_async_copy(
            input_refs[3].at[:, pl.ds(pl.multiple_of(number * lasting, lasting), lasting)],
            act_in,
            load_sem.at[2, 0],
        )

    def last_load():
        return pltpu.make_async_copy(gradient_refs[3], last_in, load_sem.at[2, 1])

    def put_halves(k, owner, span, lower, upper):
        own[k % 2, owner, :, span] = jnp.where(core == 0, lower, upper).astype(f32)
        to_core[k % 2, owner, :, span] = jnp.where(core == 0, upper, lower).astype(bf16)

    def stage_product(k):
        start_pair(k + 1)

        @pl.when(k >= 2)
        def _():
            give_copy(k - 2).wait_send()

        @pl.when(k < len(products))
        def _():
            slot_of = k % 2
            for side_of in range(2):
                buffer = pair.at[slot_of, side_of]
                pltpu.make_async_copy(buffer, buffer, load_sem.at[slot_of, side_of]).wait()
            for start in range(0, WIDTH, STRIP):
                span = slice(start, start + STRIP)
                value = dot_s(pair[slot_of, 0], pair[slot_of, 1, :, span])
                for owner in range(n_narrow):
                    top = owner * 2 * half
                    put_halves(
                        k,
                        owner,
                        span,
                        value[top : top + half],
                        value[top + half : top + 2 * half],
                    )

        @pl.when(k >= len(products))
        def _():
            for owner in range(n_narrow):
                block = owner * 4 + k - len(products)
                put_halves(
                    k,
                    owner,
                    slice(None),
                    blocks[block, 0:half, :].astype(f32),
                    blocks[block, half : 2 * half, :].astype(f32),
                )

        give_copy(k).start()

    def last_product(number):
        act_load(number).wait()
        for start in range(0, WIDTH, STRIP):
            span = slice(start, start + STRIP)
            value = dot_s(act_in[...], last_in[:, span]).astype(bf16)
            for piece in range(n_narrow):
                top = piece * 2 * half
                blocks[number * n_narrow + piece, :, span] = value[top : top + 2 * half]

        @pl.when(number < 3)
        def _():
            act_load(number + 1).start()

    def near_copy(path, k, step):
        bit, masks = leaving[path][step]
        spots = pl.ds(min(masks.values()), len(masks))
        return remote(
            to_near.at[path, k % RING, spots],
            from_near.at[path, k % RING, spots],
            near_sem.at[0, path, k, step],
            near_sem.at[1, path, k, step],
            "narrow",
            flipped(here, bit, n_bits),
        )

    def far_copy(k, step, part):
        return remote(
            to_far.at[(k % RING, step) + window(part)],
            from_far.at[(k % RING, step) + window(part)],
            far_sem.at[0, k, step],
            far_sem.at[1, k, step],
            "wide",
            flipped(there, 2 << step, w_bits),
        )

    def back_copy(k, step, part):
        place = (k, core) + window(part)
        return remote(
            out_ref.at[place],
            out_ref.at[place],
            back_sem.at[0, k, step],
            back_sem.at[1, k, step],
            "wide",
            flipped(there, 2 << step, w_bits),
        )

    def last_copy(k, side_of):
        return remote(
            out_ref.at[k, side_of],
            out_ref.at[k, side_of],
            last_sem.at[0, k],
            last_sem.at[1, k],
            "wide",
            sibling,
        )

    def place_near(path, k, step, mask, total):
        columns = pl.ds(path * side, side)
        ring_slot = k % RING
        if step == n_bits:
            acc_far[ring_slot, :, columns] = total
        elif mask in leaving[path][step][1]:
            to_near[path, ring_slot, leaving[path][step][1][mask]] = total.astype(bf16)
        else:
            acc[ring_slot, mask, :, columns] = total

    def before(k, wait):
        @pl.when(k >= RING)
        def _():
            wait()

    def stage_core(k):
        give_copy(k).wait_recv()
        for path in range(2):
            before(k, lambda path=path: near_copy(path, k - RING, 0).wait_send())
            columns = pl.ds(path * side, side)
            for mask in range(n_narrow):
                owner = flipped(here, mask, n_bits)
                total = own[k % 2, owner, :, columns] + from_core[
                    k % RING, owner, :, columns
                ].astype(f32)
                place_near(path, k, 0, mask, total)
            near_copy(path, k, 0).start()

    def stage_near(step, k):
        ring_slot = k % RING
        for path in range(2):
            columns = pl.ds(path * side, side)
            near_copy(path, k, step).wait_recv()
            if step + 1 < n_bits:
                before(k, lambda path=path: near_copy(path, k - RING, step + 1).wait_send())
            bit, masks = leaving[path][step]
            for mask, spot in masks.items():
                total = acc[ring_slot, mask - bit, :, columns] + from_near[path, ring_slot, spot].astype(f32)
                place_near(path, k, step + 1, mask - bit, total)
            if step + 1 < n_bits:
                near_copy(path, k, step + 1).start()
        if step + 1 == n_bits:
            start_far(0, k)

    def start_far(step, k):
        ring_slot = k % RING
        if step < far_steps:
            place = window(gives[step])
            before(k, lambda: far_copy(k - RING, step, gives[step]).wait_send())
            to_far[(ring_slot, step) + place] = acc_far[(ring_slot,) + place].astype(bf16)
            far_copy(k, step, gives[step]).start()
        else:
            place = window(parts[step])
            out_ref[(k, core) + place] = acc_far[(ring_slot,) + place].astype(bf16)
            start_back(far_steps - 1, k)

    def stage_far(step, k):
        ring_slot = k % RING
        far_copy(k, step, parts[step + 1]).wait_recv()
        place = window(parts[step + 1])
        if traded[step]:
            mine = acc_far[(ring_slot,) + place]
        else:
            mine = to_far[(ring_slot, step) + place].astype(f32)
        acc_far[(ring_slot,) + place] = mine + from_far[(ring_slot, step) + place].astype(f32)
        start_far(step + 1, k)

    def start_back(step, k):
        while step >= 0 and not traded[step]:
            step = step - 1
        if step >= 0:
            back_copy(k, step, parts[step + 1]).start()
        else:
            last_copy(k, core).start()

    def stage_back(step, k):
        back_copy(k, step, gives[step]).wait_recv()
        start_back(step - 1, k)

    def add_squares(value):
        squares[...] += jnp.sum(value * value, axis=0, keepdims=True)

    def turned_copy(slot, tile):
        return pltpu.make_async_copy(ring.at[slot], turned_out.at[tile], ring_sem.at[slot])

    def turn(high, rest, stack, tile, slot, used):
        @pl.when(used)
        def _():
            turned_copy(slot, tile).wait()

        left, left_rest = spread_left(lefts[stack])
        for start in range(0, WIDTH, STRIP):
            span = slice(start, start + STRIP)
            group = tile * (WIDTH // BLOCK // 4) + start // BLOCK // 4
            right, right_rest = halves(spread_right(rights[group], rights[group + 1]))
            value = dot(high[:, span], right) + dot(high[:, span], right_rest)
            if rest is not None:
                value = value + dot(rest[:, span], right)
            part, part_rest = halves(value)
            ring[slot, :, span] = dot_s(left, part) + (
                dot_s(left_rest, part) + dot_s(left, part_rest)
            )
        turned_copy(slot, tile).start()

    def stage_last(k):
        last_copy(k, 1 - core).wait_recv()
        for number in range(2):
            add_squares(out_ref[k, number].astype(f32))
        value = out_ref[k].reshape(2 * half, width)
        turn(value, None, left_number(k), k, k % 2, k >= 2)

    stages = [stage_product, stage_core]
    stages += [partial(stage_near, step) for step in range(n_bits)]
    stages += [partial(stage_far, step) for step in range(far_steps)]
    stages += [partial(stage_back, step) for step in reversed(range(far_steps)) if traded[step]]
    stages += [stage_last]

    places = hop_order(n_wide, n_narrow)
    near_places = [("narrow", bit, n_bits) for bit in range(n_bits)]
    hops = len(places)
    slot = slot_of(n_wide, n_narrow)
    count = n_wide * n_narrow * images

    def beside(axis, bit, bits, source, target, sem, position):
        return remote(
            source,
            target,
            sem.at[0, position],
            sem.at[1, position],
            axis,
            flipped(lax.axis_index(axis), 1 << bit, bits),
        )

    column_bits = n_wide // 2
    half_rows = small_out.shape[1]
    own_rows = pl.ds(pl.multiple_of(half_rows * core, 8), half_rows)
    small_places = places[hops - 1 :] + places[: hops - 1]

    def mods_copy(position):
        width = 1 << position
        block = mods_all.at[pl.ds(slot // width * width, width)]
        return beside(*places[position], block, block, mods_sem, position)

    def mods_near(path, step, mask, arrived):
        owner = flipped(here, arrived if mask is None else mask, n_bits)
        bit = 1 << route(path, step, n_bits)
        block = mods_all.at[
            pl.ds(column_bits * (owner + n_narrow * core), column_bits),
            :,
            pl.ds(path * side, side),
        ]
        return remote(
            block,
            block,
            mods_near_sem.at[0, path, arrived - 1],
            mods_near_sem.at[1, path, arrived - 1],
            "narrow",
            flipped(here, bit, n_bits),
        )

    def near_masks(path, step):
        done = sum(1 << route(path, earlier, n_bits) for earlier in range(step))
        bit = 1 << route(path, step, n_bits)
        return [(mask, mask | bit) for mask in range(n_narrow) if not mask & ~done]

    def small_copy(position):
        if position == 0:
            return beside(
                *small_places[0], small_first.at[0], small_first.at[1], small_sem, position
            )
        if position == hops:
            block = small_all.at[own_rows]
            return beside(*small_places[0], block, block, small_sem, position)
        return beside(
            *small_places[position],
            small_out.at[position],
            small_in.at[position],
            small_sem,
            position,
        )

    def act_copy(position):
        width = 1 << position
        block = act_all.at[pl.ds(here // width * width, width)]
        return beside(*near_places[position], block, block, act_sem, position)

    def small_total():
        return small_all[...]

    def rows_copy(start, rows, position):
        return pltpu.make_async_copy(
            stage.at[pl.ds(0, rows)], rows_out.at[pl.ds(start, rows)], rows_sem.at[position]
        )

    height = window_out.shape[0]

    def window_copies():
        start = here * shard // (WIDTH * ALIGN) * ALIGN
        source = rows_out.at[pl.ds(pl.multiple_of(start, ALIGN), height)]
        return [
            pltpu.make_async_copy(source, stage.at[pl.ds(0, height)], rows_sem.at[2]),
            pltpu.make_async_copy(stage.at[pl.ds(0, height)], window_out, rows_sem.at[3]),
        ]

    def mods_hop(position):
        if position == 0:
            mods_all[slot] = g_mods_ref[...].astype(bf16)
        elif position <= far_steps or position == hops:
            mods_copy(position - 1).wait_recv()
        else:
            step = position - 1 - far_steps
            for path in range(2):
                for _, arrived in near_masks(path, step):
                    mods_near(path, step, None, arrived).wait_recv()
        if position < far_steps or position == hops - 1:
            mods_copy(position).start()
        elif position < hops:
            step = position - far_steps
            for path in range(2):
                for mask, arrived in near_masks(path, step):
                    mods_near(path, step, mask, arrived).start()

    def small_hop(position):
        if position == 0:
            small_first[0, 0:PATCH] = g_patch_ref[...]
            small_first[0, PATCH : 2 * PATCH] = g_final_ref[...]
            small_first[0, 2 * PATCH : 2 * PATCH + 8] = g_bias_ref[...]
            small_first[0, 2 * PATCH + 8 :] = jnp.zeros(
                (small_first.shape[1] - 2 * PATCH - 8, WIDTH), f32
            )
        else:
            small_copy(position - 1).wait_recv()
            if position == 1:
                total = small_first[0, own_rows] + small_first[1, own_rows]
            else:
                total = small_out[position - 1] + small_in[position - 1]
            if position < hops:
                small_out[position] = total
            else:
                small_all[own_rows] = total
        small_copy(position).start()

    def small_end():
        other = pl.ds(pl.multiple_of(half_rows * (1 - core), 8), half_rows)
        block = small_all.at[other]
        beside(*small_places[0], block, block, small_sem, hops).wait_recv()

    def sort_mods():
        together = 8
        size = together * images * 8
        row = lax.broadcasted_iota(jnp.int32, (size, size), 0)
        column = lax.broadcasted_iota(jnp.int32, (size, size), 1)
        span = together * images
        order = jnp.where(column == row % span * 8 + row // span, 1.0, 0.0).astype(bf16)
        for block in range(mods_all.shape[0] // together):
            value = mods_all[block * together : (block + 1) * together].reshape(size, WIDTH)
            value = dot(order, value).astype(bf16)
            for index in range(8):
                by_mod[index, block * span : (block + 1) * span, :] = value[
                    index * span : (index + 1) * span
                ]

    def send_act():
        sort_mods()
        total = jnp.zeros(act_all.shape[1:], f32)
        for index in range(8):
            span = slice(index * WIDTH, (index + 1) * WIDTH)
            total = total + dot_t(by_mod[index], adaptive_low[:, span])
        act_all[here] = total
        act_copy(0).start()

    def act_hop(position):
        act_copy(position - 1).wait_recv()
        if position < n_bits:
            act_copy(position).start()

    def start_rows():
        grad = jnp.concatenate([act_all[number] for number in range(n_narrow)], axis=1)
        grad = grad * silu_slope(condition[...])
        high, rest = halves(grad)
        before = time_pre[...]
        first = (dot_t(high, time_two[...]) * silu_slope(before)).astype(bf16)
        product_parts[0:count] = high
        product_parts[count : 2 * count] = rest
        first_part[...] = first
        biases[0:1, :] = jnp.sum(first.astype(f32), axis=0, keepdims=True)
        biases[1:2, :] = jnp.sum(high.astype(f32), axis=0, keepdims=True)

    def upper_rows():
        stage[0:PATCH, :] = small_total()[0:PATCH]
        stage[ROW_TIME_ONE:ROW_TIME_TWO, :] = dot_s(
            sheet[:, :FREQS].astype(bf16), first_part[...]
        )
        act = jax.nn.silu(time_pre[...]).astype(bf16)
        stage[ROW_TIME_TWO:ROW_TABLE, :] = dot_s(act, product_parts[0:count])
        rows_copy(0, ROW_TABLE, 0).start()

    def table_rows(half_of):
        if half_of == 0:
            rows_copy(0, ROW_TABLE, 0).wait()
        size = 504
        labels = lax.broadcasted_iota(jnp.int32, (count, size), 1) + half_of * size
        pick = jnp.where(sheet[:, FREQS : FREQS + 1] == labels.astype(f32), 1.0, 0.0)
        pick = pick.astype(bf16)
        pick = jnp.concatenate([pick, pick], axis=0)
        stage[half_of * size : (half_of + 1) * size, :] = dot_s(pick, product_parts[...])

    def lower_rows():
        small = small_total()
        base = ROW_FINAL - ROW_TABLE
        stage[base : base + PATCH, :] = small[PATCH : 2 * PATCH]
        base = ROW_BIAS - ROW_TABLE
        bias = small[2 * PATCH : 2 * PATCH + 8]
        stage[base : base + 1, :] = bias[0:1]
        stage[base + 1 : base + 3, :] = biases[0:2, :]
        stage[base + 3 : base + 4, :] = bias[1:2]
        stage[base + 4 : base + 8, :] = bias[4:8]
        stage[base + 8 : base + 9, :] = bias[2:3]
        for index in range(8):
            stage[base + 9 + index : base + 10 + index, :] = jnp.sum(
                by_mod[index].astype(f32), axis=0, keepdims=True
            )
        lane = lax.broadcasted_iota(jnp.int32, (1, WIDTH), 1)
        stage[base + 17 : base + 18, :] = jnp.where(lane < PATCH, bias[3:4], 0.0)
        stage[base + 18 :, :] = jnp.zeros((stage.shape[0] - base - 18, WIDTH), f32)
        totals_out[...] = bias
        rows_copy(ROW_TABLE, stage.shape[0], 1).start()

    first_turn = chunks

    def adaptive_columns(index):
        value = dot_s(own_act[...], by_mod[index])
        add_squares(value)
        high, rest = halves(value)
        turn(high, rest, lefts.shape[0] - 1, first_turn + index, 2 + index % 2, index >= 2)

    def start_window():
        rows_copy(ROW_TABLE, stage.shape[0], 1).wait()
        window_copies()[0].start()

    def window_squares():
        window_copies()[0].wait()
        window_copies()[1].start()
        start = here * shard // (WIDTH * ALIGN) * ALIGN
        first = here * shard - start * WIDTH
        value = stage[0:height, :]
        spot = (
            lax.broadcasted_iota(jnp.int32, value.shape, 0) * WIDTH
            + lax.broadcasted_iota(jnp.int32, value.shape, 1)
        )
        inside = jnp.logical_and(spot >= first, spot < first + shard)
        add_squares(jnp.where(inside, value, 0.0))

    def together(*steps):
        return lambda: [step() for step in steps]

    asides = [
        together(partial(mods_hop, position), partial(small_hop, position))
        for position in range(hops)
    ]
    asides += [together(partial(mods_hop, hops), partial(small_hop, hops), send_act)]
    first_act = len(asides)
    asides += [partial(act_hop, position) for position in range(1, n_bits)]
    asides[-1] = together(asides[-1], small_end)
    asides += [
        together(partial(act_hop, n_bits), start_rows),
        upper_rows,
        partial(table_rows, 0),
        partial(table_rows, 1),
        lower_rows,
        start_window,
        window_squares,
    ]

    squares[...] = jnp.zeros_like(squares)
    greet(n_wide, n_narrow)
    start_pair(jnp.int32(0))
    last_load().start()
    act_load(0).start()
    late_copies = [
        pltpu.make_async_copy(source, target, late_sem.at[number])
        for number, (source, target) in enumerate(zip(late_inputs, late_buffers))
    ]
    for copy in late_copies:
        copy.start()

    def wave(t, carry):
        for number, stage in enumerate(stages):
            k = t - number

            @pl.when(jnp.logical_and(k >= 0, k < chunks))
            def _(stage=stage, k=k):
                stage(k)

        @pl.when(t == 1)
        def _():
            last_load().wait()
            for copy in late_copies:
                copy.wait()

        @pl.when(jnp.logical_and(t % 2 == 1, t < 8))
        def _():
            last_product(t // 2)

        for number, aside in enumerate(asides):

            @pl.when(t == number + 2)
            def _(aside=aside):
                aside()

        index = t - first_act - 2

        @pl.when(jnp.logical_and(index >= 0, index < 8))
        def _():
            adaptive_columns(index)

        return carry

    lax.fori_loop(0, max(chunks + len(stages) - 1, len(asides) + 2, first_act + 8 + 2), wave, 0)

    def finish(k, carry):
        for step in range(far_steps):
            if traded[step]:
                back_copy(k, step, parts[step + 1]).wait_send()
        last_copy(k, core).wait_send()
        return carry

    lax.fori_loop(0, chunks, finish, 0)
    for k in range(chunks - 2, chunks):
        give_copy(k).wait_send()

    def finish_ring(k, carry):
        for path in range(2):
            for step in range(n_bits):
                near_copy(path, k, step).wait_send()
        for step in range(far_steps):
            far_copy(k, step, gives[step]).wait_send()
        return carry

    lax.fori_loop(chunks - RING, chunks, finish_ring, 0)
    for position in [*range(far_steps), hops - 1]:
        mods_copy(position).wait_send()
    for path in range(2):
        for step in range(n_bits):
            for mask, arrived in near_masks(path, step):
                mods_near(path, step, mask, arrived).wait_send()
    for position in range(hops + 1):
        small_copy(position).wait_send()
    for position in range(n_bits):
        act_copy(position).wait_send()
    for slot_of_ring in range(4):
        turned_copy(slot_of_ring, 0).wait()
    window_copies()[1].wait()

    total = jnp.sum(squares[...], axis=1, keepdims=True)
    value = jnp.broadcast_to(total, norm_out.shape[1:])
    for position in range(n_bits):
        norm_out[position] = value
        copy = beside(
            *near_places[position],
            norm_out.at[position],
            norm_in.at[position],
            norm_sem,
            position,
        )
        copy.start()
        copy.wait()
        value = value + norm_in[position]
    norm = jnp.sqrt(value)
    row = lax.broadcasted_iota(jnp.int32, value.shape, 0)
    clip_out[...] = jnp.where(row == 0, norm, clip_limit / jnp.maximum(norm, clip_limit))


def reduce_all(n_wide, n_narrow, images, shard, inputs, gradients, asides):
    rows = WIDTH // n_narrow
    chunks = 12
    tokens = inputs[0].shape[0]
    half = rows // 2
    far = bits_of(n_wide) - 1
    devices = n_wide * n_narrow
    hops = bits_of(devices)
    count = devices * images
    dma = pltpu.SemaphoreType.DMA
    any_space = pl.BlockSpec(memory_space=pl.ANY)
    vmem = pl.BlockSpec(memory_space=pltpu.VMEM)
    height = flat_rows(n_narrow, shard)
    turned, _, window, totals, clip = pl.pallas_call(
        partial(reduce_kernel, n_wide, n_narrow, images, shard),
        in_specs=[any_space] * 8 + [vmem] * 4 + [any_space] * (len(asides) - 4),
        out_specs=[any_space, any_space, any_space, vmem, vmem],
        out_shape=[
            jax.ShapeDtypeStruct((chunks + 8, rows, WIDTH), f32),
            jax.ShapeDtypeStruct((height, WIDTH), f32),
            jax.ShapeDtypeStruct((shard_rows(shard), WIDTH), f32),
            jax.ShapeDtypeStruct((8, WIDTH), f32),
            jax.ShapeDtypeStruct((8, 128), f32),
        ],
        scratch_shapes=[
            pltpu.VMEM((chunks, 2, half, WIDTH), bf16),
            pltpu.VMEM((2, 2, tokens, WIDTH), bf16),
            pltpu.VMEM((tokens, WIDTH), bf16),
            pltpu.VMEM((tokens, WIDTH), bf16),
            pltpu.VMEM((4 * n_narrow, rows, WIDTH), bf16),
            pltpu.VMEM((2, n_narrow, half, WIDTH), bf16),
            *[pltpu.VMEM(array.shape, array.dtype) for array in asides[4:]],
            pltpu.VMEM((2, n_narrow, half, WIDTH), f32),
            pltpu.VMEM((RING, n_narrow, half, WIDTH), bf16),
            pltpu.VMEM((2, RING, n_narrow - 1, half, WIDTH // 2), bf16),
            pltpu.VMEM((2, RING, n_narrow - 1, half, WIDTH // 2), bf16),
            pltpu.VMEM((RING, far, half, WIDTH), bf16),
            pltpu.VMEM((RING, far, half, WIDTH), bf16),
            pltpu.VMEM((RING, n_narrow, half, WIDTH), f32),
            pltpu.VMEM((RING, half, WIDTH), f32),
            dma((3, 2)),
            dma((2, chunks)),
            dma((2, 2, chunks, bits_of(n_narrow))),
            dma((2, chunks, far)),
            dma((2, chunks, far)),
            dma((2, chunks)),
            pltpu.VMEM((devices, images * 8, WIDTH), bf16),
            pltpu.VMEM((8, count, WIDTH), bf16),
            pltpu.VMEM((2 * count, WIDTH), bf16),
            pltpu.VMEM((count, WIDTH), bf16),
            pltpu.VMEM((8, WIDTH), f32),
            pltpu.VMEM((2, 3 * PATCH, WIDTH), f32),
            pltpu.VMEM((hops, 3 * PATCH // 2, WIDTH), f32),
            pltpu.VMEM((hops, 3 * PATCH // 2, WIDTH), f32),
            pltpu.VMEM((3 * PATCH, WIDTH), f32),
            dma((len(asides) - 4,)),
            pltpu.VMEM((n_narrow, count, rows), f32),
            pltpu.VMEM((height - ROW_TABLE, WIDTH), f32),
            pltpu.VMEM((bits_of(n_narrow), 8, 128), f32),
            pltpu.VMEM((bits_of(n_narrow), 8, 128), f32),
            pltpu.VMEM((1, WIDTH), f32),
            pltpu.VMEM((4, rows, WIDTH), f32),
            dma((2, hops)),
            dma((2, 2, n_narrow - 1)),
            dma((2, hops + 1)),
            dma((2, bits_of(n_narrow))),
            dma((4,)),
            dma((2, bits_of(n_narrow))),
            dma((4,)),
        ],
        compiler_params=pltpu.CompilerParams(
            collective_id=1, has_side_effects=True, vmem_limit_bytes=63 * 1024 * 1024
        ),
        cost_estimate=pl.CostEstimate(
            flops=10**8, bytes_accessed=300 * 10**6, transcendentals=0
        ),
        name="reduce_gradients",
    )(*inputs, *gradients, *asides)
    return turned, window, totals, clip


def dot_s(left, right):
    return lax.dot_general(left, right, (((0,), (0,)), ((), ())), preferred_element_type=f32)


def center_back(grad, normal, scale):
    return (
        grad
        - jnp.mean(grad, axis=-1, keepdims=True)
        - normal * jnp.mean(grad * normal, axis=-1, keepdims=True)
    ) * scale


def gelu_pair(value):
    rate = math.sqrt(2.0 / math.pi)
    square = value * value
    bend = jnp.tanh(rate * value * (1.0 + 0.044715 * square))
    half = 0.5 * (1.0 + bend)
    slope = half + 0.5 * value * (1.0 - bend * bend) * (rate * (1.0 + 3.0 * 0.044715 * square))
    return value * half, slope


def layer_kernel(
    numbers,
    latent_ref,
    noise_ref,
    mods_ref,
    triple,
    mixed_ref,
    probs,
    place_ref,
    patch_ref,
    final_ref,
    tail_ref,
    attend_ref,
    output_ref,
    expand_ref,
    shrink_ref,
    normed_two_ref,
    act_ref,
    g_branch_two_ref,
    g_pre_ref,
    g_branch_ref,
    g_triple_ref,
    g_mods_ref,
    g_patch_ref,
    g_final_ref,
    g_bias_ref,
    slope,
    normal_one,
    normal_two,
    hidden,
    branch,
    g_mixed,
):
    image = pl.program_id(0)
    tokens = SEQUENCE
    wide = 256

    def bias(index):
        spot = ROW_BIAS - ROW_TAIL + index
        return tail_ref[spot : spot + 1, :]

    def bias_wide(ref, first, index):
        across = WIDTH // wide
        return (
            pl.ds(first + index // across, 1),
            pl.ds(pl.multiple_of(index % across * wide, wide), wide),
        )

    def row(index):
        return mods_ref[0, index : index + 1, :]

    @pl.when(image == 0)
    def _():
        for ref in (g_patch_ref, g_final_ref, g_bias_ref):
            ref[...] = jnp.zeros_like(ref)

    moment = numbers[0, image]
    blended = ((1.0 - moment) * latent_ref[0] + moment * noise_ref[0]).astype(bf16)
    target = noise_ref[0] - latent_ref[0]
    start = dot(blended, patch_ref[...]) + bias(0) + place_ref[...]
    hidden[...] = start
    normal, scale_one = center(start)
    normal_one[...] = normal
    zero = jnp.zeros((), bf16)
    masks = head_masks(tokens)
    first_half = masks[0]
    rate = HEAD_DIM ** (-0.5)

    value = dot(mixed_ref[...], output_ref[...]) + bias(3)
    branch[...] = value
    value = hidden[...] + row(2) * value
    hidden[...] = value
    normal, scale_two = center(value)
    normal_two[...] = normal
    normed_two_ref[...] = (normal * (1.0 + row(4)) + row(3)).astype(bf16)

    def widen(index, carry):
        span = pl.ds(pl.multiple_of(index * wide, wide), wide)
        before = dot(normed_two_ref[...], expand_ref[:, span])
        before = before + tail_ref[bias_wide(tail_ref, ROW_BIAS - ROW_TAIL + 4, index)]
        after, steep = gelu_pair(before)
        act_ref[:, span] = after.astype(bf16)
        slope[:, span] = steep
        return carry

    lax.fori_loop(0, MLP_WIDTH // wide, widen, 0, unroll=True)

    branch_two = dot(act_ref[...], shrink_ref[...]) + bias(8)
    upper = hidden[...] + row(5) * branch_two
    normal, scale_three = center(upper)
    final = (normal * (1.0 + row(7)) + row(6)).astype(bf16)
    mismatch = dot(final, final_ref[...]) + bias(17)[:, :PATCH] - target
    loss = numbers[2, image] * jnp.sum(mismatch * mismatch)
    grad_out = (numbers[1, image] * mismatch).astype(bf16)

    g_final_ref[...] += dot_s(final, grad_out)
    sums = jnp.sum(grad_out.astype(f32), axis=0, keepdims=True)
    spot = lax.broadcasted_iota(jnp.int32, (1, WIDTH), 1)
    sums = jnp.concatenate([sums, jnp.zeros((1, WIDTH - PATCH), f32)], axis=1)
    g_bias_ref[3:4, :] += jnp.where(spot == PATCH, loss, sums)
    grad = dot_t(grad_out, final_ref[...])
    shift_f = jnp.sum(grad, axis=0, keepdims=True)
    scale_f = jnp.sum(grad * normal, axis=0, keepdims=True)
    grad_upper = center_back((1.0 + row(7)) * grad, normal, scale_three)
    gate_two = jnp.sum(branch_two * grad_upper, axis=0, keepdims=True)
    grad_branch = (row(5) * grad_upper).astype(bf16)
    g_branch_two_ref[...] = grad_branch
    g_bias_ref[2:3, :] += jnp.sum(grad_branch.astype(f32), axis=0, keepdims=True)
    hidden[...] = grad_upper

    def narrow(index, carry):
        span = pl.ds(pl.multiple_of(index * wide, wide), wide)
        grad_act = dot_t(g_branch_two_ref[...], shrink_ref[span, :])
        grad_pre = (grad_act * slope[:, span]).astype(bf16)
        g_pre_ref[:, span] = grad_pre
        g_bias_ref[bias_wide(g_bias_ref, 4, index)] += jnp.sum(grad_pre.astype(f32), axis=0, keepdims=True)
        return carry

    lax.fori_loop(0, MLP_WIDTH // wide, narrow, 0, unroll=True)

    grad = dot_t(g_pre_ref[...], expand_ref[...])
    normal = normal_two[...]
    shift_two = jnp.sum(grad, axis=0, keepdims=True)
    scale_mod_two = jnp.sum(grad * normal, axis=0, keepdims=True)
    grad_middle = hidden[...] + center_back((1.0 + row(4)) * grad, normal, scale_two)
    gate_one = jnp.sum(branch[...] * grad_middle, axis=0, keepdims=True)
    grad_branch = (row(2) * grad_middle).astype(bf16)
    g_branch_ref[...] = grad_branch
    g_bias_ref[1:2, :] += jnp.sum(grad_branch.astype(f32), axis=0, keepdims=True)
    hidden[...] = grad_middle
    g_mixed[...] = dot_t(grad_branch, output_ref[...]).astype(bf16)

    def attend_back(pair, carry):
        query_span, key_span, value_span = pair_spans(pair)
        query = triple[:, query_span]
        keys = triple[:, key_span]
        values = triple[:, value_span]
        grad_mixed = g_mixed[:, query_span]
        results = []
        for side in range(2):
            low_weights = probs[2 * pair + side]
            weights = low_weights.astype(f32)
            grad_weights = dot_t(jnp.where(masks[side], grad_mixed, zero), values)
            grad_values = dot_s(low_weights, grad_mixed)
            grad_scores = weights * (
                grad_weights - jnp.sum(weights * grad_weights, axis=-1, keepdims=True)
            )
            grad_scores = grad_scores.astype(bf16)
            grad_query = dot(grad_scores, keys)
            grad_keys = dot_s(grad_scores, query)
            results.append((grad_query, grad_keys, grad_values))
        for part, span in enumerate((query_span, key_span, value_span)):
            merged = jnp.where(first_half, results[0][part], results[1][part])
            if part < 2:
                merged = merged * rate
            g_triple_ref[:, span] = merged.astype(bf16)
        return carry

    lax.fori_loop(0, HEADS // 2, attend_back, 0, unroll=3)

    grad = dot_t(g_triple_ref[...], attend_ref[...])
    normal = normal_one[...]
    shift_one = jnp.sum(grad, axis=0, keepdims=True)
    scale_mod_one = jnp.sum(grad * normal, axis=0, keepdims=True)
    grad_start = hidden[...] + center_back((1.0 + row(1)) * grad, normal, scale_one)
    grad_start = grad_start.astype(bf16)
    g_patch_ref[...] += dot_s(blended, grad_start)
    g_bias_ref[0:1, :] += jnp.sum(grad_start.astype(f32), axis=0, keepdims=True)
    for index, value in enumerate(
        (shift_one, scale_mod_one, gate_one, shift_two, scale_mod_two, gate_two, shift_f, scale_f)
    ):
        g_mods_ref[0, index : index + 1, :] = value


def layer(numbers, latent, noisy, mods, attention, patch_w, final_w, tail, weights):
    images = latent.shape[0]
    tokens = images * SEQUENCE
    once = pl.Buffered(1)

    def whole(array):
        return pl.BlockSpec(
            array.shape, lambda i: (0,) * len(array.shape), pipeline_mode=once
        )

    def fixed(shape, dtype=f32):
        return pl.BlockSpec(shape, lambda i: (0,) * len(shape)), jax.ShapeDtypeStruct(shape, dtype)

    def per_image(width):
        return (
            pl.BlockSpec((SEQUENCE, width), lambda i: (i, 0)),
            jax.ShapeDtypeStruct((tokens, width), bf16),
        )

    outs = [
        per_image(WIDTH),
        per_image(MLP_WIDTH),
        per_image(WIDTH),
        per_image(MLP_WIDTH),
        per_image(WIDTH),
        per_image(3 * WIDTH),
        (
            pl.BlockSpec((1, 8, WIDTH), lambda i: (i, 0, 0)),
            jax.ShapeDtypeStruct((images, 8, WIDTH), f32),
        ),
        fixed((PATCH, WIDTH)),
        fixed((WIDTH, PATCH)),
        fixed((8, WIDTH)),
    ]
    place = positions(SEQUENCE, WIDTH)
    fixed_args = (place, patch_w, final_w, tail) + tuple(weights)
    flops = 2 * 2 * 7078 * 1000 * tokens
    return pl.pallas_call(
        layer_kernel,
        grid=(images,),
        in_specs=[
            pl.BlockSpec(memory_space=pltpu.SMEM),
            pl.BlockSpec((1, SEQUENCE, PATCH), lambda i: (i, 0, 0)),
            pl.BlockSpec((1, SEQUENCE, PATCH), lambda i: (i, 0, 0)),
            pl.BlockSpec((1, 8, WIDTH), lambda i: (i, 0, 0)),
            pl.BlockSpec((SEQUENCE, 3 * WIDTH), lambda i: (i, 0)),
            pl.BlockSpec((SEQUENCE, WIDTH), lambda i: (i, 0)),
            pl.BlockSpec((HEADS, SEQUENCE, SEQUENCE), lambda i: (i, 0, 0)),
        ]
        + [whole(array) for array in fixed_args],
        out_specs=[spec for spec, _ in outs],
        out_shape=[shape for _, shape in outs],
        scratch_shapes=[
            pltpu.VMEM((SEQUENCE, MLP_WIDTH), f32),
            pltpu.VMEM((SEQUENCE, WIDTH), f32),
            pltpu.VMEM((SEQUENCE, WIDTH), f32),
            pltpu.VMEM((SEQUENCE, WIDTH), f32),
            pltpu.VMEM((SEQUENCE, WIDTH), f32),
            pltpu.VMEM((SEQUENCE, WIDTH), bf16),
        ],
        compiler_params=pltpu.CompilerParams(vmem_limit_bytes=56 * 1024 * 1024),
        cost_estimate=pl.CostEstimate(
            flops=flops, bytes_accessed=60 * 10**6, transcendentals=0
        ),
        name="layer",
    )(numbers, latent, noisy, mods, *attention, *fixed_args)


def local(
    n_wide,
    n_narrow,
    latents,
    noise_field,
    labels,
    label_drop,
    time_steps,
    loss_weights,
    attend_weight,
    attend_first,
    attend_second,
    attend_left,
    attend_right,
    output_weight,
    output_first,
    output_second,
    output_left,
    output_right,
    expand_weight,
    expand_first,
    expand_second,
    expand_left,
    expand_right,
    shrink_weight,
    shrink_first,
    shrink_second,
    shrink_left,
    shrink_right,
    adaptive_weight,
    adaptive_first,
    adaptive_second,
    adaptive_left,
    adaptive_right,
    shared_weight,
    shared_first,
    shared_second,
):
    column = lax.axis_index("narrow")
    images = labels.shape[0] * labels.shape[1]

    moment = (time_steps.reshape(images).astype(f32) + 0.5) / TIMESTEPS
    chosen = jnp.where(label_drop == 1, CLASSES - 1, labels).reshape(images, 1).astype(f32)
    weights_here = loss_weights.reshape(images)
    info = jnp.concatenate(
        [rounded(frequencies(moment, FREQS)).astype(f32), chosen, weights_here[:, None]], axis=1
    )
    info = jnp.pad(info, ((0, 8 - images), (0, SHEET - info.shape[1])))[None]

    shape = (images,) + latents.shape[2:]

    shard = shared_weight.shape[0]
    rows = shard_rows(shard)
    row_start = column * shard // (WIDTH * ALIGN) * ALIGN
    offset = column * shard - row_start * WIDTH
    margin = -(-(ALIGN + 1) * WIDTH // 1024) * 1024
    own = lax.pad(shared_weight, f32(0.0), [(margin, rows * WIDTH - shard, 0)])
    own = lax.dynamic_slice(own, (margin - offset,), (rows * WIDTH,)).reshape(rows, WIDTH)

    (
        *full,
        patch_w,
        final_rows,
        tail,
        time_two,
        sheet,
        time_pre,
        condition,
        own_act,
        adaptive_low,
        mods,
        total,
        lefts,
        rights,
        normed,
        triple,
        mixed,
        probs,
    ) = gather_all(
        n_wide,
        n_narrow,
        images,
        shard,
        (own, attend_weight, output_weight, expand_weight, shrink_weight),
        adaptive_weight,
        info,
        (attend_left, output_left, expand_left, shrink_left, adaptive_left),
        [
            blocks.transpose(1, 2, 0) if blocks.shape[0] > BLOCK else blocks
            for blocks in (attend_right, output_right, expand_right, shrink_right, adaptive_right)
        ],
        (
            moment,
            latents.reshape(shape),
            noise_field.reshape(shape),
            positions(SEQUENCE, WIDTH),
        ),
    )
    lefts = lefts.reshape(8, -1, BLOCK)
    rights = rights.reshape(-1, BLOCK, 4 * BLOCK)
    weight_sum = total[0, 0]

    entries = SEQUENCE * PATCH
    numbers = jnp.stack(
        [moment, 2.0 * weights_here / (entries * weight_sum), weights_here / entries]
    )
    (
        normed_two,
        act,
        g_branch_two,
        g_pre,
        g_branch,
        g_triple,
        g_mods,
        g_patch,
        g_final,
        g_bias,
    ) = layer(
        numbers,
        latents.reshape(shape),
        noise_field.reshape(shape),
        mods,
        (triple, mixed, probs),
        patch_w,
        final_rows.astype(bf16).reshape(WIDTH, PATCH),
        tail,
        full,
    )

    turned, window, totals, clip = reduce_all(
        n_wide,
        n_narrow,
        images,
        shard,
        (normed, mixed, normed_two, act),
        (g_triple, g_branch, g_pre, g_branch_two),
        (
            g_mods.reshape(images * 8, WIDTH),
            g_patch,
            g_final.reshape(PATCH, WIDTH),
            g_bias,
            adaptive_low,
            sheet,
            time_pre,
            condition,
            own_act,
            time_two,
            lefts,
            rights,
        ),
    )
    loss_sum = totals[3, PATCH]
    clip_norm = clip[0, 0]
    factor = clip[1, 0]
    grad_shared = lax.dynamic_slice(window.reshape(-1), (offset,), (shard,))

    results = rotated_update(
        clip,
        turned,
        lefts,
        rights,
        (
            (attend_weight, attend_first, attend_second),
            (output_weight, output_first, output_second),
            (expand_weight, expand_first, expand_second),
            (shrink_weight, shrink_first, shrink_second),
            (adaptive_weight, adaptive_first, adaptive_second),
        ),
    )
    fresh = plain_update(shared_weight, shared_first, shared_second, grad_shared * factor)
    results = [*results, fresh[0], fresh[1], fresh[2], fresh[0].astype(jnp.bfloat16)]
    return tuple(results) + (loss_sum, weight_sum, clip_norm)


def solution(mesh):
    data = P(None, ("wide", "narrow"))
    state = (P("narrow", None),) * 3 + (P("narrow", None, None), P())
    return jax.shard_map(
        partial(local, mesh.shape["wide"], mesh.shape["narrow"]),
        mesh=mesh,
        in_specs=(P(None, ("wide", "narrow"), None, None),) * 2
        + (data,) * 4
        + state * 5
        + (P("narrow"),) * 3,
        out_specs=(P("narrow", None),) * 20 + (P("narrow"),) * 4 + (P(),) * 3,
        check_vma=False,
    )
```
